32 devices in a mesh: areal: 8 (over y, x, core), layer: 4 (over z).
Axes of the slice: x: 2, y: 2, z: 4, core: 2. Of those that a mesh axis runs over, the one named last changes fastest.
Arguments:
- pressure: float32 [8, 256, 1024], P(None, 'areal', 'layer'), may hold values from 0.7 to 1.4
- composition: float32 [9, 8, 256, 1024], P(None, None, 'areal', 'layer'), may hold values from 0.02 to 1
- mass_old: float32 [9, 8, 256, 1024], P(None, None, 'areal', 'layer'), may hold values from 0 to 0.3
- pore_volume: float32 [8, 256, 1024], P(None, 'areal', 'layer'), may hold values from 0.5 to 2
- trans_x: float32 [8, 256, 1024], P(None, 'areal', 'layer'), may hold values from 0.3 to 3
- trans_y: float32 [8, 256, 1024], P(None, 'areal', 'layer'), may hold values from 0.3 to 3
- trans_z: float32 [8, 256, 1024], P(None, 'areal', 'layer'), may hold values from 0.3 to 3
- volatility: float32 [9], replicated, may hold values from 1.5 to 3
- pressure_slope: float32 [9], replicated, may hold values from 0.2 to 1
- mixing: float32 [9, 9], replicated, may hold values from -3.5 to 3.5
- two_phase: int32 [4, 64], P(None, 'areal'), may hold values from 0 to 1, as said below
Outputs:
- residual: float32 [9, 8, 256, 1024], P(None, None, 'areal', 'layer')
- new_pressure: float32 [8, 256, 1024], P(None, 'areal', 'layer')
The draws below stay inside these ranges and needn't reach their ends.
Inputs may be any that keep to these rules, and one draw needn't show every extreme that they name: `two_phase`: for each areal index, the 4 rows together flag exactly 16 of their bricks of that areal index, and one of the rows flags all of its 8 bricks of that areal index.
All inputs are finite; a program needn't handle non-finite values.
Results may differ from the reference program's by a relative error of at most 0.0003.
Values sent between devices are 32-bit elements; how exact they have to be, the bound alone decides.
No kernel may reach another device: no remote copies, remote signals or barrier semaphores. Data moves between devices by JAX's collectives and lax.ppermute only.
A program may use at most 128 MiB of HBM per device.

```python
import math
import jax
import jax.numpy as jnp
from jax import lax

NCOMP = 9
NZ = 8
BX = 4
CY = 256
BRICKS = 8
SS_ITERS = 3
RR_ITERS = 3
NX = 256
NY = 1024
XBRICKS = 64
N_LAYER = 4


def draw_two_phase(key, part):
    groups = XBRICKS // BRICKS
    spare_units = (N_LAYER - 2) * (BRICKS // 2)
    key_heavy = jax.random.fold_in(key, 11)
    key_units = jax.random.fold_in(key, 23)
    key_scores = jax.random.fold_in(key, 37)
    heavy_device = jax.random.randint(key_heavy, (groups,), 0, N_LAYER)
    picked_units = jax.random.randint(key_units, (groups, spare_units), 0, N_LAYER - 1)
    target = (heavy_device[:, None] + 1 + picked_units) % N_LAYER
    counts = jnp.sum((target[:, :, None] == jnp.arange(N_LAYER)[None, None, :]).astype(jnp.int32), axis=1)
    counts = jnp.where(jnp.arange(N_LAYER)[None, :] == heavy_device[:, None], BRICKS, counts)
    scores = jax.random.randint(key_scores, (groups, N_LAYER, BRICKS), 0, 1 << 20) * BRICKS + jnp.arange(BRICKS)[None, None, :]
    ranking = jnp.argsort(jnp.argsort(scores, axis=-1), axis=-1)
    flagged = (ranking < counts[:, :, None]).astype(jnp.int32)
    return jnp.transpose(flagged, (1, 0, 2)).reshape(N_LAYER, groups * BRICKS)


def steps_of(key, shape, shards, low, largest):
    factor_of, own = 1.0, jax.random.fold_in(key, 6)
    for position, shards_of in shards:
        heights = jnp.exp(jax.random.uniform(jax.random.fold_in(own, position), (shards_of,), jnp.float32, low / len(shards), largest / len(shards)))
        factor_of = factor_of * jnp.repeat(heights, shape[position] // shards_of).reshape([-1 if axis == position else 1 for axis in range(len(shape))])
    return factor_of


def normal_values(rng, extent, deviation, most, held_as=jnp.bfloat16):
    entries = jax.random.normal(rng, extent, jnp.float32) * deviation
    return jnp.minimum(jnp.maximum(entries, -most), most).astype(held_as)


def setup_inputs(seed: int = 0) -> dict:
    key_list = jax.random.split(jax.random.key(seed), 12)
    return {
        "pressure": jnp.clip(0.7 + 0.7 * jax.random.uniform(key_list[0], (NZ, NX, NY), jnp.float32) ** steps_of(key_list[0], (NZ, NX, NY), ((1, 8), (2, 4)), -0.2, 0.2), 0.7, 1.4),
        "composition": jnp.clip(jnp.exp(math.log(1.0) - 3.912023 * jax.random.uniform(key_list[1], (NCOMP, NZ, NX, NY), jnp.float32) ** steps_of(key_list[1], (NCOMP, NZ, NX, NY), ((2, 8), (3, 4)), -0.2, 0.2)), 0.02, 1.0),
        "mass_old": jnp.clip(0.3 * jax.random.uniform(key_list[2], (NCOMP, NZ, NX, NY), jnp.float32) ** steps_of(key_list[2], (NCOMP, NZ, NX, NY), ((2, 8), (3, 4)), -0.2, 0.2), 0.0, 0.3),
        "pore_volume": jnp.clip(jnp.exp(math.log(2.0) - 1.3862944 * jax.random.uniform(key_list[3], (NZ, NX, NY), jnp.float32) ** steps_of(key_list[3], (NZ, NX, NY), ((1, 8), (2, 4)), -0.2, 0.2)), 0.5, 2.0),
        "trans_x": jnp.clip(jnp.exp(math.log(3.0) - 2.3025851 * jax.random.uniform(key_list[4], (NZ, NX, NY), jnp.float32) ** steps_of(key_list[4], (NZ, NX, NY), ((1, 8), (2, 4)), -0.2, 0.2)), 0.3, 3.0),
        "trans_y": jnp.clip(jnp.exp(math.log(3.0) - 2.3025851 * jax.random.uniform(key_list[5], (NZ, NX, NY), jnp.float32) ** steps_of(key_list[5], (NZ, NX, NY), ((1, 8), (2, 4)), -0.2, 0.2)), 0.3, 3.0),
        "trans_z": jnp.clip(jnp.exp(math.log(3.0) - 2.3025851 * jax.random.uniform(key_list[6], (NZ, NX, NY), jnp.float32) ** steps_of(key_list[6], (NZ, NX, NY), ((1, 8), (2, 4)), -0.2, 0.2)), 0.3, 3.0),
        "volatility": jnp.clip(jax.random.uniform(key_list[7], (NCOMP,), jnp.float32, 1.5, 3.0), 1.5, 3.0),
        "pressure_slope": jnp.clip(jax.random.uniform(key_list[8], (NCOMP,), jnp.float32, 0.2, 1.0), 0.2, 1.0),
        "mixing": normal_values(key_list[9], (NCOMP, NCOMP), 3 ** -0.5, 3.5, jnp.float32),
        "two_phase": draw_two_phase(jax.random.fold_in(key_list[11], 71), 0),
    }


light_count = 4
liquid_visc = 1.0
vapour_visc = 0.25
time_step = 4.0
compress = 0.2


def flash(pressure, feed, volatility, pressure_slope, mixing):
    expand = (-1,) + (1,) * pressure.ndim
    component_sign = jnp.where(jnp.arange(feed.shape[0]) < light_count, 1.0, -1.0).astype(jnp.float32)
    base_log = (component_sign * volatility).reshape(expand) - pressure_slope.reshape(expand) * jnp.log(pressure)[None]
    liquid = feed
    vapour = feed
    fraction = jnp.zeros(pressure.shape, jnp.float32)
    for outer_step in range(SS_ITERS):
        log_ratio = base_log + jnp.tanh(jnp.tensordot(mixing, liquid - vapour, axes=1, precision=lax.Precision.HIGHEST))
        k_value = jnp.exp(log_ratio)
        excess = k_value - 1.0
        fraction = jnp.full(pressure.shape, 0.5, jnp.float32)
        for inner_step in range(RR_ITERS):
            scaled = excess / (1.0 + fraction[None] * excess)
            mismatch = jnp.sum(feed * scaled, axis=0)
            gradient = jnp.sum(feed * scaled * scaled, axis=0)
            fraction = jnp.clip(fraction + mismatch / gradient, 0.0, 1.0)
        liquid = feed / (1.0 + fraction[None] * excess)
        vapour = k_value * liquid
    return ((1.0 - fraction) ** 2 / liquid_visc) * liquid + (fraction ** 2 / vapour_visc) * vapour


def neighbours(field):
    centre = field[..., 1:-1, 1:-1, 1:-1]
    beside = [field[..., 2:, 1:-1, 1:-1], field[..., :-2, 1:-1, 1:-1],
              field[..., 1:-1, 2:, 1:-1], field[..., 1:-1, :-2, 1:-1],
              field[..., 1:-1, 1:-1, 2:], field[..., 1:-1, 1:-1, :-2]]
    return centre, beside


def assemble(pressure, mobility, trans_z, trans_x, trans_y):
    press_here, press_near = neighbours(pressure)
    mobility_here, mobility_near = neighbours(mobility)
    total_here = jnp.sum(mobility_here, axis=0)
    depth_faces = neighbours(trans_z)
    first_faces = neighbours(trans_x)
    second_faces = neighbours(trans_y)
    faces = [depth_faces[0], depth_faces[1][1], first_faces[0], first_faces[1][3], second_faces[0], second_faces[1][5]]
    flux = jnp.zeros(mobility_here.shape, jnp.float32)
    couplings = []
    for face_index in range(6):
        strength = time_step * faces[face_index]
        flux = flux + strength * (press_here - press_near[face_index]) * (0.5 * (mobility_here + mobility_near[face_index]))
        couplings.append(strength * (0.5 * (total_here + jnp.sum(mobility_near[face_index], axis=0))))
    return flux, couplings


def reference(pressure, composition, mass_old, pore_volume, trans_x, trans_y, trans_z, volatility, pressure_slope, mixing, two_phase):
    feed_norm = composition / jnp.sum(composition, axis=0, keepdims=True)

    def flash_level(pieces):
        return flash(pieces[0], pieces[1], volatility, pressure_slope, mixing)

    two_mobility = lax.map(flash_level, (pressure, jnp.moveaxis(feed_norm, 1, 0)))
    two_mobility = jnp.moveaxis(two_mobility, 0, 1)
    cell_flags = jnp.transpose(jnp.repeat(jnp.repeat(two_phase, CY, axis=0), BX, axis=1))
    mobility = jnp.where(cell_flags[None, None, :, :] > 0, two_mobility, feed_norm / liquid_visc)
    keep_x = jnp.where(jnp.arange(NX)[None, :, None] < NX - 1, trans_x, 0.0)
    keep_y = jnp.where(jnp.arange(NY)[None, None, :] < NY - 1, trans_y, 0.0)
    keep_z = jnp.where(jnp.arange(NZ)[:, None, None] < NZ - 1, trans_z, 0.0)
    flux, couplings = assemble(jnp.pad(pressure, 1), jnp.pad(mobility, ((0, 0), (1, 1), (1, 1), (1, 1))),
                               jnp.pad(keep_z, 1), jnp.pad(keep_x, 1), jnp.pad(keep_y, 1))
    residual = pore_volume * feed_norm - mass_old + flux
    total = jnp.sum(residual, axis=0)
    diagonal = pore_volume * compress
    for face_index in range(6):
        diagonal = diagonal + couplings[face_index]
    first = -total / diagonal
    near = neighbours(jnp.pad(first, 1))[1]
    gathered = -total
    for face_index in range(6):
        gathered = gathered + couplings[face_index] * near[face_index]
    second = gathered / diagonal
    return residual, pressure + second
```

```python
import jax
import jax.numpy as jnp
from jax import lax
from jax.experimental import pallas as pl
from jax.experimental.pallas import tpu as pltpu
from jax.sharding import PartitionSpec as P

SS_ITERS = 3
RR_ITERS = 3
LIGHT = 4
COMPS = 9
FIELDS = 16
PRESS, TX, TY, TZ, PORE, MASS, FLAG = range(COMPS, FIELDS)
TIME_STEP = 4.0
COMPRESS = 0.2
VAPOUR_WEIGHT = 1.0 / 0.25
LANES = 128
ROWS = 8
VMEM_LIMIT = 48 * 1024 * 1024


def rcp(x):
    return pltpu.reciprocal(x, approx=True)


def total_of(terms):
    terms = list(terms)
    while len(terms) > 1:
        terms = [a + b for a, b in zip(terms[::2], terms[1::2])] + (
            [terms[-1]] if len(terms) % 2 else []
        )
    return terms[0]


def flash(feed, pressure, signed, slope, mixing):
    log_press = jnp.log(pressure)
    base = [signed[i] - slope[i] * log_press for i in range(COMPS)]
    spread = None
    for outer in range(SS_ITERS):
        if outer == 0:
            log_k = base
        else:
            log_k = [
                base[i] - jnp.tanh(total_of(mixing(i, j) * spread[j] for j in range(COMPS)))
                for i in range(COMPS)
            ]
        w = [rcp(jnp.exp(log_k[i]) - 1.0) for i in range(COMPS)]
        fraction = jnp.full(pressure.shape, 0.5, jnp.float32)
        for _ in range(RR_ITERS):
            q = [rcp(w[i] + fraction) for i in range(COMPS)]
            part = [feed[i] * q[i] for i in range(COMPS)]
            mismatch = total_of(part)
            gradient = total_of(part[i] * q[i] for i in range(COMPS))
            fraction = jnp.clip(fraction + mismatch * rcp(gradient), 0.0, 1.0)
        spread = [feed[i] * rcp(w[i] + fraction) for i in range(COMPS)]
    liquid_part = (1.0 - fraction) * (1.0 - fraction)
    vapour_part = VAPOUR_WEIGHT * (fraction * fraction)
    both = liquid_part + vapour_part
    return [spread[i] * (both * w[i] + vapour_part) for i in range(COMPS)]


def parameters(vol_ref, slope_ref, mix_ref):
    signed = [vol_ref[i] if i < LIGHT else -vol_ref[i] for i in range(COMPS)]
    slope = [slope_ref[i] for i in range(COMPS)]
    return signed, slope, lambda i, j: mix_ref[i, j]


def lane_of(shape):
    return lax.broadcasted_iota(jnp.int32, shape, len(shape) - 1)


def row_of(shape):
    return lax.broadcasted_iota(jnp.int32, shape, len(shape) - 2)


def field_plane(index, comp, press, tx, ty, tz, pore, mass):
    if index < COMPS:
        return comp[index, 0]
    if index == MASS:
        return total_of(mass[i, 0] for i in range(COMPS))
    return {PRESS: press, TX: tx, TY: ty, TZ: tz, PORE: pore}[index][0]


def pack_columns(flags, comp, press, tx, ty, tz, pore, mass, low_ref, high_ref):
    z = pl.program_id(0)
    layer = lax.axis_index("layer")
    rows = low_ref.shape[0]
    shape = (rows, LANES)
    lane = lane_of(shape)
    brick = rows // flags.shape[1]
    row = row_of(shape)
    flag = jnp.zeros(shape, jnp.float32)
    for b in range(flags.shape[1]):
        flag = jnp.where(row // brick == b, flags[layer, b].astype(jnp.float32), flag)

    @pl.when(z == 0)
    def _():
        low_ref[...] = jnp.zeros(low_ref.shape, jnp.float32)
        high_ref[...] = jnp.zeros(high_ref.shape, jnp.float32)

    for tile in range(FIELDS // 4):
        low = jnp.zeros(shape, jnp.float32)
        high = jnp.zeros(shape, jnp.float32)
        for quarter in range(4):
            index = 4 * tile + quarter
            if index == FLAG:
                first, last = flag, flag
            else:
                plane = field_plane(index, comp, press, tx, ty, tz, pore, mass)
                first, last = plane[:, :LANES], plane[:, -LANES:]
            at = 32 * quarter
            low = jnp.where((lane >= at + 2) & (lane < at + 4), pltpu.roll(first, at + 2, 1), low)
            high = jnp.where((lane >= at) & (lane < at + 2), pltpu.roll(last, (at + 2) % LANES, 1), high)
        span = pl.ds(tile * LANES, LANES)
        low_ref[:, span] += pltpu.roll(low, 4 * z, 1)
        high_ref[:, span] += pltpu.roll(high, 4 * z, 1)


def pack_rows(flags, *refs):
    low_in, high_in = refs[:7], refs[7:14]
    left, right, low_ref, high_ref = refs[14:]
    step = pl.program_id(0)
    layer = lax.axis_index("layer")
    bricks = flags.shape[1]
    shape = (ROWS, low_ref.shape[2])
    row = row_of(shape)

    def plane(refs_of, z, index, flag):
        comp, press, tx, ty, tz, pore, mass = refs_of
        if index < COMPS:
            return comp[index, z]
        if index == MASS:
            return total_of(mass[i, z] for i in range(COMPS))
        if index == FLAG:
            return jnp.full(shape, flag, jnp.float32)
        return {PRESS: press, TX: tx, TY: ty, TZ: tz, PORE: pore}[index][z]

    low_flag = flags[layer, 0].astype(jnp.float32)
    high_flag = flags[layer, bricks - 1].astype(jnp.float32)
    half = FIELDS // 2
    for k in range(half):
        low, high = None, None
        for z in range(2):
            near = jnp.where(
                row % 4 >= 2,
                pltpu.roll(plane(low_in, z, k, low_flag), 2, 0),
                plane(low_in, z, k + half, low_flag),
            )
            far = jnp.where(
                row % 4 < 2,
                pltpu.roll(plane(high_in, z, k, high_flag), 2, 0),
                pltpu.roll(plane(high_in, z, k + half, high_flag), 4, 0),
            )
            if z == 0:
                low, high = near, far
            else:
                low = jnp.where(row < 4, low, pltpu.roll(near, 4, 0))
                high = jnp.where(row < 4, high, pltpu.roll(far, 4, 0))
        low_ref[k] = low
        high_ref[k] = high
    rows = left.shape[0]
    width = shape[1]
    for part in range(2):
        @pl.when(step == part)
        def _():
            span = pl.ds(part * width, width)
            low_ref[half] = left[pl.ds(0, ROWS), span] + right[pl.ds(0, ROWS), span]
            high_ref[half] = left[pl.ds(rows - ROWS, ROWS), span] + right[pl.ds(rows - ROWS, ROWS), span]

    @pl.when(step >= 2)
    def _():
        low_ref[half] = jnp.zeros(shape, jnp.float32)
        high_ref[half] = jnp.zeros(shape, jnp.float32)


def own_cells(flags, vol, slope, mix, comp, press, pore, mass, *rest):
    mob_ref, acc_ref, mob_sum, acc_sum = rest[-4:]
    layer = lax.axis_index("layer")
    signed, slopes, mixing = parameters(vol, slope, mix)
    rows, width = press.shape[1:]
    bricks = flags.shape[1]
    brick = rows // bricks
    shape = (ROWS, width)
    per_tile = ROWS // brick

    def tile(t, carry):
        at = pl.ds(pl.multiple_of(t * ROWS, ROWS), ROWS)
        raw = [comp[i, 0, at, :] for i in range(COMPS)]
        inverse = rcp(total_of(raw))
        feed = [raw[i] * inverse for i in range(COMPS)]
        volume = pore[0, at, :]
        acc = [volume * feed[i] - mass[i, 0, at, :] for i in range(COMPS)]
        for i in range(COMPS):
            acc_ref[i, 0, at, :] = acc[i]
        acc_sum[0, at, :] = total_of(acc)
        tile_flags = [flags[layer, t * per_tile + b] for b in range(per_tile)]
        some = tile_flags[0]
        for flag in tile_flags[1:]:
            some = some + flag

        @pl.when(some > 0)
        def _():
            row = row_of(shape)
            marked = jnp.zeros(shape, jnp.int32)
            for b in range(per_tile):
                marked = jnp.where(row // brick == b, tile_flags[b], marked)
            two = flash(feed, press[0, at, :], signed, slopes, mixing)
            mobility = [jnp.where(marked > 0, two[i], feed[i]) for i in range(COMPS)]
            for i in range(COMPS):
                mob_ref[i, 0, at, :] = mobility[i]
            mob_sum[0, at, :] = total_of(mobility)

        @pl.when(some == 0)
        def _():
            for i in range(COMPS):
                mob_ref[i, 0, at, :] = feed[i]
            mob_sum[0, at, :] = total_of(feed)

        return carry

    lax.fori_loop(0, rows // ROWS, tile, 0)


def finish(
    flags, vol, slope, mix,
    left, right, above, below,
    press, tx, ty, tz, pore, mob_sum, acc_sum, mob, acc,
    res_ref, new_ref,
    raw, mob_h, e_press, e_tx, e_ty, e_tz, e_pore, e_mob, e_acc,
    g_x, g_y, g_z, c_x, c_y, c_z, first,
):
    z_now = pl.program_id(0)
    depth, rows, width = press.shape
    layer, layers = lax.axis_index("layer"), lax.axis_size("layer")
    areal, areals = lax.axis_index("areal"), lax.axis_size("areal")
    half = FIELDS // 2
    tall, wide = rows + ROWS, width + LANES
    halo_rows = raw.shape[1]
    y_at = rows * (width // LANES)

    def x_tile(ref, lead, z):
        parts = []
        for g in range(width // LANES):
            at = pl.multiple_of(g * rows + (z // 2) * ROWS, ROWS)
            parts.append(ref[lead, pl.ds(at, ROWS), :])
        tile = jnp.concatenate(parts, axis=1)
        return pltpu.roll(tile, 6 - 4 * (z % 2), 0)

    def y_tile(ref, lead, z, count):
        return pltpu.roll(ref[lead, pl.ds(y_at, count), :], 126 - 4 * z, 1)

    @pl.when(z_now == 0)
    def _():
        shape = (rows, width)
        upper = row_of(shape) % 4 < 2
        for k in range(half):
            up, down = above[k], below[k]
            near = jnp.where(upper, up, down)
            far = jnp.where(upper, pltpu.roll(up, rows - 2, 0), pltpu.roll(down, 2, 0))
            for g in range(width // LANES):
                span = slice(g * LANES, (g + 1) * LANES)
                raw[k, pl.ds(g * rows, rows), :] = near[:, span]
                raw[k + half, pl.ds(g * rows, rows), :] = far[:, span]
        corner_row = row_of((ROWS, LANES))
        for tile in range(FIELDS // 4):
            span = slice(tile * LANES, (tile + 1) * LANES)
            columns = left[:, span] + right[:, span]
            part, within = (tile * LANES) // width, (tile * LANES) % width
            from_up = above[half, pl.ds(part * ROWS, ROWS), :][:, within : within + LANES]
            from_down = below[half, pl.ds(part * ROWS, ROWS), :][:, within : within + LANES]
            corner = jnp.where(corner_row < 4, from_down, from_up)
            for quarter in range(4):
                k = 4 * tile + quarter
                turn = (LANES - 32 * quarter) % LANES
                raw[k, pl.ds(y_at, rows), :] = pltpu.roll(columns, turn, 1) if turn else columns
                raw[k, pl.ds(y_at + rows, ROWS), :] = pltpu.roll(corner, turn, 1) if turn else corner
                raw[k, pl.ds(y_at + rows + ROWS, ROWS), :] = jnp.zeros((ROWS, LANES), jnp.float32)

        signed, slopes, mixing = parameters(vol, slope, mix)
        chunk = 2 * ROWS

        def halo_chunk(t, carry):
            at = pl.ds(pl.multiple_of(t * chunk, chunk), chunk)
            comp = [raw[i, at, :] for i in range(COMPS)]
            total = total_of(comp)
            there = total > 0.0
            inverse = rcp(jnp.where(there, total, 1.0))
            feed = [jnp.where(there, comp[i] * inverse, 1.0) for i in range(COMPS)]
            cell_press = raw[PRESS, at, :]
            two = flash(
                feed, jnp.where(cell_press > 0.0, cell_press, 1.0), signed, slopes, mixing
            )
            marked = raw[FLAG, at, :] > 0.0
            mobility = [
                jnp.where(there, jnp.where(marked, two[i], feed[i]), 0.0) for i in range(COMPS)
            ]
            for i in range(COMPS):
                mob_h[i, at, :] = mobility[i]
            mob_h[COMPS, at, :] = total_of(mobility)
            raw[MASS, at, :] = raw[PORE, at, :] - raw[MASS, at, :]
            return carry

        lax.fori_loop(0, halo_rows // chunk, halo_chunk, 0)

        last_row = row_of((rows, width)) == rows - 1
        for z in range(depth):
            for extended, own, ref, lead in (
                (e_press, press, raw, PRESS),
                (e_tx, tx, raw, TX),
                (e_ty, ty, raw, TY),
                (e_tz, tz, raw, TZ),
                (e_pore, pore, raw, PORE),
                (e_mob, mob_sum, mob_h, COMPS),
                (e_acc, acc_sum, raw, MASS),
            ):
                extended[z, pl.ds(0, rows), pl.ds(0, width)] = own[z]
                extended[z, pl.ds(rows, ROWS), pl.ds(0, width)] = x_tile(ref, lead, z)
                extended[z, pl.ds(0, tall), pl.ds(width, LANES)] = y_tile(ref, lead, z, tall)

        full = (tall, wide)
        end_x = (row_of(full) == rows - 1) & (areal == areals - 1)
        end_y = (lane_of(full) == width - 1) & (layer == layers - 1)
        scale = 0.5 * TIME_STEP

        def faces(z, carry):
            p, m = e_press[z], e_mob[z]
            strength_x = jnp.where(end_x, 0.0, scale * e_tx[z])
            strength_y = jnp.where(end_y, 0.0, scale * e_ty[z])
            strength_z = jnp.where(z < depth - 1, scale, 0.0) * e_tz[z]
            up = jnp.minimum(z + 1, depth - 1)
            for strength, p_next, m_next, g_ref, c_ref in (
                (strength_x, pltpu.roll(p, tall - 1, 0), pltpu.roll(m, tall - 1, 0), g_x, c_x),
                (strength_y, pltpu.roll(p, wide - 1, 1), pltpu.roll(m, wide - 1, 1), g_y, c_y),
                (strength_z, e_press[up], e_mob[up], g_z, c_z),
            ):
                g_ref[z] = strength * (p - p_next)
                c_ref[z] = strength * (m + m_next)
            return carry

        lax.fori_loop(0, depth, faces, 0)

        def update(z, carry):
            p = e_press[z]
            down = jnp.maximum(z - 1, 0)
            cx, cy, cz = c_x[z], c_y[z], c_z[z]
            cz_low = jnp.where(z > 0, 1.0, 0.0) * c_z[down]
            fx = cx * (p - pltpu.roll(p, tall - 1, 0))
            fy = cy * (p - pltpu.roll(p, wide - 1, 1))
            fz = cz * (p - e_press[jnp.minimum(z + 1, depth - 1)])
            fz_low = cz_low * (e_press[down] - p)
            total = (
                e_acc[z]
                + (fx - pltpu.roll(fx, 1, 0))
                + (fy - pltpu.roll(fy, 1, 1))
                + (fz - fz_low)
            )
            diagonal = (
                COMPRESS * e_pore[z]
                + (cx + pltpu.roll(cx, 1, 0))
                + (cy + pltpu.roll(cy, 1, 1))
                + (cz + cz_low)
            )
            inverse = rcp(jnp.where(diagonal > 0.0, diagonal, 1.0))
            first[z] = jnp.where(diagonal > 0.0, -total * inverse, 0.0)
            e_acc[z] = total
            e_pore[z] = inverse
            return carry

        lax.fori_loop(0, depth, update, 0)

        def second(z, carry):
            here = first[z]
            down, up = jnp.maximum(z - 1, 0), jnp.minimum(z + 1, depth - 1)
            cx, cy, cz = c_x[z], c_y[z], c_z[z]
            cz_low = jnp.where(z > 0, 1.0, 0.0) * c_z[down]
            own = (slice(0, rows), slice(0, width))
            gathered = (
                (cx * pltpu.roll(here, tall - 1, 0))[own]
                + pltpu.roll(cx * here, 1, 0)[own]
                + (cy * pltpu.roll(here, wide - 1, 1))[own]
                + pltpu.roll(cy * here, 1, 1)[own]
                + (cz * first[up] + cz_low * first[down])[own]
                - e_acc[z][own]
            )
            new_ref[z] = e_press[z][own] + gathered * e_pore[z][own]
            return carry

        lax.fori_loop(0, depth, second, 0)

    z = z_now
    own = (slice(0, rows), slice(0, width))
    down, up = jnp.maximum(z - 1, 0), jnp.minimum(z + 1, depth - 1)
    gx, gy = g_x[z], g_y[z]
    gx_low = -pltpu.roll(gx, 1, 0)[own]
    gy_low = -pltpu.roll(gy, 1, 1)[own]
    gz = g_z[z][own]
    gz_low = jnp.where(z > 0, -1.0, 0.0) * g_z[down][own]
    gx, gy = gx[own], gy[own]
    middle = (gx + gx_low) + (gy + gy_low) + (gz + gz_low)

    def component(i, carry):
        here = mob[i, z]
        tall_here = jnp.concatenate([here, x_tile(mob_h, i, z)], axis=0)
        wide_here = jnp.concatenate([here, y_tile(mob_h, i, z, rows)], axis=1)
        res_ref[i, 0] = (
            acc[i, 0]
            + middle * here
            + gx * pltpu.roll(tall_here, tall - 1, 0)[own]
            + gx_low * pltpu.roll(tall_here, 1, 0)[own]
            + gy * pltpu.roll(wide_here, wide - 1, 1)[own]
            + gy_low * pltpu.roll(wide_here, 1, 1)[own]
            + gz * mob[i, up]
            + gz_low * mob[i, down]
        )
        return carry

    lax.fori_loop(0, COMPS, component, 0)


def on_device(
    pressure, composition, mass_old, pore_volume, trans_x, trans_y, trans_z,
    volatility, pressure_slope, mixing, two_phase,
):
    depth, rows, width = pressure.shape
    f32 = jnp.float32
    smem = pl.BlockSpec(memory_space=pltpu.SMEM)
    vmem = pl.BlockSpec(memory_space=pltpu.VMEM)
    params = pltpu.CompilerParams(vmem_limit_bytes=VMEM_LIMIT)
    scalars = (two_phase, volatility, pressure_slope, mixing)

    def moved(block, axis, shift):
        count = lax.axis_size(axis)
        pairs = [(i, i + shift) for i in range(count) if 0 <= i + shift < count]
        return lax.ppermute(block, axis, pairs)

    plane = pl.BlockSpec((1, rows, width), lambda z: (z, 0, 0))
    planes = pl.BlockSpec((COMPS, 1, rows, width), lambda z: (0, z, 0, 0))
    columns = jax.ShapeDtypeStruct((rows, FIELDS * 32), f32)
    low, high = pl.pallas_call(
        pack_columns,
        grid=(depth,),
        in_specs=[smem, planes, plane, plane, plane, plane, plane, planes],
        out_specs=[vmem, vmem],
        out_shape=[columns, columns],
        compiler_params=params,
        name="pack_columns",
    )(two_phase, composition, pressure, trans_x, trans_y, trans_z, pore_volume, mass_old)
    left = moved(high, "layer", 1)
    right = moved(low, "layer", -1)

    whole = jax.ShapeDtypeStruct((COMPS, depth, rows, width), f32)
    sums = jax.ShapeDtypeStruct((depth, rows, width), f32)
    part = depth // 2

    def own(start, before):
        plane = pl.BlockSpec((1, rows, width), lambda z: (z + start, 0, 0))
        planes = pl.BlockSpec((COMPS, 1, rows, width), lambda z: (0, z + start, 0, 0))
        return pl.pallas_call(
            own_cells,
            grid=(part,),
            in_specs=[smem] * 4
            + [planes, plane, plane, planes]
            + [pl.BlockSpec(memory_space=pl.ANY)] * len(before),
            out_specs=[planes, planes, plane, plane],
            out_shape=[whole, whole, sums, sums],
            input_output_aliases={8 + k: k for k in range(len(before))},
            compiler_params=params,
            cost_estimate=pl.CostEstimate(
                flops=900 * part * rows * width,
                transcendentals=190 * part * rows * width,
                bytes_accessed=4 * 39 * part * rows * width,
            ),
            name="own_cells",
        )(*scalars, composition, pressure, pore_volume, mass_old, *before)

    begun = own(0, ())

    left, right, begun = lax.optimization_barrier((left, right, begun))
    tiles = rows // ROWS

    def edge(row):
        return [
            pl.BlockSpec((COMPS, 2, ROWS, width), lambda s: (0, s, row, 0)),
            *[pl.BlockSpec((2, ROWS, width), lambda s: (s, row, 0))] * 5,
            pl.BlockSpec((COMPS, 2, ROWS, width), lambda s: (0, s, row, 0)),
        ]

    fields = (composition, pressure, trans_x, trans_y, trans_z, pore_volume, mass_old)
    packed = jax.ShapeDtypeStruct((FIELDS // 2 + 1, 4 * depth, width), f32)
    packed_spec = pl.BlockSpec((FIELDS // 2 + 1, ROWS, width), lambda s: (0, s, 0))
    low, high = pl.pallas_call(
        pack_rows,
        grid=(depth // 2,),
        in_specs=[smem, *edge(0), *edge(tiles - 1), vmem, vmem],
        out_specs=[packed_spec, packed_spec],
        out_shape=[packed, packed],
        compiler_params=params,
        name="pack_rows",
    )(two_phase, *fields, *fields, left, right)
    above = moved(high, "areal", 1)
    below = moved(low, "areal", -1)

    mob, acc, mob_sum, acc_sum = own(part, begun)

    halo_rows = rows * (width // LANES) + rows + 2 * ROWS
    extended = pltpu.VMEM((depth, rows + ROWS, width + LANES), f32)
    return pl.pallas_call(
        finish,
        grid=(depth,),
        in_specs=[smem] * 4 + [vmem] * 12 + [planes],
        out_specs=[planes, vmem],
        out_shape=[whole, sums],
        scratch_shapes=[
            pltpu.VMEM((FIELDS, halo_rows, LANES), f32),
            pltpu.VMEM((COMPS + 1, halo_rows, LANES), f32),
            *[extended] * 14,
        ],
        compiler_params=params,
        name="finish",
    )(
        *scalars, left, right, above, below,
        pressure, trans_x, trans_y, trans_z, pore_volume, mob_sum, acc_sum, mob, acc,
    )


def solution(mesh):
    placed = (
        P(None, "areal", "layer"),
        P(None, None, "areal", "layer"),
        P(None, None, "areal", "layer"),
        P(None, "areal", "layer"),
        P(None, "areal", "layer"),
        P(None, "areal", "layer"),
        P(None, "areal", "layer"),
        P(),
        P(),
        P(),
        P(None, "areal"),
    )
    return jax.shard_map(
        on_device,
        mesh=mesh,
        in_specs=placed,
        out_specs=(P(None, None, "areal", "layer"), P(None, "areal", "layer")),
        check_vma=False,
    )
```

```python
import jax
import jax.numpy as jnp
from jax import lax
from jax.experimental import pallas as pl
from jax.experimental.pallas import tpu as pltpu
from jax.sharding import PartitionSpec as P

SS_ITERS = 3
RR_ITERS = 3
LIGHT = 4
COMPS = 9
FIELDS = 16
PRESS, TX, TY, TZ, PORE, MASS, FLAG = range(COMPS, FIELDS)
TIME_STEP = 4.0
COMPRESS = 0.2
VAPOUR_WEIGHT = 1.0 / 0.25
LANES = 128
ROWS = 8
VMEM_LIMIT = 48 * 1024 * 1024


def rcp(x):
    return pltpu.reciprocal(x, approx=True)


def total_of(terms):
    terms = list(terms)
    while len(terms) > 1:
        terms = [a + b for a, b in zip(terms[::2], terms[1::2])] + (
            [terms[-1]] if len(terms) % 2 else []
        )
    return terms[0]


def flash(feed, pressure, signed, slope, mixing):
    log_press = jnp.log(pressure)
    base = [signed[i] - slope[i] * log_press for i in range(COMPS)]
    spread = None
    for outer in range(SS_ITERS):
        if outer == 0:
            log_k = base
        else:
            log_k = [
                base[i] - jnp.tanh(total_of(mixing(i, j) * spread[j] for j in range(COMPS)))
                for i in range(COMPS)
            ]
        w = [rcp(jnp.exp(log_k[i]) - 1.0) for i in range(COMPS)]
        fraction = jnp.full(pressure.shape, 0.5, jnp.float32)
        for _ in range(RR_ITERS):
            q = [rcp(w[i] + fraction) for i in range(COMPS)]
            part = [feed[i] * q[i] for i in range(COMPS)]
            mismatch = total_of(part)
            gradient = total_of(part[i] * q[i] for i in range(COMPS))
            fraction = jnp.clip(fraction + mismatch * rcp(gradient), 0.0, 1.0)
        spread = [feed[i] * rcp(w[i] + fraction) for i in range(COMPS)]
    liquid_part = (1.0 - fraction) * (1.0 - fraction)
    vapour_part = VAPOUR_WEIGHT * (fraction * fraction)
    both = liquid_part + vapour_part
    return [spread[i] * (both * w[i] + vapour_part) for i in range(COMPS)]


def parameters(vol_ref, slope_ref, mix_ref):
    signed = [vol_ref[i] if i < LIGHT else -vol_ref[i] for i in range(COMPS)]
    slope = [slope_ref[i] for i in range(COMPS)]
    return signed, slope, lambda i, j: mix_ref[i, j]


def lane_of(shape):
    return lax.broadcasted_iota(jnp.int32, shape, len(shape) - 1)


def row_of(shape):
    return lax.broadcasted_iota(jnp.int32, shape, len(shape) - 2)


def field_plane(index, z, comp, press, tx, ty, tz, pore, mass):
    if index < COMPS:
        return comp[index, z]
    if index == MASS:
        return total_of(mass[i, z] for i in range(COMPS))
    return {PRESS: press, TX: tx, TY: ty, TZ: tz, PORE: pore}[index][z]


def pack_columns(flags, comp, press, tx, ty, tz, pore, mass, out_ref):
    step = pl.program_id(0)
    planes = press.shape[0]
    layer = lax.axis_index("layer")
    rows = out_ref.shape[0]
    shape = (rows, LANES)
    lane = lane_of(shape)
    brick = rows // flags.shape[1]
    row = row_of(shape)
    flag = jnp.zeros(shape, jnp.float32)
    for b in range(flags.shape[1]):
        flag = jnp.where(row // brick == b, flags[layer, b].astype(jnp.float32), flag)

    @pl.when(step == 0)
    def _():
        out_ref[...] = jnp.zeros(out_ref.shape, jnp.float32)

    for tile in range(FIELDS // 4):
        packed = jnp.zeros(shape, jnp.float32)
        for quarter in range(4):
            index = 4 * tile + quarter
            for z in range(planes):
                if index == FLAG:
                    first, last = flag, flag
                else:
                    plane = field_plane(index, z, comp, press, tx, ty, tz, pore, mass)
                    first, last = plane[:, :LANES], plane[:, -LANES:]
                at = 32 * quarter + 4 * z
                both = jnp.where(lane < LANES // 2, first, last)
                both = pltpu.roll(both, at + 2, 1)
                packed = jnp.where((lane >= at) & (lane < at + 4), both, packed)
        span = pl.ds(tile * LANES, LANES)
        out_ref[:, span] += pltpu.roll(packed, 4 * planes * step, 1)


def columns_of(gathered, rows, lanes):
    layer, layers = lax.axis_index("layer"), lax.axis_size("layer")
    left = gathered[jnp.maximum(layer - 1, 0), rows, lanes]
    right = gathered[jnp.minimum(layer + 1, layers - 1), rows, lanes]
    lane = lane_of(left.shape)
    left = jnp.where(layer > 0, left, 0.0)
    right = jnp.where(layer < layers - 1, right, 0.0)
    return jnp.where(lane % 4 < 2, left, right)


def pack_rows(flags, *refs):
    low_in, high_in = refs[:7], refs[7:14]
    gathered, low_ref, high_ref = refs[14:]
    step = pl.program_id(0)
    layer = lax.axis_index("layer")
    bricks = flags.shape[1]
    shape = (ROWS, low_ref.shape[2])
    row = row_of(shape)

    def plane(refs_of, z, index, flag):
        if index == FLAG:
            return jnp.full(shape, flag, jnp.float32)
        return field_plane(index, z, *refs_of)

    low_flag = flags[layer, 0].astype(jnp.float32)
    high_flag = flags[layer, bricks - 1].astype(jnp.float32)
    half = FIELDS // 2
    for k in range(half):
        low, high = None, None
        for z in range(2):
            near = jnp.where(
                row % 4 >= 2,
                pltpu.roll(plane(low_in, z, k, low_flag), 2, 0),
                plane(low_in, z, k + half, low_flag),
            )
            far = jnp.where(
                row % 4 < 2,
                pltpu.roll(plane(high_in, z, k, high_flag), 2, 0),
                pltpu.roll(plane(high_in, z, k + half, high_flag), 4, 0),
            )
            if z == 0:
                low, high = near, far
            else:
                low = jnp.where(row < 4, low, pltpu.roll(near, 4, 0))
                high = jnp.where(row < 4, high, pltpu.roll(far, 4, 0))
        low_ref[k] = low
        high_ref[k] = high
    rows = gathered.shape[1]
    width = shape[1]
    for part in range(2):
        @pl.when(step == part)
        def _():
            span = pl.ds(part * width, width)
            low_ref[half] = columns_of(gathered, pl.ds(0, ROWS), span)
            high_ref[half] = columns_of(gathered, pl.ds(rows - ROWS, ROWS), span)

    @pl.when(step >= 2)
    def _():
        low_ref[half] = jnp.zeros(shape, jnp.float32)
        high_ref[half] = jnp.zeros(shape, jnp.float32)


def own_cells(flags, vol, slope, mix, comp, press, pore, mass, *rest):
    mob_ref, acc_ref, mob_sum, acc_sum = rest[-4:]
    layer = lax.axis_index("layer")
    signed, slopes, mixing = parameters(vol, slope, mix)
    planes, rows, width = press.shape
    bricks = flags.shape[1]
    brick = rows // bricks
    shape = (planes, ROWS, width)
    per_tile = ROWS // brick

    def tile(t, carry):
        at = pl.ds(pl.multiple_of(t * ROWS, ROWS), ROWS)
        raw = [comp[i, :, at, :] for i in range(COMPS)]
        inverse = rcp(total_of(raw))
        feed = [raw[i] * inverse for i in range(COMPS)]
        volume = pore[:, at, :]
        acc = [volume * feed[i] - mass[i, :, at, :] for i in range(COMPS)]
        for i in range(COMPS):
            acc_ref[i, :, at, :] = acc[i]
        acc_sum[:, at, :] = total_of(acc)
        tile_flags = [flags[layer, t * per_tile + b] for b in range(per_tile)]
        some = tile_flags[0]
        for flag in tile_flags[1:]:
            some = some + flag

        @pl.when(some > 0)
        def _():
            row = row_of(shape)
            marked = jnp.zeros(shape, jnp.int32)
            for b in range(per_tile):
                marked = jnp.where(row // brick == b, tile_flags[b], marked)
            two = flash(feed, press[:, at, :], signed, slopes, mixing)
            mobility = [jnp.where(marked > 0, two[i], feed[i]) for i in range(COMPS)]
            for i in range(COMPS):
                mob_ref[i, :, at, :] = mobility[i]
            mob_sum[:, at, :] = total_of(mobility)

        @pl.when(some == 0)
        def _():
            for i in range(COMPS):
                mob_ref[i, :, at, :] = feed[i]
            mob_sum[:, at, :] = total_of(feed)

        return carry

    lax.fori_loop(0, rows // ROWS, tile, 0)


def finish(
    flags, vol, slope, mix,
    gathered, above, below,
    press, tx, ty, tz, pore, mob_sum, acc_sum, mob, acc,
    res_ref, new_ref,
    raw, mob_h, e_press, e_tx, e_ty, e_tz, e_pore, e_mob, e_acc,
    g_x, g_y, g_z, c_x, c_y, c_z, first,
):
    step = pl.program_id(0)
    planes = res_ref.shape[1]
    depth, rows, width = press.shape
    layer, layers = lax.axis_index("layer"), lax.axis_size("layer")
    areal, areals = lax.axis_index("areal"), lax.axis_size("areal")
    half = FIELDS // 2
    tall, wide = rows + ROWS, width + LANES
    halo_rows = raw.shape[1]
    y_at = rows * (width // LANES)

    def x_tile(ref, lead, z):
        parts = []
        for g in range(width // LANES):
            at = pl.multiple_of(g * rows + (z // 2) * ROWS, ROWS)
            parts.append(ref[lead, pl.ds(at, ROWS), :])
        tile = jnp.concatenate(parts, axis=1)
        return pltpu.roll(tile, 6 - 4 * (z % 2), 0)

    def y_tile(ref, lead, z, count):
        return pltpu.roll(ref[lead, pl.ds(y_at, count), :], 126 - 4 * z, 1)

    @pl.when(step == 0)
    def _():
        shape = (rows, width)
        upper = row_of(shape) % 4 < 2
        for k in range(half):
            up, down = above[k], below[k]
            near = jnp.where(upper, up, down)
            far = jnp.where(upper, pltpu.roll(up, rows - 2, 0), pltpu.roll(down, 2, 0))
            for g in range(width // LANES):
                span = slice(g * LANES, (g + 1) * LANES)
                raw[k, pl.ds(g * rows, rows), :] = near[:, span]
                raw[k + half, pl.ds(g * rows, rows), :] = far[:, span]
        corner_row = row_of((ROWS, LANES))
        for tile in range(FIELDS // 4):
            span = slice(tile * LANES, (tile + 1) * LANES)
            columns = columns_of(gathered, slice(None), span)
            part, within = (tile * LANES) // width, (tile * LANES) % width
            from_up = above[half, pl.ds(part * ROWS, ROWS), :][:, within : within + LANES]
            from_down = below[half, pl.ds(part * ROWS, ROWS), :][:, within : within + LANES]
            corner = jnp.where(corner_row < 4, from_down, from_up)
            for quarter in range(4):
                k = 4 * tile + quarter
                turn = (LANES - 32 * quarter) % LANES
                raw[k, pl.ds(y_at, rows), :] = pltpu.roll(columns, turn, 1) if turn else columns
                raw[k, pl.ds(y_at + rows, ROWS), :] = pltpu.roll(corner, turn, 1) if turn else corner
                raw[k, pl.ds(y_at + tall, halo_rows - y_at - tall), :] = jnp.zeros(
                    (halo_rows - y_at - tall, LANES), jnp.float32
                )

        signed, slopes, mixing = parameters(vol, slope, mix)
        chunk = 4 * ROWS

        def halo_chunk(t, carry):
            at = pl.ds(pl.multiple_of(t * chunk, chunk), chunk)
            comp = [raw[i, at, :] for i in range(COMPS)]
            total = total_of(comp)
            there = total > 0.0
            inverse = rcp(jnp.where(there, total, 1.0))
            feed = [jnp.where(there, comp[i] * inverse, 1.0) for i in range(COMPS)]
            cell_press = raw[PRESS, at, :]
            two = flash(
                feed, jnp.where(cell_press > 0.0, cell_press, 1.0), signed, slopes, mixing
            )
            marked = raw[FLAG, at, :] > 0.0
            mobility = [
                jnp.where(there, jnp.where(marked, two[i], feed[i]), 0.0) for i in range(COMPS)
            ]
            for i in range(COMPS):
                mob_h[i, at, :] = mobility[i]
            mob_h[COMPS, at, :] = total_of(mobility)
            raw[MASS, at, :] = raw[PORE, at, :] - raw[MASS, at, :]
            return carry

        lax.fori_loop(0, halo_rows // chunk, halo_chunk, 0)

        last_row = row_of((rows, width)) == rows - 1
        for z in range(depth):
            for extended, own, ref, lead in (
                (e_press, press, raw, PRESS),
                (e_tx, tx, raw, TX),
                (e_ty, ty, raw, TY),
                (e_tz, tz, raw, TZ),
                (e_pore, pore, raw, PORE),
                (e_mob, mob_sum, mob_h, COMPS),
                (e_acc, acc_sum, raw, MASS),
            ):
                extended[z, pl.ds(0, rows), pl.ds(0, width)] = own[z]
                extended[z, pl.ds(rows, ROWS), pl.ds(0, width)] = x_tile(ref, lead, z)
                extended[z, pl.ds(0, tall), pl.ds(width, LANES)] = y_tile(ref, lead, z, tall)

        full = (tall, wide)
        end_x = (row_of(full) == rows - 1) & (areal == areals - 1)
        end_y = (lane_of(full) == width - 1) & (layer == layers - 1)
        scale = 0.5 * TIME_STEP

        low_z = jnp.zeros(full, jnp.float32), jnp.zeros(full, jnp.float32)
        for z in range(depth):
            p, m = e_press[z], e_mob[z]
            strength = [
                jnp.where(end_x, 0.0, scale * e_tx[z]),
                jnp.where(end_y, 0.0, scale * e_ty[z]),
                scale * e_tz[z],
            ]
            p_next = [pltpu.roll(p, tall - 1, 0), pltpu.roll(p, wide - 1, 1)]
            m_next = [pltpu.roll(m, tall - 1, 0), pltpu.roll(m, wide - 1, 1)]
            if z < depth - 1:
                p_next.append(e_press[z + 1])
                m_next.append(e_mob[z + 1])
            g = [strength[d] * (p - p_next[d]) for d in range(len(p_next))]
            c = [strength[d] * (m + m_next[d]) for d in range(len(p_next))]
            f = [g[d] * (m + m_next[d]) for d in range(len(p_next))]
            g_x[z], g_y[z], c_x[z], c_y[z] = g[0], g[1], c[0], c[1]
            total = e_acc[z] + (f[0] - pltpu.roll(f[0], 1, 0)) + (f[1] - pltpu.roll(f[1], 1, 1))
            diagonal = (
                COMPRESS * e_pore[z]
                + (c[0] + pltpu.roll(c[0], 1, 0))
                + (c[1] + pltpu.roll(c[1], 1, 1))
            )
            if z > 0:
                total = total - low_z[0]
                diagonal = diagonal + low_z[1]
            if z < depth - 1:
                total = total + f[2]
                diagonal = diagonal + c[2]
                g_z[z], c_z[z] = g[2], c[2]
                low_z = f[2], c[2]
            inverse = rcp(jnp.where(diagonal > 0.0, diagonal, 1.0))
            first[z] = jnp.where(diagonal > 0.0, -total * inverse, 0.0)
            e_acc[z] = total
            e_pore[z] = inverse

        own = (slice(0, rows), slice(0, width))
        for z in range(depth):
            here = first[z]
            cx, cy = c_x[z], c_y[z]
            gathered_sum = (
                (cx * pltpu.roll(here, tall - 1, 0))[own]
                + pltpu.roll(cx * here, 1, 0)[own]
                + (cy * pltpu.roll(here, wide - 1, 1))[own]
                + pltpu.roll(cy * here, 1, 1)[own]
                - e_acc[z][own]
            )
            if z < depth - 1:
                gathered_sum = gathered_sum + (c_z[z] * first[z + 1])[own]
            if z > 0:
                gathered_sum = gathered_sum + (c_z[z - 1] * first[z - 1])[own]
            new_ref[z] = e_press[z][own] + gathered_sum * e_pore[z][own]

    own = (slice(0, rows), slice(0, width))
    for plane in range(planes):
        z = step * planes + plane
        down, up = jnp.maximum(z - 1, 0), jnp.minimum(z + 1, depth - 1)
        gx, gy = g_x[z], g_y[z]
        gx_low = -pltpu.roll(gx, 1, 0)[own]
        gy_low = -pltpu.roll(gy, 1, 1)[own]
        gz = jnp.where(z < depth - 1, g_z[z][own], 0.0)
        gz_low = jnp.where(z > 0, -g_z[down][own], 0.0)
        gx, gy = gx[own], gy[own]
        middle = (gx + gx_low) + (gy + gy_low) + (gz + gz_low)
        for i in range(COMPS):
            here = mob[i, z]
            tall_here = jnp.concatenate([here, x_tile(mob_h, i, z)], axis=0)
            wide_here = jnp.concatenate([here, y_tile(mob_h, i, z, rows)], axis=1)
            res_ref[i, plane] = (
                acc[i, z]
                + middle * here
                + gx * pltpu.roll(tall_here, tall - 1, 0)[own]
                + gx_low * pltpu.roll(tall_here, 1, 0)[own]
                + gy * pltpu.roll(wide_here, wide - 1, 1)[own]
                + gy_low * pltpu.roll(wide_here, 1, 1)[own]
                + gz * mob[i, up]
                + gz_low * mob[i, down]
            )


def on_device(
    pressure, composition, mass_old, pore_volume, trans_x, trans_y, trans_z,
    volatility, pressure_slope, mixing, two_phase,
):
    depth, rows, width = pressure.shape
    f32 = jnp.float32
    smem = pl.BlockSpec(memory_space=pltpu.SMEM)
    vmem = pl.BlockSpec(memory_space=pltpu.VMEM)
    params = pltpu.CompilerParams(vmem_limit_bytes=VMEM_LIMIT)
    scalars = (two_phase, volatility, pressure_slope, mixing)

    def moved(block, axis, shift):
        count = lax.axis_size(axis)
        pairs = [(i, i + shift) for i in range(count) if 0 <= i + shift < count]
        return lax.ppermute(block, axis, pairs)

    def blocks(count, start=0):
        plane = pl.BlockSpec((count, rows, width), lambda s: (s + start, 0, 0))
        planes = pl.BlockSpec((COMPS, count, rows, width), lambda s: (0, s + start, 0, 0))
        return plane, planes

    fields = (composition, pressure, trans_x, trans_y, trans_z, pore_volume, mass_old)
    plane, planes = blocks(2)
    packet = pl.pallas_call(
        pack_columns,
        grid=(depth // 2,),
        in_specs=[smem, planes, plane, plane, plane, plane, plane, planes],
        out_specs=vmem,
        out_shape=jax.ShapeDtypeStruct((rows, FIELDS * 32), f32),
        compiler_params=params,
        name="pack_columns",
    )(two_phase, *[pltpu.with_memory_space_constraint(field, pltpu.HBM) for field in fields])
    gathered = lax.all_gather(packet, "layer")

    whole = jax.ShapeDtypeStruct((COMPS, depth, rows, width), f32)
    sums = jax.ShapeDtypeStruct((depth, rows, width), f32)
    part = depth // 4

    def own(start, before):
        plane, planes = blocks(2, start)
        return pl.pallas_call(
            own_cells,
            grid=(part,),
            in_specs=[smem] * 4
            + [planes, plane, plane, planes]
            + [pl.BlockSpec(memory_space=pl.ANY)] * len(before),
            out_specs=[planes, planes, plane, plane],
            out_shape=[whole, whole, sums, sums],
            input_output_aliases={8 + k: k for k in range(len(before))},
            compiler_params=params,
            cost_estimate=pl.CostEstimate(
                flops=1800 * part * rows * width,
                transcendentals=380 * part * rows * width,
                bytes_accessed=8 * 39 * part * rows * width,
            ),
            name="own_cells",
        )(*scalars, composition, pressure, pore_volume, mass_old, *before)

    begun = own(0, ())

    gathered, begun = lax.optimization_barrier((gathered, begun))
    tiles = rows // ROWS

    def edge(row):
        return [
            pl.BlockSpec((COMPS, 2, ROWS, width), lambda s: (0, s, row, 0)),
            *[pl.BlockSpec((2, ROWS, width), lambda s: (s, row, 0))] * 5,
            pl.BlockSpec((COMPS, 2, ROWS, width), lambda s: (0, s, row, 0)),
        ]

    packed = jax.ShapeDtypeStruct((FIELDS // 2 + 1, 4 * depth, width), f32)
    packed_spec = pl.BlockSpec((FIELDS // 2 + 1, ROWS, width), lambda s: (0, s, 0))
    low, high = pl.pallas_call(
        pack_rows,
        grid=(depth // 2,),
        in_specs=[smem, *edge(0), *edge(tiles - 1), vmem],
        out_specs=[packed_spec, packed_spec],
        out_shape=[packed, packed],
        compiler_params=params,
        name="pack_rows",
    )(two_phase, *fields, *fields, gathered)
    above = moved(high, "areal", 1)
    below = moved(low, "areal", -1)

    mob, acc, mob_sum, acc_sum = own(part, begun)

    halo_rows = pl.cdiv(rows * (width // LANES) + rows + ROWS, 4 * ROWS) * 4 * ROWS
    extended = pltpu.VMEM((depth, rows + ROWS, width + LANES), f32)
    return pl.pallas_call(
        finish,
        grid=(depth // 2,),
        in_specs=[smem] * 4 + [vmem] * 12,
        out_specs=[planes, vmem],
        out_shape=[whole, sums],
        scratch_shapes=[
            pltpu.VMEM((FIELDS, halo_rows, LANES), f32),
            pltpu.VMEM((COMPS + 1, halo_rows, LANES), f32),
            *[extended] * 14,
        ],
        compiler_params=params,
        name="finish",
    )(
        *scalars, gathered, above, below,
        pressure, trans_x, trans_y, trans_z, pore_volume, mob_sum, acc_sum, mob, acc,
    )


def solution(mesh):
    placed = (
        P(None, "areal", "layer"),
        P(None, None, "areal", "layer"),
        P(None, None, "areal", "layer"),
        P(None, "areal", "layer"),
        P(None, "areal", "layer"),
        P(None, "areal", "layer"),
        P(None, "areal", "layer"),
        P(),
        P(),
        P(),
        P(None, "areal"),
    )
    return jax.shard_map(
        on_device,
        mesh=mesh,
        in_specs=placed,
        out_specs=(P(None, None, "areal", "layer"), P(None, "areal", "layer")),
        check_vma=False,
    )
```

```python
import functools

import jax
import jax.numpy as jnp
from jax import lax
from jax.experimental import pallas as pl
from jax.experimental.pallas import tpu as pltpu
from jax.sharding import PartitionSpec as P

SS_ITERS = 3
RR_ITERS = 3
LIGHT = 4
COMPS = 9
FIELDS = 16
PRESS, TX, TY, TZ, PORE, MASS, FLAG = range(COMPS, FIELDS)
H_MOB, H_PRESS, H_TX, H_TY, H_TZ, H_PORE, H_ACC = range(COMPS, FIELDS)
CORNER = (H_MOB, H_PRESS, H_TX, H_TY)
TIME_STEP = 4.0
COMPRESS = 0.2
VAPOUR_WEIGHT = 1.0 / 0.25
LANES = 128
ROWS = 8
MIB = 1024 * 1024
PLANES = 4


def rcp(x):
    return pltpu.reciprocal(x, approx=True)


def total_of(terms):
    terms = list(terms)
    while len(terms) > 1:
        terms = [a + b for a, b in zip(terms[::2], terms[1::2])] + (
            [terms[-1]] if len(terms) % 2 else []
        )
    return terms[0]


def flash(feed, pressure, signed, slope, mixing):
    log_press = jnp.log(pressure)
    base = [signed[i] - slope[i] * log_press for i in range(COMPS)]
    spread = None
    for outer in range(SS_ITERS):
        if outer == 0:
            log_k = base
        else:
            log_k = [
                base[i] - jnp.tanh(total_of(mixing(i, j) * spread[j] for j in range(COMPS)))
                for i in range(COMPS)
            ]
        w = [rcp(jnp.exp(log_k[i]) - 1.0) for i in range(COMPS)]
        fraction = jnp.full(pressure.shape, 0.5, jnp.float32)
        for _ in range(RR_ITERS):
            q = [rcp(w[i] + fraction) for i in range(COMPS)]
            part = [feed[i] * q[i] for i in range(COMPS)]
            mismatch = total_of(part)
            gradient = total_of(part[i] * q[i] for i in range(COMPS))
            fraction = jnp.clip(fraction + mismatch * rcp(gradient), 0.0, 1.0)
        spread = [feed[i] * rcp(w[i] + fraction) for i in range(COMPS)]
    liquid_part = (1.0 - fraction) * (1.0 - fraction)
    vapour_part = VAPOUR_WEIGHT * (fraction * fraction)
    both = liquid_part + vapour_part
    return [spread[i] * (both * w[i] + vapour_part) for i in range(COMPS)]


def parameters(vol_ref, slope_ref, mix_ref):
    signed = [vol_ref[i] if i < LIGHT else -vol_ref[i] for i in range(COMPS)]
    slope = [slope_ref[i] for i in range(COMPS)]
    return signed, slope, lambda i, j: mix_ref[i, j]


def lane_of(shape):
    return lax.broadcasted_iota(jnp.int32, shape, len(shape) - 1)


def row_of(shape):
    return lax.broadcasted_iota(jnp.int32, shape, len(shape) - 2)


def field_plane(index, z, comp, press, tx, ty, tz, pore, mass):
    if index < COMPS:
        return comp[index, z]
    if index == MASS:
        return total_of(mass[i, z] for i in range(COMPS))
    return {PRESS: press, TX: tx, TY: ty, TZ: tz, PORE: pore}[index][z]


def pack_columns(flags, comp, press, tx, ty, tz, pore, mass, out_ref):
    step = pl.program_id(0)
    planes = press.shape[0]
    layer = lax.axis_index("layer")
    rows = out_ref.shape[0]
    shape = (rows, LANES)
    lane = lane_of(shape)
    brick = rows // flags.shape[1]
    row = row_of(shape)
    flag = jnp.zeros(shape, jnp.float32)
    for b in range(flags.shape[1]):
        flag = jnp.where(row // brick == b, flags[layer, b].astype(jnp.float32), flag)

    @pl.when(step == 0)
    def _():
        out_ref[...] = jnp.zeros(out_ref.shape, jnp.float32)

    for tile in range(FIELDS // 4):
        packed = jnp.zeros(shape, jnp.float32)
        for quarter in range(4):
            index = 4 * tile + quarter
            for z in range(planes):
                if index == FLAG:
                    first, last = flag, flag
                else:
                    plane = field_plane(index, z, comp, press, tx, ty, tz, pore, mass)
                    first, last = plane[:, :LANES], plane[:, -LANES:]
                at = 32 * quarter + 4 * z
                both = jnp.where(lane < LANES // 2, first, last)
                both = pltpu.roll(both, at + 2, 1)
                packed = jnp.where((lane >= at) & (lane < at + 4), both, packed)
        span = pl.ds(tile * LANES, LANES)
        out_ref[:, span] += pltpu.roll(packed, 4 * planes * step, 1)


def own_cells(pack, flags, vol, slope, mix, comp, press, pore, mass, *rest):
    per_tile = 2
    if pack:
        tx, ty, tz, mob_ref, acc_ref, mob_sum, acc_sum, low_ref, high_ref = rest
        tile_row = pl.program_id(0) * (flags.shape[1] // per_tile - 1)
    else:
        mob_ref, acc_ref, mob_sum, acc_sum = rest[-4:]
        tile_row = pl.program_id(0) + 1
    layer = lax.axis_index("layer")
    signed, slopes, mixing = parameters(vol, slope, mix)
    shape = press.shape
    planes = shape[0]
    raw = [comp[i] for i in range(COMPS)]
    inverse = rcp(total_of(raw))
    feed = [raw[i] * inverse for i in range(COMPS)]
    volume = pore[...]
    acc = [volume * feed[i] - mass[i] for i in range(COMPS)]
    for i in range(COMPS):
        acc_ref[i] = acc[i]
    acc_sum[...] = total_of(acc)
    tile_flags = [flags[layer, tile_row * per_tile + b] for b in range(per_tile)]
    some = tile_flags[0] + tile_flags[1]

    @pl.when(some > 0)
    def _():
        marked = jnp.where(row_of(shape) < ROWS // per_tile, tile_flags[0], tile_flags[1])
        two = flash(feed, press[...], signed, slopes, mixing)
        mobility = [jnp.where(marked > 0, two[i], feed[i]) for i in range(COMPS)]
        for i in range(COMPS):
            mob_ref[i] = mobility[i]
        mob_sum[...] = total_of(mobility)

    @pl.when(some == 0)
    def _():
        for i in range(COMPS):
            mob_ref[i] = feed[i]
        mob_sum[...] = total_of(feed)

    if not pack:
        return
    rest_fields = {
        H_MOB: mob_sum, H_PRESS: press, H_TX: tx, H_TY: ty, H_TZ: tz, H_PORE: pore, H_ACC: acc_sum,
    }

    def field(k, z):
        return mob_ref[k, z] if k < COMPS else rest_fields[k][z]

    half = FIELDS // 2
    row = row_of(shape[1:])

    @pl.when(pl.program_id(0) == 0)
    def _():
        for k in range(half):
            for pair in range(planes // 2):
                near, far = [
                    jnp.where(row % 4 >= 2, pltpu.roll(field(k, z), 2, 0), field(k + half, z))
                    for z in (2 * pair, 2 * pair + 1)
                ]
                low_ref[k, pl.ds(pair * ROWS, ROWS), :] = jnp.where(row < 4, near, pltpu.roll(far, 4, 0))

    @pl.when(pl.program_id(0) == 1)
    def _():
        for k in range(half):
            for pair in range(planes // 2):
                near, far = [
                    jnp.where(
                        row % 4 < 2, pltpu.roll(field(k, z), 2, 0), pltpu.roll(field(k + half, z), 4, 0)
                    )
                    for z in (2 * pair, 2 * pair + 1)
                ]
                high_ref[k, pl.ds(pair * ROWS, ROWS), :] = jnp.where(row < 4, near, pltpu.roll(far, 4, 0))


def column_cells(vol, slope, mix, left, right, low_in, high_in, out_ref, low_ref, high_ref):
    del low_in, high_in
    rows = left.shape[0]
    shape = (rows, LANES)
    lane = lane_of(shape)
    raw = []
    for tile in range(FIELDS // 4):
        span = slice(tile * LANES, (tile + 1) * LANES)
        columns = jnp.where(lane % 4 < 2, left[:, span], right[:, span])
        for quarter in range(4):
            turn = (LANES - 32 * quarter) % LANES
            raw.append(pltpu.roll(columns, turn, 1) if turn else columns)
    total = total_of(raw[:COMPS])
    there = (total > 0.0) & (lane < 32)
    inverse = rcp(jnp.where(there, total, 1.0))
    feed = [jnp.where(there, raw[i] * inverse, 1.0) for i in range(COMPS)]
    signed, slopes, mixing = parameters(vol, slope, mix)
    two = flash(feed, jnp.where(there, raw[PRESS], 1.0), signed, slopes, mixing)
    marked = raw[FLAG] > 0.0
    mobility = [jnp.where(there, jnp.where(marked, two[i], feed[i]), 0.0) for i in range(COMPS)]
    fields = mobility + [total_of(mobility), raw[PRESS], raw[TX], raw[TY], raw[TZ], raw[PORE]]
    fields.append(raw[PORE] - raw[MASS])
    for k in range(FIELDS):
        out_ref[k] = fields[k]
    corner = fields[CORNER[0]]
    for quarter in range(1, 4):
        at = 32 * quarter
        corner = jnp.where(
            (lane >= at) & (lane < at + 32), pltpu.roll(fields[CORNER[quarter]], at, 1), corner
        )
    low_ref[0] = corner[:ROWS]
    high_ref[0] = corner[rows - ROWS :]


def finish(
    columns, above, below,
    press, tx, ty, tz, pore, mob_sum, acc_sum, mob, acc,
    res_ref, new_ref,
    rows_h, columns_h, e_press, e_tx, e_ty, e_tz, e_pore, e_mob, e_acc,
    g_x, g_y, g_z, c_x, c_y, c_z, first,
):
    step = pl.program_id(0)
    planes = res_ref.shape[1]
    depth, rows, width = press.shape
    layer, layers = lax.axis_index("layer"), lax.axis_size("layer")
    areal, areals = lax.axis_index("areal"), lax.axis_size("areal")
    half = FIELDS // 2
    tall, wide = rows + ROWS, width + LANES
    full = (tall, wide)
    own = (slice(0, rows), slice(0, width))
    extended = {
        H_MOB: (e_mob, mob_sum), H_PRESS: (e_press, press), H_TX: (e_tx, tx), H_TY: (e_ty, ty),
        H_TZ: (e_tz, tz), H_PORE: (e_pore, pore), H_ACC: (e_acc, acc_sum),
    }

    @pl.when(step == 0)
    def _():
        upper = row_of((rows, width)) % 4 < 2
        corner_row = row_of((ROWS, LANES))
        corners = jnp.where(corner_row < 4, below[half, 0:ROWS, 0:LANES], above[half, 0:ROWS, 0:LANES])
        for k in range(FIELDS):
            up, down = above[k % half], below[k % half]
            if k < half:
                beside = jnp.where(upper, up, down)
            else:
                beside = jnp.where(upper, pltpu.roll(up, rows - 2, 0), pltpu.roll(down, 2, 0))
            column = columns[k]
            for z in range(depth):
                at = (z // 2) * ROWS
                tile = pltpu.roll(beside[at : at + ROWS], 6 - 4 * (z % 2), 0)
                turn = (LANES + LANES - 2 - 4 * z) % LANES
                side = pltpu.roll(column, turn, 1)
                if k < COMPS:
                    rows_h[k, z] = tile
                    columns_h[k, z] = side
                else:
                    e_ref, own_ref = extended[k]
                    e_ref[z, pl.ds(0, rows), pl.ds(0, width)] = own_ref[z]
                    e_ref[z, pl.ds(rows, ROWS), pl.ds(0, width)] = tile
                    e_ref[z, pl.ds(0, rows), pl.ds(width, LANES)] = side
                    if k in CORNER:
                        turn = (turn + LANES - 32 * CORNER.index(k)) % LANES
                        e_ref[z, pl.ds(rows, ROWS), pl.ds(width, LANES)] = pltpu.roll(corners, turn, 1)

        end_x = (row_of(full) == rows - 1) & (areal == areals - 1)
        end_y = (lane_of(full) == width - 1) & (layer == layers - 1)
        scale = 0.5 * TIME_STEP
        nothing = jnp.zeros(full, jnp.float32)
        g_z[0] = nothing
        c_z[0] = nothing

        def update(z):
            p, m = e_press[z], e_mob[z]
            up, down = jnp.minimum(z + 1, depth - 1), jnp.maximum(z - 1, 0)
            strength_x = jnp.where(end_x, 0.0, scale * e_tx[z])
            strength_y = jnp.where(end_y, 0.0, scale * e_ty[z])
            strength_z = jnp.where(z < depth - 1, scale, 0.0) * e_tz[z]
            dx = p - pltpu.roll(p, tall - 1, 0)
            dy = p - pltpu.roll(p, wide - 1, 1)
            dz = p - e_press[up]
            cx = strength_x * (m + pltpu.roll(m, tall - 1, 0))
            cy = strength_y * (m + pltpu.roll(m, wide - 1, 1))
            cz = strength_z * (m + e_mob[up])
            cz_low = c_z[z]
            g_x[z], g_y[z], g_z[z + 1] = strength_x * dx, strength_y * dy, strength_z * dz
            c_x[z], c_y[z], c_z[z + 1] = cx, cy, cz
            fx, fy = cx * dx, cy * dy
            total = (
                e_acc[z]
                + (fx - pltpu.roll(fx, 1, 0))
                + (fy - pltpu.roll(fy, 1, 1))
                + (cz * dz + cz_low * (p - e_press[down]))
            )
            diagonal = (
                COMPRESS * e_pore[z]
                + (cx + pltpu.roll(cx, 1, 0))
                + (cy + pltpu.roll(cy, 1, 1))
                + (cz + cz_low)
            )
            inverse = rcp(jnp.where(diagonal > 0.0, diagonal, 1.0))
            first[z] = jnp.where(diagonal > 0.0, -total * inverse, 0.0)
            e_acc[z] = total
            e_pore[z] = inverse

        def second(z):
            here = first[z]
            up, down = jnp.minimum(z + 1, depth - 1), jnp.maximum(z - 1, 0)
            cx, cy = c_x[z], c_y[z]
            near = (
                (cx * pltpu.roll(here, tall - 1, 0))[own]
                + pltpu.roll(cx * here, 1, 0)[own]
                + (cy * pltpu.roll(here, wide - 1, 1))[own]
                + pltpu.roll(cy * here, 1, 1)[own]
                + (c_z[z + 1] * first[up] + c_z[z] * first[down])[own]
                - e_acc[z][own]
            )
            new_ref[z] = e_press[z][own] + near * e_pore[z][own]

        for body in (update, second):
            def pair(t, carry):
                body(2 * t)
                body(2 * t + 1)
                return carry

            lax.fori_loop(0, depth // 2, pair, 0)

    for plane in range(planes):
        z = step * planes + plane
        down, up = jnp.maximum(z - 1, 0), jnp.minimum(z + 1, depth - 1)
        gx, gy = g_x[z], g_y[z]
        gx_low = -pltpu.roll(gx, 1, 0)[own]
        gy_low = -pltpu.roll(gy, 1, 1)[own]
        gz, gz_low = g_z[z + 1][own], -g_z[z][own]
        gx, gy = gx[own], gy[own]
        middle = (gx + gx_low) + (gy + gy_low) + (gz + gz_low)
        for i in range(COMPS):
            here = mob[i, z]
            tall_here = jnp.concatenate([here, rows_h[i, z]], axis=0)
            wide_here = jnp.concatenate([here, columns_h[i, z]], axis=1)
            res_ref[i, plane] = (
                acc[i, z]
                + middle * here
                + gx * pltpu.roll(tall_here, tall - 1, 0)[own]
                + gx_low * pltpu.roll(tall_here, 1, 0)[own]
                + gy * pltpu.roll(wide_here, wide - 1, 1)[own]
                + gy_low * pltpu.roll(wide_here, 1, 1)[own]
                + gz * mob[i, up]
                + gz_low * mob[i, down]
            )


def on_device(
    pressure, composition, mass_old, pore_volume, trans_x, trans_y, trans_z,
    volatility, pressure_slope, mixing, two_phase,
):
    depth, rows, width = pressure.shape
    f32 = jnp.float32
    smem = pl.BlockSpec(memory_space=pltpu.SMEM)
    vmem = pl.BlockSpec(memory_space=pltpu.VMEM)
    half = FIELDS // 2

    def params(mib):
        return pltpu.CompilerParams(vmem_limit_bytes=mib * MIB)

    scalars = (two_phase, volatility, pressure_slope, mixing)

    def moved(block, axis, shift):
        count = lax.axis_size(axis)
        pairs = [(i, i + shift) for i in range(count) if 0 <= i + shift < count]
        return lax.ppermute(block, axis, pairs)

    fields = (composition, pressure, trans_x, trans_y, trans_z, pore_volume, mass_old)
    plane = pl.BlockSpec((2, rows, width), lambda s: (s, 0, 0))
    planes = pl.BlockSpec((COMPS, 2, rows, width), lambda s: (0, s, 0, 0))
    packet = pl.pallas_call(
        pack_columns,
        grid=(depth // 2,),
        in_specs=[smem, planes, plane, plane, plane, plane, plane, planes],
        out_specs=vmem,
        out_shape=jax.ShapeDtypeStruct((rows, FIELDS * 32), f32),
        compiler_params=params(24),
        name="pack_columns",
    )(two_phase, *[pltpu.with_memory_space_constraint(field, pltpu.HBM) for field in fields])
    left = moved(packet, "layer", 1)
    right = moved(packet, "layer", -1)

    whole = jax.ShapeDtypeStruct((COMPS, depth, rows, width), f32)
    sums = jax.ShapeDtypeStruct((depth, rows, width), f32)
    packed = jax.ShapeDtypeStruct((half + 1, 4 * depth, width), f32)
    parts = depth // PLANES
    tiles = rows // ROWS

    def own(pack, before):
        tile_row = (lambda g: g * (tiles - 1)) if pack else (lambda g: g + 1)
        plane = pl.BlockSpec((PLANES, ROWS, width), lambda g, z: (z, tile_row(g), 0))
        planes = pl.BlockSpec((COMPS, PLANES, ROWS, width), lambda g, z: (0, z, tile_row(g), 0))
        block = (half, 4 * PLANES, width)
        low = pl.BlockSpec(block, lambda g, z: (0, jnp.where(g == 0, z, parts - 1), 0))
        high = pl.BlockSpec(block, lambda g, z: (0, jnp.where(g == 0, 0, z), 0))
        count = 2 if pack else tiles - 2
        cells = count * ROWS * depth * width
        return pl.pallas_call(
            functools.partial(own_cells, pack),
            grid=(count, parts),
            in_specs=[smem] * 4
            + [planes, plane, plane, planes]
            + [plane] * (3 if pack else 0)
            + [pl.BlockSpec(memory_space=pl.ANY)] * len(before),
            out_specs=[planes, planes, plane, plane] + ([low, high] if pack else []),
            out_shape=[whole, whole, sums, sums] + ([packed, packed] if pack else []),
            input_output_aliases={8 + k: k for k in range(len(before))},
            compiler_params=params(24),
            cost_estimate=pl.CostEstimate(
                flops=900 * cells, transcendentals=190 * cells, bytes_accessed=4 * 39 * cells
            ),
            name="edge_cells" if pack else "inner_cells",
        )(
            *scalars, composition, pressure, pore_volume, mass_old,
            *((trans_x, trans_y, trans_z) if pack else ()), *before,
        )

    *begun, low, high = own(True, ())

    left, right, low, high, begun = lax.optimization_barrier((left, right, low, high, begun))
    corner = pl.BlockSpec((1, ROWS, LANES), lambda s: (half, 0, 0))
    columns, low, high = pl.pallas_call(
        column_cells,
        grid=(1,),
        in_specs=[smem] * 3 + [vmem] * 2 + [pl.BlockSpec(memory_space=pl.ANY)] * 2,
        out_specs=[vmem, corner, corner],
        out_shape=[jax.ShapeDtypeStruct((FIELDS, rows, LANES), f32), packed, packed],
        input_output_aliases={5: 1, 6: 2},
        compiler_params=params(16),
        name="column_cells",
    )(*scalars[1:], left, right, low, high)
    above = moved(high, "areal", 1)
    below = moved(low, "areal", -1)

    mob, acc, mob_sum, acc_sum = own(False, begun)

    planes = pl.BlockSpec((COMPS, 2, rows, width), lambda s: (0, s, 0, 0))
    extended = pltpu.VMEM((depth, rows + ROWS, width + LANES), f32)
    above_faces = pltpu.VMEM((depth + 1, rows + ROWS, width + LANES), f32)
    return pl.pallas_call(
        finish,
        grid=(depth // 2,),
        in_specs=[vmem] * 12,
        out_specs=[planes, vmem],
        out_shape=[whole, sums],
        scratch_shapes=[
            pltpu.VMEM((COMPS, depth, ROWS, width), f32),
            pltpu.VMEM((COMPS, depth, rows, LANES), f32),
            *[extended] * 7,
            *[extended, extended, above_faces] * 2,
            extended,
        ],
        compiler_params=params(28),
        name="finish",
    )(
        columns, above, below,
        pressure, trans_x, trans_y, trans_z, pore_volume, mob_sum, acc_sum, mob, acc,
    )


def solution(mesh):
    placed = (
        P(None, "areal", "layer"),
        P(None, None, "areal", "layer"),
        P(None, None, "areal", "layer"),
        P(None, "areal", "layer"),
        P(None, "areal", "layer"),
        P(None, "areal", "layer"),
        P(None, "areal", "layer"),
        P(),
        P(),
        P(),
        P(None, "areal"),
    )
    return jax.shard_map(
        on_device,
        mesh=mesh,
        in_specs=placed,
        out_specs=(P(None, None, "areal", "layer"), P(None, "areal", "layer")),
        check_vma=False,
    )
```

```python
import functools

import jax
import jax.numpy as jnp
from jax import lax
from jax.experimental import pallas as pl
from jax.experimental.pallas import tpu as pltpu
from jax.sharding import PartitionSpec as P

SS_ITERS = 3
RR_ITERS = 3
LIGHT = 4
COMPS = 9
FIELDS = 16
PRESS, TX, TY, TZ, PORE, MASS = range(COMPS, FIELDS - 1)
H_MOB, H_PRESS, H_TX, H_TY, H_TZ, H_PORE, H_ACC = range(COMPS, FIELDS)
CORNER = (H_MOB, H_PRESS, H_TX, H_TY)
TIME_STEP = 4.0
COMPRESS = 0.2
VAPOUR_WEIGHT = 1.0 / 0.25
LANES = 128
ROWS = 8
MIB = 1024 * 1024
PART = (COMPS + 1) * ROWS
DEEP = 256
PLANES = 4


def rcp(x):
    return pltpu.reciprocal(x, approx=True)


def total_of(terms):
    terms = list(terms)
    while len(terms) > 1:
        terms = [a + b for a, b in zip(terms[::2], terms[1::2])] + (
            [terms[-1]] if len(terms) % 2 else []
        )
    return terms[0]


def split(x):
    high = x.astype(jnp.bfloat16)
    return high, (x - high.astype(jnp.float32)).astype(jnp.bfloat16)


def mixing_operand(mix_ref):
    shape = (ROWS, DEEP)
    lane, row = lane_of(shape), row_of(shape)
    part = lax.div(lane, PART)
    within = lane - PART * part
    column = lax.div(within, ROWS)
    on = (within - ROWS * column == row) & (part < 3)
    blocks = []
    for i in range(COMPS):
        value = jnp.zeros(shape, jnp.float32)
        for j in range(COMPS):
            value = jnp.where(column == j, mix_ref[i, j], value)
        high, low = split(value)
        value = jnp.where(part == 2, low.astype(jnp.float32), high.astype(jnp.float32))
        blocks.append(jnp.where(on, value, 0.0))
    blocks.append(jnp.zeros(shape, jnp.float32))
    return jnp.concatenate(blocks, axis=0).astype(jnp.bfloat16)


def mixed(operand, spread):
    shape = spread[0].shape
    high, low = split(jnp.concatenate(spread + [jnp.zeros(shape, jnp.float32)], axis=0))
    tail = jnp.zeros((DEEP - 3 * PART, shape[1]), jnp.bfloat16)
    out = jnp.dot(
        operand,
        jnp.concatenate([high, low, high, tail], axis=0),
        preferred_element_type=jnp.float32,
    )
    return [out[ROWS * i : ROWS * (i + 1)] for i in range(COMPS)]


def flash(feed, pressure, signed, slope, operand):
    log_press = jnp.log(pressure)
    base = [signed[i] - slope[i] * log_press for i in range(COMPS)]
    spread = None
    for outer in range(SS_ITERS):
        if outer == 0:
            log_k = base
        else:
            mix = mixed(operand, spread)
            log_k = [base[i] - jnp.tanh(mix[i]) for i in range(COMPS)]
        w = [rcp(jnp.exp(log_k[i]) - 1.0) for i in range(COMPS)]
        fraction = jnp.full(pressure.shape, 0.5, jnp.float32)
        for _ in range(RR_ITERS):
            q = [rcp(w[i] + fraction) for i in range(COMPS)]
            part = [feed[i] * q[i] for i in range(COMPS)]
            mismatch = total_of(part)
            gradient = total_of(part[i] * q[i] for i in range(COMPS))
            fraction = jnp.clip(fraction + mismatch * rcp(gradient), 0.0, 1.0)
        spread = [feed[i] * rcp(w[i] + fraction) for i in range(COMPS)]
    liquid_part = (1.0 - fraction) * (1.0 - fraction)
    vapour_part = VAPOUR_WEIGHT * (fraction * fraction)
    both = liquid_part + vapour_part
    return [spread[i] * (both * w[i] + vapour_part) for i in range(COMPS)]


def parameters(vol_ref, slope_ref):
    signed = [vol_ref[i] if i < LIGHT else -vol_ref[i] for i in range(COMPS)]
    return signed, [slope_ref[i] for i in range(COMPS)]


def lane_of(shape):
    return lax.broadcasted_iota(jnp.int32, shape, len(shape) - 1)


def row_of(shape):
    return lax.broadcasted_iota(jnp.int32, shape, len(shape) - 2)


def field_plane(index, z, comp, press, tx, ty, tz, pore, mass):
    if index < COMPS:
        return comp[index, z]
    if index == MASS:
        return total_of(mass[i, z] for i in range(COMPS))
    return {PRESS: press, TX: tx, TY: ty, TZ: tz, PORE: pore}[index][z]


def pack_columns(comp, press, tx, ty, tz, pore, mass, out_ref):
    step = pl.program_id(0)
    planes = press.shape[0]
    shape = (out_ref.shape[0], LANES)
    lane = lane_of(shape)

    @pl.when(step == 0)
    def _():
        out_ref[...] = jnp.zeros(out_ref.shape, jnp.float32)

    for tile in range(FIELDS // 4):
        packed = jnp.zeros(shape, jnp.float32)
        for quarter in range(4):
            index = 4 * tile + quarter
            for z in range(planes if index <= MASS else 0):
                plane = field_plane(index, z, comp, press, tx, ty, tz, pore, mass)
                first, last = plane[:, :LANES], plane[:, -LANES:]
                at = 32 * quarter + 4 * z
                both = jnp.where(lane < LANES // 2, first, last)
                both = pltpu.roll(both, at + 2, 1)
                packed = jnp.where((lane >= at) & (lane < at + 4), both, packed)
        span = pl.ds(tile * LANES, LANES)
        out_ref[:, span] += pltpu.roll(packed, 4 * planes * step, 1)


def own_cells(pack, flags, vol, slope, mix, comp, press, pore, mass, *rest):
    per_tile = 2
    if pack:
        tx, ty, tz, mob_ref, acc_ref, mob_sum, acc_sum, low_ref, high_ref, operand = rest
        tile_row = pl.program_id(0) * (flags.shape[1] // per_tile - 1)
    else:
        mob_ref, acc_ref, mob_sum, acc_sum, operand = rest[-5:]
        tile_row = pl.program_id(0) + 1
    layer = lax.axis_index("layer")
    signed, slopes = parameters(vol, slope)
    planes, _, width = press.shape

    @pl.when((pl.program_id(0) == 0) & (pl.program_id(1) == 0))
    def _():
        operand[...] = mixing_operand(mix)

    raw = [comp[i] for i in range(COMPS)]
    inverse = rcp(total_of(raw))
    feed = [raw[i] * inverse for i in range(COMPS)]
    volume = pore[...]
    acc = [volume * feed[i] - mass[i] for i in range(COMPS)]
    for i in range(COMPS):
        acc_ref[i] = acc[i]
    acc_sum[...] = total_of(acc)
    tile_flags = [flags[layer, tile_row * per_tile + b] for b in range(per_tile)]
    some = tile_flags[0] + tile_flags[1]

    @pl.when(some > 0)
    def _():
        def beside(x):
            return jnp.concatenate([x[z] for z in range(planes)], axis=1)

        here = [beside(feed[i]) for i in range(COMPS)]
        two = flash(here, beside(press), signed, slopes, operand[...])
        marked = jnp.where(row_of(here[0].shape) < ROWS // per_tile, tile_flags[0], tile_flags[1])
        mobility = [jnp.where(marked > 0, two[i], here[i]) for i in range(COMPS)]
        total = total_of(mobility)
        for z in range(planes):
            span = slice(z * width, (z + 1) * width)
            for i in range(COMPS):
                mob_ref[i, z] = mobility[i][:, span]
            mob_sum[z] = total[:, span]

    @pl.when(some == 0)
    def _():
        for i in range(COMPS):
            mob_ref[i] = feed[i]
        mob_sum[...] = total_of(feed)

    if not pack:
        return
    rest_fields = {
        H_MOB: mob_sum, H_PRESS: press, H_TX: tx, H_TY: ty, H_TZ: tz, H_PORE: pore, H_ACC: acc_sum,
    }

    def field(k, z):
        return mob_ref[k, z] if k < COMPS else rest_fields[k][z]

    half = FIELDS // 2
    row = row_of((ROWS, width))

    @pl.when(pl.program_id(0) == 0)
    def _():
        for k in range(half):
            for pair in range(planes // 2):
                near, far = [
                    jnp.where(row % 4 >= 2, pltpu.roll(field(k, z), 2, 0), field(k + half, z))
                    for z in (2 * pair, 2 * pair + 1)
                ]
                low_ref[k, pl.ds(pair * ROWS, ROWS), :] = jnp.where(row < 4, near, pltpu.roll(far, 4, 0))

    @pl.when(pl.program_id(0) == 1)
    def _():
        for k in range(half):
            for pair in range(planes // 2):
                near, far = [
                    jnp.where(
                        row % 4 < 2, pltpu.roll(field(k, z), 2, 0), pltpu.roll(field(k + half, z), 4, 0)
                    )
                    for z in (2 * pair, 2 * pair + 1)
                ]
                high_ref[k, pl.ds(pair * ROWS, ROWS), :] = jnp.where(row < 4, near, pltpu.roll(far, 4, 0))


def column_cells(flags, vol, slope, mix, left, right, low_in, high_in, out_ref, low_ref, high_ref):
    del low_in, high_in
    rows = left.shape[0]
    shape = (rows, LANES)
    lane = lane_of(shape)
    raw = []
    for tile in range(FIELDS // 4):
        span = slice(tile * LANES, (tile + 1) * LANES)
        columns = jnp.where(lane % 4 < 2, left[:, span], right[:, span])
        for quarter in range(4):
            turn = (LANES - 32 * quarter) % LANES
            raw.append(pltpu.roll(columns, turn, 1) if turn else columns)
    total = total_of(raw[:COMPS])
    there = (total > 0.0) & (lane < 32)
    inverse = rcp(jnp.where(there, total, 1.0))
    feed = [jnp.where(there, raw[i] * inverse, 1.0) for i in range(COMPS)]
    signed, slopes = parameters(vol, slope)
    layer, layers = lax.axis_index("layer"), lax.axis_size("layer")
    bricks = flags.shape[1]
    brick = lax.div(row_of(shape), rows // bricks)
    marked = jnp.zeros(shape, jnp.int32)
    for b in range(bricks):
        both = jnp.where(
            lane % 4 < 2, flags[jnp.maximum(layer - 1, 0), b], flags[jnp.minimum(layer + 1, layers - 1), b]
        )
        marked = jnp.where(brick == b, both, marked)

    def beside(x):
        return jnp.concatenate([x[t : t + ROWS] for t in range(0, rows, ROWS)], axis=1)

    def above(x):
        return jnp.concatenate([x[:, t : t + LANES] for t in range(0, x.shape[1], LANES)], axis=0)

    pressure = jnp.where(there, raw[PRESS], 1.0)
    two = flash([beside(x) for x in feed], beside(pressure), signed, slopes, mixing_operand(mix))
    mobility = [
        jnp.where(there, jnp.where(marked > 0, above(two[i]), feed[i]), 0.0) for i in range(COMPS)
    ]
    fields = mobility + [total_of(mobility), raw[PRESS], raw[TX], raw[TY], raw[TZ], raw[PORE]]
    fields.append(raw[PORE] - raw[MASS])
    for k in range(FIELDS):
        out_ref[k] = fields[k]
    corner = fields[CORNER[0]]
    for quarter in range(1, 4):
        at = 32 * quarter
        corner = jnp.where(
            (lane >= at) & (lane < at + 32), pltpu.roll(fields[CORNER[quarter]], at, 1), corner
        )
    low_ref[0] = corner[:ROWS]
    high_ref[0] = corner[rows - ROWS :]


def finish(
    columns, above, below,
    press, tx, ty, tz, pore, mob_sum, acc_sum, mob, acc,
    res_ref, new_ref,
    rows_h, columns_h, e_press, e_tx, e_ty, e_tz, e_pore, e_mob, e_acc,
    g_x, g_y, g_z, c_x, c_y, c_z, first,
):
    step = pl.program_id(0)
    planes = res_ref.shape[1]
    depth, rows, width = press.shape
    layer, layers = lax.axis_index("layer"), lax.axis_size("layer")
    areal, areals = lax.axis_index("areal"), lax.axis_size("areal")
    half = FIELDS // 2
    tall, wide = rows + ROWS, width + LANES
    full = (tall, wide)
    own = (slice(0, rows), slice(0, width))
    extended = {
        H_MOB: (e_mob, mob_sum), H_PRESS: (e_press, press), H_TX: (e_tx, tx), H_TY: (e_ty, ty),
        H_TZ: (e_tz, tz), H_PORE: (e_pore, pore), H_ACC: (e_acc, acc_sum),
    }

    @pl.when(step == 0)
    def _():
        upper = row_of((rows, width)) % 4 < 2
        corner_row = row_of((ROWS, LANES))
        corners = jnp.where(corner_row < 4, below[half, 0:ROWS, 0:LANES], above[half, 0:ROWS, 0:LANES])
        for k in range(FIELDS):
            up, down = above[k % half], below[k % half]
            if k < half:
                beside = jnp.where(upper, up, down)
            else:
                beside = jnp.where(upper, pltpu.roll(up, rows - 2, 0), pltpu.roll(down, 2, 0))
            column = columns[k]
            for z in range(depth):
                at = (z // 2) * ROWS
                tile = pltpu.roll(beside[at : at + ROWS], 6 - 4 * (z % 2), 0)
                turn = (LANES + LANES - 2 - 4 * z) % LANES
                side = pltpu.roll(column, turn, 1)
                if k < COMPS:
                    rows_h[k, z] = tile
                    columns_h[k, z] = side
                else:
                    e_ref, own_ref = extended[k]
                    e_ref[z, pl.ds(0, rows), pl.ds(0, width)] = own_ref[z]
                    e_ref[z, pl.ds(rows, ROWS), pl.ds(0, width)] = tile
                    e_ref[z, pl.ds(0, rows), pl.ds(width, LANES)] = side
                    if k in CORNER:
                        turn = (turn + LANES - 32 * CORNER.index(k)) % LANES
                        e_ref[z, pl.ds(rows, ROWS), pl.ds(width, LANES)] = pltpu.roll(corners, turn, 1)

        end_x = (row_of(full) == rows - 1) & (areal == areals - 1)
        end_y = (lane_of(full) == width - 1) & (layer == layers - 1)
        scale = 0.5 * TIME_STEP
        nothing = jnp.zeros(full, jnp.float32)
        g_z[0] = nothing
        c_z[0] = nothing

        def update(z):
            p, m = e_press[z], e_mob[z]
            up, down = jnp.minimum(z + 1, depth - 1), jnp.maximum(z - 1, 0)
            strength_x = jnp.where(end_x, 0.0, scale * e_tx[z])
            strength_y = jnp.where(end_y, 0.0, scale * e_ty[z])
            strength_z = jnp.where(z < depth - 1, scale, 0.0) * e_tz[z]
            dx = p - pltpu.roll(p, tall - 1, 0)
            dy = p - pltpu.roll(p, wide - 1, 1)
            dz = p - e_press[up]
            cx = strength_x * (m + pltpu.roll(m, tall - 1, 0))
            cy = strength_y * (m + pltpu.roll(m, wide - 1, 1))
            cz = strength_z * (m + e_mob[up])
            cz_low = c_z[z]
            g_x[z], g_y[z], g_z[z + 1] = strength_x * dx, strength_y * dy, strength_z * dz
            c_x[z], c_y[z], c_z[z + 1] = cx, cy, cz
            fx, fy = cx * dx, cy * dy
            total = (
                e_acc[z]
                + (fx - pltpu.roll(fx, 1, 0))
                + (fy - pltpu.roll(fy, 1, 1))
                + (cz * dz + cz_low * (p - e_press[down]))
            )
            diagonal = (
                COMPRESS * e_pore[z]
                + (cx + pltpu.roll(cx, 1, 0))
                + (cy + pltpu.roll(cy, 1, 1))
                + (cz + cz_low)
            )
            inverse = rcp(jnp.where(diagonal > 0.0, diagonal, 1.0))
            first[z] = jnp.where(diagonal > 0.0, -total * inverse, 0.0)
            e_acc[z] = total
            e_pore[z] = inverse

        def second(z):
            here = first[z]
            up, down = jnp.minimum(z + 1, depth - 1), jnp.maximum(z - 1, 0)
            cx, cy = c_x[z], c_y[z]
            near = (
                (cx * pltpu.roll(here, tall - 1, 0))[own]
                + pltpu.roll(cx * here, 1, 0)[own]
                + (cy * pltpu.roll(here, wide - 1, 1))[own]
                + pltpu.roll(cy * here, 1, 1)[own]
                + (c_z[z + 1] * first[up] + c_z[z] * first[down])[own]
                - e_acc[z][own]
            )
            new_ref[z] = e_press[z][own] + near * e_pore[z][own]

        for body in (update, second):
            def pair(t, carry):
                body(2 * t)
                body(2 * t + 1)
                return carry

            lax.fori_loop(0, depth // 2, pair, 0)

    for plane in range(planes):
        z = step * planes + plane
        down, up = jnp.maximum(z - 1, 0), jnp.minimum(z + 1, depth - 1)
        gx, gy = g_x[z], g_y[z]
        gx_low = -pltpu.roll(gx, 1, 0)[own]
        gy_low = -pltpu.roll(gy, 1, 1)[own]
        gz, gz_low = g_z[z + 1][own], -g_z[z][own]
        gx, gy = gx[own], gy[own]
        middle = (gx + gx_low) + (gy + gy_low) + (gz + gz_low)
        for i in range(COMPS):
            here = mob[i, z]
            tall_here = jnp.concatenate([here, rows_h[i, z]], axis=0)
            wide_here = jnp.concatenate([here, columns_h[i, z]], axis=1)
            res_ref[i, plane] = (
                acc[i, z]
                + middle * here
                + gx * pltpu.roll(tall_here, tall - 1, 0)[own]
                + gx_low * pltpu.roll(tall_here, 1, 0)[own]
                + gy * pltpu.roll(wide_here, wide - 1, 1)[own]
                + gy_low * pltpu.roll(wide_here, 1, 1)[own]
                + gz * mob[i, up]
                + gz_low * mob[i, down]
            )


def on_device(
    pressure, composition, mass_old, pore_volume, trans_x, trans_y, trans_z,
    volatility, pressure_slope, mixing, two_phase,
):
    depth, rows, width = pressure.shape
    f32 = jnp.float32
    smem = pl.BlockSpec(memory_space=pltpu.SMEM)
    vmem = pl.BlockSpec(memory_space=pltpu.VMEM)
    half = FIELDS // 2

    def params(mib):
        return pltpu.CompilerParams(vmem_limit_bytes=mib * MIB)

    scalars = (two_phase, volatility, pressure_slope, mixing)

    def moved(block, axis, shift):
        count = lax.axis_size(axis)
        pairs = [(i, i + shift) for i in range(count) if 0 <= i + shift < count]
        return lax.ppermute(block, axis, pairs)

    fields = (composition, pressure, trans_x, trans_y, trans_z, pore_volume, mass_old)
    plane = pl.BlockSpec((PLANES, rows, width), lambda s: (s, 0, 0))
    planes = pl.BlockSpec((COMPS, PLANES, rows, width), lambda s: (0, s, 0, 0))
    packet = pl.pallas_call(
        pack_columns,
        grid=(depth // PLANES,),
        in_specs=[planes, plane, plane, plane, plane, plane, planes],
        out_specs=vmem,
        out_shape=jax.ShapeDtypeStruct((rows, FIELDS * 32), f32),
        compiler_params=params(24),
        name="pack_columns",
    )(*[pltpu.with_memory_space_constraint(field, pltpu.HBM) for field in fields])
    left = moved(packet, "layer", 1)
    right = moved(packet, "layer", -1)

    whole = jax.ShapeDtypeStruct((COMPS, depth, rows, width), f32)
    sums = jax.ShapeDtypeStruct((depth, rows, width), f32)
    packed = jax.ShapeDtypeStruct((half + 1, 4 * depth, width), f32)
    parts = depth // PLANES
    tiles = rows // ROWS

    def own(pack, before):
        tile_row = (lambda g: g * (tiles - 1)) if pack else (lambda g: g + 1)
        plane = pl.BlockSpec((PLANES, ROWS, width), lambda g, z: (z, tile_row(g), 0))
        planes = pl.BlockSpec((COMPS, PLANES, ROWS, width), lambda g, z: (0, z, tile_row(g), 0))
        block = (half, 4 * PLANES, width)
        low = pl.BlockSpec(block, lambda g, z: (0, jnp.where(g == 0, z, parts - 1), 0))
        high = pl.BlockSpec(block, lambda g, z: (0, jnp.where(g == 0, 0, z), 0))
        count = 2 if pack else tiles - 2
        cells = count * ROWS * depth * width
        return pl.pallas_call(
            functools.partial(own_cells, pack),
            grid=(count, parts),
            in_specs=[smem] * 4
            + [planes, plane, plane, planes]
            + [plane] * (3 if pack else 0)
            + [pl.BlockSpec(memory_space=pl.ANY)] * len(before),
            out_specs=[planes, planes, plane, plane] + ([low, high] if pack else []),
            out_shape=[whole, whole, sums, sums] + ([packed, packed] if pack else []),
            input_output_aliases={8 + k: k for k in range(len(before))},
            scratch_shapes=[pltpu.VMEM((PART, DEEP), jnp.bfloat16)],
            compiler_params=params(24),
            cost_estimate=pl.CostEstimate(
                flops=900 * cells, transcendentals=190 * cells, bytes_accessed=4 * 39 * cells
            ),
            name="edge_cells" if pack else "inner_cells",
        )(
            *scalars, composition, pressure, pore_volume, mass_old,
            *((trans_x, trans_y, trans_z) if pack else ()), *before,
        )

    *begun, low, high = own(True, ())

    left, right, low, high, begun = lax.optimization_barrier((left, right, low, high, begun))
    corner = pl.BlockSpec((1, ROWS, LANES), lambda s: (half, 0, 0))
    columns, low, high = pl.pallas_call(
        column_cells,
        grid=(1,),
        in_specs=[smem] * 4 + [vmem] * 2 + [pl.BlockSpec(memory_space=pl.ANY)] * 2,
        out_specs=[vmem, corner, corner],
        out_shape=[jax.ShapeDtypeStruct((FIELDS, rows, LANES), f32), packed, packed],
        input_output_aliases={6: 1, 7: 2},
        compiler_params=params(16),
        name="column_cells",
    )(*scalars, left, right, low, high)
    above = moved(high, "areal", 1)
    below = moved(low, "areal", -1)

    mob, acc, mob_sum, acc_sum = own(False, begun)

    planes = pl.BlockSpec((COMPS, 2, rows, width), lambda s: (0, s, 0, 0))
    extended = pltpu.VMEM((depth, rows + ROWS, width + LANES), f32)
    above_faces = pltpu.VMEM((depth + 1, rows + ROWS, width + LANES), f32)
    return pl.pallas_call(
        finish,
        grid=(depth // 2,),
        in_specs=[vmem] * 12,
        out_specs=[planes, vmem],
        out_shape=[whole, sums],
        scratch_shapes=[
            pltpu.VMEM((COMPS, depth, ROWS, width), f32),
            pltpu.VMEM((COMPS, depth, rows, LANES), f32),
            *[extended] * 7,
            *[extended, extended, above_faces] * 2,
            extended,
        ],
        compiler_params=params(28),
        name="finish",
    )(
        columns, above, below,
        pressure, trans_x, trans_y, trans_z, pore_volume, mob_sum, acc_sum, mob, acc,
    )


def solution(mesh):
    placed = (
        P(None, "areal", "layer"),
        P(None, None, "areal", "layer"),
        P(None, None, "areal", "layer"),
        P(None, "areal", "layer"),
        P(None, "areal", "layer"),
        P(None, "areal", "layer"),
        P(None, "areal", "layer"),
        P(),
        P(),
        P(),
        P(None, "areal"),
    )
    return jax.shard_map(
        on_device,
        mesh=mesh,
        in_specs=placed,
        out_specs=(P(None, None, "areal", "layer"), P(None, "areal", "layer")),
        check_vma=False,
    )
```

```python
import functools

import jax
import jax.numpy as jnp
from jax import lax
from jax.experimental import pallas as pl
from jax.experimental.pallas import tpu as pltpu
from jax.sharding import PartitionSpec as P

SS_ITERS = 3
RR_ITERS = 3
LIGHT = 4
COMPS = 9
FIELDS = 16
PRESS, TX, TY, TZ, PORE, MASS = range(COMPS, FIELDS - 1)
H_MOB, H_PRESS, H_TX, H_TY, H_TZ, H_PORE, H_ACC = range(COMPS, FIELDS)
CORNER = (H_MOB, H_PRESS, H_TX, H_TY)
TIME_STEP = 4.0
COMPRESS = 0.2
VAPOUR_WEIGHT = 1.0 / 0.25
LANES = 128
ROWS = 8
MIB = 1024 * 1024
PART = (COMPS + 1) * ROWS
DEEP = 256
PLANES = 4


def rcp(x):
    return pltpu.reciprocal(x, approx=True)


def total_of(terms):
    terms = list(terms)
    while len(terms) > 1:
        terms = [a + b for a, b in zip(terms[::2], terms[1::2])] + (
            [terms[-1]] if len(terms) % 2 else []
        )
    return terms[0]


def inverses(values):
    out = []
    for a, b in zip(values[::2], values[1::2]):
        both = rcp(a * b)
        out += [b * both, a * both]
    if len(values) % 2:
        out.append(rcp(values[-1]))
    return out


def split(x):
    high = x.astype(jnp.bfloat16)
    return high, (x - high.astype(jnp.float32)).astype(jnp.bfloat16)


def mixing_operand(mix_ref):
    shape = (ROWS, DEEP)
    lane, row = lane_of(shape), row_of(shape)
    part = lax.div(lane, PART)
    within = lane - PART * part
    column = lax.div(within, ROWS)
    on = (within - ROWS * column == row) & (part < 3)
    blocks = []
    for i in range(COMPS):
        value = jnp.zeros(shape, jnp.float32)
        for j in range(COMPS):
            value = jnp.where(column == j, mix_ref[i, j], value)
        high, low = split(value)
        value = jnp.where(part == 2, low.astype(jnp.float32), high.astype(jnp.float32))
        blocks.append(jnp.where(on, value, 0.0))
    blocks.append(jnp.zeros(shape, jnp.float32))
    return jnp.concatenate(blocks, axis=0).astype(jnp.bfloat16)


def mixed(operand, spread):
    shape = spread[0].shape
    high, low = split(jnp.concatenate(spread + [jnp.zeros(shape, jnp.float32)], axis=0))
    tail = jnp.zeros((DEEP - 3 * PART, shape[1]), jnp.bfloat16)
    out = jnp.dot(
        operand,
        jnp.concatenate([high, low, high, tail], axis=0),
        preferred_element_type=jnp.float32,
    )
    return [out[ROWS * i : ROWS * (i + 1)] for i in range(COMPS)]


def flash(feed, pressure, signed, slope, operand):
    log_press = jnp.log(pressure)
    base = [signed[i] - slope[i] * log_press for i in range(COMPS)]
    spread = None
    for outer in range(SS_ITERS):
        if outer == 0:
            log_k = base
        else:
            mix = mixed(operand, spread)
            log_k = [base[i] - jnp.tanh(mix[i]) for i in range(COMPS)]
        w = inverses([jnp.exp(log_k[i]) - 1.0 for i in range(COMPS)])
        fraction = jnp.full(pressure.shape, 0.5, jnp.float32)
        for _ in range(RR_ITERS):
            q = inverses([w[i] + fraction for i in range(COMPS)])
            part = [feed[i] * q[i] for i in range(COMPS)]
            mismatch = total_of(part)
            gradient = total_of(part[i] * q[i] for i in range(COMPS))
            fraction = jnp.clip(fraction + mismatch * rcp(gradient), 0.0, 1.0)
        q = inverses([w[i] + fraction for i in range(COMPS)])
        spread = [feed[i] * q[i] for i in range(COMPS)]
    liquid_part = (1.0 - fraction) * (1.0 - fraction)
    vapour_part = VAPOUR_WEIGHT * (fraction * fraction)
    both = liquid_part + vapour_part
    return [spread[i] * (both * w[i] + vapour_part) for i in range(COMPS)]


def parameters(vol_ref, slope_ref):
    signed = [vol_ref[i] if i < LIGHT else -vol_ref[i] for i in range(COMPS)]
    return signed, [slope_ref[i] for i in range(COMPS)]


def lane_of(shape):
    return lax.broadcasted_iota(jnp.int32, shape, len(shape) - 1)


def row_of(shape):
    return lax.broadcasted_iota(jnp.int32, shape, len(shape) - 2)


def field_plane(index, z, comp, press, tx, ty, tz, pore, mass):
    if index < COMPS:
        return comp[index, z]
    if index == MASS:
        return total_of(mass[i, z] for i in range(COMPS))
    return {PRESS: press, TX: tx, TY: ty, TZ: tz, PORE: pore}[index][z]


def pack_columns(step, fields, out_ref):
    planes = fields[1].shape[0]
    shape = (out_ref.shape[0], LANES)
    lane = lane_of(shape)

    @pl.when(step == 0)
    def _():
        out_ref[...] = jnp.zeros(out_ref.shape, jnp.float32)

    for tile in range(FIELDS // 4):
        packed = jnp.zeros(shape, jnp.float32)
        for quarter in range(4):
            index = 4 * tile + quarter
            for z in range(planes if index <= MASS else 0):
                plane = field_plane(index, z, *fields)
                first, last = plane[:, :LANES], plane[:, -LANES:]
                at = 32 * quarter + 4 * z
                both = jnp.where(lane < LANES // 2, first, last)
                both = pltpu.roll(both, at + 2, 1)
                packed = jnp.where((lane >= at) & (lane < at + 4), both, packed)
        span = pl.ds(tile * LANES, LANES)
        out_ref[:, span] += pltpu.roll(packed, 4 * planes * step, 1)


def flash_tiles(tiles, flags, vol, slope, operand, comp, press, pore, mass, mob_ref, acc_ref, mob_sum, acc_sum):
    layer = lax.axis_index("layer")
    planes, _, width = press.shape
    places = [(z, slice(at, at + ROWS), tile) for z in range(planes) for at, tile in tiles]

    def beside(parts):
        return jnp.concatenate(parts, axis=1)

    def store(ref, value, *lead):
        for n, (z, at, _) in enumerate(places):
            ref[(*lead, z, at)] = value[:, n * width : (n + 1) * width]

    def load(ref, *lead):
        return beside([ref[(*lead, z, at)] for z, at, _ in places])

    raw = [load(comp, i) for i in range(COMPS)]
    inverse = rcp(total_of(raw))
    feed = [raw[i] * inverse for i in range(COMPS)]
    volume = load(pore)
    acc = [volume * feed[i] - load(mass, i) for i in range(COMPS)]
    for i in range(COMPS):
        store(acc_ref, acc[i], i)
    store(acc_sum, total_of(acc))
    some = total_of(flags[layer, 2 * tile] + flags[layer, 2 * tile + 1] for _, tile in tiles)

    @pl.when(some > 0)
    def _():
        signed, slopes = parameters(vol, slope)
        two = flash(feed, load(press), signed, slopes, operand[...])
        row = row_of((ROWS, width))
        marked = beside(
            [
                jnp.where(row < ROWS // 2, flags[layer, 2 * tile], flags[layer, 2 * tile + 1])
                for _, _, tile in places
            ]
        )
        mobility = [jnp.where(marked > 0, two[i], feed[i]) for i in range(COMPS)]
        for i in range(COMPS):
            store(mob_ref, mobility[i], i)
        store(mob_sum, total_of(mobility))

    @pl.when(some == 0)
    def _():
        for i in range(COMPS):
            store(mob_ref, feed[i], i)
        store(mob_sum, total_of(feed))


def edge_cells(
    flags, vol, slope, mix, comp, press, tx, ty, tz, pore, mass,
    mob_ref, acc_ref, mob_sum, acc_sum, packet, low_ref, high_ref, operand,
):
    step = pl.program_id(0)
    planes, rows, width = press.shape

    @pl.when(step == 0)
    def _():
        operand[...] = mixing_operand(mix)

    pack_columns(step, (comp, press, tx, ty, tz, pore, mass), packet)
    ends = ((0, 0), (rows - ROWS, rows // ROWS - 1))
    flash_tiles(
        ends, flags, vol, slope, operand, comp, press, pore, mass, mob_ref, acc_ref, mob_sum, acc_sum
    )
    rest_fields = {
        H_MOB: mob_sum, H_PRESS: press, H_TX: tx, H_TY: ty, H_TZ: tz, H_PORE: pore, H_ACC: acc_sum,
    }
    half = FIELDS // 2
    row = row_of((ROWS, width))
    for k in range(half):
        for pair in range(planes // 2):
            near, far = [], []
            for z in (2 * pair, 2 * pair + 1):
                here = mob_ref[k, z]
                beside = rest_fields[k + half][z] if k + half >= COMPS else mob_ref[k + half, z]
                low, high = here[:ROWS], here[rows - ROWS :]
                near.append(jnp.where(row % 4 >= 2, pltpu.roll(low, 2, 0), beside[:ROWS]))
                far.append(
                    jnp.where(
                        row % 4 < 2, pltpu.roll(high, 2, 0), pltpu.roll(beside[rows - ROWS :], 4, 0)
                    )
                )
            at = pl.ds(pair * ROWS, ROWS)
            low_ref[k, at, :] = jnp.where(row < 4, near[0], pltpu.roll(near[1], 4, 0))
            high_ref[k, at, :] = jnp.where(row < 4, far[0], pltpu.roll(far[1], 4, 0))


def inner_cells(start, flags, vol, slope, mix, comp, press, pore, mass, *rest):
    outs, operand = rest[-5:-1], rest[-1]

    @pl.when((pl.program_id(0) == 0) & (pl.program_id(1) == 0))
    def _():
        operand[...] = mixing_operand(mix)

    tiles = ((0, pl.program_id(0) + start),)
    flash_tiles(tiles, flags, vol, slope, operand, comp, press, pore, mass, *outs)


def column_cells(flags, vol, slope, mix, left, right, low_in, high_in, out_ref, low_ref, high_ref):
    del low_in, high_in
    rows = left.shape[0]
    shape = (rows, LANES)
    lane = lane_of(shape)
    raw = []
    for tile in range(FIELDS // 4):
        span = slice(tile * LANES, (tile + 1) * LANES)
        columns = jnp.where(lane % 4 < 2, left[:, span], right[:, span])
        for quarter in range(4):
            turn = (LANES - 32 * quarter) % LANES
            raw.append(pltpu.roll(columns, turn, 1) if turn else columns)
    total = total_of(raw[:COMPS])
    there = (total > 0.0) & (lane < 32)
    inverse = rcp(jnp.where(there, total, 1.0))
    feed = [jnp.where(there, raw[i] * inverse, 1.0) for i in range(COMPS)]
    signed, slopes = parameters(vol, slope)
    layer, layers = lax.axis_index("layer"), lax.axis_size("layer")
    bricks = flags.shape[1]
    brick = lax.div(row_of(shape), rows // bricks)
    marked = jnp.zeros(shape, jnp.int32)
    for b in range(bricks):
        both = jnp.where(
            lane % 4 < 2, flags[jnp.maximum(layer - 1, 0), b], flags[jnp.minimum(layer + 1, layers - 1), b]
        )
        marked = jnp.where(brick == b, both, marked)

    def beside(x):
        return jnp.concatenate([x[t : t + ROWS] for t in range(0, rows, ROWS)], axis=1)

    def above(x):
        return jnp.concatenate([x[:, t : t + LANES] for t in range(0, x.shape[1], LANES)], axis=0)

    pressure = jnp.where(there, raw[PRESS], 1.0)
    two = flash([beside(x) for x in feed], beside(pressure), signed, slopes, mixing_operand(mix))
    mobility = [
        jnp.where(there, jnp.where(marked > 0, above(two[i]), feed[i]), 0.0) for i in range(COMPS)
    ]
    fields = mobility + [total_of(mobility), raw[PRESS], raw[TX], raw[TY], raw[TZ], raw[PORE]]
    fields.append(raw[PORE] - raw[MASS])
    for k in range(FIELDS):
        out_ref[k] = fields[k]
    corner = fields[CORNER[0]]
    for quarter in range(1, 4):
        at = 32 * quarter
        corner = jnp.where(
            (lane >= at) & (lane < at + 32), pltpu.roll(fields[CORNER[quarter]], at, 1), corner
        )
    low_ref[0] = corner[:ROWS]
    high_ref[0] = corner[rows - ROWS :]


def finish(
    columns, above, below,
    press, tx, ty, tz, pore, mob_sum, acc_sum, mob, acc,
    res_ref, new_ref,
    rows_h, columns_h, e_press, e_tx, e_ty, e_tz, e_pore, e_mob, e_acc,
    g_x, g_y, g_z, c_x, c_y, c_z, first,
):
    step = pl.program_id(0)
    planes = res_ref.shape[1]
    depth, rows, width = press.shape
    layer, layers = lax.axis_index("layer"), lax.axis_size("layer")
    areal, areals = lax.axis_index("areal"), lax.axis_size("areal")
    half = FIELDS // 2
    tall, wide = rows + ROWS, width + LANES
    full = (tall, wide)
    own = (slice(0, rows), slice(0, width))
    extended = {
        H_MOB: (e_mob, mob_sum), H_PRESS: (e_press, press), H_TX: (e_tx, tx), H_TY: (e_ty, ty),
        H_TZ: (e_tz, tz), H_PORE: (e_pore, pore), H_ACC: (e_acc, acc_sum),
    }

    @pl.when(step == 0)
    def _():
        upper = row_of((rows, width)) % 4 < 2
        corner_row = row_of((ROWS, LANES))
        corners = jnp.where(corner_row < 4, below[half, 0:ROWS, 0:LANES], above[half, 0:ROWS, 0:LANES])
        for k in range(FIELDS):
            up, down = above[k % half], below[k % half]
            if k < half:
                beside = jnp.where(upper, up, down)
            else:
                beside = jnp.where(upper, pltpu.roll(up, rows - 2, 0), pltpu.roll(down, 2, 0))
            column = columns[k]
            for z in range(depth):
                at = (z // 2) * ROWS
                tile = pltpu.roll(beside[at : at + ROWS], 6 - 4 * (z % 2), 0)
                turn = (LANES + LANES - 2 - 4 * z) % LANES
                side = pltpu.roll(column, turn, 1)
                if k < COMPS:
                    rows_h[k, z] = tile
                    columns_h[k, z] = side
                else:
                    e_ref, own_ref = extended[k]
                    e_ref[z, pl.ds(0, rows), pl.ds(0, width)] = own_ref[z]
                    e_ref[z, pl.ds(rows, ROWS), pl.ds(0, width)] = tile
                    e_ref[z, pl.ds(0, rows), pl.ds(width, LANES)] = side
                    if k in CORNER:
                        turn = (turn + LANES - 32 * CORNER.index(k)) % LANES
                        e_ref[z, pl.ds(rows, ROWS), pl.ds(width, LANES)] = pltpu.roll(corners, turn, 1)

        end_x = (row_of(full) == rows - 1) & (areal == areals - 1)
        end_y = (lane_of(full) == width - 1) & (layer == layers - 1)
        scale = 0.5 * TIME_STEP
        nothing = jnp.zeros(full, jnp.float32)
        g_z[0] = nothing
        c_z[0] = nothing

        def update(z):
            p, m = e_press[z], e_mob[z]
            up, down = jnp.minimum(z + 1, depth - 1), jnp.maximum(z - 1, 0)
            strength_x = jnp.where(end_x, 0.0, scale * e_tx[z])
            strength_y = jnp.where(end_y, 0.0, scale * e_ty[z])
            strength_z = jnp.where(z < depth - 1, scale, 0.0) * e_tz[z]
            dx = p - pltpu.roll(p, tall - 1, 0)
            dy = p - pltpu.roll(p, wide - 1, 1)
            dz = p - e_press[up]
            cx = strength_x * (m + pltpu.roll(m, tall - 1, 0))
            cy = strength_y * (m + pltpu.roll(m, wide - 1, 1))
            cz = strength_z * (m + e_mob[up])
            cz_low = c_z[z]
            g_x[z], g_y[z], g_z[z + 1] = strength_x * dx, strength_y * dy, strength_z * dz
            c_x[z], c_y[z], c_z[z + 1] = cx, cy, cz
            fx, fy = cx * dx, cy * dy
            total = (
                e_acc[z]
                + (fx - pltpu.roll(fx, 1, 0))
                + (fy - pltpu.roll(fy, 1, 1))
                + (cz * dz + cz_low * (p - e_press[down]))
            )
            diagonal = (
                COMPRESS * e_pore[z]
                + (cx + pltpu.roll(cx, 1, 0))
                + (cy + pltpu.roll(cy, 1, 1))
                + (cz + cz_low)
            )
            inverse = rcp(jnp.where(diagonal > 0.0, diagonal, 1.0))
            first[z] = jnp.where(diagonal > 0.0, -total * inverse, 0.0)
            e_acc[z] = total
            e_pore[z] = inverse

        def second(z):
            here = first[z]
            up, down = jnp.minimum(z + 1, depth - 1), jnp.maximum(z - 1, 0)
            cx, cy = c_x[z], c_y[z]
            near = (
                (cx * pltpu.roll(here, tall - 1, 0))[own]
                + pltpu.roll(cx * here, 1, 0)[own]
                + (cy * pltpu.roll(here, wide - 1, 1))[own]
                + pltpu.roll(cy * here, 1, 1)[own]
                + (c_z[z + 1] * first[up] + c_z[z] * first[down])[own]
                - e_acc[z][own]
            )
            new_ref[z] = e_press[z][own] + near * e_pore[z][own]

        for body in (update, second):
            def pair(t, carry):
                body(2 * t)
                body(2 * t + 1)
                return carry

            lax.fori_loop(0, depth // 2, pair, 0)

    for plane in range(planes):
        z = step * planes + plane
        down, up = jnp.maximum(z - 1, 0), jnp.minimum(z + 1, depth - 1)
        gx, gy = g_x[z], g_y[z]
        gx_low = -pltpu.roll(gx, 1, 0)[own]
        gy_low = -pltpu.roll(gy, 1, 1)[own]
        gz, gz_low = g_z[z + 1][own], -g_z[z][own]
        gx, gy = gx[own], gy[own]
        middle = (gx + gx_low) + (gy + gy_low) + (gz + gz_low)
        for i in range(COMPS):
            here = mob[i, z]
            tall_here = jnp.concatenate([here, rows_h[i, z]], axis=0)
            wide_here = jnp.concatenate([here, columns_h[i, z]], axis=1)
            res_ref[i, plane] = (
                acc[i, z]
                + middle * here
                + gx * pltpu.roll(tall_here, tall - 1, 0)[own]
                + gx_low * pltpu.roll(tall_here, 1, 0)[own]
                + gy * pltpu.roll(wide_here, wide - 1, 1)[own]
                + gy_low * pltpu.roll(wide_here, 1, 1)[own]
                + gz * mob[i, up]
                + gz_low * mob[i, down]
            )


def on_device(
    pressure, composition, mass_old, pore_volume, trans_x, trans_y, trans_z,
    volatility, pressure_slope, mixing, two_phase,
):
    depth, rows, width = pressure.shape
    f32 = jnp.float32
    smem = pl.BlockSpec(memory_space=pltpu.SMEM)
    vmem = pl.BlockSpec(memory_space=pltpu.VMEM)
    half = FIELDS // 2

    def params(mib):
        return pltpu.CompilerParams(vmem_limit_bytes=mib * MIB)

    scalars = (two_phase, volatility, pressure_slope, mixing)

    def moved(block, axis, shift):
        count = lax.axis_size(axis)
        pairs = [(i, i + shift) for i in range(count) if 0 <= i + shift < count]
        return lax.ppermute(block, axis, pairs)

    whole = jax.ShapeDtypeStruct((COMPS, depth, rows, width), f32)
    sums = jax.ShapeDtypeStruct((depth, rows, width), f32)
    packed = jax.ShapeDtypeStruct((half + 1, 4 * depth, width), f32)
    tiles = rows // ROWS
    operand = pltpu.VMEM((PART, DEEP), jnp.bfloat16)
    plane = pl.BlockSpec((2, rows, width), lambda s: (s, 0, 0))
    planes = pl.BlockSpec((COMPS, 2, rows, width), lambda s: (0, s, 0, 0))
    edge = pl.BlockSpec((half, 2 * 4, width), lambda s: (0, s, 0))
    fields = (composition, pressure, trans_x, trans_y, trans_z, pore_volume, mass_old)
    *begun, packet, low, high = pl.pallas_call(
        edge_cells,
        grid=(depth // 2,),
        in_specs=[smem] * 4 + [planes, plane, plane, plane, plane, plane, planes],
        out_specs=[planes, planes, plane, plane, vmem, edge, edge],
        out_shape=[
            whole, whole, sums, sums, jax.ShapeDtypeStruct((rows, FIELDS * 32), f32), packed, packed
        ],
        scratch_shapes=[operand],
        compiler_params=params(24),
        name="edge_cells",
    )(*[pltpu.with_memory_space_constraint(x, pltpu.HBM) for x in (*scalars, *fields)])
    left = moved(packet, "layer", 1)
    right = moved(packet, "layer", -1)

    def inner(start, count, before):
        plane = pl.BlockSpec((PLANES, ROWS, width), lambda t, z: (z, start + t, 0))
        planes = pl.BlockSpec((COMPS, PLANES, ROWS, width), lambda t, z: (0, z, start + t, 0))
        cells = count * ROWS * depth * width
        return pl.pallas_call(
            functools.partial(inner_cells, start),
            grid=(count, depth // PLANES),
            in_specs=[smem] * 4
            + [planes, plane, plane, planes]
            + [pl.BlockSpec(memory_space=pl.ANY)] * len(before),
            out_specs=[planes, planes, plane, plane],
            out_shape=[whole, whole, sums, sums],
            input_output_aliases={8 + k: k for k in range(len(before))},
            scratch_shapes=[operand],
            compiler_params=params(24),
            cost_estimate=pl.CostEstimate(
                flops=900 * cells, transcendentals=190 * cells, bytes_accessed=4 * 39 * cells
            ),
            name="inner_cells",
        )(*scalars, composition, pressure, pore_volume, mass_old, *before)

    early = (tiles - 2) // 2
    begun = inner(1, early, begun)

    left, right, low, high, begun = lax.optimization_barrier((left, right, low, high, begun))
    corner = pl.BlockSpec((1, ROWS, LANES), lambda s: (half, 0, 0))
    columns, low, high = pl.pallas_call(
        column_cells,
        grid=(1,),
        in_specs=[smem] * 4 + [vmem] * 2 + [pl.BlockSpec(memory_space=pl.ANY)] * 2,
        out_specs=[vmem, corner, corner],
        out_shape=[jax.ShapeDtypeStruct((FIELDS, rows, LANES), f32), packed, packed],
        input_output_aliases={6: 1, 7: 2},
        compiler_params=params(16),
        name="column_cells",
    )(*scalars, left, right, low, high)
    above = moved(high, "areal", 1)
    below = moved(low, "areal", -1)

    mob, acc, mob_sum, acc_sum = inner(1 + early, tiles - 2 - early, begun)

    planes = pl.BlockSpec((COMPS, 2, rows, width), lambda s: (0, s, 0, 0))
    extended = pltpu.VMEM((depth, rows + ROWS, width + LANES), f32)
    above_faces = pltpu.VMEM((depth + 1, rows + ROWS, width + LANES), f32)
    return pl.pallas_call(
        finish,
        grid=(depth // 2,),
        in_specs=[vmem] * 12,
        out_specs=[planes, vmem],
        out_shape=[whole, sums],
        scratch_shapes=[
            pltpu.VMEM((COMPS, depth, ROWS, width), f32),
            pltpu.VMEM((COMPS, depth, rows, LANES), f32),
            *[extended] * 7,
            *[extended, extended, above_faces] * 2,
            extended,
        ],
        compiler_params=params(28),
        name="finish",
    )(
        columns, above, below,
        pressure, trans_x, trans_y, trans_z, pore_volume, mob_sum, acc_sum, mob, acc,
    )


def solution(mesh):
    placed = (
        P(None, "areal", "layer"),
        P(None, None, "areal", "layer"),
        P(None, None, "areal", "layer"),
        P(None, "areal", "layer"),
        P(None, "areal", "layer"),
        P(None, "areal", "layer"),
        P(None, "areal", "layer"),
        P(),
        P(),
        P(),
        P(None, "areal"),
    )
    return jax.shard_map(
        on_device,
        mesh=mesh,
        in_specs=placed,
        out_specs=(P(None, None, "areal", "layer"), P(None, "areal", "layer")),
        check_vma=False,
    )
```

```python
import functools

import jax
import jax.numpy as jnp
from jax import lax
from jax.experimental import pallas as pl
from jax.experimental.pallas import tpu as pltpu
from jax.sharding import PartitionSpec as P

SS_ITERS = 3
RR_ITERS = 3
LIGHT = 4
COMPS = 9
FIELDS = 16
MOB, PRESS, TX, TY, TZ, PORE, ACC = range(COMPS, FIELDS)
UNITS = (MOB, PRESS, TX, (0, 1), (2, 3), (4, 5), (6, 7), (8, TY), (TZ, PORE), (ACC, ACC))
DEPTH_SLOTS = 4
TIME_STEP = 4.0
COMPRESS = 0.2
VAPOUR_WEIGHT = 1.0 / 0.25
LANES = 128
ROWS = 8
MIB = 1024 * 1024
PART = (COMPS + 1) * ROWS
DEEP = 256
PLANES = 4


def rcp(x):
    return pltpu.reciprocal(x, approx=True)


def total_of(terms):
    terms = list(terms)
    while len(terms) > 1:
        terms = [a + b for a, b in zip(terms[::2], terms[1::2])] + (
            [terms[-1]] if len(terms) % 2 else []
        )
    return terms[0]


def split(x):
    high = x.astype(jnp.bfloat16)
    return high, (x - high.astype(jnp.float32)).astype(jnp.bfloat16)


def mixing_operand(mix_ref):
    shape = (ROWS, DEEP)
    lane, row = lane_of(shape), row_of(shape)
    part = lax.div(lane, PART)
    within = lane - PART * part
    column = lax.div(within, ROWS)
    on = (within - ROWS * column == row) & (part < 3)
    blocks = []
    for i in range(COMPS):
        value = jnp.zeros(shape, jnp.float32)
        for j in range(COMPS):
            value = jnp.where(column == j, 2.0 * mix_ref[i, j], value)
        high, low = split(value)
        value = jnp.where(part == 2, low.astype(jnp.float32), high.astype(jnp.float32))
        blocks.append(jnp.where(on, value, 0.0))
    blocks.append(jnp.zeros(shape, jnp.float32))
    return jnp.concatenate(blocks, axis=0).astype(jnp.bfloat16)


def mixed(operand, spread):
    shape = spread[0].shape
    high, low = split(jnp.concatenate(spread + [jnp.zeros(shape, jnp.float32)], axis=0))
    tail = jnp.zeros((DEEP - 3 * PART, shape[1]), jnp.bfloat16)
    out = jnp.dot(
        operand,
        jnp.concatenate([high, low, high, tail], axis=0),
        preferred_element_type=jnp.float32,
    )
    return [out[ROWS * i : ROWS * (i + 1)] for i in range(COMPS)]


def flash(feed, pressure, signed, slope, operand):
    log_press = jnp.log(pressure)
    half_base = [0.5 * signed[i] - (0.5 * slope[i]) * log_press for i in range(COMPS)]
    spread = None
    for outer in range(SS_ITERS):
        if outer == 0:
            half_log = half_base
        else:
            mix = mixed(operand, spread)
            half_log = [half_base[i] - 0.5 * jnp.tanh(mix[i]) for i in range(COMPS)]
        t = [jnp.tanh(half_log[i]) for i in range(COMPS)]
        u = [rcp(t[i]) for i in range(COMPS)]
        psi = None
        for inner in range(RR_ITERS):
            q = t if inner == 0 else [rcp(u[i] + psi) for i in range(COMPS)]
            part = [feed[i] * q[i] for i in range(COMPS)]
            step = total_of(part) * rcp(total_of(part[i] * q[i] for i in range(COMPS)))
            psi = jnp.clip(step if inner == 0 else psi + step, -1.0, 1.0)
        spread = [feed[i] * rcp(u[i] + psi) for i in range(COMPS)]
    liquid_part = (0.25 * (1.0 - psi)) * (1.0 - psi)
    vapour_part = (0.25 * VAPOUR_WEIGHT * (1.0 + psi)) * (1.0 + psi)
    both, apart = vapour_part + liquid_part, vapour_part - liquid_part
    return [spread[i] * (both * u[i] + apart) for i in range(COMPS)]


def parameters(vol_ref, slope_ref):
    signed = [vol_ref[i] if i < LIGHT else -vol_ref[i] for i in range(COMPS)]
    return signed, [slope_ref[i] for i in range(COMPS)]


def lane_of(shape):
    return lax.broadcasted_iota(jnp.int32, shape, len(shape) - 1)


def row_of(shape):
    return lax.broadcasted_iota(jnp.int32, shape, len(shape) - 2)


def pack_rows(field, low_ref, high_ref, planes):
    row = None
    for n in range(0, len(UNITS), 2):
        lows, highs = [], []
        for z in range(planes):
            for unit in UNITS[n : n + 2]:
                if isinstance(unit, tuple):
                    (first_a, last_a), (first_b, last_b) = (field(k, z) for k in unit)
                    if row is None:
                        row = row_of(first_a.shape)
                    low = jnp.where(row == 2, pltpu.roll(first_a, 2, 0), pltpu.roll(first_b, 3, 0))
                    high = jnp.where(row == 0, pltpu.roll(last_b, 1, 0), pltpu.roll(last_a, 2, 0))
                else:
                    first, last = field(unit, z)
                    if row is None:
                        row = row_of(first.shape)
                    low, high = pltpu.roll(first, 2, 0), pltpu.roll(last, 2, 0)
                lows.append(low)
                highs.append(high)
        for pair in range(planes // 2):
            at = pl.ds(pair * ROWS, ROWS)
            l, h = lows[4 * pair : 4 * pair + 4], highs[4 * pair : 4 * pair + 4]
            if low_ref is not None:
                low_ref[n // 2, at, :] = jnp.where(
                    row < 4,
                    jnp.where(row >= 2, l[0], pltpu.roll(l[1], 6, 0)),
                    jnp.where(row >= 6, pltpu.roll(l[2], 4, 0), pltpu.roll(l[3], 2, 0)),
                )
            if high_ref is not None:
                high_ref[n // 2, at, :] = jnp.where(
                    row < 4,
                    jnp.where(row < 2, h[0], pltpu.roll(h[1], 2, 0)),
                    jnp.where(row < 6, pltpu.roll(h[2], 4, 0), pltpu.roll(h[3], 6, 0)),
                )


def row_tiles(above, below, wanted):
    shape = above.shape[1:]
    upper = row_of(shape) % DEPTH_SLOTS < 2
    tile_row = row_of((ROWS, shape[1]))
    depth = shape[0] // DEPTH_SLOTS
    tiles = {}
    for n, unit in enumerate(UNITS):
        fields = unit if isinstance(unit, tuple) else (unit,)
        if not any(k in wanted for k in fields):
            continue
        up, down = above[n // 2], below[n // 2]
        if n % 2:
            up, down = pltpu.roll(up, shape[0] - 2, 0), pltpu.roll(down, 2, 0)
        both = jnp.where(upper, up, down)
        for z in range(depth):
            at = (z // 2) * ROWS
            tile = pltpu.roll(both[at : at + ROWS], 6 - 4 * (z % 2), 0)
            if fields[0] in wanted:
                tiles.setdefault(fields[0], []).append(tile)
            if fields[-1] in wanted and fields[-1] != fields[0]:
                other = jnp.where(tile_row < 4, pltpu.roll(tile, ROWS - 1, 0), pltpu.roll(tile, 1, 0))
                tiles.setdefault(fields[-1], []).append(other)
    return tiles


def pack_columns(above, below, mob, mob_sum, press, tx, ty, tz, pore, acc_sum, out_ref):
    depth, rows, width = press.shape
    shape = (rows + ROWS, LANES)
    lane = lane_of(shape)
    corner_fields = {MOB: mob_sum, PRESS: press, TX: tx, TY: ty}
    others = {TZ: tz, PORE: pore, ACC: acc_sum, **corner_fields}
    corners = row_tiles(above, below, corner_fields)
    nothing = jnp.zeros((ROWS, LANES), jnp.float32)
    for tile in range(FIELDS // 4):
        packed = jnp.zeros(shape, jnp.float32)
        for quarter in range(4):
            k = 4 * tile + quarter
            for z in range(depth):
                plane = mob[k, z] if k < COMPS else others[k][z]
                first, last = plane[:, :LANES], plane[:, -LANES:]
                at = 32 * quarter + 4 * z
                if k < COMPS:
                    one = pltpu.roll(jnp.concatenate([first, nothing], axis=0), at + 1, 1)
                    two = pltpu.roll(jnp.concatenate([last, nothing], axis=0), (at + 3) % LANES, 1)
                    packed = jnp.where(lane == at + 1, one, jnp.where(lane == at + 2, two, packed))
                    continue
                both = jnp.where(lane_of(first.shape) < LANES // 2, first, last)
                end = nothing
                if k in corner_fields:
                    end = corners[k][z]
                    end = jnp.where(lane_of(end[:, :LANES].shape) < LANES // 2, end[:, :LANES], end[:, -LANES:])
                both = pltpu.roll(jnp.concatenate([both, end], axis=0), (at + 2) % LANES, 1)
                packed = jnp.where((lane >= at) & (lane < at + 4), both, packed)
        out_ref[:, tile * LANES : (tile + 1) * LANES] = packed


def side_fields(left, right):
    fields = []
    lane = lane_of((left.shape[0], LANES))
    for tile in range(FIELDS // 4):
        span = slice(tile * LANES, (tile + 1) * LANES)
        l, r = left[:, span], right[:, span]
        one = jnp.where(lane % 4 < 2, r, l)
        other = jnp.where(lane % 4 < 2, l, r)
        for quarter in range(4):
            turn = (LANES - 32 * quarter) % LANES
            both = one if 4 * tile + quarter < COMPS else other
            fields.append(pltpu.roll(both, turn, 1) if turn else both)
    return fields


def own_cells(pack, flags, vol, slope, mix, comp, press, pore, mass, *rest):
    per_tile = 2
    if pack:
        tx, ty, tz, mob_ref, acc_ref, mob_sum, acc_sum, low_ref, high_ref, operand = rest
        tile_row = pl.program_id(0) * (flags.shape[1] // per_tile - 1)
    else:
        mob_ref, acc_ref, mob_sum, acc_sum, operand = rest[-5:]
        tile_row = pl.program_id(0) + 1
    layer = lax.axis_index("layer")
    signed, slopes = parameters(vol, slope)
    planes, _, width = press.shape

    @pl.when((pl.program_id(0) == 0) & (pl.program_id(1) == 0))
    def _():
        operand[...] = mixing_operand(mix)

    raw = [comp[i] for i in range(COMPS)]
    inverse = rcp(total_of(raw))
    feed = [raw[i] * inverse for i in range(COMPS)]
    volume = pore[...]
    acc = [volume * feed[i] - mass[i] for i in range(COMPS)]
    for i in range(COMPS):
        acc_ref[i] = acc[i]
    acc_sum[...] = total_of(acc)
    tile_flags = [flags[layer, tile_row * per_tile + b] for b in range(per_tile)]
    some = tile_flags[0] + tile_flags[1]

    @pl.when(some > 0)
    def _():
        def beside(x):
            return jnp.concatenate([x[z] for z in range(planes)], axis=1)

        here = [beside(feed[i]) for i in range(COMPS)]
        two = flash(here, beside(press), signed, slopes, operand[...])
        marked = jnp.where(row_of(here[0].shape) < ROWS // per_tile, tile_flags[0], tile_flags[1])
        mobility = [jnp.where(marked > 0, two[i], here[i]) for i in range(COMPS)]
        total = total_of(mobility)
        for z in range(planes):
            span = slice(z * width, (z + 1) * width)
            for i in range(COMPS):
                mob_ref[i, z] = mobility[i][:, span]
            mob_sum[z] = total[:, span]

    @pl.when(some == 0)
    def _():
        for i in range(COMPS):
            mob_ref[i] = feed[i]
        mob_sum[...] = total_of(feed)

    if not pack:
        return
    rest_fields = {
        MOB: mob_sum, PRESS: press, TX: tx, TY: ty, TZ: tz, PORE: pore, ACC: acc_sum,
    }

    def field(k, z):
        here = mob_ref[k, z] if k < COMPS else rest_fields[k][z]
        return here, here

    @pl.when(pl.program_id(0) == 0)
    def _():
        pack_rows(field, low_ref, None, planes)

    @pl.when(pl.program_id(0) == 1)
    def _():
        pack_rows(field, None, high_ref, planes)


def near_residual(above, below, press, tx, ty, tz, mob, acc, out_ref, rows_h, press_h, tx_h):
    step = pl.program_id(0)
    planes = out_ref.shape[1]
    depth, rows, width = press.shape
    areal, areals = lax.axis_index("areal"), lax.axis_size("areal")
    tall = rows + ROWS

    @pl.when(step == 0)
    def _():
        tiles = row_tiles(above, below, (PRESS, TX, *range(COMPS)))
        for z in range(depth):
            press_h[z] = tiles[PRESS][z]
            tx_h[z] = tiles[TX][z]
            for i in range(COMPS):
                rows_h[i, z] = tiles[i][z]

    own = slice(0, rows)
    scale = 0.5 * TIME_STEP
    end_x = (row_of((tall, width)) == rows - 1) & (areal == areals - 1)
    end_y = lane_of((rows, width)) == width - 1
    for plane in range(planes):
        z = step * planes + plane
        down, up = jnp.maximum(z - 1, 0), jnp.minimum(z + 1, depth - 1)
        p = press[z]
        p_tall = jnp.concatenate([p, press_h[z]], axis=0)
        t_tall = jnp.where(end_x, 0.0, scale * jnp.concatenate([tx[z], tx_h[z]], axis=0))
        gx = t_tall * (p_tall - pltpu.roll(p_tall, tall - 1, 0))
        gx_low = -pltpu.roll(gx, 1, 0)[own]
        gx = gx[own]
        gy = jnp.where(end_y, 0.0, scale * ty[z]) * (p - pltpu.roll(p, width - 1, 1))
        gy_low = -pltpu.roll(gy, 1, 1)
        gz = jnp.where(z < depth - 1, scale, 0.0) * tz[z] * (p - press[up])
        gz_low = jnp.where(z > 0, scale, 0.0) * tz[down] * (p - press[down])
        middle = (gx + gx_low) + (gy + gy_low) + (gz + gz_low)
        for i in range(COMPS):
            here = mob[i, z]
            tall_here = jnp.concatenate([here, rows_h[i, z]], axis=0)
            out_ref[i, plane] = (
                acc[i, z]
                + middle * here
                + gx * pltpu.roll(tall_here, tall - 1, 0)[own]
                + gx_low * pltpu.roll(tall_here, 1, 0)[own]
                + gy * pltpu.roll(here, width - 1, 1)
                + gy_low * pltpu.roll(here, 1, 1)
                + gz * mob[i, up]
                + gz_low * mob[i, down]
            )


def finish(
    left, right, above, below,
    press, tx, ty, tz, pore, mob_sum, acc_sum, mob, near,
    res_ref, new_ref,
    side_h, e_press, e_tx, e_ty, e_tz, e_pore, e_mob, e_acc,
    c_x, c_y, c_z, first, g_first, g_last,
):
    step = pl.program_id(0)
    planes = res_ref.shape[1]
    depth, rows, width = press.shape
    layer, layers = lax.axis_index("layer"), lax.axis_size("layer")
    areal, areals = lax.axis_index("areal"), lax.axis_size("areal")
    tall, wide = rows + ROWS, width + LANES
    full = (tall, wide)
    own = (slice(0, rows), slice(0, width))

    @pl.when(step == 0)
    def _():
        extended = {
            MOB: (e_mob, mob_sum), PRESS: (e_press, press), TX: (e_tx, tx), TY: (e_ty, ty),
            TZ: (e_tz, tz), PORE: (e_pore, pore), ACC: (e_acc, acc_sum),
        }
        tiles = row_tiles(above, below, extended)
        columns = side_fields(left, right)
        for i in range(COMPS):
            side_h[i] = columns[i][:rows]
        for k, (e_ref, own_ref) in extended.items():
            for z in range(depth):
                e_ref[z, pl.ds(0, rows), pl.ds(0, width)] = own_ref[z]
                e_ref[z, pl.ds(rows, ROWS), pl.ds(0, width)] = tiles[k][z]
                e_ref[z, :, pl.ds(width, LANES)] = pltpu.roll(columns[k], LANES - 2 - 4 * z, 1)

        end_x = (row_of(full) == rows - 1) & (areal == areals - 1)
        end_y = (lane_of(full) == width - 1) & (layer == layers - 1)
        scale = 0.5 * TIME_STEP
        lane = lane_of((rows, LANES))
        c_z[0] = jnp.zeros(full, jnp.float32)

        def update(z):
            p, m = e_press[z], e_mob[z]
            up, down = jnp.minimum(z + 1, depth - 1), jnp.maximum(z - 1, 0)
            strength_x = jnp.where(end_x, 0.0, scale * e_tx[z])
            strength_y = jnp.where(end_y, 0.0, scale * e_ty[z])
            strength_z = jnp.where(z < depth - 1, scale, 0.0) * e_tz[z]
            dx = p - pltpu.roll(p, tall - 1, 0)
            dy = p - pltpu.roll(p, wide - 1, 1)
            dz = p - e_press[up]
            cx = strength_x * (m + pltpu.roll(m, tall - 1, 0))
            cy = strength_y * (m + pltpu.roll(m, wide - 1, 1))
            cz = strength_z * (m + e_mob[up])
            cz_low = c_z[z]
            gy = (strength_y * dy)[:rows]
            g_first[z] = jnp.where(lane == 0, -pltpu.roll(gy[:, width:], 1, 1), 0.0)
            g_last[z] = jnp.where(lane == LANES - 1, gy[:, width - LANES : width], 0.0)
            c_x[z], c_y[z], c_z[z + 1] = cx, cy, cz
            fx, fy = cx * dx, cy * dy
            total = (
                e_acc[z]
                + (fx - pltpu.roll(fx, 1, 0))
                + (fy - pltpu.roll(fy, 1, 1))
                + (cz * dz + cz_low * (p - e_press[down]))
            )
            diagonal = (
                COMPRESS * e_pore[z]
                + (cx + pltpu.roll(cx, 1, 0))
                + (cy + pltpu.roll(cy, 1, 1))
                + (cz + cz_low)
            )
            inverse = rcp(jnp.where(diagonal > 0.0, diagonal, 1.0))
            first[z] = jnp.where(diagonal > 0.0, -total * inverse, 0.0)
            e_acc[z] = total
            e_pore[z] = inverse

        def second(z):
            here = first[z]
            up, down = jnp.minimum(z + 1, depth - 1), jnp.maximum(z - 1, 0)
            cx, cy = c_x[z], c_y[z]
            gathered = (
                (cx * pltpu.roll(here, tall - 1, 0))[own]
                + pltpu.roll(cx * here, 1, 0)[own]
                + (cy * pltpu.roll(here, wide - 1, 1))[own]
                + pltpu.roll(cy * here, 1, 1)[own]
                + (c_z[z + 1] * first[up] + c_z[z] * first[down])[own]
                - e_acc[z][own]
            )
            new_ref[z] = e_press[z][own] + gathered * e_pore[z][own]

        for body in (update, second):
            def pair(t, carry):
                body(2 * t)
                body(2 * t + 1)
                return carry

            lax.fori_loop(0, depth // 2, pair, 0)

    low, high = slice(0, LANES), slice(width - LANES, width)
    for plane in range(planes):
        z = step * planes + plane
        for i in range(COMPS):
            side = pltpu.roll(side_h[i], LANES - 2 - 4 * z, 1)
            here = mob[i, z]
            for span, face in ((low, g_first[z]), (high, g_last[z])):
                res_ref[i, plane, :, span] = near[i, plane, :, span] + face * (here[:, span] + side)


def on_device(
    pressure, composition, mass_old, pore_volume, trans_x, trans_y, trans_z,
    volatility, pressure_slope, mixing, two_phase,
):
    depth, rows, width = pressure.shape
    f32 = jnp.float32
    smem = pl.BlockSpec(memory_space=pltpu.SMEM)
    vmem = pl.BlockSpec(memory_space=pltpu.VMEM)
    def params(mib):
        return pltpu.CompilerParams(vmem_limit_bytes=mib * MIB)

    scalars = (two_phase, volatility, pressure_slope, mixing)

    def moved(block, axis, shift):
        count = lax.axis_size(axis)
        pairs = [(i, i + shift) for i in range(count) if 0 <= i + shift < count]
        return lax.ppermute(block, axis, pairs)

    whole = jax.ShapeDtypeStruct((COMPS, depth, rows, width), f32)
    sums = jax.ShapeDtypeStruct((depth, rows, width), f32)
    packed = jax.ShapeDtypeStruct((len(UNITS) // 2, DEPTH_SLOTS * depth, width), f32)
    parts = depth // PLANES
    tiles = rows // ROWS

    fields = (composition, pressure, pore_volume, mass_old, trans_x, trans_y, trans_z)

    def pinned(x):
        return pltpu.with_memory_space_constraint(x, pltpu.HBM)

    def own(pack, before):
        tile_row = (lambda g: g * (tiles - 1)) if pack else (lambda g: g + 1)
        plane = pl.BlockSpec((PLANES, ROWS, width), lambda g, z: (z, tile_row(g), 0))
        planes = pl.BlockSpec((COMPS, PLANES, ROWS, width), lambda g, z: (0, z, tile_row(g), 0))
        block = (len(UNITS) // 2, DEPTH_SLOTS * PLANES, width)
        low = pl.BlockSpec(block, lambda g, z: (0, jnp.where(g == 0, z, parts - 1), 0))
        high = pl.BlockSpec(block, lambda g, z: (0, jnp.where(g == 0, 0, z), 0))
        count = 2 if pack else tiles - 2
        cells = count * ROWS * depth * width
        return pl.pallas_call(
            functools.partial(own_cells, pack),
            grid=(count, parts),
            in_specs=[smem] * 4
            + [planes, plane, plane, planes]
            + [plane] * (3 if pack else 0)
            + [pl.BlockSpec(memory_space=pl.ANY)] * len(before),
            out_specs=[planes, planes, plane, plane] + ([low, high] if pack else []),
            out_shape=[whole, whole, sums, sums] + ([packed, packed] if pack else []),
            input_output_aliases={8 + k: k for k in range(len(before))},
            scratch_shapes=[pltpu.VMEM((PART, DEEP), jnp.bfloat16)],
            compiler_params=params(24),
            cost_estimate=pl.CostEstimate(
                flops=900 * cells, transcendentals=190 * cells, bytes_accessed=4 * 39 * cells
            ),
            name="edge_cells" if pack else "inner_cells",
        )(*(pinned(x) if pack else x for x in (*scalars, *fields[: None if pack else 4])), *before)

    *begun, low, high = own(True, ())

    above = moved(high, "areal", 1)
    below = moved(low, "areal", -1)
    mob, acc, mob_sum, acc_sum = own(False, begun)

    packet = pl.pallas_call(
        pack_columns,
        in_specs=[vmem] * 10,
        out_specs=vmem,
        out_shape=jax.ShapeDtypeStruct((rows + ROWS, FIELDS * 32), f32),
        compiler_params=params(24),
        name="pack_columns",
    )(above, below, mob, mob_sum, pressure, trans_x, trans_y, trans_z, pore_volume, acc_sum)
    left = moved(packet, "layer", 1)
    right = moved(packet, "layer", -1)
    planes = pl.BlockSpec((COMPS, 2, rows, width), lambda s: (0, s, 0, 0))
    row_tile = pltpu.VMEM((depth, ROWS, width), f32)
    cells = rows * depth * width
    near = pl.pallas_call(
        near_residual,
        grid=(depth // 2,),
        in_specs=[vmem] * 8,
        out_specs=planes,
        out_shape=whole,
        scratch_shapes=[pltpu.VMEM((COMPS, depth, ROWS, width), f32), row_tile, row_tile],
        compiler_params=params(24),
        cost_estimate=pl.CostEstimate(flops=150 * cells, transcendentals=0, bytes_accessed=4 * 31 * cells),
        name="near_residual",
    )(above, below, pressure, trans_x, trans_y, trans_z, mob, acc)

    extended = pltpu.VMEM((depth, rows + ROWS, width + LANES), f32)
    side = pltpu.VMEM((depth, rows, LANES), f32)
    return pl.pallas_call(
        finish,
        grid=(depth // 2,),
        in_specs=[vmem] * 12 + [planes],
        out_specs=[planes, vmem],
        out_shape=[whole, sums],
        scratch_shapes=[
            pltpu.VMEM((COMPS, rows, LANES), f32),
            *[extended] * 9,
            pltpu.VMEM((depth + 1, rows + ROWS, width + LANES), f32),
            extended,
            side,
            side,
        ],
        compiler_params=params(28),
        name="finish",
    )(
        left, right, above, below,
        pressure, trans_x, trans_y, trans_z, pore_volume, mob_sum, acc_sum, mob, near,
    )


def solution(mesh):
    placed = (
        P(None, "areal", "layer"),
        P(None, None, "areal", "layer"),
        P(None, None, "areal", "layer"),
        P(None, "areal", "layer"),
        P(None, "areal", "layer"),
        P(None, "areal", "layer"),
        P(None, "areal", "layer"),
        P(),
        P(),
        P(),
        P(None, "areal"),
    )
    return jax.shard_map(
        on_device,
        mesh=mesh,
        in_specs=placed,
        out_specs=(P(None, None, "areal", "layer"), P(None, "areal", "layer")),
        check_vma=False,
    )
```

```python
import functools

import jax
import jax.numpy as jnp
from jax import lax
from jax.experimental import pallas as pl
from jax.experimental.pallas import tpu as pltpu
from jax.sharding import PartitionSpec as P

SS_ITERS = 3
RR_ITERS = 3
LIGHT = 4
COMPS = 9
FIELDS = 16
MOB, PRESS, TX, TY, TZ, PORE, ACC = range(COMPS, FIELDS)
UNITS = (MOB, PRESS, TX, (0, 1), (2, 3), (4, 5), (6, 7), (8, TY), (TZ, PORE), (ACC, ACC))
DEPTH_SLOTS = 4
TIME_STEP = 4.0
COMPRESS = 0.2
VAPOUR_WEIGHT = 1.0 / 0.25
LANES = 128
ROWS = 8
MIB = 1024 * 1024
PART = (COMPS + 1) * ROWS
DEEP = 256
PLANES = 4


def rcp(x):
    return pltpu.reciprocal(x, approx=True)


def total_of(terms):
    terms = list(terms)
    while len(terms) > 1:
        terms = [a + b for a, b in zip(terms[::2], terms[1::2])] + (
            [terms[-1]] if len(terms) % 2 else []
        )
    return terms[0]


def split(x):
    high = x.astype(jnp.bfloat16)
    return high, (x - high.astype(jnp.float32)).astype(jnp.bfloat16)


def mixing_operand(mix_ref):
    shape = (ROWS, DEEP)
    lane, row = lane_of(shape), row_of(shape)
    part = lax.div(lane, PART)
    within = lane - PART * part
    column = lax.div(within, ROWS)
    on = (within - ROWS * column == row) & (part < 3)
    blocks = []
    for i in range(COMPS):
        value = jnp.zeros(shape, jnp.float32)
        for j in range(COMPS):
            value = jnp.where(column == j, 2.0 * mix_ref[i, j], value)
        high, low = split(value)
        value = jnp.where(part == 2, low.astype(jnp.float32), high.astype(jnp.float32))
        blocks.append(jnp.where(on, value, 0.0))
    blocks.append(jnp.zeros(shape, jnp.float32))
    return jnp.concatenate(blocks, axis=0).astype(jnp.bfloat16)


def mixed(operand, spread):
    shape = spread[0].shape
    high, low = split(jnp.concatenate(spread + [jnp.zeros(shape, jnp.float32)], axis=0))
    tail = jnp.zeros((DEEP - 3 * PART, shape[1]), jnp.bfloat16)
    out = jnp.dot(
        operand,
        jnp.concatenate([high, low, high, tail], axis=0),
        preferred_element_type=jnp.float32,
    )
    return [out[ROWS * i : ROWS * (i + 1)] for i in range(COMPS)]


def flash(feed, pressure, signed, slope, operand):
    log_press = jnp.log(pressure)
    half_base = [0.5 * signed[i] - (0.5 * slope[i]) * log_press for i in range(COMPS)]
    spread = None
    for outer in range(SS_ITERS):
        if outer == 0:
            half_log = half_base
        else:
            mix = mixed(operand, spread)
            half_log = [half_base[i] - 0.5 * jnp.tanh(mix[i]) for i in range(COMPS)]
        t = [jnp.tanh(half_log[i]) for i in range(COMPS)]
        u = [rcp(t[i]) for i in range(COMPS)]
        psi = None
        for inner in range(RR_ITERS):
            q = t if inner == 0 else [rcp(u[i] + psi) for i in range(COMPS)]
            part = [feed[i] * q[i] for i in range(COMPS)]
            step = total_of(part) * rcp(total_of(part[i] * q[i] for i in range(COMPS)))
            psi = jnp.clip(step if inner == 0 else psi + step, -1.0, 1.0)
        spread = [feed[i] * rcp(u[i] + psi) for i in range(COMPS)]
    liquid_part = (0.25 * (1.0 - psi)) * (1.0 - psi)
    vapour_part = (0.25 * VAPOUR_WEIGHT * (1.0 + psi)) * (1.0 + psi)
    both, apart = vapour_part + liquid_part, vapour_part - liquid_part
    return [spread[i] * (both * u[i] + apart) for i in range(COMPS)]


def parameters(vol_ref, slope_ref):
    signed = [vol_ref[i] if i < LIGHT else -vol_ref[i] for i in range(COMPS)]
    return signed, [slope_ref[i] for i in range(COMPS)]


def lane_of(shape):
    return lax.broadcasted_iota(jnp.int32, shape, len(shape) - 1)


def row_of(shape):
    return lax.broadcasted_iota(jnp.int32, shape, len(shape) - 2)


def pack_rows(field, low_ref, high_ref, planes):
    row = None
    for n in range(0, len(UNITS), 2):
        lows, highs = [], []
        for z in range(planes):
            for unit in UNITS[n : n + 2]:
                if isinstance(unit, tuple):
                    (first_a, last_a), (first_b, last_b) = (field(k, z) for k in unit)
                    if row is None:
                        row = row_of(first_a.shape)
                    low = jnp.where(row == 2, pltpu.roll(first_a, 2, 0), pltpu.roll(first_b, 3, 0))
                    high = jnp.where(row == 0, pltpu.roll(last_b, 1, 0), pltpu.roll(last_a, 2, 0))
                else:
                    first, last = field(unit, z)
                    if row is None:
                        row = row_of(first.shape)
                    low, high = pltpu.roll(first, 2, 0), pltpu.roll(last, 2, 0)
                lows.append(low)
                highs.append(high)
        for pair in range(planes // 2):
            at = pl.ds(pair * ROWS, ROWS)
            l, h = lows[4 * pair : 4 * pair + 4], highs[4 * pair : 4 * pair + 4]
            if low_ref is not None:
                low_ref[n // 2, at, :] = jnp.where(
                    row < 4,
                    jnp.where(row >= 2, l[0], pltpu.roll(l[1], 6, 0)),
                    jnp.where(row >= 6, pltpu.roll(l[2], 4, 0), pltpu.roll(l[3], 2, 0)),
                )
            if high_ref is not None:
                high_ref[n // 2, at, :] = jnp.where(
                    row < 4,
                    jnp.where(row < 2, h[0], pltpu.roll(h[1], 2, 0)),
                    jnp.where(row < 6, pltpu.roll(h[2], 4, 0), pltpu.roll(h[3], 6, 0)),
                )


def row_tiles(above, below, wanted, start=0, stop=None):
    shape = above.shape[1:]
    upper = row_of(shape) % DEPTH_SLOTS < 2
    tile_row = row_of((ROWS, shape[1]))
    stop = stop or shape[0] // DEPTH_SLOTS
    tiles = {}
    for n, unit in enumerate(UNITS):
        fields = unit if isinstance(unit, tuple) else (unit,)
        if not any(k in wanted for k in fields):
            continue
        up, down = above[n // 2], below[n // 2]
        if n % 2:
            up, down = pltpu.roll(up, shape[0] - 2, 0), pltpu.roll(down, 2, 0)
        both = jnp.where(upper, up, down)
        for z in range(start, stop):
            at = (z // 2) * ROWS
            tile = pltpu.roll(both[at : at + ROWS], 6 - 4 * (z % 2), 0)
            if fields[0] in wanted:
                tiles.setdefault(fields[0], []).append(tile)
            if fields[-1] in wanted and fields[-1] != fields[0]:
                other = jnp.where(tile_row < 4, pltpu.roll(tile, ROWS - 1, 0), pltpu.roll(tile, 1, 0))
                tiles.setdefault(fields[-1], []).append(other)
    return tiles


def pack_columns(above, below, mob, mob_sum, press, tx, ty, tz, pore, acc_sum, out_ref):
    depth, rows, width = press.shape
    shape = (rows + ROWS, LANES)
    lane = lane_of(shape)
    corner_fields = {MOB: mob_sum, PRESS: press, TX: tx, TY: ty}
    others = {TZ: tz, PORE: pore, ACC: acc_sum, **corner_fields}
    corners = row_tiles(above, below, corner_fields)
    nothing = jnp.zeros((ROWS, LANES), jnp.float32)
    for tile in range(FIELDS // 4):
        packed = jnp.zeros(shape, jnp.float32)
        for quarter in range(4):
            k = 4 * tile + quarter
            for z in range(depth):
                plane = mob[k, z] if k < COMPS else others[k][z]
                first, last = plane[:, :LANES], plane[:, -LANES:]
                at = 32 * quarter + 4 * z
                if k < COMPS:
                    one = pltpu.roll(jnp.concatenate([first, nothing], axis=0), at + 1, 1)
                    two = pltpu.roll(jnp.concatenate([last, nothing], axis=0), (at + 3) % LANES, 1)
                    packed = jnp.where(lane == at + 1, one, jnp.where(lane == at + 2, two, packed))
                    continue
                both = jnp.where(lane_of(first.shape) < LANES // 2, first, last)
                end = nothing
                if k in corner_fields:
                    end = corners[k][z]
                    end = jnp.where(lane_of(end[:, :LANES].shape) < LANES // 2, end[:, :LANES], end[:, -LANES:])
                both = pltpu.roll(jnp.concatenate([both, end], axis=0), (at + 2) % LANES, 1)
                packed = jnp.where((lane >= at) & (lane < at + 4), both, packed)
        out_ref[:, tile * LANES : (tile + 1) * LANES] = packed


def side_fields(left, right):
    fields = []
    lane = lane_of((left.shape[0], LANES))
    for tile in range(FIELDS // 4):
        span = slice(tile * LANES, (tile + 1) * LANES)
        l, r = left[:, span], right[:, span]
        one = jnp.where(lane % 4 < 2, r, l)
        other = jnp.where(lane % 4 < 2, l, r)
        for quarter in range(4):
            turn = (LANES - 32 * quarter) % LANES
            both = one if 4 * tile + quarter < COMPS else other
            fields.append(pltpu.roll(both, turn, 1) if turn else both)
    return fields


def own_cells(edge, start, flags, vol, slope, mix, comp, press, pore, mass, *rest):
    per_tile = 2
    if edge:
        tx, ty, tz, mob_ref, acc_ref, mob_sum, acc_sum, low_ref, high_ref, operand = rest
        tile_row = pl.program_id(0) * (flags.shape[1] // per_tile - 1)

        @pl.when((pl.program_id(0) == 0) & (pl.program_id(1) == 0))
        def _():
            operand[...] = mixing_operand(mix)

    else:
        mob_ref, acc_ref, mob_sum, acc_sum = rest[-4:]
        operand = mix
        tile_row = pl.program_id(0) + start
    layer = lax.axis_index("layer")
    signed, slopes = parameters(vol, slope)
    planes, _, width = press.shape

    raw = [comp[i] for i in range(COMPS)]
    inverse = rcp(total_of(raw))
    feed = [raw[i] * inverse for i in range(COMPS)]
    volume = pore[...]
    acc = [volume * feed[i] - mass[i] for i in range(COMPS)]
    for i in range(COMPS):
        acc_ref[i] = acc[i]
    acc_sum[...] = total_of(acc)
    tile_flags = [flags[layer, tile_row * per_tile + b] for b in range(per_tile)]
    some = tile_flags[0] + tile_flags[1]

    @pl.when(some > 0)
    def _():
        def beside(x):
            return jnp.concatenate([x[z] for z in range(planes)], axis=1)

        here = [beside(feed[i]) for i in range(COMPS)]
        two = flash(here, beside(press), signed, slopes, operand[...])
        marked = jnp.where(row_of(here[0].shape) < ROWS // per_tile, tile_flags[0], tile_flags[1])
        mobility = [jnp.where(marked > 0, two[i], here[i]) for i in range(COMPS)]
        total = total_of(mobility)
        for z in range(planes):
            span = slice(z * width, (z + 1) * width)
            for i in range(COMPS):
                mob_ref[i, z] = mobility[i][:, span]
            mob_sum[z] = total[:, span]

    @pl.when(some == 0)
    def _():
        for i in range(COMPS):
            mob_ref[i] = feed[i]
        mob_sum[...] = total_of(feed)

    if not edge:
        return
    rest_fields = {
        MOB: mob_sum, PRESS: press, TX: tx, TY: ty, TZ: tz, PORE: pore, ACC: acc_sum,
    }

    def field(k, z):
        here = mob_ref[k, z] if k < COMPS else rest_fields[k][z]
        return here, here

    @pl.when(pl.program_id(0) == 0)
    def _():
        pack_rows(field, low_ref, None, planes)

    @pl.when(pl.program_id(0) == 1)
    def _():
        pack_rows(field, None, high_ref, planes)


def near_residual(start, count, above, below, press, tx, ty, tz, mob, acc, *rest):
    out_ref, rows_h, press_h, tx_h = rest[-4:]
    step = pl.program_id(0)
    planes = out_ref.shape[1]
    depth, rows, width = press.shape
    areal, areals = lax.axis_index("areal"), lax.axis_size("areal")
    tall = rows + ROWS

    @pl.when(step == 0)
    def _():
        tiles = row_tiles(above, below, (PRESS, TX, *range(COMPS)), start, start + count)
        for n in range(count):
            press_h[n] = tiles[PRESS][n]
            tx_h[n] = tiles[TX][n]
            for i in range(COMPS):
                rows_h[i, n] = tiles[i][n]

    own = slice(0, rows)
    scale = 0.5 * TIME_STEP
    end_x = (row_of((tall, width)) == rows - 1) & (areal == areals - 1)
    end_y = lane_of((rows, width)) == width - 1
    for plane in range(planes):
        n = step * planes + plane
        z = start + n
        down, up = jnp.maximum(z - 1, 0), jnp.minimum(z + 1, depth - 1)
        p = press[z]
        p_tall = jnp.concatenate([p, press_h[n]], axis=0)
        t_tall = jnp.where(end_x, 0.0, scale * jnp.concatenate([tx[z], tx_h[n]], axis=0))
        gx = t_tall * (p_tall - pltpu.roll(p_tall, tall - 1, 0))
        gx_low = -pltpu.roll(gx, 1, 0)[own]
        gx = gx[own]
        gy = jnp.where(end_y, 0.0, scale * ty[z]) * (p - pltpu.roll(p, width - 1, 1))
        gy_low = -pltpu.roll(gy, 1, 1)
        gz = jnp.where(z < depth - 1, scale, 0.0) * tz[z] * (p - press[up])
        gz_low = jnp.where(z > 0, scale, 0.0) * tz[down] * (p - press[down])
        middle = (gx + gx_low) + (gy + gy_low) + (gz + gz_low)
        for i in range(COMPS):
            here = mob[i, z]
            tall_here = jnp.concatenate([here, rows_h[i, n]], axis=0)
            out_ref[i, plane] = (
                acc[i, z]
                + middle * here
                + gx * pltpu.roll(tall_here, tall - 1, 0)[own]
                + gx_low * pltpu.roll(tall_here, 1, 0)[own]
                + gy * pltpu.roll(here, width - 1, 1)
                + gy_low * pltpu.roll(here, 1, 1)
                + gz * mob[i, up]
                + gz_low * mob[i, down]
            )


def finish(
    left, right, above, below,
    press, tx, ty, tz, pore, mob_sum, acc_sum, mob, near,
    res_ref, new_ref,
    side_h, e_press, e_tx, e_ty, e_tz, e_pore, e_mob, e_acc,
    c_x, c_y, c_z, first, g_first, g_last,
):
    step = pl.program_id(0)
    planes = res_ref.shape[1]
    depth, rows, width = press.shape
    layer, layers = lax.axis_index("layer"), lax.axis_size("layer")
    areal, areals = lax.axis_index("areal"), lax.axis_size("areal")
    tall, wide = rows + ROWS, width + LANES
    full = (tall, wide)
    own = (slice(0, rows), slice(0, width))

    @pl.when(step == 0)
    def _():
        extended = {
            MOB: (e_mob, mob_sum), PRESS: (e_press, press), TX: (e_tx, tx), TY: (e_ty, ty),
            TZ: (e_tz, tz), PORE: (e_pore, pore), ACC: (e_acc, acc_sum),
        }
        tiles = row_tiles(above, below, extended)
        columns = side_fields(left, right)
        for i in range(COMPS):
            side_h[i] = columns[i][:rows]
        for k, (e_ref, own_ref) in extended.items():
            for z in range(depth):
                e_ref[z, pl.ds(0, rows), pl.ds(0, width)] = own_ref[z]
                e_ref[z, pl.ds(rows, ROWS), pl.ds(0, width)] = tiles[k][z]
                e_ref[z, :, pl.ds(width, LANES)] = pltpu.roll(columns[k], LANES - 2 - 4 * z, 1)

        end_x = (row_of(full) == rows - 1) & (areal == areals - 1)
        end_y = (lane_of(full) == width - 1) & (layer == layers - 1)
        scale = 0.5 * TIME_STEP
        lane = lane_of((rows, LANES))
        c_z[0] = jnp.zeros(full, jnp.float32)

        def update(z):
            p, m = e_press[z], e_mob[z]
            up, down = jnp.minimum(z + 1, depth - 1), jnp.maximum(z - 1, 0)
            strength_x = jnp.where(end_x, 0.0, scale * e_tx[z])
            strength_y = jnp.where(end_y, 0.0, scale * e_ty[z])
            strength_z = jnp.where(z < depth - 1, scale, 0.0) * e_tz[z]
            dx = p - pltpu.roll(p, tall - 1, 0)
            dy = p - pltpu.roll(p, wide - 1, 1)
            dz = p - e_press[up]
            cx = strength_x * (m + pltpu.roll(m, tall - 1, 0))
            cy = strength_y * (m + pltpu.roll(m, wide - 1, 1))
            cz = strength_z * (m + e_mob[up])
            cz_low = c_z[z]
            gy = (strength_y * dy)[:rows]
            g_first[z] = jnp.where(lane == 0, -pltpu.roll(gy[:, width:], 1, 1), 0.0)
            g_last[z] = jnp.where(lane == LANES - 1, gy[:, width - LANES : width], 0.0)
            c_x[z], c_y[z], c_z[z + 1] = cx, cy, cz
            fx, fy = cx * dx, cy * dy
            total = (
                e_acc[z]
                + (fx - pltpu.roll(fx, 1, 0))
                + (fy - pltpu.roll(fy, 1, 1))
                + (cz * dz + cz_low * (p - e_press[down]))
            )
            diagonal = (
                COMPRESS * e_pore[z]
                + (cx + pltpu.roll(cx, 1, 0))
                + (cy + pltpu.roll(cy, 1, 1))
                + (cz + cz_low)
            )
            inverse = rcp(jnp.where(diagonal > 0.0, diagonal, 1.0))
            first[z] = jnp.where(diagonal > 0.0, -total * inverse, 0.0)
            e_acc[z] = total
            e_pore[z] = inverse

        def second(z):
            here = first[z]
            up, down = jnp.minimum(z + 1, depth - 1), jnp.maximum(z - 1, 0)
            cx, cy = c_x[z], c_y[z]
            gathered = (
                (cx * pltpu.roll(here, tall - 1, 0))[own]
                + pltpu.roll(cx * here, 1, 0)[own]
                + (cy * pltpu.roll(here, wide - 1, 1))[own]
                + pltpu.roll(cy * here, 1, 1)[own]
                + (c_z[z + 1] * first[up] + c_z[z] * first[down])[own]
                - e_acc[z][own]
            )
            new_ref[z] = e_press[z][own] + gathered * e_pore[z][own]

        for body in (update, second):
            def pair(t, carry):
                body(2 * t)
                body(2 * t + 1)
                return carry

            lax.fori_loop(0, depth // 2, pair, 0)

    low, high = slice(0, LANES), slice(width - LANES, width)
    for plane in range(planes):
        z = step * planes + plane
        for i in range(COMPS):
            side = pltpu.roll(side_h[i], LANES - 2 - 4 * z, 1)
            here = mob[i, z]
            for span, face in ((low, g_first[z]), (high, g_last[z])):
                res_ref[i, plane, :, span] = near[i, plane, :, span] + face * (here[:, span] + side)


def on_device(
    pressure, composition, mass_old, pore_volume, trans_x, trans_y, trans_z,
    volatility, pressure_slope, mixing, two_phase,
):
    depth, rows, width = pressure.shape
    f32 = jnp.float32
    smem = pl.BlockSpec(memory_space=pltpu.SMEM)
    vmem = pl.BlockSpec(memory_space=pltpu.VMEM)
    def params(mib):
        return pltpu.CompilerParams(vmem_limit_bytes=mib * MIB)

    scalars = (two_phase, volatility, pressure_slope, mixing)

    def moved(block, axis, shift):
        count = lax.axis_size(axis)
        pairs = [(i, i + shift) for i in range(count) if 0 <= i + shift < count]
        return lax.ppermute(block, axis, pairs)

    whole = jax.ShapeDtypeStruct((COMPS, depth, rows, width), f32)
    sums = jax.ShapeDtypeStruct((depth, rows, width), f32)
    packed = jax.ShapeDtypeStruct((len(UNITS) // 2, DEPTH_SLOTS * depth, width), f32)
    parts = depth // PLANES
    tiles = rows // ROWS

    fields = (composition, pressure, pore_volume, mass_old, trans_x, trans_y, trans_z)

    def pinned(x):
        return pltpu.with_memory_space_constraint(x, pltpu.HBM)

    operand = jax.ShapeDtypeStruct((PART, DEEP), jnp.bfloat16)
    anywhere = pl.BlockSpec(memory_space=pl.ANY)

    def own(edge, start, count, small, before):
        tile_row = (lambda t: t * (tiles - 1)) if edge else (lambda t: start + t)
        plane = pl.BlockSpec((PLANES, ROWS, width), lambda t, z: (z, tile_row(t), 0))
        planes = pl.BlockSpec((COMPS, PLANES, ROWS, width), lambda t, z: (0, z, tile_row(t), 0))
        block = (len(UNITS) // 2, DEPTH_SLOTS * PLANES, width)
        low = pl.BlockSpec(block, lambda t, z: (0, jnp.where(t == 0, z, parts - 1), 0))
        high = pl.BlockSpec(block, lambda t, z: (0, jnp.where(t == 0, 0, z), 0))
        cells = count * ROWS * depth * width
        used = fields if edge else fields[:4]
        return pl.pallas_call(
            functools.partial(own_cells, edge, start),
            grid=(count, parts),
            in_specs=[smem] * 3
            + [smem if edge else vmem]
            + [planes, plane, plane, planes]
            + [plane] * (len(used) - 4)
            + [anywhere] * len(before),
            out_specs=[planes, planes, plane, plane] + ([low, high, vmem] if edge else []),
            out_shape=[whole, whole, sums, sums] + ([packed, packed, operand] if edge else []),
            input_output_aliases={4 + len(used) + k: k for k in range(len(before))},
            compiler_params=params(24),
            cost_estimate=pl.CostEstimate(flops=cells, transcendentals=0, bytes_accessed=cells),
            name="edge_cells" if edge else "inner_cells",
        )(*(pinned(x) if edge else x for x in (*small, *used)), *before)

    *begun, low, high, mixer = own(True, 0, 2, scalars, ())
    small = (*scalars[:3], mixer)
    early = (tiles - 2) // 2
    below = moved(low, "areal", -1)
    begun = own(False, 1, early, small, begun)
    high, begun = lax.optimization_barrier((high, begun))
    above = moved(high, "areal", 1)
    mob, acc, mob_sum, acc_sum = own(False, 1 + early, tiles - 2 - early, small, begun)

    packet = pl.pallas_call(
        pack_columns,
        in_specs=[vmem] * 10,
        out_specs=vmem,
        out_shape=jax.ShapeDtypeStruct((rows + ROWS, FIELDS * 32), f32),
        compiler_params=params(24),
        name="pack_columns",
    )(above, below, mob, mob_sum, pressure, trans_x, trans_y, trans_z, pore_volume, acc_sum)

    def residual(start, count, before):
        cells = rows * count * width
        row_tile = pltpu.VMEM((count, ROWS, width), f32)
        return pl.pallas_call(
            functools.partial(near_residual, start, count),
            grid=(count // 2,),
            in_specs=[vmem] * 8 + [anywhere] * len(before),
            out_specs=pl.BlockSpec((COMPS, 2, rows, width), lambda s: (0, s + start // 2, 0, 0)),
            out_shape=whole,
            input_output_aliases={8: 0} if before else {},
            scratch_shapes=[pltpu.VMEM((COMPS, count, ROWS, width), f32), row_tile, row_tile],
            compiler_params=params(24),
            cost_estimate=pl.CostEstimate(
                flops=150 * cells, transcendentals=0, bytes_accessed=4 * 31 * cells
            ),
            name="near_residual",
        )(above, below, pressure, trans_x, trans_y, trans_z, mob, acc, *before)

    left = moved(packet, "layer", 1)
    near = residual(0, depth // 2, ())
    packet, near = lax.optimization_barrier((packet, near))
    right = moved(packet, "layer", -1)
    near = residual(depth // 2, depth - depth // 2, (near,))
    planes = pl.BlockSpec((COMPS, 2, rows, width), lambda s: (0, s, 0, 0))

    extended = pltpu.VMEM((depth, rows + ROWS, width + LANES), f32)
    side = pltpu.VMEM((depth, rows, LANES), f32)
    return pl.pallas_call(
        finish,
        grid=(depth // 2,),
        in_specs=[vmem] * 12 + [planes],
        out_specs=[planes, vmem],
        out_shape=[whole, sums],
        scratch_shapes=[
            pltpu.VMEM((COMPS, rows, LANES), f32),
            *[extended] * 9,
            pltpu.VMEM((depth + 1, rows + ROWS, width + LANES), f32),
            extended,
            side,
            side,
        ],
        compiler_params=params(28),
        name="finish",
    )(
        left, right, above, below,
        pressure, trans_x, trans_y, trans_z, pore_volume, mob_sum, acc_sum, mob, near,
    )


def solution(mesh):
    placed = (
        P(None, "areal", "layer"),
        P(None, None, "areal", "layer"),
        P(None, None, "areal", "layer"),
        P(None, "areal", "layer"),
        P(None, "areal", "layer"),
        P(None, "areal", "layer"),
        P(None, "areal", "layer"),
        P(),
        P(),
        P(),
        P(None, "areal"),
    )
    return jax.shard_map(
        on_device,
        mesh=mesh,
        in_specs=placed,
        out_specs=(P(None, None, "areal", "layer"), P(None, "areal", "layer")),
        check_vma=False,
    )
```

```python
import functools

import jax
import jax.numpy as jnp
from jax import lax
from jax.experimental import pallas as pl
from jax.experimental.pallas import tpu as pltpu
from jax.sharding import PartitionSpec as P

SS_ITERS = 3
RR_ITERS = 3
LIGHT = 4
COMPS = 9
FIELDS = 16
MOB, PRESS, TX, TY, TZ, PORE, ACC = range(COMPS, FIELDS)
UNITS = (MOB, PRESS, TX, (0, 1), (2, 3), (4, 5), (6, 7), (8, TY), (TZ, PORE), (ACC, ACC))
DEPTH_SLOTS = 4
TIME_STEP = 4.0
COMPRESS = 0.2
VAPOUR_WEIGHT = 1.0 / 0.25
LANES = 128
ROWS = 8
MIB = 1024 * 1024
PART = (COMPS + 1) * ROWS
DEEP = 256
PLANES = 4


def rcp(x):
    return pltpu.reciprocal(x, approx=True)


def total_of(terms):
    terms = list(terms)
    while len(terms) > 1:
        terms = [a + b for a, b in zip(terms[::2], terms[1::2])] + (
            [terms[-1]] if len(terms) % 2 else []
        )
    return terms[0]


def split(x):
    high = x.astype(jnp.bfloat16)
    return high, (x - high.astype(jnp.float32)).astype(jnp.bfloat16)


def mixing_operand(mix_ref):
    shape = (ROWS, DEEP)
    lane, row = lane_of(shape), row_of(shape)
    part = lax.div(lane, PART)
    within = lane - PART * part
    column = lax.div(within, ROWS)
    on = (within - ROWS * column == row) & (part < 3)
    blocks = []
    for i in range(COMPS):
        value = jnp.zeros(shape, jnp.float32)
        for j in range(COMPS):
            value = jnp.where(column == j, 2.0 * mix_ref[i, j], value)
        high, low = split(value)
        value = jnp.where(part == 2, low.astype(jnp.float32), high.astype(jnp.float32))
        blocks.append(jnp.where(on, value, 0.0))
    blocks.append(jnp.zeros(shape, jnp.float32))
    return jnp.concatenate(blocks, axis=0).astype(jnp.bfloat16)


def mixed(operand, spread):
    shape = spread[0].shape
    high, low = split(jnp.concatenate(spread + [jnp.zeros(shape, jnp.float32)], axis=0))
    tail = jnp.zeros((DEEP - 3 * PART, shape[1]), jnp.bfloat16)
    out = jnp.dot(
        operand,
        jnp.concatenate([high, low, high, tail], axis=0),
        preferred_element_type=jnp.float32,
    )
    return [out[ROWS * i : ROWS * (i + 1)] for i in range(COMPS)]


def flash(feed, pressure, signed, slope, operand):
    log_press = jnp.log(pressure)
    half_base = [0.5 * signed[i] - (0.5 * slope[i]) * log_press for i in range(COMPS)]
    spread = None
    for outer in range(SS_ITERS):
        if outer == 0:
            half_log = half_base
        else:
            mix = mixed(operand, spread)
            half_log = [half_base[i] - 0.5 * jnp.tanh(mix[i]) for i in range(COMPS)]
        t = [jnp.tanh(half_log[i]) for i in range(COMPS)]
        u = [rcp(t[i]) for i in range(COMPS)]
        psi = None
        for inner in range(RR_ITERS):
            q = t if inner == 0 else [rcp(u[i] + psi) for i in range(COMPS)]
            part = [feed[i] * q[i] for i in range(COMPS)]
            step = total_of(part) * rcp(total_of(part[i] * q[i] for i in range(COMPS)))
            psi = jnp.clip(step if inner == 0 else psi + step, -1.0, 1.0)
        spread = [feed[i] * rcp(u[i] + psi) for i in range(COMPS)]
    liquid_part = (0.25 * (1.0 - psi)) * (1.0 - psi)
    vapour_part = (0.25 * VAPOUR_WEIGHT * (1.0 + psi)) * (1.0 + psi)
    both, apart = vapour_part + liquid_part, vapour_part - liquid_part
    return [spread[i] * (both * u[i] + apart) for i in range(COMPS)]


def parameters(vol_ref, slope_ref):
    signed = [vol_ref[i] if i < LIGHT else -vol_ref[i] for i in range(COMPS)]
    return signed, [slope_ref[i] for i in range(COMPS)]


def lane_of(shape):
    return lax.broadcasted_iota(jnp.int32, shape, len(shape) - 1)


def row_of(shape):
    return lax.broadcasted_iota(jnp.int32, shape, len(shape) - 2)


def pack_rows(field, low_ref, high_ref, planes):
    row = None
    for n in range(0, len(UNITS), 2):
        lows, highs = [], []
        for z in range(planes):
            for unit in UNITS[n : n + 2]:
                if isinstance(unit, tuple):
                    (first_a, last_a), (first_b, last_b) = (field(k, z) for k in unit)
                    if row is None:
                        row = row_of(first_a.shape)
                    low = jnp.where(row == 2, pltpu.roll(first_a, 2, 0), pltpu.roll(first_b, 3, 0))
                    high = jnp.where(row == 0, pltpu.roll(last_b, 1, 0), pltpu.roll(last_a, 2, 0))
                else:
                    first, last = field(unit, z)
                    if row is None:
                        row = row_of(first.shape)
                    low, high = pltpu.roll(first, 2, 0), pltpu.roll(last, 2, 0)
                lows.append(low)
                highs.append(high)
        for pair in range(planes // 2):
            at = pl.ds(pair * ROWS, ROWS)
            l, h = lows[4 * pair : 4 * pair + 4], highs[4 * pair : 4 * pair + 4]
            if low_ref is not None:
                low_ref[n // 2, at, :] = jnp.where(
                    row < 4,
                    jnp.where(row >= 2, l[0], pltpu.roll(l[1], 6, 0)),
                    jnp.where(row >= 6, pltpu.roll(l[2], 4, 0), pltpu.roll(l[3], 2, 0)),
                )
            if high_ref is not None:
                high_ref[n // 2, at, :] = jnp.where(
                    row < 4,
                    jnp.where(row < 2, h[0], pltpu.roll(h[1], 2, 0)),
                    jnp.where(row < 6, pltpu.roll(h[2], 4, 0), pltpu.roll(h[3], 6, 0)),
                )


def row_tiles(one, two, wanted, start=0, stop=None):
    shape = one.shape[1:]
    upper = row_of(shape) % DEPTH_SLOTS < 2
    tile_row = row_of((ROWS, shape[1]))
    stop = stop or shape[0] // DEPTH_SLOTS
    tiles = {}
    for n, unit in enumerate(UNITS):
        fields = unit if isinstance(unit, tuple) else (unit,)
        if not any(k in wanted for k in fields):
            continue
        up, down = by_side("areal", one[n // 2], two[n // 2])
        if n % 2:
            up, down = pltpu.roll(up, shape[0] - 2, 0), pltpu.roll(down, 2, 0)
        both = jnp.where(upper, up, down)
        for z in range(start, stop):
            at = (z // 2) * ROWS
            tile = pltpu.roll(both[at : at + ROWS], 6 - 4 * (z % 2), 0)
            if fields[0] in wanted:
                tiles.setdefault(fields[0], []).append(tile)
            if fields[-1] in wanted and fields[-1] != fields[0]:
                other = jnp.where(tile_row < 4, pltpu.roll(tile, ROWS - 1, 0), pltpu.roll(tile, 1, 0))
                tiles.setdefault(fields[-1], []).append(other)
    return tiles


def pack_columns(rows_one, rows_two, mob, mob_sum, press, tx, ty, tz, pore, acc_sum, out_ref):
    depth, rows, width = press.shape
    shape = (rows + ROWS, LANES)
    lane = lane_of(shape)
    corner_fields = {MOB: mob_sum, PRESS: press, TX: tx, TY: ty}
    others = {TZ: tz, PORE: pore, ACC: acc_sum, **corner_fields}
    corners = row_tiles(rows_one, rows_two, corner_fields)
    nothing = jnp.zeros((ROWS, LANES), jnp.float32)
    for tile in range(FIELDS // 4):
        packed = jnp.zeros(shape, jnp.float32)
        for quarter in range(4):
            k = 4 * tile + quarter
            for z in range(depth):
                plane = mob[k, z] if k < COMPS else others[k][z]
                first, last = plane[:, :LANES], plane[:, -LANES:]
                at = 32 * quarter + 4 * z
                if k < COMPS:
                    one = pltpu.roll(jnp.concatenate([first, nothing], axis=0), at + 1, 1)
                    two = pltpu.roll(jnp.concatenate([last, nothing], axis=0), (at + 3) % LANES, 1)
                    packed = jnp.where(lane == at + 1, one, jnp.where(lane == at + 2, two, packed))
                    continue
                both = jnp.where(lane_of(first.shape) < LANES // 2, first, last)
                end = nothing
                if k in corner_fields:
                    end = corners[k][z]
                    end = jnp.where(lane_of(end[:, :LANES].shape) < LANES // 2, end[:, :LANES], end[:, -LANES:])
                both = pltpu.roll(jnp.concatenate([both, end], axis=0), (at + 2) % LANES, 1)
                packed = jnp.where((lane >= at) & (lane < at + 4), both, packed)
        out_ref[:, tile * LANES : (tile + 1) * LANES] = packed


def side_fields(one, two):
    fields = []
    lane = lane_of((one.shape[0], LANES))
    for tile in range(FIELDS // 4):
        span = slice(tile * LANES, (tile + 1) * LANES)
        l, r = by_side("layer", one[:, span], two[:, span])
        mobility = jnp.where(lane % 4 < 2, r, l)
        other = jnp.where(lane % 4 < 2, l, r)
        for quarter in range(4):
            turn = (LANES - 32 * quarter) % LANES
            both = mobility if 4 * tile + quarter < COMPS else other
            fields.append(pltpu.roll(both, turn, 1) if turn else both)
    return fields


def own_cells(edge, start, flags, vol, slope, mix, comp, press, pore, mass, *rest):
    per_tile = 2
    if edge:
        tx, ty, tz, mob_ref, acc_ref, mob_sum, acc_sum, one_ref, two_ref, operand = rest
        tile_row = pl.program_id(0) * (flags.shape[1] // per_tile - 1)

        @pl.when((pl.program_id(0) == 0) & (pl.program_id(1) == 0))
        def _():
            operand[...] = mixing_operand(mix)

    else:
        mob_ref, acc_ref, mob_sum, acc_sum = rest[-4:]
        operand = mix
        tile_row = pl.program_id(0) + start
    layer = lax.axis_index("layer")
    signed, slopes = parameters(vol, slope)
    planes, _, width = press.shape

    raw = [comp[i] for i in range(COMPS)]
    inverse = rcp(total_of(raw))
    feed = [raw[i] * inverse for i in range(COMPS)]
    volume = pore[...]
    acc = [volume * feed[i] - mass[i] for i in range(COMPS)]
    for i in range(COMPS):
        acc_ref[i] = acc[i]
    acc_sum[...] = total_of(acc)
    tile_flags = [flags[layer, tile_row * per_tile + b] for b in range(per_tile)]
    some = tile_flags[0] + tile_flags[1]

    @pl.when(some > 0)
    def _():
        def beside(x):
            return jnp.concatenate([x[z] for z in range(planes)], axis=1)

        here = [beside(feed[i]) for i in range(COMPS)]
        two = flash(here, beside(press), signed, slopes, operand[...])
        marked = jnp.where(row_of(here[0].shape) < ROWS // per_tile, tile_flags[0], tile_flags[1])
        mobility = [jnp.where(marked > 0, two[i], here[i]) for i in range(COMPS)]
        total = total_of(mobility)
        for z in range(planes):
            span = slice(z * width, (z + 1) * width)
            for i in range(COMPS):
                mob_ref[i, z] = mobility[i][:, span]
            mob_sum[z] = total[:, span]

    @pl.when(some == 0)
    def _():
        for i in range(COMPS):
            mob_ref[i] = feed[i]
        mob_sum[...] = total_of(feed)

    if not edge:
        return
    rest_fields = {
        MOB: mob_sum, PRESS: press, TX: tx, TY: ty, TZ: tz, PORE: pore, ACC: acc_sum,
    }

    def field(k, z):
        here = mob_ref[k, z] if k < COMPS else rest_fields[k][z]
        return here, here

    count = DEPTH_SLOTS * planes
    at = pl.multiple_of(pl.program_id(1) * count, count)
    odd = lax.axis_index("areal") % 2
    for end in range(2):
        for turn, ref in enumerate((one_ref, two_ref)):
            @pl.when((pl.program_id(0) == end) & ((odd == 1) == (end == turn)))
            def _():
                here = ref.at[:, pl.ds(at, count), :]
                pack_rows(field, *((here, None) if end == 0 else (None, here)), planes)


def by_side(axis, one, two):
    odd = lax.axis_index(axis) % 2 == 1
    return jnp.where(odd, one, two), jnp.where(odd, two, one)


def near_residual(start, count, rows_one, rows_two, press, tx, ty, tz, mob, acc, *rest):
    out_ref, rows_h, press_h, tx_h = rest[-4:]
    step = pl.program_id(0)
    planes = out_ref.shape[1]
    depth, rows, width = press.shape
    areal, areals = lax.axis_index("areal"), lax.axis_size("areal")
    tall = rows + ROWS

    @pl.when(step == 0)
    def _():
        tiles = row_tiles(rows_one, rows_two, (PRESS, TX, *range(COMPS)), start, start + count)
        for n in range(count):
            press_h[n] = tiles[PRESS][n]
            tx_h[n] = tiles[TX][n]
            for i in range(COMPS):
                rows_h[i, n] = tiles[i][n]

    own = slice(0, rows)
    scale = 0.5 * TIME_STEP
    end_x = (row_of((tall, width)) == rows - 1) & (areal == areals - 1)
    end_y = lane_of((rows, width)) == width - 1
    for plane in range(planes):
        n = step * planes + plane
        z = start + n
        down, up = jnp.maximum(z - 1, 0), jnp.minimum(z + 1, depth - 1)
        p = press[z]
        p_tall = jnp.concatenate([p, press_h[n]], axis=0)
        t_tall = jnp.where(end_x, 0.0, scale * jnp.concatenate([tx[z], tx_h[n]], axis=0))
        gx = t_tall * (p_tall - pltpu.roll(p_tall, tall - 1, 0))
        gx_low = -pltpu.roll(gx, 1, 0)[own]
        gx = gx[own]
        gy = jnp.where(end_y, 0.0, scale * ty[z]) * (p - pltpu.roll(p, width - 1, 1))
        gy_low = -pltpu.roll(gy, 1, 1)
        gz = jnp.where(z < depth - 1, scale, 0.0) * tz[z] * (p - press[up])
        gz_low = jnp.where(z > 0, scale, 0.0) * tz[down] * (p - press[down])
        middle = (gx + gx_low) + (gy + gy_low) + (gz + gz_low)
        for i in range(COMPS):
            here = mob[i, z]
            tall_here = jnp.concatenate([here, rows_h[i, n]], axis=0)
            out_ref[i, plane] = (
                acc[i, z]
                + middle * here
                + gx * pltpu.roll(tall_here, tall - 1, 0)[own]
                + gx_low * pltpu.roll(tall_here, 1, 0)[own]
                + gy * pltpu.roll(here, width - 1, 1)
                + gy_low * pltpu.roll(here, 1, 1)
                + gz * mob[i, up]
                + gz_low * mob[i, down]
            )


def finish(
    columns_one, columns_two, rows_one, rows_two,
    press, tx, ty, tz, pore, mob_sum, acc_sum, mob, near,
    res_ref, new_ref,
    side_h, e_press, e_tx, e_ty, e_tz, e_pore, e_mob, e_acc,
    c_x, c_y, c_z, first, g_first, g_last,
):
    step = pl.program_id(0)
    planes = res_ref.shape[1]
    depth, rows, width = press.shape
    layer, layers = lax.axis_index("layer"), lax.axis_size("layer")
    areal, areals = lax.axis_index("areal"), lax.axis_size("areal")
    tall, wide = rows + ROWS, width + LANES
    full = (tall, wide)
    own = (slice(0, rows), slice(0, width))

    @pl.when(step == 0)
    def _():
        extended = {
            MOB: (e_mob, mob_sum), PRESS: (e_press, press), TX: (e_tx, tx), TY: (e_ty, ty),
            TZ: (e_tz, tz), PORE: (e_pore, pore), ACC: (e_acc, acc_sum),
        }
        tiles = row_tiles(rows_one, rows_two, extended)
        columns = side_fields(columns_one, columns_two)
        for i in range(COMPS):
            side_h[i] = columns[i][:rows]
        for k, (e_ref, own_ref) in extended.items():
            for z in range(depth):
                e_ref[z, pl.ds(0, rows), pl.ds(0, width)] = own_ref[z]
                e_ref[z, pl.ds(rows, ROWS), pl.ds(0, width)] = tiles[k][z]
                e_ref[z, :, pl.ds(width, LANES)] = pltpu.roll(columns[k], LANES - 2 - 4 * z, 1)

        end_x = (row_of(full) == rows - 1) & (areal == areals - 1)
        end_y = (lane_of(full) == width - 1) & (layer == layers - 1)
        scale = 0.5 * TIME_STEP
        lane = lane_of((rows, LANES))
        c_z[0] = jnp.zeros(full, jnp.float32)

        def update(z):
            p, m = e_press[z], e_mob[z]
            up, down = jnp.minimum(z + 1, depth - 1), jnp.maximum(z - 1, 0)
            strength_x = jnp.where(end_x, 0.0, scale * e_tx[z])
            strength_y = jnp.where(end_y, 0.0, scale * e_ty[z])
            strength_z = jnp.where(z < depth - 1, scale, 0.0) * e_tz[z]
            dx = p - pltpu.roll(p, tall - 1, 0)
            dy = p - pltpu.roll(p, wide - 1, 1)
            dz = p - e_press[up]
            cx = strength_x * (m + pltpu.roll(m, tall - 1, 0))
            cy = strength_y * (m + pltpu.roll(m, wide - 1, 1))
            cz = strength_z * (m + e_mob[up])
            cz_low = c_z[z]
            gy = (strength_y * dy)[:rows]
            g_first[z] = jnp.where(lane == 0, -pltpu.roll(gy[:, width:], 1, 1), 0.0)
            g_last[z] = jnp.where(lane == LANES - 1, gy[:, width - LANES : width], 0.0)
            c_x[z], c_y[z], c_z[z + 1] = cx, cy, cz
            fx, fy = cx * dx, cy * dy
            total = (
                e_acc[z]
                + (fx - pltpu.roll(fx, 1, 0))
                + (fy - pltpu.roll(fy, 1, 1))
                + (cz * dz + cz_low * (p - e_press[down]))
            )
            diagonal = (
                COMPRESS * e_pore[z]
                + (cx + pltpu.roll(cx, 1, 0))
                + (cy + pltpu.roll(cy, 1, 1))
                + (cz + cz_low)
            )
            inverse = rcp(jnp.where(diagonal > 0.0, diagonal, 1.0))
            first[z] = jnp.where(diagonal > 0.0, -total * inverse, 0.0)
            e_acc[z] = total
            e_pore[z] = inverse

        def second(z):
            here = first[z]
            up, down = jnp.minimum(z + 1, depth - 1), jnp.maximum(z - 1, 0)
            cx, cy = c_x[z], c_y[z]
            gathered = (
                (cx * pltpu.roll(here, tall - 1, 0))[own]
                + pltpu.roll(cx * here, 1, 0)[own]
                + (cy * pltpu.roll(here, wide - 1, 1))[own]
                + pltpu.roll(cy * here, 1, 1)[own]
                + (c_z[z + 1] * first[up] + c_z[z] * first[down])[own]
                - e_acc[z][own]
            )
            new_ref[z] = e_press[z][own] + gathered * e_pore[z][own]

        for body in (update, second):
            def pair(t, carry):
                body(2 * t)
                body(2 * t + 1)
                return carry

            lax.fori_loop(0, depth // 2, pair, 0)

    low, high = slice(0, LANES), slice(width - LANES, width)
    for plane in range(planes):
        z = step * planes + plane
        for i in range(COMPS):
            side = pltpu.roll(side_h[i], LANES - 2 - 4 * z, 1)
            here = mob[i, z]
            for span, face in ((low, g_first[z]), (high, g_last[z])):
                res_ref[i, plane, :, span] = near[i, plane, :, span] + face * (here[:, span] + side)


def on_device(
    pressure, composition, mass_old, pore_volume, trans_x, trans_y, trans_z,
    volatility, pressure_slope, mixing, two_phase,
):
    depth, rows, width = pressure.shape
    f32 = jnp.float32
    smem = pl.BlockSpec(memory_space=pltpu.SMEM)
    vmem = pl.BlockSpec(memory_space=pltpu.VMEM)
    def params(mib):
        return pltpu.CompilerParams(vmem_limit_bytes=mib * MIB)

    scalars = (two_phase, volatility, pressure_slope, mixing)

    def swapped(block, axis, first):
        count = lax.axis_size(axis)
        pairs = [(i, i + 1) for i in range(first, count - 1, 2)]
        return lax.ppermute(block, axis, pairs + [(j, i) for i, j in pairs])

    whole = jax.ShapeDtypeStruct((COMPS, depth, rows, width), f32)
    sums = jax.ShapeDtypeStruct((depth, rows, width), f32)
    packed = jax.ShapeDtypeStruct((len(UNITS) // 2, DEPTH_SLOTS * depth, width), f32)
    parts = depth // PLANES
    tiles = rows // ROWS

    fields = (composition, pressure, pore_volume, mass_old, trans_x, trans_y, trans_z)

    def pinned(x):
        return pltpu.with_memory_space_constraint(x, pltpu.HBM)

    operand = jax.ShapeDtypeStruct((PART, DEEP), jnp.bfloat16)
    anywhere = pl.BlockSpec(memory_space=pl.ANY)

    def own(edge, start, count, small, before):
        tile_row = (lambda t: t * (tiles - 1)) if edge else (lambda t: start + t)
        plane = pl.BlockSpec((PLANES, ROWS, width), lambda t, z: (z, tile_row(t), 0))
        planes = pl.BlockSpec((COMPS, PLANES, ROWS, width), lambda t, z: (0, z, tile_row(t), 0))
        cells = count * ROWS * depth * width
        used = fields if edge else fields[:4]
        return pl.pallas_call(
            functools.partial(own_cells, edge, start),
            grid=(count, parts),
            in_specs=[smem] * 3
            + [smem if edge else vmem]
            + [planes, plane, plane, planes]
            + [plane] * (len(used) - 4)
            + [anywhere] * len(before),
            out_specs=[planes, planes, plane, plane] + ([vmem] * 3 if edge else []),
            out_shape=[whole, whole, sums, sums] + ([packed, packed, operand] if edge else []),
            input_output_aliases={4 + len(used) + k: k for k in range(len(before))},
            compiler_params=params(24),
            cost_estimate=pl.CostEstimate(
                flops=900 * cells, transcendentals=190 * cells, bytes_accessed=4 * 39 * cells
            ),
            name="edge_cells" if edge else "inner_cells",
        )(*(pinned(x) if edge else x for x in (*small, *used)), *before)

    *begun, one, two, mixer = own(True, 0, 2, scalars, ())
    rows_one = swapped(one, "areal", 0)
    rows_two = swapped(two, "areal", 1)
    mob, acc, mob_sum, acc_sum = own(False, 1, tiles - 2, (*scalars[:3], mixer), begun)

    packet = pl.pallas_call(
        pack_columns,
        in_specs=[vmem] * 10,
        out_specs=vmem,
        out_shape=jax.ShapeDtypeStruct((rows + ROWS, FIELDS * 32), f32),
        compiler_params=params(24),
        name="pack_columns",
    )(rows_one, rows_two, mob, mob_sum, pressure, trans_x, trans_y, trans_z, pore_volume, acc_sum)

    def residual(start, count, before):
        cells = rows * count * width
        row_tile = pltpu.VMEM((count, ROWS, width), f32)
        return pl.pallas_call(
            functools.partial(near_residual, start, count),
            grid=(count // 2,),
            in_specs=[vmem] * 8 + [anywhere] * len(before),
            out_specs=pl.BlockSpec((COMPS, 2, rows, width), lambda s: (0, s + start // 2, 0, 0)),
            out_shape=whole,
            input_output_aliases={8: 0} if before else {},
            scratch_shapes=[pltpu.VMEM((COMPS, count, ROWS, width), f32), row_tile, row_tile],
            compiler_params=params(24),
            cost_estimate=pl.CostEstimate(
                flops=150 * cells, transcendentals=0, bytes_accessed=4 * 31 * cells
            ),
            name="near_residual",
        )(rows_one, rows_two, pressure, trans_x, trans_y, trans_z, mob, acc, *before)

    columns_one = swapped(packet, "layer", 0)
    columns_two = swapped(packet, "layer", 1)
    near = residual(0, depth, ())
    planes = pl.BlockSpec((COMPS, 2, rows, width), lambda s: (0, s, 0, 0))

    extended = pltpu.VMEM((depth, rows + ROWS, width + LANES), f32)
    side = pltpu.VMEM((depth, rows, LANES), f32)
    return pl.pallas_call(
        finish,
        grid=(depth // 2,),
        in_specs=[vmem] * 12 + [planes],
        out_specs=[planes, vmem],
        out_shape=[whole, sums],
        scratch_shapes=[
            pltpu.VMEM((COMPS, rows, LANES), f32),
            *[extended] * 9,
            pltpu.VMEM((depth + 1, rows + ROWS, width + LANES), f32),
            extended,
            side,
            side,
        ],
        compiler_params=params(28),
        name="finish",
    )(
        columns_one, columns_two, rows_one, rows_two,
        pressure, trans_x, trans_y, trans_z, pore_volume, mob_sum, acc_sum, mob, near,
    )


def solution(mesh):
    placed = (
        P(None, "areal", "layer"),
        P(None, None, "areal", "layer"),
        P(None, None, "areal", "layer"),
        P(None, "areal", "layer"),
        P(None, "areal", "layer"),
        P(None, "areal", "layer"),
        P(None, "areal", "layer"),
        P(),
        P(),
        P(),
        P(None, "areal"),
    )
    return jax.shard_map(
        on_device,
        mesh=mesh,
        in_specs=placed,
        out_specs=(P(None, None, "areal", "layer"), P(None, "areal", "layer")),
        check_vma=False,
    )
```

```python
import functools

import jax
import jax.numpy as jnp
from jax import lax
from jax.experimental import pallas as pl
from jax.experimental.pallas import tpu as pltpu
from jax.sharding import PartitionSpec as P

SS_ITERS = 3
RR_ITERS = 3
LIGHT = 4
COMPS = 9
FIELDS = 16
MOB, PRESS, TX, TY, TZ, PORE, ACC = range(COMPS, FIELDS)
UNITS = (MOB, PRESS, TX, (0, 1), (2, 3), (4, 5), (6, 7), (8, TY), (TZ, PORE), (ACC, ACC))
DEPTH_SLOTS = 4
TIME_STEP = 4.0
COMPRESS = 0.2
VAPOUR_WEIGHT = 1.0 / 0.25
LANES = 128
ROWS = 8
MIB = 1024 * 1024
PART = (COMPS + 1) * ROWS
DEEP = 256
PLANES = 4


def rcp(x):
    return pltpu.reciprocal(x, approx=True)


def total_of(terms):
    terms = list(terms)
    while len(terms) > 1:
        terms = [a + b for a, b in zip(terms[::2], terms[1::2])] + (
            [terms[-1]] if len(terms) % 2 else []
        )
    return terms[0]


def split(x):
    high = x.astype(jnp.bfloat16)
    return high, (x - high.astype(jnp.float32)).astype(jnp.bfloat16)


def mixing_operand(mix_ref):
    shape = (ROWS, DEEP)
    lane, row = lane_of(shape), row_of(shape)
    part = lax.div(lane, PART)
    within = lane - PART * part
    column = lax.div(within, ROWS)
    on = (within - ROWS * column == row) & (part < 3)
    blocks = []
    for i in range(COMPS):
        value = jnp.zeros(shape, jnp.float32)
        for j in range(COMPS):
            value = jnp.where(column == j, 2.0 * mix_ref[i, j], value)
        high, low = split(value)
        value = jnp.where(part == 2, low.astype(jnp.float32), high.astype(jnp.float32))
        blocks.append(jnp.where(on, value, 0.0))
    blocks.append(jnp.zeros(shape, jnp.float32))
    return jnp.concatenate(blocks, axis=0).astype(jnp.bfloat16)


def mixed(operand, spread):
    shape = spread[0].shape
    high, low = split(jnp.concatenate(spread + [jnp.zeros(shape, jnp.float32)], axis=0))
    tail = jnp.zeros((DEEP - 3 * PART, shape[1]), jnp.bfloat16)
    out = jnp.dot(
        operand,
        jnp.concatenate([high, low, high, tail], axis=0),
        preferred_element_type=jnp.float32,
    )
    return [out[ROWS * i : ROWS * (i + 1)] for i in range(COMPS)]


def flash(feed, pressure, signed, slope, operand):
    log_press = jnp.log(pressure)
    half_base = [0.5 * signed[i] - (0.5 * slope[i]) * log_press for i in range(COMPS)]
    spread = None
    for outer in range(SS_ITERS):
        if outer == 0:
            half_log = half_base
        else:
            mix = mixed(operand, spread)
            half_log = [half_base[i] - 0.5 * jnp.tanh(mix[i]) for i in range(COMPS)]
        t = [jnp.tanh(half_log[i]) for i in range(COMPS)]
        u = [rcp(t[i]) for i in range(COMPS)]
        psi = None
        for inner in range(RR_ITERS):
            q = t if inner == 0 else [rcp(u[i] + psi) for i in range(COMPS)]
            part = [feed[i] * q[i] for i in range(COMPS)]
            step = total_of(part) * rcp(total_of(part[i] * q[i] for i in range(COMPS)))
            psi = jnp.clip(step if inner == 0 else psi + step, -1.0, 1.0)
        spread = [feed[i] * rcp(u[i] + psi) for i in range(COMPS)]
    liquid_part = (0.25 * (1.0 - psi)) * (1.0 - psi)
    vapour_part = (0.25 * VAPOUR_WEIGHT * (1.0 + psi)) * (1.0 + psi)
    both, apart = vapour_part + liquid_part, vapour_part - liquid_part
    return [spread[i] * (both * u[i] + apart) for i in range(COMPS)]


def parameters(vol_ref, slope_ref):
    signed = [vol_ref[i] if i < LIGHT else -vol_ref[i] for i in range(COMPS)]
    return signed, [slope_ref[i] for i in range(COMPS)]


def lane_of(shape):
    return lax.broadcasted_iota(jnp.int32, shape, len(shape) - 1)


def row_of(shape):
    return lax.broadcasted_iota(jnp.int32, shape, len(shape) - 2)


def pack_rows(field, low_ref, high_ref, planes):
    row = None
    for n in range(0, len(UNITS), 2):
        lows, highs = [], []
        for z in range(planes):
            for unit in UNITS[n : n + 2]:
                if isinstance(unit, tuple):
                    (first_a, last_a), (first_b, last_b) = (field(k, z) for k in unit)
                    if row is None:
                        row = row_of(first_a.shape)
                    low = jnp.where(row == 2, pltpu.roll(first_a, 2, 0), pltpu.roll(first_b, 3, 0))
                    high = jnp.where(row == 0, pltpu.roll(last_b, 1, 0), pltpu.roll(last_a, 2, 0))
                else:
                    first, last = field(unit, z)
                    if row is None:
                        row = row_of(first.shape)
                    low, high = pltpu.roll(first, 2, 0), pltpu.roll(last, 2, 0)
                lows.append(low)
                highs.append(high)
        for pair in range(planes // 2):
            at = pl.ds(pair * ROWS, ROWS)
            l, h = lows[4 * pair : 4 * pair + 4], highs[4 * pair : 4 * pair + 4]
            if low_ref is not None:
                low_ref[n // 2, at, :] = jnp.where(
                    row < 4,
                    jnp.where(row >= 2, l[0], pltpu.roll(l[1], 6, 0)),
                    jnp.where(row >= 6, pltpu.roll(l[2], 4, 0), pltpu.roll(l[3], 2, 0)),
                )
            if high_ref is not None:
                high_ref[n // 2, at, :] = jnp.where(
                    row < 4,
                    jnp.where(row < 2, h[0], pltpu.roll(h[1], 2, 0)),
                    jnp.where(row < 6, pltpu.roll(h[2], 4, 0), pltpu.roll(h[3], 6, 0)),
                )


def row_tiles(one, two, wanted, start=0, stop=None):
    shape = one.shape[1:]
    upper = row_of(shape) % DEPTH_SLOTS < 2
    tile_row = row_of((ROWS, shape[1]))
    stop = stop or shape[0] // DEPTH_SLOTS
    tiles = {}
    for n, unit in enumerate(UNITS):
        fields = unit if isinstance(unit, tuple) else (unit,)
        if not any(k in wanted for k in fields):
            continue
        up, down = by_side("areal", one[n // 2], two[n // 2])
        if n % 2:
            up, down = pltpu.roll(up, shape[0] - 2, 0), pltpu.roll(down, 2, 0)
        both = jnp.where(upper, up, down)
        for z in range(start, stop):
            at = (z // 2) * ROWS
            tile = pltpu.roll(both[at : at + ROWS], 6 - 4 * (z % 2), 0)
            if fields[0] in wanted:
                tiles.setdefault(fields[0], []).append(tile)
            if fields[-1] in wanted and fields[-1] != fields[0]:
                other = jnp.where(tile_row < 4, pltpu.roll(tile, ROWS - 1, 0), pltpu.roll(tile, 1, 0))
                tiles.setdefault(fields[-1], []).append(other)
    return tiles


def pack_columns(rows_one, rows_two, mob, mob_sum, press, tx, ty, tz, pore, acc_sum, out_ref):
    depth, rows, width = press.shape
    shape = (rows + ROWS, LANES)
    lane = lane_of(shape)
    corner_fields = {MOB: mob_sum, PRESS: press, TX: tx, TY: ty}
    others = {TZ: tz, PORE: pore, ACC: acc_sum, **corner_fields}
    corners = row_tiles(rows_one, rows_two, corner_fields)
    nothing = jnp.zeros((ROWS, LANES), jnp.float32)
    for tile in range(FIELDS // 4):
        packed = jnp.zeros(shape, jnp.float32)
        for quarter in range(4):
            k = 4 * tile + quarter
            for z in range(depth):
                plane = mob[k, z] if k < COMPS else others[k][z]
                first, last = plane[:, :LANES], plane[:, -LANES:]
                at = 32 * quarter + 4 * z
                if k < COMPS:
                    one = pltpu.roll(jnp.concatenate([first, nothing], axis=0), at + 1, 1)
                    two = pltpu.roll(jnp.concatenate([last, nothing], axis=0), (at + 3) % LANES, 1)
                    packed = jnp.where(lane == at + 1, one, jnp.where(lane == at + 2, two, packed))
                    continue
                both = jnp.where(lane_of(first.shape) < LANES // 2, first, last)
                end = nothing
                if k in corner_fields:
                    end = corners[k][z]
                    end = jnp.where(lane_of(end[:, :LANES].shape) < LANES // 2, end[:, :LANES], end[:, -LANES:])
                both = pltpu.roll(jnp.concatenate([both, end], axis=0), (at + 2) % LANES, 1)
                packed = jnp.where((lane >= at) & (lane < at + 4), both, packed)
        out_ref[:, tile * LANES : (tile + 1) * LANES] = packed


def spread_fields(tiles):
    fields = []
    for tile in tiles:
        for quarter in range(4):
            turn = (LANES - 32 * quarter) % LANES
            fields.append(pltpu.roll(tile, turn, 1) if turn else tile)
    return fields


def side_fields(one, two):
    lane = lane_of((one.shape[0], LANES))
    tiles, mobilities = [], []
    for tile in range(FIELDS // 4):
        span = slice(tile * LANES, (tile + 1) * LANES)
        left, right = by_side("layer", one[:, span], two[:, span])
        mobilities.append(jnp.where(lane % 4 < 2, right, left))
        tiles.append(jnp.where(lane % 4 < 2, left, right))
    return spread_fields(mobilities)[:COMPS] + spread_fields(tiles)[COMPS:]


def own_cells(edge, start, flags, vol, slope, mix, comp, press, pore, mass, *rest):
    per_tile = 2
    if edge:
        tx, ty, tz, mob_ref, acc_ref, mob_sum, acc_sum, one_ref, two_ref, operand = rest
        tile_row = pl.program_id(0) * (flags.shape[1] // per_tile - 1)

        @pl.when((pl.program_id(0) == 0) & (pl.program_id(1) == 0))
        def _():
            operand[...] = mixing_operand(mix)

    else:
        mob_ref, acc_ref, mob_sum, acc_sum = rest[-4:]
        operand = mix
        tile_row = pl.program_id(0) + start
    layer = lax.axis_index("layer")
    signed, slopes = parameters(vol, slope)
    planes, _, width = press.shape

    raw = [comp[i] for i in range(COMPS)]
    inverse = rcp(total_of(raw))
    feed = [raw[i] * inverse for i in range(COMPS)]
    volume = pore[...]
    acc = [volume * feed[i] - mass[i] for i in range(COMPS)]
    for i in range(COMPS):
        acc_ref[i] = acc[i]
    acc_sum[...] = total_of(acc)
    tile_flags = [flags[layer, tile_row * per_tile + b] for b in range(per_tile)]
    some = tile_flags[0] + tile_flags[1]

    @pl.when(some > 0)
    def _():
        def beside(x):
            return jnp.concatenate([x[z] for z in range(planes)], axis=1)

        here = [beside(feed[i]) for i in range(COMPS)]
        two = flash(here, beside(press), signed, slopes, operand[...])
        marked = jnp.where(row_of(here[0].shape) < ROWS // per_tile, tile_flags[0], tile_flags[1])
        mobility = [jnp.where(marked > 0, two[i], here[i]) for i in range(COMPS)]
        total = total_of(mobility)
        for z in range(planes):
            span = slice(z * width, (z + 1) * width)
            for i in range(COMPS):
                mob_ref[i, z] = mobility[i][:, span]
            mob_sum[z] = total[:, span]

    @pl.when(some == 0)
    def _():
        for i in range(COMPS):
            mob_ref[i] = feed[i]
        mob_sum[...] = total_of(feed)

    if not edge:
        return
    rest_fields = {
        MOB: mob_sum, PRESS: press, TX: tx, TY: ty, TZ: tz, PORE: pore, ACC: acc_sum,
    }

    def field(k, z):
        here = mob_ref[k, z] if k < COMPS else rest_fields[k][z]
        return here, here

    count = DEPTH_SLOTS * planes
    at = pl.multiple_of(pl.program_id(1) * count, count)
    odd = lax.axis_index("areal") % 2
    for end in range(2):
        for turn, ref in enumerate((one_ref, two_ref)):
            @pl.when((pl.program_id(0) == end) & ((odd == 1) == (end == turn)))
            def _():
                here = ref.at[:, pl.ds(at, count), :]
                pack_rows(field, *((here, None) if end == 0 else (None, here)), planes)


def by_side(axis, one, two):
    odd = lax.axis_index(axis) % 2 == 1
    return jnp.where(odd, one, two), jnp.where(odd, two, one)


def near_residual(
    rows_one, rows_two, press, tx, ty, tz, pore, mob_sum, acc_sum, mob, acc,
    out_ref, total_ref, diagonal_ref, c_x, c_y, c_z,
    rows_h, fields_h, g_x, g_y, g_z,
):
    step = pl.program_id(0)
    planes = out_ref.shape[1]
    depth, rows, width = press.shape
    areal, areals = lax.axis_index("areal"), lax.axis_size("areal")
    tall = rows + ROWS
    full = (tall, width)
    own = slice(0, rows)

    @pl.when(step == 0)
    def _():
        fields = {MOB: mob_sum, PRESS: press, TX: tx, TY: ty, TZ: tz, PORE: pore, ACC: acc_sum}
        tiles = row_tiles(rows_one, rows_two, range(FIELDS))
        for z in range(depth):
            for i in range(COMPS):
                rows_h[i, z] = tiles[i][z]
            for n, k in enumerate(fields):
                fields_h[n, z] = tiles[k][z]

        end_x = (row_of(full) == rows - 1) & (areal == areals - 1)
        end_y = lane_of(full) == width - 1
        scale = 0.5 * TIME_STEP
        c_z[0] = jnp.zeros(full, jnp.float32)
        g_z[0] = jnp.zeros((rows, width), jnp.float32)

        def update(z):
            m, p, x, y, zz, volume, total = (
                jnp.concatenate([ref[z], fields_h[n, z]], axis=0) for n, ref in enumerate(fields.values())
            )
            up, down = jnp.minimum(z + 1, depth - 1), jnp.maximum(z - 1, 0)
            p_up = jnp.concatenate([press[up], fields_h[1, up]], axis=0)
            p_down = jnp.concatenate([press[down], fields_h[1, down]], axis=0)
            m_up = jnp.concatenate([mob_sum[up], fields_h[0, up]], axis=0)
            strength_x = jnp.where(end_x, 0.0, scale * x)
            strength_y = jnp.where(end_y, 0.0, scale * y)
            strength_z = jnp.where(z < depth - 1, scale, 0.0) * zz
            dx = p - pltpu.roll(p, tall - 1, 0)
            dy = p - pltpu.roll(p, width - 1, 1)
            dz = p - p_up
            cx = strength_x * (m + pltpu.roll(m, tall - 1, 0))
            cy = strength_y * (m + pltpu.roll(m, width - 1, 1))
            cz = strength_z * (m + m_up)
            cz_low = c_z[z]
            gx = strength_x * dx
            g_x[0, z], g_x[1, z] = gx[own], -pltpu.roll(gx, 1, 0)[own]
            g_y[z], g_z[z + 1] = (strength_y * dy)[own], (strength_z * dz)[own]
            c_x[z], c_y[z], c_z[z + 1] = cx, cy, cz
            fx, fy = cx * dx, cy * dy
            total_ref[z] = (
                total
                + (fx - pltpu.roll(fx, 1, 0))
                + (fy - pltpu.roll(fy, 1, 1))
                + (cz * dz + cz_low * (p - p_down))
            )
            diagonal_ref[z] = (
                COMPRESS * volume
                + (cx + pltpu.roll(cx, 1, 0))
                + (cy + pltpu.roll(cy, 1, 1))
                + (cz + cz_low)
            )

        def pair(t, carry):
            update(2 * t)
            update(2 * t + 1)
            return carry

        lax.fori_loop(0, depth // 2, pair, 0)

    for plane in range(planes):
        z = step * planes + plane
        down, up = jnp.maximum(z - 1, 0), jnp.minimum(z + 1, depth - 1)
        gx, gx_low, gy, gz, gz_low = g_x[0, z], g_x[1, z], g_y[z], g_z[z + 1], -g_z[z]
        gy_low = -pltpu.roll(gy, 1, 1)
        middle = (gx + gx_low) + (gy + gy_low) + (gz + gz_low)
        for i in range(COMPS):
            here = mob[i, z]
            tall_here = jnp.concatenate([here, rows_h[i, z]], axis=0)
            out_ref[i, plane] = (
                acc[i, z]
                + middle * here
                + gx * pltpu.roll(tall_here, tall - 1, 0)[own]
                + gx_low * pltpu.roll(tall_here, 1, 0)[own]
                + gy * pltpu.roll(here, width - 1, 1)
                + gy_low * pltpu.roll(here, 1, 1)
                + gz * mob[i, up]
                + gz_low * mob[i, down]
            )


def finish(
    columns_one, columns_two, packet, press, total_in, diagonal_in, c_x, c_y, c_z, mob, near,
    res_ref, new_ref,
    side_h, edge_h, first, total_ref, inverse_ref,
):
    step = pl.program_id(0)
    planes = res_ref.shape[1]
    depth, rows, width = press.shape
    layer, layers = lax.axis_index("layer"), lax.axis_size("layer")
    areal, areals = lax.axis_index("areal"), lax.axis_size("areal")
    tall = rows + ROWS
    lane = lane_of((tall, LANES))
    at_first, at_last = lane == 0, lane == LANES - 1
    low, high = slice(0, LANES), slice(width - LANES, width)
    FLUX, COUPLE, FACE, NEXT = range(4)

    def edges(which, z):
        both = pltpu.roll(edge_h[which], LANES - 1 - 4 * z, 1)
        return jnp.where(at_first, both, 0.0), jnp.where(at_last, both, 0.0)

    @pl.when(step == 0)
    def _():
        halo = side_fields(columns_one, columns_two)
        here = spread_fields([packet[:, t : t + LANES] for t in range(0, FIELDS * 32, LANES)])
        for i in range(COMPS):
            side_h[i] = halo[i][:rows]
        scale = 0.5 * TIME_STEP
        is_left = lane % 4 == 1

        def turned(x, by):
            return pltpu.roll(x, by % LANES, 1)

        def outer(x):
            return jnp.where(is_left, turned(x, 1), turned(x, -1))

        def inner(x):
            return jnp.where(is_left, turned(x, -1), turned(x, 1))

        m, p = halo[MOB], halo[PRESS]
        strength = scale * halo[TY]
        own_strength = jnp.where(layer < layers - 1, scale, 0.0) * here[TY]
        c_out = jnp.where(is_left, turned(strength, 1), strength) * (m + outer(m))
        s_in = jnp.where(is_left, strength, turned(own_strength, 1))
        c_in = s_in * (m + inner(here[MOB]))
        d_in = p - inner(here[PRESS])
        end_x = (row_of(lane.shape) == rows - 1) & (areal == areals - 1)
        cx = jnp.where(end_x, 0.0, scale * halo[TX]) * (m + pltpu.roll(m, tall - 1, 0))
        cz = jnp.where(lane < 4 * (depth - 1), scale * halo[TZ], 0.0) * (m + turned(m, -4))
        fx = cx * (p - pltpu.roll(p, tall - 1, 0))
        fz = cz * (p - turned(p, -4))
        total = (
            halo[ACC]
            + (c_out * (p - outer(p)) + c_in * d_in)
            + (fx - pltpu.roll(fx, 1, 0))
            + (fz - turned(fz, 4))
        )
        diagonal = (
            COMPRESS * halo[PORE] + (c_out + c_in) + (cx + pltpu.roll(cx, 1, 0)) + (cz + turned(cz, 4))
        )
        usable = diagonal > 0.0
        beside = jnp.where(usable, -total * rcp(jnp.where(usable, diagonal, 1.0)), 0.0)
        for which, value in (
            (FLUX, -c_in * d_in), (COUPLE, c_in), (FACE, -s_in * d_in), (NEXT, c_in * beside)
        ):
            edge_h[which] = jnp.where(is_left, value, turned(value, -2))

        def update(z):
            flux, couple = edges(FLUX, z), edges(COUPLE, z)
            for n, span in enumerate((low, high)):
                total = total_in[z, :, span] + flux[n]
                diagonal = diagonal_in[z, :, span] + couple[n]
                usable = diagonal > 0.0
                inverse = rcp(jnp.where(usable, diagonal, 1.0))
                first[z, :, span] = jnp.where(usable, -total * inverse, 0.0)
                total_ref[z, :, span] = total[:rows]
                inverse_ref[z, :, span] = inverse[:rows]

        def second(z):
            here = first[z]
            up, down = jnp.minimum(z + 1, depth - 1), jnp.maximum(z - 1, 0)
            cx, cy = c_x[z], c_y[z, :rows]
            own = here[:rows]
            gathered = (
                (cx * pltpu.roll(here, tall - 1, 0))[:rows]
                + pltpu.roll(cx * here, 1, 0)[:rows]
                + cy * pltpu.roll(own, width - 1, 1)
                + pltpu.roll(cy * own, 1, 1)
                + (c_z[z + 1, :rows] * first[up, :rows] + c_z[z, :rows] * first[down, :rows])
                - total_ref[z]
            )
            beyond = edges(NEXT, z)
            for n, span in enumerate((low, high)):
                new_ref[z, :, span] = press[z, :, span] + inverse_ref[z, :, span] * (
                    gathered[:, span] + beyond[n][:rows]
                )

        for body in (update, second):
            def pair(t, carry):
                body(2 * t)
                body(2 * t + 1)
                return carry

            lax.fori_loop(0, depth // 2, pair, 0)

    for plane in range(planes):
        z = step * planes + plane
        faces = [face[:rows] for face in edges(FACE, z)]
        for i in range(COMPS):
            side = pltpu.roll(side_h[i], LANES - 2 - 4 * z, 1)
            here = mob[i, z]
            for span, face in zip((low, high), faces):
                res_ref[i, plane, :, span] = near[i, plane, :, span] + face * (here[:, span] + side)


def on_device(
    pressure, composition, mass_old, pore_volume, trans_x, trans_y, trans_z,
    volatility, pressure_slope, mixing, two_phase,
):
    depth, rows, width = pressure.shape
    f32 = jnp.float32
    smem = pl.BlockSpec(memory_space=pltpu.SMEM)
    vmem = pl.BlockSpec(memory_space=pltpu.VMEM)
    def params(mib):
        return pltpu.CompilerParams(vmem_limit_bytes=mib * MIB)

    scalars = (two_phase, volatility, pressure_slope, mixing)

    def swapped(block, axis, first):
        count = lax.axis_size(axis)
        pairs = [(i, i + 1) for i in range(first, count - 1, 2)]
        return lax.ppermute(block, axis, pairs + [(j, i) for i, j in pairs])

    whole = jax.ShapeDtypeStruct((COMPS, depth, rows, width), f32)
    sums = jax.ShapeDtypeStruct((depth, rows, width), f32)
    packed = jax.ShapeDtypeStruct((len(UNITS) // 2, DEPTH_SLOTS * depth, width), f32)
    parts = depth // PLANES
    tiles = rows // ROWS

    fields = (composition, pressure, pore_volume, mass_old, trans_x, trans_y, trans_z)

    def pinned(x):
        return pltpu.with_memory_space_constraint(x, pltpu.HBM)

    operand = jax.ShapeDtypeStruct((PART, DEEP), jnp.bfloat16)
    anywhere = pl.BlockSpec(memory_space=pl.ANY)

    def own(edge, start, count, small, before):
        tile_row = (lambda t: t * (tiles - 1)) if edge else (lambda t: start + t)
        plane = pl.BlockSpec((PLANES, ROWS, width), lambda t, z: (z, tile_row(t), 0))
        planes = pl.BlockSpec((COMPS, PLANES, ROWS, width), lambda t, z: (0, z, tile_row(t), 0))
        cells = count * ROWS * depth * width
        used = fields if edge else fields[:4]
        return pl.pallas_call(
            functools.partial(own_cells, edge, start),
            grid=(count, parts),
            in_specs=[smem] * 3
            + [smem if edge else vmem]
            + [planes, plane, plane, planes]
            + [plane] * (len(used) - 4)
            + [anywhere] * len(before),
            out_specs=[planes, planes, plane, plane] + ([vmem] * 3 if edge else []),
            out_shape=[whole, whole, sums, sums] + ([packed, packed, operand] if edge else []),
            input_output_aliases={4 + len(used) + k: k for k in range(len(before))},
            compiler_params=params(24),
            cost_estimate=pl.CostEstimate(
                flops=900 * cells, transcendentals=190 * cells, bytes_accessed=4 * 39 * cells
            ),
            name="edge_cells" if edge else "inner_cells",
        )(*(pinned(x) if edge else x for x in (*small, *used)), *before)

    *begun, one, two, mixer = own(True, 0, 2, scalars, ())
    rows_one = swapped(one, "areal", 0)
    rows_two = swapped(two, "areal", 1)
    mob, acc, mob_sum, acc_sum = own(False, 1, tiles - 2, (*scalars[:3], mixer), begun)

    packet = pl.pallas_call(
        pack_columns,
        in_specs=[vmem] * 10,
        out_specs=vmem,
        out_shape=jax.ShapeDtypeStruct((rows + ROWS, FIELDS * 32), f32),
        compiler_params=params(24),
        name="pack_columns",
    )(rows_one, rows_two, mob, mob_sum, pressure, trans_x, trans_y, trans_z, pore_volume, acc_sum)

    columns_one = swapped(packet, "layer", 0)
    columns_two = swapped(packet, "layer", 1)

    planes = pl.BlockSpec((COMPS, 2, rows, width), lambda s: (0, s, 0, 0))
    tall = jax.ShapeDtypeStruct((depth, rows + ROWS, width), f32)
    above_faces = jax.ShapeDtypeStruct((depth + 1, rows + ROWS, width), f32)
    cells = rows * depth * width
    near, *sweep = pl.pallas_call(
        near_residual,
        grid=(depth // 2,),
        in_specs=[vmem] * 11,
        out_specs=[planes] + [vmem] * 5,
        out_shape=[whole, tall, tall, tall, tall, above_faces],
        scratch_shapes=[
            pltpu.VMEM((COMPS, depth, ROWS, width), f32),
            pltpu.VMEM((FIELDS - COMPS, depth, ROWS, width), f32),
            pltpu.VMEM((2, depth, rows, width), f32),
            pltpu.VMEM((depth, rows, width), f32),
            pltpu.VMEM((depth + 1, rows, width), f32),
        ],
        compiler_params=params(24),
        cost_estimate=pl.CostEstimate(flops=150 * cells, transcendentals=0, bytes_accessed=4 * 31 * cells),
        name="near_residual",
    )(
        rows_one, rows_two,
        pressure, trans_x, trans_y, trans_z, pore_volume, mob_sum, acc_sum, mob, acc,
    )

    return pl.pallas_call(
        finish,
        grid=(depth // 2,),
        in_specs=[vmem] * 10 + [planes],
        out_specs=[planes, vmem],
        out_shape=[whole, sums],
        scratch_shapes=[
            pltpu.VMEM((COMPS, rows, LANES), f32),
            pltpu.VMEM((4, rows + ROWS, LANES), f32),
            pltpu.VMEM((depth, rows + ROWS, width), f32),
            pltpu.VMEM((depth, rows, width), f32),
            pltpu.VMEM((depth, rows, width), f32),
        ],
        compiler_params=params(24),
        name="finish",
    )(columns_one, columns_two, packet, pressure, *sweep, mob, near)


def solution(mesh):
    placed = (
        P(None, "areal", "layer"),
        P(None, None, "areal", "layer"),
        P(None, None, "areal", "layer"),
        P(None, "areal", "layer"),
        P(None, "areal", "layer"),
        P(None, "areal", "layer"),
        P(None, "areal", "layer"),
        P(),
        P(),
        P(),
        P(None, "areal"),
    )
    return jax.shard_map(
        on_device,
        mesh=mesh,
        in_specs=placed,
        out_specs=(P(None, None, "areal", "layer"), P(None, "areal", "layer")),
        check_vma=False,
    )
```

```python
import functools

import jax
import jax.numpy as jnp
from jax import lax
from jax.experimental import pallas as pl
from jax.experimental.pallas import tpu as pltpu
from jax.sharding import PartitionSpec as P

SS_ITERS = 3
RR_ITERS = 3
LIGHT = 4
COMPS = 9
FIELDS = 16
MOB, PRESS, TX, TY, TZ, PORE, ACC = range(COMPS, FIELDS)
UNITS = (MOB, PRESS, TX, (0, 1), (2, 3), (4, 5), (6, 7), (8, TY), (TZ, PORE), (ACC, ACC))
DEPTH_SLOTS = 4
TIME_STEP = 4.0
COMPRESS = 0.2
VAPOUR_WEIGHT = 1.0 / 0.25
LANES = 128
ROWS = 8
MIB = 1024 * 1024
PART = (COMPS + 1) * ROWS
DEEP = 256
PLANES = 8


def rcp(x):
    return pltpu.reciprocal(x, approx=True)


def total_of(terms):
    terms = list(terms)
    while len(terms) > 1:
        terms = [a + b for a, b in zip(terms[::2], terms[1::2])] + (
            [terms[-1]] if len(terms) % 2 else []
        )
    return terms[0]


def split(x):
    high = x.astype(jnp.bfloat16)
    return high, (x - high.astype(jnp.float32)).astype(jnp.bfloat16)


def mixing_operand(mix_ref):
    shape = (ROWS, DEEP)
    lane, row = lane_of(shape), row_of(shape)
    part = lax.div(lane, PART)
    within = lane - PART * part
    column = lax.div(within, ROWS)
    on = (within - ROWS * column == row) & (part < 3)
    blocks = []
    for i in range(COMPS):
        value = jnp.zeros(shape, jnp.float32)
        for j in range(COMPS):
            value = jnp.where(column == j, 2.0 * mix_ref[i, j], value)
        high, low = split(value)
        value = jnp.where(part == 2, low.astype(jnp.float32), high.astype(jnp.float32))
        blocks.append(jnp.where(on, value, 0.0))
    blocks.append(jnp.zeros(shape, jnp.float32))
    return jnp.concatenate(blocks, axis=0).astype(jnp.bfloat16)


def mixed(operand, spread):
    shape = spread[0].shape
    high, low = split(jnp.concatenate(spread + [jnp.zeros(shape, jnp.float32)], axis=0))
    tail = jnp.zeros((DEEP - 3 * PART, shape[1]), jnp.bfloat16)
    out = jnp.dot(
        operand,
        jnp.concatenate([high, low, high, tail], axis=0),
        preferred_element_type=jnp.float32,
    )
    return [out[ROWS * i : ROWS * (i + 1)] for i in range(COMPS)]


def flash(feed, pressure, signed, slope, operand):
    log_press = jnp.log(pressure)
    half_base = [0.5 * signed[i] - (0.5 * slope[i]) * log_press for i in range(COMPS)]
    spread = None
    for outer in range(SS_ITERS):
        if outer == 0:
            half_log = half_base
        else:
            mix = mixed(operand, spread)
            half_log = [half_base[i] - 0.5 * jnp.tanh(mix[i]) for i in range(COMPS)]
        t = [jnp.tanh(half_log[i]) for i in range(COMPS)]
        u = [rcp(t[i]) for i in range(COMPS)]
        psi = None
        for inner in range(RR_ITERS):
            q = t if inner == 0 else [rcp(u[i] + psi) for i in range(COMPS)]
            part = [feed[i] * q[i] for i in range(COMPS)]
            step = total_of(part) * rcp(total_of(part[i] * q[i] for i in range(COMPS)))
            psi = jnp.clip(step if inner == 0 else psi + step, -1.0, 1.0)
        spread = [feed[i] * rcp(u[i] + psi) for i in range(COMPS)]
    liquid_part = (0.25 * (1.0 - psi)) * (1.0 - psi)
    vapour_part = (0.25 * VAPOUR_WEIGHT * (1.0 + psi)) * (1.0 + psi)
    both, apart = vapour_part + liquid_part, vapour_part - liquid_part
    return [spread[i] * (both * u[i] + apart) for i in range(COMPS)]


def parameters(vol_ref, slope_ref):
    signed = [vol_ref[i] if i < LIGHT else -vol_ref[i] for i in range(COMPS)]
    return signed, [slope_ref[i] for i in range(COMPS)]


def lane_of(shape):
    return lax.broadcasted_iota(jnp.int32, shape, len(shape) - 1)


def row_of(shape):
    return lax.broadcasted_iota(jnp.int32, shape, len(shape) - 2)


def pack_rows(field, low_ref, high_ref, planes):
    row = None
    for n in range(0, len(UNITS), 2):
        lows, highs = [], []
        for z in range(planes):
            for unit in UNITS[n : n + 2]:
                if isinstance(unit, tuple):
                    (first_a, last_a), (first_b, last_b) = (field(k, z) for k in unit)
                    if row is None:
                        row = row_of(first_a.shape)
                    low = jnp.where(row == 2, pltpu.roll(first_a, 2, 0), pltpu.roll(first_b, 3, 0))
                    high = jnp.where(row == 0, pltpu.roll(last_b, 1, 0), pltpu.roll(last_a, 2, 0))
                else:
                    first, last = field(unit, z)
                    if row is None:
                        row = row_of(first.shape)
                    low, high = pltpu.roll(first, 2, 0), pltpu.roll(last, 2, 0)
                lows.append(low)
                highs.append(high)
        for pair in range(planes // 2):
            at = pl.ds(pair * ROWS, ROWS)
            l, h = lows[4 * pair : 4 * pair + 4], highs[4 * pair : 4 * pair + 4]
            if low_ref is not None:
                low_ref[n // 2, at, :] = jnp.where(
                    row < 4,
                    jnp.where(row >= 2, l[0], pltpu.roll(l[1], 6, 0)),
                    jnp.where(row >= 6, pltpu.roll(l[2], 4, 0), pltpu.roll(l[3], 2, 0)),
                )
            if high_ref is not None:
                high_ref[n // 2, at, :] = jnp.where(
                    row < 4,
                    jnp.where(row < 2, h[0], pltpu.roll(h[1], 2, 0)),
                    jnp.where(row < 6, pltpu.roll(h[2], 4, 0), pltpu.roll(h[3], 6, 0)),
                )


def row_tiles(one, two, wanted, start=0, stop=None):
    shape = one.shape[1:]
    upper = row_of(shape) % DEPTH_SLOTS < 2
    tile_row = row_of((ROWS, shape[1]))
    stop = stop or shape[0] // DEPTH_SLOTS
    tiles = {}
    for n, unit in enumerate(UNITS):
        fields = unit if isinstance(unit, tuple) else (unit,)
        if not any(k in wanted for k in fields):
            continue
        up, down = by_side("areal", one[n // 2], two[n // 2])
        if n % 2:
            up, down = pltpu.roll(up, shape[0] - 2, 0), pltpu.roll(down, 2, 0)
        both = jnp.where(upper, up, down)
        for z in range(start, stop):
            at = (z // 2) * ROWS
            tile = pltpu.roll(both[at : at + ROWS], 6 - 4 * (z % 2), 0)
            if fields[0] in wanted:
                tiles.setdefault(fields[0], []).append(tile)
            if fields[-1] in wanted and fields[-1] != fields[0]:
                other = jnp.where(tile_row < 4, pltpu.roll(tile, ROWS - 1, 0), pltpu.roll(tile, 1, 0))
                tiles.setdefault(fields[-1], []).append(other)
    return tiles


def pack_columns(rows_one, rows_two, mob, mob_sum, press, tx, ty, tz, pore, acc_sum, out_ref):
    depth, rows, width = press.shape
    shape = (rows + ROWS, LANES)
    lane = lane_of(shape)
    corner_fields = {MOB: mob_sum, PRESS: press, TX: tx, TY: ty}
    others = {TZ: tz, PORE: pore, ACC: acc_sum, **corner_fields}
    corners = row_tiles(rows_one, rows_two, corner_fields)
    nothing = jnp.zeros((ROWS, LANES), jnp.float32)
    for tile in range(FIELDS // 4):
        packed = jnp.zeros(shape, jnp.float32)
        for quarter in range(4):
            k = 4 * tile + quarter
            for z in range(depth):
                plane = mob[k, z] if k < COMPS else others[k][z]
                first, last = plane[:, :LANES], plane[:, -LANES:]
                at = 32 * quarter + 4 * z
                both = jnp.where(lane_of(first.shape) < LANES // 2, first, last)
                if k < COMPS:
                    both = pltpu.roll(both, at + 1, 1)
                    on = (lane_of(first.shape) >= at) & (lane_of(first.shape) < at + 2)
                    packed = jnp.concatenate([jnp.where(on, both, packed[:rows]), nothing], axis=0)
                    continue
                end = nothing
                if k in corner_fields:
                    end = corners[k][z]
                    end = jnp.where(lane_of(end[:, :LANES].shape) < LANES // 2, end[:, :LANES], end[:, -LANES:])
                both = pltpu.roll(jnp.concatenate([both, end], axis=0), (at + 2) % LANES, 1)
                packed = jnp.where((lane >= at) & (lane < at + 4), both, packed)
        out_ref[:, tile * LANES : (tile + 1) * LANES] = packed


def spread_fields(tiles):
    fields = []
    for tile in tiles:
        for quarter in range(4):
            turn = (LANES - 32 * quarter) % LANES
            fields.append(pltpu.roll(tile, turn, 1) if turn else tile)
    return fields


def side_fields(one, two):
    lane = lane_of((one.shape[0], LANES))
    tiles, mobilities = [], []
    for tile in range(FIELDS // 4):
        span = slice(tile * LANES, (tile + 1) * LANES)
        left, right = by_side("layer", one[:, span], two[:, span])
        mobilities.append(jnp.where(lane % 4 == 1, right, pltpu.roll(left, 2, 1)))
        tiles.append(jnp.where(lane % 4 < 2, left, right))
    return spread_fields(mobilities)[:COMPS] + spread_fields(tiles)[COMPS:]


def own_cells(edge, start, flags, vol, slope, mix, comp, press, pore, mass, *rest):
    per_tile = 2
    if edge:
        tx, ty, tz, mob_ref, acc_ref, mob_sum, acc_sum, one_ref, two_ref, operand = rest
        tile_row = pl.program_id(0) * (flags.shape[1] // per_tile - 1)

        @pl.when((pl.program_id(0) == 0) & (pl.program_id(1) == 0))
        def _():
            operand[...] = mixing_operand(mix)

    else:
        mob_ref, acc_ref, mob_sum, acc_sum = rest[-4:]
        operand = mix
        tile_row = pl.program_id(0) + start
    layer = lax.axis_index("layer")
    signed, slopes = parameters(vol, slope)
    planes, _, width = press.shape

    raw = [comp[i] for i in range(COMPS)]
    inverse = rcp(total_of(raw))
    feed = [raw[i] * inverse for i in range(COMPS)]
    volume = pore[...]
    acc = [volume * feed[i] - mass[i] for i in range(COMPS)]
    for i in range(COMPS):
        acc_ref[i] = acc[i]
    acc_sum[...] = total_of(acc)
    tile_flags = [flags[layer, tile_row * per_tile + b] for b in range(per_tile)]
    some = tile_flags[0] + tile_flags[1]

    @pl.when(some > 0)
    def _():
        def beside(x):
            return jnp.concatenate([x[z] for z in range(planes)], axis=1)

        here = [beside(feed[i]) for i in range(COMPS)]
        two = flash(here, beside(press), signed, slopes, operand[...])
        marked = jnp.where(row_of(here[0].shape) < ROWS // per_tile, tile_flags[0], tile_flags[1])
        mobility = [jnp.where(marked > 0, two[i], here[i]) for i in range(COMPS)]
        total = total_of(mobility)
        for z in range(planes):
            span = slice(z * width, (z + 1) * width)
            for i in range(COMPS):
                mob_ref[i, z] = mobility[i][:, span]
            mob_sum[z] = total[:, span]

    @pl.when(some == 0)
    def _():
        for i in range(COMPS):
            mob_ref[i] = feed[i]
        mob_sum[...] = total_of(feed)

    if not edge:
        return
    rest_fields = {
        MOB: mob_sum, PRESS: press, TX: tx, TY: ty, TZ: tz, PORE: pore, ACC: acc_sum,
    }

    def field(k, z):
        here = mob_ref[k, z] if k < COMPS else rest_fields[k][z]
        return here, here

    count = DEPTH_SLOTS * planes
    at = pl.multiple_of(pl.program_id(1) * count, count)
    odd = lax.axis_index("areal") % 2
    for end in range(2):
        for turn, ref in enumerate((one_ref, two_ref)):
            @pl.when((pl.program_id(0) == end) & ((odd == 1) == (end == turn)))
            def _():
                here = ref.at[:, pl.ds(at, count), :]
                pack_rows(field, *((here, None) if end == 0 else (None, here)), planes)


def by_side(axis, one, two):
    odd = lax.axis_index(axis) % 2 == 1
    return jnp.where(odd, one, two), jnp.where(odd, two, one)


def near_residual(
    rows_one, rows_two, press, tx, ty, tz, pore, mob_sum, acc_sum, mob, acc,
    out_ref, total_ref, diagonal_ref, c_x, c_y, c_z,
    rows_h, fields_h, g_x, g_y, g_z,
):
    step = pl.program_id(0)
    planes = out_ref.shape[1]
    depth, rows, width = press.shape
    areal, areals = lax.axis_index("areal"), lax.axis_size("areal")
    tall = rows + ROWS
    full = (tall, width)
    own = slice(0, rows)

    @pl.when(step == 0)
    def _():
        fields = {MOB: mob_sum, PRESS: press, TX: tx, TY: ty, TZ: tz, PORE: pore, ACC: acc_sum}
        tiles = row_tiles(rows_one, rows_two, range(FIELDS))
        for z in range(depth):
            for i in range(COMPS):
                rows_h[i, z] = tiles[i][z]
            for n, k in enumerate(fields):
                fields_h[n, z] = tiles[k][z]

        end_x = (row_of(full) == rows - 1) & (areal == areals - 1)
        end_y = lane_of(full) == width - 1
        scale = 0.5 * TIME_STEP
        c_z[0] = jnp.zeros(full, jnp.float32)
        g_z[0] = jnp.zeros((rows, width), jnp.float32)

        def update(z):
            m, p, x, y, zz, volume, total = (
                jnp.concatenate([ref[z], fields_h[n, z]], axis=0) for n, ref in enumerate(fields.values())
            )
            up, down = jnp.minimum(z + 1, depth - 1), jnp.maximum(z - 1, 0)
            p_up = jnp.concatenate([press[up], fields_h[1, up]], axis=0)
            p_down = jnp.concatenate([press[down], fields_h[1, down]], axis=0)
            m_up = jnp.concatenate([mob_sum[up], fields_h[0, up]], axis=0)
            strength_x = jnp.where(end_x, 0.0, scale * x)
            strength_y = jnp.where(end_y, 0.0, scale * y)
            strength_z = jnp.where(z < depth - 1, scale, 0.0) * zz
            dx = p - pltpu.roll(p, tall - 1, 0)
            dy = p - pltpu.roll(p, width - 1, 1)
            dz = p - p_up
            cx = strength_x * (m + pltpu.roll(m, tall - 1, 0))
            cy = strength_y * (m + pltpu.roll(m, width - 1, 1))
            cz = strength_z * (m + m_up)
            cz_low = c_z[z]
            gx = strength_x * dx
            g_x[0, z], g_x[1, z] = gx[own], -pltpu.roll(gx, 1, 0)[own]
            g_y[z], g_z[z + 1] = (strength_y * dy)[own], (strength_z * dz)[own]
            c_x[z], c_y[z], c_z[z + 1] = cx, cy, cz
            fx, fy = cx * dx, cy * dy
            total_ref[z] = (
                total
                + (fx - pltpu.roll(fx, 1, 0))
                + (fy - pltpu.roll(fy, 1, 1))
                + (cz * dz + cz_low * (p - p_down))
            )
            diagonal_ref[z] = (
                COMPRESS * volume
                + (cx + pltpu.roll(cx, 1, 0))
                + (cy + pltpu.roll(cy, 1, 1))
                + (cz + cz_low)
            )

        def pair(t, carry):
            update(2 * t)
            update(2 * t + 1)
            return carry

        lax.fori_loop(0, depth // 2, pair, 0)

    for plane in range(planes):
        z = step * planes + plane
        down, up = jnp.maximum(z - 1, 0), jnp.minimum(z + 1, depth - 1)
        gx, gx_low, gy, gz, gz_low = g_x[0, z], g_x[1, z], g_y[z], g_z[z + 1], -g_z[z]
        gy_low = -pltpu.roll(gy, 1, 1)
        middle = (gx + gx_low) + (gy + gy_low) + (gz + gz_low)
        for i in range(COMPS):
            here = mob[i, z]
            tall_here = jnp.concatenate([here, rows_h[i, z]], axis=0)
            out_ref[i, plane] = (
                acc[i, z]
                + middle * here
                + gx * pltpu.roll(tall_here, tall - 1, 0)[own]
                + gx_low * pltpu.roll(tall_here, 1, 0)[own]
                + gy * pltpu.roll(here, width - 1, 1)
                + gy_low * pltpu.roll(here, 1, 1)
                + gz * mob[i, up]
                + gz_low * mob[i, down]
            )


def finish(
    columns_one, columns_two, packet, press, total_in, diagonal_in, c_x, c_y, c_z, mob, near,
    res_ref, new_ref,
    side_h, edge_h, first, total_ref, inverse_ref,
):
    step = pl.program_id(0)
    planes = res_ref.shape[1]
    depth, rows, width = press.shape
    layer, layers = lax.axis_index("layer"), lax.axis_size("layer")
    areal, areals = lax.axis_index("areal"), lax.axis_size("areal")
    tall = rows + ROWS
    lane = lane_of((tall, LANES))
    at_first, at_last = lane == 0, lane == LANES - 1
    low, high = slice(0, LANES), slice(width - LANES, width)
    FLUX, COUPLE, FACE, NEXT = range(4)

    def edges(which, z):
        both = pltpu.roll(edge_h[which], LANES - 1 - 4 * z, 1)
        return jnp.where(at_first, both, 0.0), jnp.where(at_last, both, 0.0)

    @pl.when(step == 0)
    def _():
        halo = side_fields(columns_one, columns_two)
        here = spread_fields([packet[:, t : t + LANES] for t in range(0, FIELDS * 32, LANES)])
        for i in range(COMPS):
            side_h[i] = halo[i][:rows]
        scale = 0.5 * TIME_STEP
        is_left = lane % 4 == 1

        def turned(x, by):
            return pltpu.roll(x, by % LANES, 1)

        def outer(x):
            return jnp.where(is_left, turned(x, 1), turned(x, -1))

        def inner(x):
            return jnp.where(is_left, turned(x, -1), turned(x, 1))

        m, p = halo[MOB], halo[PRESS]
        strength = scale * halo[TY]
        own_strength = jnp.where(layer < layers - 1, scale, 0.0) * here[TY]
        c_out = jnp.where(is_left, turned(strength, 1), strength) * (m + outer(m))
        s_in = jnp.where(is_left, strength, turned(own_strength, 1))
        c_in = s_in * (m + inner(here[MOB]))
        d_in = p - inner(here[PRESS])
        end_x = (row_of(lane.shape) == rows - 1) & (areal == areals - 1)
        cx = jnp.where(end_x, 0.0, scale * halo[TX]) * (m + pltpu.roll(m, tall - 1, 0))
        cz = jnp.where(lane < 4 * (depth - 1), scale * halo[TZ], 0.0) * (m + turned(m, -4))
        fx = cx * (p - pltpu.roll(p, tall - 1, 0))
        fz = cz * (p - turned(p, -4))
        total = (
            halo[ACC]
            + (c_out * (p - outer(p)) + c_in * d_in)
            + (fx - pltpu.roll(fx, 1, 0))
            + (fz - turned(fz, 4))
        )
        diagonal = (
            COMPRESS * halo[PORE] + (c_out + c_in) + (cx + pltpu.roll(cx, 1, 0)) + (cz + turned(cz, 4))
        )
        usable = diagonal > 0.0
        beside = jnp.where(usable, -total * rcp(jnp.where(usable, diagonal, 1.0)), 0.0)
        for which, value in (
            (FLUX, -c_in * d_in), (COUPLE, c_in), (FACE, -s_in * d_in), (NEXT, c_in * beside)
        ):
            edge_h[which] = jnp.where(is_left, value, turned(value, -2))

    def depth_pairs(body):
        def pair(t, carry):
            body(2 * t)
            body(2 * t + 1)
            return carry

        lax.fori_loop(0, depth // 2, pair, 0)

    @pl.when(step == 1)
    def _():
        def update(z):
            flux, couple = edges(FLUX, z), edges(COUPLE, z)
            for n, span in enumerate((low, high)):
                total = total_in[z, :, span] + flux[n]
                diagonal = diagonal_in[z, :, span] + couple[n]
                usable = diagonal > 0.0
                inverse = rcp(jnp.where(usable, diagonal, 1.0))
                first[z, :, span] = jnp.where(usable, -total * inverse, 0.0)
                total_ref[z, :, span] = total[:rows]
                inverse_ref[z, :, span] = inverse[:rows]

        depth_pairs(update)

    @pl.when(step == 2)
    def _():
        def second(z):
            here = first[z]
            up, down = jnp.minimum(z + 1, depth - 1), jnp.maximum(z - 1, 0)
            cx, cy = c_x[z], c_y[z, :rows]
            own = here[:rows]
            gathered = (
                (cx * pltpu.roll(here, tall - 1, 0))[:rows]
                + pltpu.roll(cx * here, 1, 0)[:rows]
                + cy * pltpu.roll(own, width - 1, 1)
                + pltpu.roll(cy * own, 1, 1)
                + (c_z[z + 1, :rows] * first[up, :rows] + c_z[z, :rows] * first[down, :rows])
                - total_ref[z]
            )
            beyond = edges(NEXT, z)
            for n, span in enumerate((low, high)):
                new_ref[z, :, span] = press[z, :, span] + inverse_ref[z, :, span] * (
                    gathered[:, span] + beyond[n][:rows]
                )

        depth_pairs(second)

    for plane in range(planes):
        z = step * planes + plane
        faces = [face[:rows] for face in edges(FACE, z)]
        for i in range(COMPS):
            side = pltpu.roll(side_h[i], LANES - 2 - 4 * z, 1)
            here = mob[i, z]
            for span, face in zip((low, high), faces):
                res_ref[i, plane, :, span] = near[i, plane, :, span] + face * (here[:, span] + side)


def on_device(
    pressure, composition, mass_old, pore_volume, trans_x, trans_y, trans_z,
    volatility, pressure_slope, mixing, two_phase,
):
    depth, rows, width = pressure.shape
    f32 = jnp.float32
    smem = pl.BlockSpec(memory_space=pltpu.SMEM)
    vmem = pl.BlockSpec(memory_space=pltpu.VMEM)
    def params(mib):
        return pltpu.CompilerParams(vmem_limit_bytes=mib * MIB)

    scalars = (two_phase, volatility, pressure_slope, mixing)

    def swapped(block, axis, first):
        count = lax.axis_size(axis)
        pairs = [(i, i + 1) for i in range(first, count - 1, 2)]
        return lax.ppermute(block, axis, pairs + [(j, i) for i, j in pairs])

    whole = jax.ShapeDtypeStruct((COMPS, depth, rows, width), f32)
    sums = jax.ShapeDtypeStruct((depth, rows, width), f32)
    packed = jax.ShapeDtypeStruct((len(UNITS) // 2, DEPTH_SLOTS * depth, width), f32)
    parts = depth // PLANES
    tiles = rows // ROWS

    fields = (composition, pressure, pore_volume, mass_old, trans_x, trans_y, trans_z)

    def pinned(x):
        return pltpu.with_memory_space_constraint(x, pltpu.HBM)

    operand = jax.ShapeDtypeStruct((PART, DEEP), jnp.bfloat16)
    anywhere = pl.BlockSpec(memory_space=pl.ANY)

    def own(edge, start, count, small, before):
        tile_row = (lambda t: t * (tiles - 1)) if edge else (lambda t: start + t)
        plane = pl.BlockSpec((PLANES, ROWS, width), lambda t, z: (z, tile_row(t), 0))
        planes = pl.BlockSpec((COMPS, PLANES, ROWS, width), lambda t, z: (0, z, tile_row(t), 0))
        cells = count * ROWS * depth * width
        used = fields if edge else fields[:4]
        return pl.pallas_call(
            functools.partial(own_cells, edge, start),
            grid=(count, parts),
            in_specs=[smem] * 3
            + [smem if edge else vmem]
            + [planes, plane, plane, planes]
            + [plane] * (len(used) - 4)
            + [anywhere] * len(before),
            out_specs=[planes, planes, plane, plane] + ([vmem] * 3 if edge else []),
            out_shape=[whole, whole, sums, sums] + ([packed, packed, operand] if edge else []),
            input_output_aliases={4 + len(used) + k: k for k in range(len(before))},
            compiler_params=params(24),
            cost_estimate=pl.CostEstimate(
                flops=900 * cells, transcendentals=190 * cells, bytes_accessed=4 * 39 * cells
            ),
            name="edge_cells" if edge else "inner_cells",
        )(*(pinned(x) if edge else x for x in (*small, *used)), *before)

    *begun, one, two, mixer = own(True, 0, 2, scalars, ())
    rows_one = swapped(one, "areal", 0)
    rows_two = swapped(two, "areal", 1)
    mob, acc, mob_sum, acc_sum = own(False, 1, tiles - 2, (*scalars[:3], mixer), begun)

    packet = pl.pallas_call(
        pack_columns,
        in_specs=[vmem] * 10,
        out_specs=vmem,
        out_shape=jax.ShapeDtypeStruct((rows + ROWS, FIELDS * 32), f32),
        compiler_params=params(24),
        name="pack_columns",
    )(rows_one, rows_two, mob, mob_sum, pressure, trans_x, trans_y, trans_z, pore_volume, acc_sum)

    columns_one = swapped(packet, "layer", 0)
    columns_two = swapped(packet, "layer", 1)

    planes = pl.BlockSpec((COMPS, 2, rows, width), lambda s: (0, s, 0, 0))
    tall = jax.ShapeDtypeStruct((depth, rows + ROWS, width), f32)
    above_faces = jax.ShapeDtypeStruct((depth + 1, rows + ROWS, width), f32)
    cells = rows * depth * width
    near, *sweep = pl.pallas_call(
        near_residual,
        grid=(depth // 2,),
        in_specs=[vmem] * 11,
        out_specs=[planes] + [vmem] * 5,
        out_shape=[whole, tall, tall, tall, tall, above_faces],
        scratch_shapes=[
            pltpu.VMEM((COMPS, depth, ROWS, width), f32),
            pltpu.VMEM((FIELDS - COMPS, depth, ROWS, width), f32),
            pltpu.VMEM((2, depth, rows, width), f32),
            pltpu.VMEM((depth, rows, width), f32),
            pltpu.VMEM((depth + 1, rows, width), f32),
        ],
        compiler_params=params(24),
        cost_estimate=pl.CostEstimate(flops=150 * cells, transcendentals=0, bytes_accessed=4 * 31 * cells),
        name="near_residual",
    )(
        rows_one, rows_two,
        pressure, trans_x, trans_y, trans_z, pore_volume, mob_sum, acc_sum, mob, acc,
    )

    return pl.pallas_call(
        finish,
        grid=(depth // 2,),
        in_specs=[vmem] * 10 + [planes],
        out_specs=[planes, vmem],
        out_shape=[whole, sums],
        scratch_shapes=[
            pltpu.VMEM((COMPS, rows, LANES), f32),
            pltpu.VMEM((4, rows + ROWS, LANES), f32),
            pltpu.VMEM((depth, rows + ROWS, width), f32),
            pltpu.VMEM((depth, rows, width), f32),
            pltpu.VMEM((depth, rows, width), f32),
        ],
        compiler_params=params(24),
        name="finish",
    )(columns_one, columns_two, packet, pressure, *sweep, mob, near)


def solution(mesh):
    placed = (
        P(None, "areal", "layer"),
        P(None, None, "areal", "layer"),
        P(None, None, "areal", "layer"),
        P(None, "areal", "layer"),
        P(None, "areal", "layer"),
        P(None, "areal", "layer"),
        P(None, "areal", "layer"),
        P(),
        P(),
        P(),
        P(None, "areal"),
    )
    return jax.shard_map(
        on_device,
        mesh=mesh,
        in_specs=placed,
        out_specs=(P(None, None, "areal", "layer"), P(None, "areal", "layer")),
        check_vma=False,
    )
```

```python
import jax
import jax.numpy as jnp
from jax import lax
from jax.experimental import pallas as pl
from jax.experimental.pallas import tpu as pltpu
from jax.sharding import PartitionSpec as P

SS_ITERS = 3
RR_ITERS = 3
LIGHT = 4
COMPS = 9
FIELDS = 16
MOB, PRESS, TX, TY, TZ, PORE, ACC = range(COMPS, FIELDS)
UNITS = (MOB, PRESS, TX, (0, 1), (2, 3), (4, 5), (6, 7), (8, TY), (TZ, PORE), (ACC, ACC))
DEPTH_SLOTS = 4
TIME_STEP = 4.0
COMPRESS = 0.2
VAPOUR_WEIGHT = 1.0 / 0.25
LANES = 128
ROWS = 8
MIB = 1024 * 1024
PART = (COMPS + 1) * ROWS
DEEP = 256


def rcp(x):
    return pltpu.reciprocal(x, approx=True)


def total_of(terms):
    terms = list(terms)
    while len(terms) > 1:
        terms = [a + b for a, b in zip(terms[::2], terms[1::2])] + (
            [terms[-1]] if len(terms) % 2 else []
        )
    return terms[0]


def split(x):
    high = x.astype(jnp.bfloat16)
    return high, (x - high.astype(jnp.float32)).astype(jnp.bfloat16)


def mixing_operand(mix_ref):
    shape = (ROWS, DEEP)
    lane, row = lane_of(shape), row_of(shape)
    part = lax.div(lane, PART)
    within = lane - PART * part
    column = lax.div(within, ROWS)
    on = (within - ROWS * column == row) & (part < 3)
    blocks = []
    for i in range(COMPS):
        value = jnp.zeros(shape, jnp.float32)
        for j in range(COMPS):
            value = jnp.where(column == j, 2.0 * mix_ref[i, j], value)
        high, low = split(value)
        value = jnp.where(part == 2, low.astype(jnp.float32), high.astype(jnp.float32))
        blocks.append(jnp.where(on, value, 0.0))
    blocks.append(jnp.zeros(shape, jnp.float32))
    return jnp.concatenate(blocks, axis=0).astype(jnp.bfloat16)


def mixed(operand, spread):
    shape = spread[0].shape
    high, low = split(jnp.concatenate(spread + [jnp.zeros(shape, jnp.float32)], axis=0))
    tail = jnp.zeros((DEEP - 3 * PART, shape[1]), jnp.bfloat16)
    out = jnp.dot(
        operand,
        jnp.concatenate([high, low, high, tail], axis=0),
        preferred_element_type=jnp.float32,
    )
    return [out[ROWS * i : ROWS * (i + 1)] for i in range(COMPS)]


def flash(feed, pressure, signed, slope, operand):
    log_press = jnp.log(pressure)
    half_base = [0.5 * signed[i] - (0.5 * slope[i]) * log_press for i in range(COMPS)]
    spread = None
    for outer in range(SS_ITERS):
        if outer == 0:
            half_log = half_base
        else:
            mix = mixed(operand, spread)
            half_log = [half_base[i] - 0.5 * jnp.tanh(mix[i]) for i in range(COMPS)]
        t = [jnp.tanh(half_log[i]) for i in range(COMPS)]
        u = [rcp(t[i]) for i in range(COMPS)]
        psi = None
        for inner in range(RR_ITERS):
            q = t if inner == 0 else [rcp(u[i] + psi) for i in range(COMPS)]
            part = [feed[i] * q[i] for i in range(COMPS)]
            step = total_of(part) * rcp(total_of(part[i] * q[i] for i in range(COMPS)))
            psi = jnp.clip(step if inner == 0 else psi + step, -1.0, 1.0)
        spread = [feed[i] * rcp(u[i] + psi) for i in range(COMPS)]
    liquid_part = (0.25 * (1.0 - psi)) * (1.0 - psi)
    vapour_part = (0.25 * VAPOUR_WEIGHT * (1.0 + psi)) * (1.0 + psi)
    both, apart = vapour_part + liquid_part, vapour_part - liquid_part
    return [spread[i] * (both * u[i] + apart) for i in range(COMPS)]


def parameters(vol_ref, slope_ref):
    signed = [vol_ref[i] if i < LIGHT else -vol_ref[i] for i in range(COMPS)]
    return signed, [slope_ref[i] for i in range(COMPS)]


def lane_of(shape):
    return lax.broadcasted_iota(jnp.int32, shape, len(shape) - 1)


def row_of(shape):
    return lax.broadcasted_iota(jnp.int32, shape, len(shape) - 2)


class Rows:
    def __init__(self, edge, inner):
        self.edge, self.inner = edge, inner

    def __getitem__(self, at):
        at = at if isinstance(at, tuple) else (at,)
        edge = self.edge[at]
        return jnp.concatenate([edge[:ROWS], self.inner[at], edge[ROWS:]], axis=0)


def pack_rows(field, low_ref, high_ref, planes):
    row = None
    for n in range(0, len(UNITS), 2):
        lows, highs = [], []
        for z in range(planes):
            for unit in UNITS[n : n + 2]:
                if isinstance(unit, tuple):
                    (first_a, last_a), (first_b, last_b) = (field(k, z) for k in unit)
                    if row is None:
                        row = row_of(first_a.shape)
                    low = jnp.where(row == 2, pltpu.roll(first_a, 2, 0), pltpu.roll(first_b, 3, 0))
                    high = jnp.where(row == 0, pltpu.roll(last_b, 1, 0), pltpu.roll(last_a, 2, 0))
                else:
                    first, last = field(unit, z)
                    if row is None:
                        row = row_of(first.shape)
                    low, high = pltpu.roll(first, 2, 0), pltpu.roll(last, 2, 0)
                lows.append(low)
                highs.append(high)
        for pair in range(planes // 2):
            at = pl.ds(pair * ROWS, ROWS)
            l, h = lows[4 * pair : 4 * pair + 4], highs[4 * pair : 4 * pair + 4]
            if low_ref is not None:
                low_ref[n // 2, at, :] = jnp.where(
                    row < 4,
                    jnp.where(row >= 2, l[0], pltpu.roll(l[1], 6, 0)),
                    jnp.where(row >= 6, pltpu.roll(l[2], 4, 0), pltpu.roll(l[3], 2, 0)),
                )
            if high_ref is not None:
                high_ref[n // 2, at, :] = jnp.where(
                    row < 4,
                    jnp.where(row < 2, h[0], pltpu.roll(h[1], 2, 0)),
                    jnp.where(row < 6, pltpu.roll(h[2], 4, 0), pltpu.roll(h[3], 6, 0)),
                )


def row_tiles(one, two, wanted, start=0, stop=None):
    shape = one.shape[1:]
    upper = row_of(shape) % DEPTH_SLOTS < 2
    tile_row = row_of((ROWS, shape[1]))
    stop = stop or shape[0] // DEPTH_SLOTS
    tiles = {}
    for n, unit in enumerate(UNITS):
        fields = unit if isinstance(unit, tuple) else (unit,)
        if not any(k in wanted for k in fields):
            continue
        up, down = by_side("areal", one[n // 2], two[n // 2])
        if n % 2:
            up, down = pltpu.roll(up, shape[0] - 2, 0), pltpu.roll(down, 2, 0)
        both = jnp.where(upper, up, down)
        for z in range(start, stop):
            at = (z // 2) * ROWS
            tile = pltpu.roll(both[at : at + ROWS], 6 - 4 * (z % 2), 0)
            if fields[0] in wanted:
                tiles.setdefault(fields[0], []).append(tile)
            if fields[-1] in wanted and fields[-1] != fields[0]:
                other = jnp.where(tile_row < 4, pltpu.roll(tile, ROWS - 1, 0), pltpu.roll(tile, 1, 0))
                tiles.setdefault(fields[-1], []).append(other)
    return tiles


def pack_columns(rows_one, rows_two, *refs):
    press, tx, ty, tz, pore, edge_mob, _, edge_mob_sum, edge_acc_sum, mob, _, mob_sum, acc_sum, out_ref = refs
    depth, rows, width = press.shape
    shape = (rows + ROWS, LANES)
    lane = lane_of(shape)
    mob, mob_sum, acc_sum = (
        Rows(*both) for both in ((edge_mob, mob), (edge_mob_sum, mob_sum), (edge_acc_sum, acc_sum))
    )
    corner_fields = {MOB: mob_sum, PRESS: press, TX: tx, TY: ty}
    others = {TZ: tz, PORE: pore, ACC: acc_sum, **corner_fields}
    corners = row_tiles(rows_one, rows_two, corner_fields)
    nothing = jnp.zeros((ROWS, LANES), jnp.float32)
    for tile in range(FIELDS // 4):
        packed = jnp.zeros(shape, jnp.float32)
        for quarter in range(4):
            k = 4 * tile + quarter
            for z in range(depth):
                plane = mob[k, z] if k < COMPS else others[k][z]
                first, last = plane[:, :LANES], plane[:, -LANES:]
                at = 32 * quarter + 4 * z
                both = jnp.where(lane_of(first.shape) < LANES // 2, first, last)
                if k < COMPS:
                    both = pltpu.roll(both, at + 1, 1)
                    on = (lane_of(first.shape) >= at) & (lane_of(first.shape) < at + 2)
                    packed = jnp.concatenate([jnp.where(on, both, packed[:rows]), nothing], axis=0)
                    continue
                end = nothing
                if k in corner_fields:
                    end = corners[k][z]
                    end = jnp.where(lane_of(end[:, :LANES].shape) < LANES // 2, end[:, :LANES], end[:, -LANES:])
                both = pltpu.roll(jnp.concatenate([both, end], axis=0), (at + 2) % LANES, 1)
                packed = jnp.where((lane >= at) & (lane < at + 4), both, packed)
        out_ref[:, tile * LANES : (tile + 1) * LANES] = packed


def spread_fields(tiles):
    fields = []
    for tile in tiles:
        for quarter in range(4):
            turn = (LANES - 32 * quarter) % LANES
            fields.append(pltpu.roll(tile, turn, 1) if turn else tile)
    return fields


def side_fields(one, two):
    lane = lane_of((one.shape[0], LANES))
    tiles, mobilities = [], []
    for tile in range(FIELDS // 4):
        span = slice(tile * LANES, (tile + 1) * LANES)
        left, right = by_side("layer", one[:, span], two[:, span])
        mobilities.append(jnp.where(lane % 4 == 1, right, pltpu.roll(left, 2, 1)))
        tiles.append(jnp.where(lane % 4 < 2, left, right))
    return spread_fields(mobilities)[:COMPS] + spread_fields(tiles)[COMPS:]


def flash_rows(source, target, tile_row, flags, vol, slope, operand, comp, press, pore, mass, outs):
    mob_ref, acc_ref, mob_sum, acc_sum = outs
    layer = lax.axis_index("layer")
    depth, _, width = press.shape

    def beside(ref, *lead):
        return jnp.concatenate([ref[(*lead, z, source)] for z in range(depth)], axis=1)

    def store(ref, value, *lead):
        for z in range(depth):
            ref[(*lead, z, target)] = value[:, z * width : (z + 1) * width]

    raw = [beside(comp, i) for i in range(COMPS)]
    inverse = rcp(total_of(raw))
    feed = [raw[i] * inverse for i in range(COMPS)]
    volume = beside(pore)
    acc = [volume * feed[i] - beside(mass, i) for i in range(COMPS)]
    for i in range(COMPS):
        store(acc_ref, acc[i], i)
    store(acc_sum, total_of(acc))
    first, last = flags[layer, 2 * tile_row], flags[layer, 2 * tile_row + 1]

    @pl.when(first + last > 0)
    def _():
        signed, slopes = parameters(vol, slope)
        two = flash(feed, beside(press), signed, slopes, operand[...])
        marked = jnp.where(row_of(feed[0].shape) < ROWS // 2, first, last) > 0
        mobility = [jnp.where(marked, two[i], feed[i]) for i in range(COMPS)]
        for i in range(COMPS):
            store(mob_ref, mobility[i], i)
        store(mob_sum, total_of(mobility))

    @pl.when(first + last == 0)
    def _():
        for i in range(COMPS):
            store(mob_ref, feed[i], i)
        store(mob_sum, total_of(feed))


def edge_cells(
    flags, vol, slope, mix, comp, press, pore, mass, tx, ty, tz,
    mob_ref, acc_ref, mob_sum, acc_sum, one_ref, two_ref, operand, comp_i, press_i, pore_i, mass_i,
    comp_s, press_s, pore_s, mass_s, tx_s, ty_s, tz_s, sems,
):
    depth, rows, _ = press.shape
    fetched = (
        (comp, comp_s), (press, press_s), (pore, pore_s), (mass, mass_s), (tx, tx_s), (ty, ty_s), (tz, tz_s)
    )

    ahead = (comp_i, press_i, pore_i, mass_i)

    def fetch(end, n):
        source, slot = fetched[n]
        at = pl.ds(end * (rows - ROWS), ROWS) if end < 2 else pl.ds(ROWS, rows - 2 * ROWS)
        return pltpu.make_async_copy(
            source.at[:, :, at, :] if len(source.shape) == 4 else source.at[:, at, :],
            slot.at[end] if end < 2 else ahead[n],
            sems.at[end, n],
        )

    for end in range(2):
        for n in range(len(fetched)):
            fetch(end, n).start()
    operand[...] = mixing_operand(mix)
    odd = lax.axis_index("areal") % 2 == 1
    for end in range(2):
        for n in range(len(fetched)):
            fetch(end, n).wait()
        if end == 0:
            for n in range(len(ahead)):
                fetch(2, n).start()
        target = slice(end * ROWS, (end + 1) * ROWS)
        flash_rows(
            slice(None), target, end * (rows // ROWS - 1), flags, vol, slope, operand,
            *(slot.at[end] for _, slot in fetched[:4]), (mob_ref, acc_ref, mob_sum, acc_sum),
        )

        def field(k, z):
            if k < COMPS:
                here = mob_ref[k, z, target]
            elif k in (MOB, ACC):
                here = (mob_sum if k == MOB else acc_sum)[z, target]
            else:
                here = {PRESS: press_s, TX: tx_s, TY: ty_s, TZ: tz_s, PORE: pore_s}[k][end, z]
            return here, here

        for turn, ref in enumerate((one_ref, two_ref)):
            @pl.when(odd == (end == turn))
            def _():
                pack_rows(field, *((ref, None) if end == 0 else (None, ref)), depth)

    for n in range(len(ahead)):
        fetch(2, n).wait()


def inner_cells(flags, vol, slope, operand, comp, press, pore, mass, *outs):
    def tile(t, carry):
        at = pl.ds(pl.multiple_of(t * ROWS, ROWS), ROWS)
        flash_rows(at, at, t + 1, flags, vol, slope, operand, comp, press, pore, mass, outs)
        return carry

    lax.fori_loop(0, press.shape[1] // ROWS, tile, 0)


def by_side(axis, one, two):
    odd = lax.axis_index(axis) % 2 == 1
    return jnp.where(odd, one, two), jnp.where(odd, two, one)


def by_pairs(count, body):
    def pair(t, carry):
        body(2 * t)
        body(2 * t + 1)
        return carry

    lax.fori_loop(0, count // 2, pair, 0)


def near_residual(
    rows_one, rows_two, press, tx, ty, tz, pore,
    edge_mob, edge_acc, edge_mob_sum, edge_acc_sum, mob, acc, mob_sum, acc_sum,
    out_ref, total_ref, diagonal_ref, c_x, c_y, c_z,
    rows_h, fields_h, g_x, g_y, g_z,
):
    depth, rows, width = press.shape
    areal, areals = lax.axis_index("areal"), lax.axis_size("areal")
    tall = rows + ROWS
    full = (tall, width)
    own = slice(0, rows)
    mob, acc, mob_sum, acc_sum = (
        Rows(*both)
        for both in ((edge_mob, mob), (edge_acc, acc), (edge_mob_sum, mob_sum), (edge_acc_sum, acc_sum))
    )
    fields = {MOB: mob_sum, PRESS: press, TX: tx, TY: ty, TZ: tz, PORE: pore, ACC: acc_sum}
    tiles = row_tiles(rows_one, rows_two, range(FIELDS))
    for z in range(depth):
        for i in range(COMPS):
            rows_h[i, z] = tiles[i][z]
        for n, k in enumerate(fields):
            fields_h[n, z] = tiles[k][z]

    end_x = (row_of(full) == rows - 1) & (areal == areals - 1)
    end_y = lane_of(full) == width - 1
    scale = 0.5 * TIME_STEP
    c_z[0] = jnp.zeros(full, jnp.float32)
    g_z[0] = jnp.zeros((rows, width), jnp.float32)

    def update(z):
        m, p, x, y, zz, volume, total = (
            jnp.concatenate([ref[z], fields_h[n, z]], axis=0) for n, ref in enumerate(fields.values())
        )
        up, down = jnp.minimum(z + 1, depth - 1), jnp.maximum(z - 1, 0)
        p_up = jnp.concatenate([press[up], fields_h[1, up]], axis=0)
        p_down = jnp.concatenate([press[down], fields_h[1, down]], axis=0)
        m_up = jnp.concatenate([mob_sum[up], fields_h[0, up]], axis=0)
        strength_x = jnp.where(end_x, 0.0, scale * x)
        strength_y = jnp.where(end_y, 0.0, scale * y)
        strength_z = jnp.where(z < depth - 1, scale, 0.0) * zz
        dx = p - pltpu.roll(p, tall - 1, 0)
        dy = p - pltpu.roll(p, width - 1, 1)
        dz = p - p_up
        cx = strength_x * (m + pltpu.roll(m, tall - 1, 0))
        cy = strength_y * (m + pltpu.roll(m, width - 1, 1))
        cz = strength_z * (m + m_up)
        cz_low = c_z[z]
        gx = strength_x * dx
        g_x[0, z], g_x[1, z] = gx[own], -pltpu.roll(gx, 1, 0)[own]
        g_y[z], g_z[z + 1] = (strength_y * dy)[own], (strength_z * dz)[own]
        c_x[z], c_y[z], c_z[z + 1] = cx, cy, cz
        fx, fy = cx * dx, cy * dy
        total_ref[z] = (
            total
            + (fx - pltpu.roll(fx, 1, 0))
            + (fy - pltpu.roll(fy, 1, 1))
            + (cz * dz + cz_low * (p - p_down))
        )
        diagonal_ref[z] = (
            COMPRESS * volume
            + (cx + pltpu.roll(cx, 1, 0))
            + (cy + pltpu.roll(cy, 1, 1))
            + (cz + cz_low)
        )

    by_pairs(depth, update)

    def residual(z):
        down, up = jnp.maximum(z - 1, 0), jnp.minimum(z + 1, depth - 1)
        gx, gx_low, gy, gz, gz_low = g_x[0, z], g_x[1, z], g_y[z], g_z[z + 1], -g_z[z]
        gy_low = -pltpu.roll(gy, 1, 1)
        middle = (gx + gx_low) + (gy + gy_low) + (gz + gz_low)
        for i in range(COMPS):
            here = mob[i, z]
            tall_here = jnp.concatenate([here, rows_h[i, z]], axis=0)
            out_ref[i, z] = (
                acc[i, z]
                + middle * here
                + gx * pltpu.roll(tall_here, tall - 1, 0)[own]
                + gx_low * pltpu.roll(tall_here, 1, 0)[own]
                + gy * pltpu.roll(here, width - 1, 1)
                + gy_low * pltpu.roll(here, 1, 1)
                + gz * mob[i, up]
                + gz_low * mob[i, down]
            )

    by_pairs(depth, residual)


def finish(
    columns_one, columns_two, packet, press, total_in, diagonal_in, c_x, c_y, c_z, edge_mob, mob, near,
    res_ref, new_ref,
    side_h, edge_h, first, total_ref, inverse_ref,
):
    step = pl.program_id(0)
    planes = res_ref.shape[1]
    depth, rows, width = press.shape
    layer, layers = lax.axis_index("layer"), lax.axis_size("layer")
    areal, areals = lax.axis_index("areal"), lax.axis_size("areal")
    tall = rows + ROWS
    lane = lane_of((tall, LANES))
    at_first, at_last = lane == 0, lane == LANES - 1
    low, high = slice(0, LANES), slice(width - LANES, width)
    FLUX, COUPLE, FACE, NEXT = range(4)
    mob = Rows(edge_mob, mob)

    def edges(which, z):
        both = pltpu.roll(edge_h[which], LANES - 1 - 4 * z, 1)
        return jnp.where(at_first, both, 0.0), jnp.where(at_last, both, 0.0)

    @pl.when(step == 0)
    def _():
        halo = side_fields(columns_one, columns_two)
        here = spread_fields([packet[:, t : t + LANES] for t in range(0, FIELDS * 32, LANES)])
        for i in range(COMPS):
            side_h[i] = halo[i][:rows]
        scale = 0.5 * TIME_STEP
        is_left = lane % 4 == 1

        def turned(x, by):
            return pltpu.roll(x, by % LANES, 1)

        def outer(x):
            return jnp.where(is_left, turned(x, 1), turned(x, -1))

        def inner(x):
            return jnp.where(is_left, turned(x, -1), turned(x, 1))

        m, p = halo[MOB], halo[PRESS]
        strength = scale * halo[TY]
        own_strength = jnp.where(layer < layers - 1, scale, 0.0) * here[TY]
        c_out = jnp.where(is_left, turned(strength, 1), strength) * (m + outer(m))
        s_in = jnp.where(is_left, strength, turned(own_strength, 1))
        c_in = s_in * (m + inner(here[MOB]))
        d_in = p - inner(here[PRESS])
        end_x = (row_of(lane.shape) == rows - 1) & (areal == areals - 1)
        cx = jnp.where(end_x, 0.0, scale * halo[TX]) * (m + pltpu.roll(m, tall - 1, 0))
        cz = jnp.where(lane < 4 * (depth - 1), scale * halo[TZ], 0.0) * (m + turned(m, -4))
        fx = cx * (p - pltpu.roll(p, tall - 1, 0))
        fz = cz * (p - turned(p, -4))
        total = (
            halo[ACC]
            + (c_out * (p - outer(p)) + c_in * d_in)
            + (fx - pltpu.roll(fx, 1, 0))
            + (fz - turned(fz, 4))
        )
        diagonal = (
            COMPRESS * halo[PORE] + (c_out + c_in) + (cx + pltpu.roll(cx, 1, 0)) + (cz + turned(cz, 4))
        )
        usable = diagonal > 0.0
        beside = jnp.where(usable, -total * rcp(jnp.where(usable, diagonal, 1.0)), 0.0)
        for which, value in (
            (FLUX, -c_in * d_in), (COUPLE, c_in), (FACE, -s_in * d_in), (NEXT, c_in * beside)
        ):
            edge_h[which] = jnp.where(is_left, value, turned(value, -2))

    @pl.when(step == 1)
    def _():
        def update(z):
            flux, couple = edges(FLUX, z), edges(COUPLE, z)
            for n, span in enumerate((low, high)):
                total = total_in[z, :, span] + flux[n]
                diagonal = diagonal_in[z, :, span] + couple[n]
                usable = diagonal > 0.0
                inverse = rcp(jnp.where(usable, diagonal, 1.0))
                first[z, :, span] = jnp.where(usable, -total * inverse, 0.0)
                total_ref[z, :, span] = total[:rows]
                inverse_ref[z, :, span] = inverse[:rows]

        by_pairs(depth, update)

    @pl.when(step == 2)
    def _():
        def second(z):
            here = first[z]
            up, down = jnp.minimum(z + 1, depth - 1), jnp.maximum(z - 1, 0)
            cx, cy = c_x[z], c_y[z, :rows]
            own = here[:rows]
            gathered = (
                (cx * pltpu.roll(here, tall - 1, 0))[:rows]
                + pltpu.roll(cx * here, 1, 0)[:rows]
                + cy * pltpu.roll(own, width - 1, 1)
                + pltpu.roll(cy * own, 1, 1)
                + (c_z[z + 1, :rows] * first[up, :rows] + c_z[z, :rows] * first[down, :rows])
                - total_ref[z]
            )
            beyond = edges(NEXT, z)
            for n, span in enumerate((low, high)):
                new_ref[z, :, span] = press[z, :, span] + inverse_ref[z, :, span] * (
                    gathered[:, span] + beyond[n][:rows]
                )

        by_pairs(depth, second)

    for plane in range(planes):
        z = step * planes + plane
        faces = [face[:rows] for face in edges(FACE, z)]
        for i in range(COMPS):
            side = pltpu.roll(side_h[i], LANES - 2 - 4 * z, 1)
            here = mob[i, z]
            for span, face in zip((low, high), faces):
                res_ref[i, plane, :, span] = near[i, z, :, span] + face * (here[:, span] + side)


def on_device(
    pressure, composition, mass_old, pore_volume, trans_x, trans_y, trans_z,
    volatility, pressure_slope, mixing, two_phase,
):
    depth, rows, width = pressure.shape
    f32 = jnp.float32
    smem = pl.BlockSpec(memory_space=pltpu.SMEM)
    vmem = pl.BlockSpec(memory_space=pltpu.VMEM)
    def params(mib):
        return pltpu.CompilerParams(vmem_limit_bytes=mib * MIB)

    scalars = (two_phase, volatility, pressure_slope, mixing)

    def swapped(block, axis, first):
        count = lax.axis_size(axis)
        pairs = [(i, i + 1) for i in range(first, count - 1, 2)]
        return lax.ppermute(block, axis, pairs + [(j, i) for i, j in pairs])

    whole = jax.ShapeDtypeStruct((COMPS, depth, rows, width), f32)
    sums = jax.ShapeDtypeStruct((depth, rows, width), f32)
    packed = jax.ShapeDtypeStruct((len(UNITS) // 2, DEPTH_SLOTS * depth, width), f32)
    fields = (composition, pressure, pore_volume, mass_old, trans_x, trans_y, trans_z)

    def parts(count):
        planes = jax.ShapeDtypeStruct((COMPS, depth, count, width), f32)
        plane = jax.ShapeDtypeStruct((depth, count, width), f32)
        return [planes, planes, plane, plane]

    between = [jax.ShapeDtypeStruct((*x.shape[:-2], rows - 2 * ROWS, width), f32) for x in fields[:4]]
    *results, operand, comp, press, pore, mass = pl.pallas_call(
        edge_cells,
        in_specs=[smem] * 4 + [pl.BlockSpec(memory_space=pl.ANY)] * len(fields),
        out_specs=[vmem] * 11,
        out_shape=parts(2 * ROWS)
        + [packed, packed, jax.ShapeDtypeStruct((PART, DEEP), jnp.bfloat16), *between],
        scratch_shapes=[pltpu.VMEM((2, *x.shape[:-2], ROWS, width), f32) for x in fields]
        + [pltpu.SemaphoreType.DMA((3, len(fields)))],
        compiler_params=params(24),
        name="edge_cells",
    )(*(pltpu.with_memory_space_constraint(x, pltpu.HBM) for x in (*scalars, *fields)))
    *edge, one, two = results
    rows_one = swapped(one, "areal", 0)
    rows_two = swapped(two, "areal", 1)
    cells = rows * depth * width
    inner = pl.pallas_call(
        inner_cells,
        in_specs=[smem] * 3 + [vmem] * 5,
        out_specs=[vmem] * 4,
        out_shape=parts(rows - 2 * ROWS),
        compiler_params=params(24),
        cost_estimate=pl.CostEstimate(
            flops=450 * cells, transcendentals=95 * cells, bytes_accessed=2 * 39 * cells
        ),
        name="inner_cells",
    )(*scalars[:3], operand, comp, press, pore, mass)
    planes_of = (pressure, trans_x, trans_y, trans_z, pore_volume)

    packet = pl.pallas_call(
        pack_columns,
        in_specs=[vmem] * 15,
        out_specs=vmem,
        out_shape=jax.ShapeDtypeStruct((rows + ROWS, FIELDS * 32), f32),
        compiler_params=params(24),
        name="pack_columns",
    )(rows_one, rows_two, *planes_of, *edge, *inner)

    columns_one = swapped(packet, "layer", 0)
    columns_two = swapped(packet, "layer", 1)

    planes = pl.BlockSpec((COMPS, 2, rows, width), lambda s: (0, s, 0, 0))
    tall = jax.ShapeDtypeStruct((depth, rows + ROWS, width), f32)
    above_faces = jax.ShapeDtypeStruct((depth + 1, rows + ROWS, width), f32)
    near, *sweep = pl.pallas_call(
        near_residual,
        in_specs=[vmem] * 15,
        out_specs=[vmem] * 6,
        out_shape=[whole, tall, tall, tall, tall, above_faces],
        scratch_shapes=[
            pltpu.VMEM((COMPS, depth, ROWS, width), f32),
            pltpu.VMEM((FIELDS - COMPS, depth, ROWS, width), f32),
            pltpu.VMEM((2, depth, rows, width), f32),
            pltpu.VMEM((depth, rows, width), f32),
            pltpu.VMEM((depth + 1, rows, width), f32),
        ],
        compiler_params=params(24),
        cost_estimate=pl.CostEstimate(flops=150 * cells, transcendentals=0, bytes_accessed=4 * 31 * cells),
        name="near_residual",
    )(rows_one, rows_two, *planes_of, *edge, *inner)

    return pl.pallas_call(
        finish,
        grid=(depth // 2,),
        in_specs=[vmem] * 12,
        out_specs=[planes, vmem],
        out_shape=[whole, sums],
        scratch_shapes=[
            pltpu.VMEM((COMPS, rows, LANES), f32),
            pltpu.VMEM((4, rows + ROWS, LANES), f32),
            pltpu.VMEM((depth, rows + ROWS, width), f32),
            pltpu.VMEM((depth, rows, width), f32),
            pltpu.VMEM((depth, rows, width), f32),
        ],
        compiler_params=params(24),
        name="finish",
    )(columns_one, columns_two, packet, pressure, *sweep, edge[0], inner[0], near)


def solution(mesh):
    placed = (
        P(None, "areal", "layer"),
        P(None, None, "areal", "layer"),
        P(None, None, "areal", "layer"),
        P(None, "areal", "layer"),
        P(None, "areal", "layer"),
        P(None, "areal", "layer"),
        P(None, "areal", "layer"),
        P(),
        P(),
        P(),
        P(None, "areal"),
    )
    return jax.shard_map(
        on_device,
        mesh=mesh,
        in_specs=placed,
        out_specs=(P(None, None, "areal", "layer"), P(None, "areal", "layer")),
        check_vma=False,
    )
```

```python
import jax
import jax.numpy as jnp
from jax import lax
from jax.experimental import pallas as pl
from jax.experimental.pallas import tpu as pltpu
from jax.sharding import PartitionSpec as P

SS_ITERS = 3
RR_ITERS = 3
LIGHT = 4
COMPS = 9
FIELDS = 16
MOB, PRESS, TX, TY, TZ, PORE, ACC = range(COMPS, FIELDS)
UNITS = (MOB, PRESS, TX, (0, 1), (2, 3), (4, 5), (6, 7), (8, TY), (TZ, PORE), (ACC, ACC))
DEPTH_SLOTS = 4
TIME_STEP = 4.0
COMPRESS = 0.2
VAPOUR_WEIGHT = 1.0 / 0.25
LANES = 128
ROWS = 8
MIB = 1024 * 1024
PART = (COMPS + 1) * ROWS
DEEP = 256


def rcp(x):
    return pltpu.reciprocal(x, approx=True)


def total_of(terms):
    terms = list(terms)
    while len(terms) > 1:
        terms = [a + b for a, b in zip(terms[::2], terms[1::2])] + (
            [terms[-1]] if len(terms) % 2 else []
        )
    return terms[0]


def split(x):
    high = x.astype(jnp.bfloat16)
    return high, (x - high.astype(jnp.float32)).astype(jnp.bfloat16)


def mixing_operand(mix_ref):
    shape = (ROWS, DEEP)
    lane, row = lane_of(shape), row_of(shape)
    part = lax.div(lane, PART)
    within = lane - PART * part
    column = lax.div(within, ROWS)
    on = (within - ROWS * column == row) & (part < 3)
    blocks = []
    for i in range(COMPS):
        value = jnp.zeros(shape, jnp.float32)
        for j in range(COMPS):
            value = jnp.where(column == j, 2.0 * mix_ref[i, j], value)
        high, low = split(value)
        value = jnp.where(part == 2, low.astype(jnp.float32), high.astype(jnp.float32))
        blocks.append(jnp.where(on, value, 0.0))
    blocks.append(jnp.zeros(shape, jnp.float32))
    return jnp.concatenate(blocks, axis=0).astype(jnp.bfloat16)


def mixed(operand, spread):
    shape = spread[0].shape
    high, low = split(jnp.concatenate(spread + [jnp.zeros(shape, jnp.float32)], axis=0))
    tail = jnp.zeros((DEEP - 3 * PART, shape[1]), jnp.bfloat16)
    out = jnp.dot(
        operand,
        jnp.concatenate([high, low, high, tail], axis=0),
        preferred_element_type=jnp.float32,
    )
    return [out[ROWS * i : ROWS * (i + 1)] for i in range(COMPS)]


def flash(feed, pressure, signed, slope, operand):
    log_press = jnp.log(pressure)
    half_base = [0.5 * signed[i] - (0.5 * slope[i]) * log_press for i in range(COMPS)]
    spread = None
    for outer in range(SS_ITERS):
        if outer == 0:
            half_log = half_base
        else:
            mix = mixed(operand, spread)
            half_log = [half_base[i] - 0.5 * jnp.tanh(mix[i]) for i in range(COMPS)]
        t = [jnp.tanh(half_log[i]) for i in range(COMPS)]
        u = [rcp(t[i]) for i in range(COMPS)]
        psi = None
        for inner in range(RR_ITERS):
            q = t if inner == 0 else [rcp(u[i] + psi) for i in range(COMPS)]
            part = [feed[i] * q[i] for i in range(COMPS)]
            step = total_of(part) * rcp(total_of(part[i] * q[i] for i in range(COMPS)))
            psi = jnp.clip(step if inner == 0 else psi + step, -1.0, 1.0)
        spread = [feed[i] * rcp(u[i] + psi) for i in range(COMPS)]
    liquid_part = (0.25 * (1.0 - psi)) * (1.0 - psi)
    vapour_part = (0.25 * VAPOUR_WEIGHT * (1.0 + psi)) * (1.0 + psi)
    both, apart = vapour_part + liquid_part, vapour_part - liquid_part
    return [spread[i] * (both * u[i] + apart) for i in range(COMPS)]


def parameters(vol_ref, slope_ref):
    signed = [vol_ref[i] if i < LIGHT else -vol_ref[i] for i in range(COMPS)]
    return signed, [slope_ref[i] for i in range(COMPS)]


def lane_of(shape):
    return lax.broadcasted_iota(jnp.int32, shape, len(shape) - 1)


def row_of(shape):
    return lax.broadcasted_iota(jnp.int32, shape, len(shape) - 2)


class Rows:
    def __init__(self, edge, inner):
        self.edge, self.inner = edge, inner

    def __getitem__(self, at):
        at = at if isinstance(at, tuple) else (at,)
        edge = self.edge[at]
        return jnp.concatenate([edge[:ROWS], self.inner[at], edge[ROWS:]], axis=0)


def pack_rows(field, low, out_ref, depth):
    row = None
    for n in range(0, len(UNITS), 2):
        for pair in range(depth // 2):
            tile = None
            for z in (2 * pair, 2 * pair + 1):
                order = (1, 0) if low else (0, 1)
                for which in order:
                    unit = UNITS[n + which]
                    at = 4 * (z % 2) + (2 if low == (which == 0) else 0)
                    first = 0 if low else ROWS - 1
                    if isinstance(unit, tuple):
                        a, b = unit
                        pieces = [(at, a, at - first), (at + 1, b, at + 1 - first)]
                        if not low:
                            pieces = [(at, b, at - first), (at + 1, a, at + 1 - first)]
                    else:
                        pieces = [(at, unit, at if low else at + 2)]
                    for start, k, turn in pieces:
                        here = field(k, z)
                        if row is None:
                            row = row_of(here.shape)
                        if turn % ROWS:
                            here = pltpu.roll(here, turn % ROWS, 0)
                        tile = here if tile is None else jnp.where(row < start, tile, here)
            out_ref[n // 2, pl.ds(pair * ROWS, ROWS), :] = tile


def row_tiles(one, two, wanted, start=0, stop=None):
    shape = one.shape[1:]
    upper = row_of(shape) % DEPTH_SLOTS < 2
    tile_row = row_of((ROWS, shape[1]))
    stop = stop or shape[0] // DEPTH_SLOTS
    tiles = {}
    for n, unit in enumerate(UNITS):
        fields = unit if isinstance(unit, tuple) else (unit,)
        if not any(k in wanted for k in fields):
            continue
        up, down = by_side("areal", one[n // 2], two[n // 2])
        if n % 2:
            up, down = pltpu.roll(up, shape[0] - 2, 0), pltpu.roll(down, 2, 0)
        both = jnp.where(upper, up, down)
        for z in range(start, stop):
            at = (z // 2) * ROWS
            tile = pltpu.roll(both[at : at + ROWS], 6 - 4 * (z % 2), 0)
            if fields[0] in wanted:
                tiles.setdefault(fields[0], []).append(tile)
            if fields[-1] in wanted and fields[-1] != fields[0]:
                other = jnp.where(tile_row < 4, pltpu.roll(tile, ROWS - 1, 0), pltpu.roll(tile, 1, 0))
                tiles.setdefault(fields[-1], []).append(other)
    return tiles


def pack_columns(rows_one, rows_two, *refs):
    press, tx, ty, tz, pore, edge_mob, _, edge_mob_sum, edge_acc_sum, mob, _, mob_sum, acc_sum, out_ref = refs
    depth, rows, width = press.shape
    shape = (rows + ROWS, LANES)
    lane = lane_of(shape)
    mob, mob_sum, acc_sum = (
        Rows(*both) for both in ((edge_mob, mob), (edge_mob_sum, mob_sum), (edge_acc_sum, acc_sum))
    )
    corner_fields = {MOB: mob_sum, PRESS: press, TX: tx, TY: ty}
    others = {TZ: tz, PORE: pore, ACC: acc_sum, **corner_fields}
    corners = row_tiles(rows_one, rows_two, corner_fields)
    nothing = jnp.zeros((ROWS, LANES), jnp.float32)
    for tile in range(FIELDS // 4):
        packed = jnp.zeros(shape, jnp.float32)
        for quarter in range(4):
            k = 4 * tile + quarter
            for z in range(depth):
                plane = mob[k, z] if k < COMPS else others[k][z]
                first, last = plane[:, :LANES], plane[:, -LANES:]
                at = 32 * quarter + 4 * z
                both = jnp.where(lane_of(first.shape) < LANES // 2, first, last)
                if k < COMPS:
                    both = pltpu.roll(both, at + 1, 1)
                    on = (lane_of(first.shape) >= at) & (lane_of(first.shape) < at + 2)
                    packed = jnp.concatenate([jnp.where(on, both, packed[:rows]), nothing], axis=0)
                    continue
                end = nothing
                if k in corner_fields:
                    end = corners[k][z]
                    end = jnp.where(lane_of(end[:, :LANES].shape) < LANES // 2, end[:, :LANES], end[:, -LANES:])
                both = pltpu.roll(jnp.concatenate([both, end], axis=0), (at + 2) % LANES, 1)
                packed = jnp.where((lane >= at) & (lane < at + 4), both, packed)
        out_ref[:, tile * LANES : (tile + 1) * LANES] = packed


def spread_fields(tiles):
    fields = []
    for tile in tiles:
        for quarter in range(4):
            turn = (LANES - 32 * quarter) % LANES
            fields.append(pltpu.roll(tile, turn, 1) if turn else tile)
    return fields


def side_fields(one, two):
    lane = lane_of((one.shape[0], LANES))
    tiles, mobilities = [], []
    for tile in range(FIELDS // 4):
        span = slice(tile * LANES, (tile + 1) * LANES)
        left, right = by_side("layer", one[:, span], two[:, span])
        mobilities.append(jnp.where(lane % 4 == 1, right, pltpu.roll(left, 2, 1)))
        tiles.append(jnp.where(lane % 4 < 2, left, right))
    return spread_fields(mobilities)[:COMPS] + spread_fields(tiles)[COMPS:]


def flash_rows(source, target, tile_row, flags, vol, slope, operand, comp, press, pore, mass, outs):
    mob_ref, acc_ref, mob_sum, acc_sum = outs
    layer = lax.axis_index("layer")
    depth, _, width = press.shape

    def beside(ref, *lead):
        return jnp.concatenate([ref[(*lead, z, source)] for z in range(depth)], axis=1)

    def store(ref, value, *lead):
        for z in range(depth):
            ref[(*lead, z, target)] = value[:, z * width : (z + 1) * width]

    raw = [beside(comp, i) for i in range(COMPS)]
    inverse = rcp(total_of(raw))
    feed = [raw[i] * inverse for i in range(COMPS)]
    volume = beside(pore)
    acc = [volume * feed[i] - beside(mass, i) for i in range(COMPS)]
    for i in range(COMPS):
        store(acc_ref, acc[i], i)
    store(acc_sum, total_of(acc))
    first, last = flags[layer, 2 * tile_row], flags[layer, 2 * tile_row + 1]

    @pl.when(first + last > 0)
    def _():
        signed, slopes = parameters(vol, slope)
        two = flash(feed, beside(press), signed, slopes, operand[...])
        marked = jnp.where(row_of(feed[0].shape) < ROWS // 2, first, last) > 0
        mobility = [jnp.where(marked, two[i], feed[i]) for i in range(COMPS)]
        for i in range(COMPS):
            store(mob_ref, mobility[i], i)
        store(mob_sum, total_of(mobility))

    @pl.when(first + last == 0)
    def _():
        for i in range(COMPS):
            store(mob_ref, feed[i], i)
        store(mob_sum, total_of(feed))


def edge_cells(
    flags_in, vol_in, slope_in, mix_in, comp, press, pore, mass, tx, ty, tz,
    mob_ref, acc_ref, mob_sum, acc_sum, one_ref, two_ref, operand, comp_i, press_i, pore_i, mass_i,
    flags, vol, slope, mix, comp_s, press_s, pore_s, mass_s, tx_s, ty_s, tz_s, sems, scalar_sems,
):
    depth, rows, _ = press.shape
    fetched = (
        (comp, comp_s), (press, press_s), (pore, pore_s), (mass, mass_s), (tx, tx_s), (ty, ty_s), (tz, tz_s)
    )

    ahead = (comp_i, press_i, pore_i, mass_i)

    def fetch(end, n):
        source, slot = fetched[n]
        at = pl.ds(end * (rows - ROWS), ROWS) if end < 2 else pl.ds(ROWS, rows - 2 * ROWS)
        return pltpu.make_async_copy(
            source.at[:, :, at, :] if len(source.shape) == 4 else source.at[:, at, :],
            slot.at[end] if end < 2 else ahead[n],
            sems.at[end, n],
        )

    scalars = [
        pltpu.make_async_copy(source, slot, scalar_sems.at[n])
        for n, (source, slot) in enumerate(
            ((flags_in, flags), (vol_in, vol), (slope_in, slope), (mix_in, mix))
        )
    ]
    for copy in scalars:
        copy.start()
    for end in range(2):
        for n in range(len(fetched)):
            fetch(end, n).start()
    for copy in scalars:
        copy.wait()
    operand[...] = mixing_operand(mix)
    odd = lax.axis_index("areal") % 2 == 1
    for end in range(2):
        for n in range(len(fetched)):
            fetch(end, n).wait()
        if end == 0:
            for n in range(len(ahead)):
                fetch(2, n).start()
        target = slice(end * ROWS, (end + 1) * ROWS)
        flash_rows(
            slice(None), target, end * (rows // ROWS - 1), flags, vol, slope, operand,
            *(slot.at[end] for _, slot in fetched[:4]), (mob_ref, acc_ref, mob_sum, acc_sum),
        )

        def field(k, z):
            if k < COMPS:
                here = mob_ref[k, z, target]
            elif k in (MOB, ACC):
                here = (mob_sum if k == MOB else acc_sum)[z, target]
            else:
                here = {PRESS: press_s, TX: tx_s, TY: ty_s, TZ: tz_s, PORE: pore_s}[k][end, z]
            return here

        for turn, ref in enumerate((one_ref, two_ref)):
            @pl.when(odd == (end == turn))
            def _():
                pack_rows(field, end == 0, ref, depth)

    for n in range(len(ahead)):
        fetch(2, n).wait()


def inner_cells(flags, vol, slope, operand, comp, press, pore, mass, *outs):
    def tile(t, carry):
        at = pl.ds(pl.multiple_of(t * ROWS, ROWS), ROWS)
        flash_rows(at, at, t + 1, flags, vol, slope, operand, comp, press, pore, mass, outs)
        return carry

    lax.fori_loop(0, press.shape[1] // ROWS, tile, 0)


def by_side(axis, one, two):
    odd = lax.axis_index(axis) % 2 == 1
    return jnp.where(odd, one, two), jnp.where(odd, two, one)


def by_pairs(count, body):
    def pair(t, carry):
        body(2 * t)
        body(2 * t + 1)
        return carry

    lax.fori_loop(0, count // 2, pair, 0)


def near_residual(
    rows_one, rows_two, press, tx, ty, tz, pore,
    edge_mob, edge_acc, edge_mob_sum, edge_acc_sum, mob, acc, mob_sum, acc_sum,
    out_ref, total_ref, diagonal_ref, c_x, c_y, c_z,
    rows_h, fields_h, g_x, g_y, g_z,
):
    depth, rows, width = press.shape
    areal, areals = lax.axis_index("areal"), lax.axis_size("areal")
    tall = rows + ROWS
    full = (tall, width)
    own = slice(0, rows)
    mob, acc, mob_sum, acc_sum = (
        Rows(*both)
        for both in ((edge_mob, mob), (edge_acc, acc), (edge_mob_sum, mob_sum), (edge_acc_sum, acc_sum))
    )
    fields = {MOB: mob_sum, PRESS: press, TX: tx, TY: ty, TZ: tz, PORE: pore, ACC: acc_sum}
    tiles = row_tiles(rows_one, rows_two, range(FIELDS))
    for z in range(depth):
        for i in range(COMPS):
            rows_h[i, z] = tiles[i][z]
        for n, k in enumerate(fields):
            fields_h[n, z] = tiles[k][z]

    end_x = (row_of(full) == rows - 1) & (areal == areals - 1)
    end_y = lane_of(full) == width - 1
    scale = 0.5 * TIME_STEP
    c_z[0] = jnp.zeros(full, jnp.float32)
    g_z[0] = jnp.zeros((rows, width), jnp.float32)

    def update(z):
        m, p, x, y, zz, volume, total = (
            jnp.concatenate([ref[z], fields_h[n, z]], axis=0) for n, ref in enumerate(fields.values())
        )
        up, down = jnp.minimum(z + 1, depth - 1), jnp.maximum(z - 1, 0)
        p_up = jnp.concatenate([press[up], fields_h[1, up]], axis=0)
        p_down = jnp.concatenate([press[down], fields_h[1, down]], axis=0)
        m_up = jnp.concatenate([mob_sum[up], fields_h[0, up]], axis=0)
        strength_x = jnp.where(end_x, 0.0, scale * x)
        strength_y = jnp.where(end_y, 0.0, scale * y)
        strength_z = jnp.where(z < depth - 1, scale, 0.0) * zz
        dx = p - pltpu.roll(p, tall - 1, 0)
        dy = p - pltpu.roll(p, width - 1, 1)
        dz = p - p_up
        cx = strength_x * (m + pltpu.roll(m, tall - 1, 0))
        cy = strength_y * (m + pltpu.roll(m, width - 1, 1))
        cz = strength_z * (m + m_up)
        cz_low = c_z[z]
        gx = strength_x * dx
        g_x[0, z], g_x[1, z] = gx[own], -pltpu.roll(gx, 1, 0)[own]
        g_y[z], g_z[z + 1] = (strength_y * dy)[own], (strength_z * dz)[own]
        c_x[z], c_y[z], c_z[z + 1] = cx, cy, cz
        fx, fy = cx * dx, cy * dy
        total_ref[z] = (
            total
            + (fx - pltpu.roll(fx, 1, 0))
            + (fy - pltpu.roll(fy, 1, 1))
            + (cz * dz + cz_low * (p - p_down))
        )
        diagonal_ref[z] = (
            COMPRESS * volume
            + (cx + pltpu.roll(cx, 1, 0))
            + (cy + pltpu.roll(cy, 1, 1))
            + (cz + cz_low)
        )

    by_pairs(depth, update)

    def residual(z):
        down, up = jnp.maximum(z - 1, 0), jnp.minimum(z + 1, depth - 1)
        gx, gx_low, gy, gz, gz_low = g_x[0, z], g_x[1, z], g_y[z], g_z[z + 1], -g_z[z]
        gy_low = -pltpu.roll(gy, 1, 1)
        middle = (gx + gx_low) + (gy + gy_low) + (gz + gz_low)
        for i in range(COMPS):
            here = mob[i, z]
            tall_here = jnp.concatenate([here, rows_h[i, z]], axis=0)
            out_ref[i, z] = (
                acc[i, z]
                + middle * here
                + gx * pltpu.roll(tall_here, tall - 1, 0)[own]
                + gx_low * pltpu.roll(tall_here, 1, 0)[own]
                + gy * pltpu.roll(here, width - 1, 1)
                + gy_low * pltpu.roll(here, 1, 1)
                + gz * mob[i, up]
                + gz_low * mob[i, down]
            )

    by_pairs(depth, residual)


def finish(
    columns_one, columns_two, packet, press, total_in, diagonal_in, c_x, c_y, c_z, edge_mob, mob, near,
    res_ref, new_ref,
    side_h, edge_h, first, total_ref, inverse_ref, res_s, sems,
):
    depth, rows, width = press.shape
    layer, layers = lax.axis_index("layer"), lax.axis_size("layer")
    areal, areals = lax.axis_index("areal"), lax.axis_size("areal")
    tall = rows + ROWS
    lane = lane_of((tall, LANES))
    at_first, at_last = lane == 0, lane == LANES - 1
    low, high = slice(0, LANES), slice(width - LANES, width)
    FLUX, COUPLE, FACE, NEXT = range(4)
    mob = Rows(edge_mob, mob)

    def edges(which, z):
        both = pltpu.roll(edge_h[which], LANES - 1 - 4 * z, 1)
        return jnp.where(at_first, both, 0.0), jnp.where(at_last, both, 0.0)

    halo = side_fields(columns_one, columns_two)
    here = spread_fields([packet[:, t : t + LANES] for t in range(0, FIELDS * 32, LANES)])
    for i in range(COMPS):
        side_h[i] = halo[i][:rows]
    scale = 0.5 * TIME_STEP
    is_left = lane % 4 == 1

    def turned(x, by):
        return pltpu.roll(x, by % LANES, 1)

    def outer(x):
        return jnp.where(is_left, turned(x, 1), turned(x, -1))

    def inner(x):
        return jnp.where(is_left, turned(x, -1), turned(x, 1))

    m, p = halo[MOB], halo[PRESS]
    strength = scale * halo[TY]
    own_strength = jnp.where(layer < layers - 1, scale, 0.0) * here[TY]
    c_out = jnp.where(is_left, turned(strength, 1), strength) * (m + outer(m))
    s_in = jnp.where(is_left, strength, turned(own_strength, 1))
    c_in = s_in * (m + inner(here[MOB]))
    d_in = p - inner(here[PRESS])
    end_x = (row_of(lane.shape) == rows - 1) & (areal == areals - 1)
    cx = jnp.where(end_x, 0.0, scale * halo[TX]) * (m + pltpu.roll(m, tall - 1, 0))
    cz = jnp.where(lane < 4 * (depth - 1), scale * halo[TZ], 0.0) * (m + turned(m, -4))
    fx = cx * (p - pltpu.roll(p, tall - 1, 0))
    fz = cz * (p - turned(p, -4))
    total = (
        halo[ACC]
        + (c_out * (p - outer(p)) + c_in * d_in)
        + (fx - pltpu.roll(fx, 1, 0))
        + (fz - turned(fz, 4))
    )
    diagonal = (
        COMPRESS * halo[PORE] + (c_out + c_in) + (cx + pltpu.roll(cx, 1, 0)) + (cz + turned(cz, 4))
    )
    usable = diagonal > 0.0
    beside = jnp.where(usable, -total * rcp(jnp.where(usable, diagonal, 1.0)), 0.0)
    for which, value in (
        (FLUX, -c_in * d_in), (COUPLE, c_in), (FACE, -s_in * d_in), (NEXT, c_in * beside)
    ):
        edge_h[which] = jnp.where(is_left, value, turned(value, -2))

    def leave(z):
        return pltpu.make_async_copy(res_s.at[:, z], res_ref.at[:, z], sems.at[z])

    def update(z):
        faces = [face[:rows] for face in edges(FACE, z)]
        for i in range(COMPS):
            side = pltpu.roll(side_h[i], LANES - 2 - 4 * z, 1)
            cells = mob[i, z]
            for span, face in zip((low, high), faces):
                res_s[i, z, :, span] = near[i, z, :, span] + face * (cells[:, span] + side)
        leave(z).start()
        flux, couple = edges(FLUX, z), edges(COUPLE, z)
        for n, span in enumerate((low, high)):
            total = total_in[z, :, span] + flux[n]
            diagonal = diagonal_in[z, :, span] + couple[n]
            usable = diagonal > 0.0
            inverse = rcp(jnp.where(usable, diagonal, 1.0))
            first[z, :, span] = jnp.where(usable, -total * inverse, 0.0)
            total_ref[z, :, span] = total[:rows]
            inverse_ref[z, :, span] = inverse[:rows]

    by_pairs(depth, update)

    def second(z):
        here = first[z]
        up, down = jnp.minimum(z + 1, depth - 1), jnp.maximum(z - 1, 0)
        cx, cy = c_x[z], c_y[z, :rows]
        own = here[:rows]
        gathered = (
            (cx * pltpu.roll(here, tall - 1, 0))[:rows]
            + pltpu.roll(cx * here, 1, 0)[:rows]
            + cy * pltpu.roll(own, width - 1, 1)
            + pltpu.roll(cy * own, 1, 1)
            + (c_z[z + 1, :rows] * first[up, :rows] + c_z[z, :rows] * first[down, :rows])
            - total_ref[z]
        )
        beyond = edges(NEXT, z)
        for n, span in enumerate((low, high)):
            new_ref[z, :, span] = press[z, :, span] + inverse_ref[z, :, span] * (
                gathered[:, span] + beyond[n][:rows]
            )

    by_pairs(depth, second)

    def left(z):
        leave(z).wait()

    by_pairs(depth, left)


def on_device(
    pressure, composition, mass_old, pore_volume, trans_x, trans_y, trans_z,
    volatility, pressure_slope, mixing, two_phase,
):
    depth, rows, width = pressure.shape
    f32 = jnp.float32
    smem = pl.BlockSpec(memory_space=pltpu.SMEM)
    vmem = pl.BlockSpec(memory_space=pltpu.VMEM)
    def params(mib):
        return pltpu.CompilerParams(vmem_limit_bytes=mib * MIB)

    scalars = (two_phase, volatility, pressure_slope, mixing)

    def swapped(block, axis, first):
        count = lax.axis_size(axis)
        pairs = [(i, i + 1) for i in range(first, count - 1, 2)]
        return lax.ppermute(block, axis, pairs + [(j, i) for i, j in pairs])

    whole = jax.ShapeDtypeStruct((COMPS, depth, rows, width), f32)
    sums = jax.ShapeDtypeStruct((depth, rows, width), f32)
    packed = jax.ShapeDtypeStruct((len(UNITS) // 2, DEPTH_SLOTS * depth, width), f32)
    fields = (composition, pressure, pore_volume, mass_old, trans_x, trans_y, trans_z)

    def parts(count):
        planes = jax.ShapeDtypeStruct((COMPS, depth, count, width), f32)
        plane = jax.ShapeDtypeStruct((depth, count, width), f32)
        return [planes, planes, plane, plane]

    between = [jax.ShapeDtypeStruct((*x.shape[:-2], rows - 2 * ROWS, width), f32) for x in fields[:4]]
    *results, operand, comp, press, pore, mass = pl.pallas_call(
        edge_cells,
        in_specs=[pl.BlockSpec(memory_space=pl.ANY)] * (4 + len(fields)),
        out_specs=[vmem] * 11,
        out_shape=parts(2 * ROWS)
        + [packed, packed, jax.ShapeDtypeStruct((PART, DEEP), jnp.bfloat16), *between],
        scratch_shapes=[pltpu.SMEM(x.shape, x.dtype) for x in scalars]
        + [pltpu.VMEM((2, *x.shape[:-2], ROWS, width), f32) for x in fields]
        + [pltpu.SemaphoreType.DMA((3, len(fields))), pltpu.SemaphoreType.DMA((4,))],
        compiler_params=params(24),
        name="edge_cells",
    )(*(pltpu.with_memory_space_constraint(x, pltpu.HBM) for x in (*scalars, *fields)))
    *edge, one, two = results
    rows_one = swapped(one, "areal", 0)
    rows_two = swapped(two, "areal", 1)
    cells = rows * depth * width
    inner = pl.pallas_call(
        inner_cells,
        in_specs=[smem] * 3 + [vmem] * 5,
        out_specs=[vmem] * 4,
        out_shape=parts(rows - 2 * ROWS),
        compiler_params=params(24),
        cost_estimate=pl.CostEstimate(
            flops=450 * cells, transcendentals=95 * cells, bytes_accessed=2 * 39 * cells
        ),
        name="inner_cells",
    )(*scalars[:3], operand, comp, press, pore, mass)
    planes_of = (pressure, trans_x, trans_y, trans_z, pore_volume)

    packet = pl.pallas_call(
        pack_columns,
        in_specs=[vmem] * 15,
        out_specs=vmem,
        out_shape=jax.ShapeDtypeStruct((rows + ROWS, FIELDS * 32), f32),
        compiler_params=params(24),
        name="pack_columns",
    )(rows_one, rows_two, *planes_of, *edge, *inner)

    columns_one = swapped(packet, "layer", 0)
    columns_two = swapped(packet, "layer", 1)

    tall = jax.ShapeDtypeStruct((depth, rows + ROWS, width), f32)
    above_faces = jax.ShapeDtypeStruct((depth + 1, rows + ROWS, width), f32)
    near, *sweep = pl.pallas_call(
        near_residual,
        in_specs=[vmem] * 15,
        out_specs=[vmem] * 6,
        out_shape=[whole, tall, tall, tall, tall, above_faces],
        scratch_shapes=[
            pltpu.VMEM((COMPS, depth, ROWS, width), f32),
            pltpu.VMEM((FIELDS - COMPS, depth, ROWS, width), f32),
            pltpu.VMEM((2, depth, rows, width), f32),
            pltpu.VMEM((depth, rows, width), f32),
            pltpu.VMEM((depth + 1, rows, width), f32),
        ],
        compiler_params=params(24),
        cost_estimate=pl.CostEstimate(flops=150 * cells, transcendentals=0, bytes_accessed=4 * 31 * cells),
        name="near_residual",
    )(rows_one, rows_two, *planes_of, *edge, *inner)

    return pl.pallas_call(
        finish,
        in_specs=[vmem] * 12,
        out_specs=[pl.BlockSpec(memory_space=pl.ANY), vmem],
        out_shape=[whole, sums],
        scratch_shapes=[
            pltpu.VMEM((COMPS, rows, LANES), f32),
            pltpu.VMEM((4, rows + ROWS, LANES), f32),
            pltpu.VMEM((depth, rows + ROWS, width), f32),
            pltpu.VMEM((depth, rows, width), f32),
            pltpu.VMEM((depth, rows, width), f32),
            pltpu.VMEM((COMPS, depth, rows, width), f32),
            pltpu.SemaphoreType.DMA((depth,)),
        ],
        compiler_params=params(24),
        name="finish",
    )(columns_one, columns_two, packet, pressure, *sweep, edge[0], inner[0], near)


def solution(mesh):
    placed = (
        P(None, "areal", "layer"),
        P(None, None, "areal", "layer"),
        P(None, None, "areal", "layer"),
        P(None, "areal", "layer"),
        P(None, "areal", "layer"),
        P(None, "areal", "layer"),
        P(None, "areal", "layer"),
        P(),
        P(),
        P(),
        P(None, "areal"),
    )
    return jax.shard_map(
        on_device,
        mesh=mesh,
        in_specs=placed,
        out_specs=(P(None, None, "areal", "layer"), P(None, "areal", "layer")),
        check_vma=False,
    )
```

```python
import jax
import jax.numpy as jnp
from jax import lax
from jax.experimental import pallas as pl
from jax.experimental.pallas import tpu as pltpu
from jax.sharding import PartitionSpec as P

SS_ITERS = 3
RR_ITERS = 3
LIGHT = 4
COMPS = 9
FIELDS = 16
MOB, PRESS, TX, TY, TZ, PORE, ACC = range(COMPS, FIELDS)
UNITS = (MOB, PRESS, TX, (0, 1), (2, 3), (4, 5), (6, 7), (8, TY), (TZ, PORE), (ACC, ACC))
DEPTH_SLOTS = 4
TIME_STEP = 4.0
COMPRESS = 0.2
VAPOUR_WEIGHT = 1.0 / 0.25
LANES = 128
ROWS = 8
MIB = 1024 * 1024
PART = (COMPS + 1) * ROWS
DEEP = 256


def rcp(x):
    return pltpu.reciprocal(x, approx=True)


def total_of(terms):
    terms = list(terms)
    while len(terms) > 1:
        terms = [a + b for a, b in zip(terms[::2], terms[1::2])] + (
            [terms[-1]] if len(terms) % 2 else []
        )
    return terms[0]


def split(x):
    high = x.astype(jnp.bfloat16)
    return high, (x - high.astype(jnp.float32)).astype(jnp.bfloat16)


def mixing_operand(mix_ref):
    shape = (ROWS, DEEP)
    lane, row = lane_of(shape), row_of(shape)
    part = lax.div(lane, PART)
    within = lane - PART * part
    column = lax.div(within, ROWS)
    on = (within - ROWS * column == row) & (part < 3)
    blocks = []
    for i in range(COMPS):
        value = jnp.zeros(shape, jnp.float32)
        for j in range(COMPS):
            value = jnp.where(column == j, 2.0 * mix_ref[i, j], value)
        high, low = split(value)
        value = jnp.where(part == 2, low.astype(jnp.float32), high.astype(jnp.float32))
        blocks.append(jnp.where(on, value, 0.0))
    blocks.append(jnp.zeros(shape, jnp.float32))
    return jnp.concatenate(blocks, axis=0).astype(jnp.bfloat16)


def mixed(operand, spread):
    shape = spread[0].shape
    high, low = split(jnp.concatenate(spread + [jnp.zeros(shape, jnp.float32)], axis=0))
    tail = jnp.zeros((DEEP - 3 * PART, shape[1]), jnp.bfloat16)
    out = jnp.dot(
        operand,
        jnp.concatenate([high, low, high, tail], axis=0),
        preferred_element_type=jnp.float32,
    )
    return [out[ROWS * i : ROWS * (i + 1)] for i in range(COMPS)]


def flash(feed, pressure, signed, slope, operand):
    log_press = jnp.log(pressure)
    half_base = [0.5 * signed[i] - (0.5 * slope[i]) * log_press for i in range(COMPS)]
    spread = None
    for outer in range(SS_ITERS):
        if outer == 0:
            half_log = half_base
        else:
            mix = mixed(operand, spread)
            half_log = [half_base[i] - 0.5 * jnp.tanh(mix[i]) for i in range(COMPS)]
        t = [jnp.tanh(half_log[i]) for i in range(COMPS)]
        u = [rcp(t[i]) for i in range(COMPS)]
        psi = None
        for inner in range(RR_ITERS):
            q = t if inner == 0 else [rcp(u[i] + psi) for i in range(COMPS)]
            part = [feed[i] * q[i] for i in range(COMPS)]
            step = total_of(part) * rcp(total_of(part[i] * q[i] for i in range(COMPS)))
            psi = jnp.clip(step if inner == 0 else psi + step, -1.0, 1.0)
        spread = [feed[i] * rcp(u[i] + psi) for i in range(COMPS)]
    liquid_part = (0.25 * (1.0 - psi)) * (1.0 - psi)
    vapour_part = (0.25 * VAPOUR_WEIGHT * (1.0 + psi)) * (1.0 + psi)
    both, apart = vapour_part + liquid_part, vapour_part - liquid_part
    return [spread[i] * (both * u[i] + apart) for i in range(COMPS)]


def parameters(vol_ref, slope_ref):
    signed = [vol_ref[i] if i < LIGHT else -vol_ref[i] for i in range(COMPS)]
    return signed, [slope_ref[i] for i in range(COMPS)]


def lane_of(shape):
    return lax.broadcasted_iota(jnp.int32, shape, len(shape) - 1)


def row_of(shape):
    return lax.broadcasted_iota(jnp.int32, shape, len(shape) - 2)


class Rows:
    def __init__(self, edge, inner):
        self.edge, self.inner = edge, inner

    def __getitem__(self, at):
        at = at if isinstance(at, tuple) else (at,)
        edge = self.edge[at]
        return jnp.concatenate([edge[:ROWS], self.inner[at], edge[ROWS:]], axis=0)


def pack_rows(field, low, out_ref, depth):
    row = None
    for n in range(0, len(UNITS), 2):
        for pair in range(depth // 2):
            tile = None
            for z in (2 * pair, 2 * pair + 1):
                order = (1, 0) if low else (0, 1)
                for which in order:
                    unit = UNITS[n + which]
                    at = 4 * (z % 2) + (2 if low == (which == 0) else 0)
                    first = 0 if low else ROWS - 1
                    if isinstance(unit, tuple):
                        a, b = unit
                        pieces = [(at, a, at - first), (at + 1, b, at + 1 - first)]
                        if not low:
                            pieces = [(at, b, at - first), (at + 1, a, at + 1 - first)]
                    else:
                        pieces = [(at, unit, at if low else at + 2)]
                    for start, k, turn in pieces:
                        here = field(k, z)
                        if row is None:
                            row = row_of(here.shape)
                        if turn % ROWS:
                            here = pltpu.roll(here, turn % ROWS, 0)
                        tile = here if tile is None else jnp.where(row < start, tile, here)
            out_ref[n // 2, pl.ds(pair * ROWS, ROWS), :] = tile


def row_tiles(one, two, wanted, start=0, stop=None):
    shape = one.shape[1:]
    upper = row_of(shape) % DEPTH_SLOTS < 2
    tile_row = row_of((ROWS, shape[1]))
    stop = stop or shape[0] // DEPTH_SLOTS
    tiles = {}
    for n, unit in enumerate(UNITS):
        fields = unit if isinstance(unit, tuple) else (unit,)
        if not any(k in wanted for k in fields):
            continue
        up, down = by_side("areal", one[n // 2], two[n // 2])
        if n % 2:
            up, down = pltpu.roll(up, shape[0] - 2, 0), pltpu.roll(down, 2, 0)
        both = jnp.where(upper, up, down)
        for z in range(start, stop):
            at = (z // 2) * ROWS
            tile = pltpu.roll(both[at : at + ROWS], 6 - 4 * (z % 2), 0)
            if fields[0] in wanted:
                tiles.setdefault(fields[0], []).append(tile)
            if fields[-1] in wanted and fields[-1] != fields[0]:
                other = jnp.where(tile_row < 4, pltpu.roll(tile, ROWS - 1, 0), pltpu.roll(tile, 1, 0))
                tiles.setdefault(fields[-1], []).append(other)
    return tiles


def pack_columns(rows_one, rows_two, *refs):
    (
        press, tx, ty, tz, pore, edge_mob, _, edge_mob_sum, edge_acc_sum, mob, _, mob_sum, acc_sum,
        one_ref, two_ref, own_ref,
    ) = refs
    depth, rows, width = press.shape
    shape = (rows + ROWS, LANES)
    lane = lane_of(shape)
    mob, mob_sum, acc_sum = (
        Rows(*both) for both in ((edge_mob, mob), (edge_mob_sum, mob_sum), (edge_acc_sum, acc_sum))
    )
    corner_fields = {MOB: mob_sum, PRESS: press, TX: tx, TY: ty}
    others = {TZ: tz, PORE: pore, ACC: acc_sum, **corner_fields}
    corners = row_tiles(rows_one, rows_two, corner_fields)
    nothing = jnp.zeros((ROWS, LANES), jnp.float32)
    for tile in range(FIELDS // 4):
        packed = jnp.zeros(shape, jnp.float32)
        for quarter in range(4):
            k = 4 * tile + quarter
            for z in range(depth):
                plane = mob[k, z] if k < COMPS else others[k][z]
                first, last = plane[:, :LANES], plane[:, -LANES:]
                at = 32 * quarter + 4 * z
                both = jnp.where(lane_of(first.shape) < LANES // 2, first, last)
                if k < COMPS:
                    both = pltpu.roll(both, at + 2, 1)
                    on = (lane_of(first.shape) >= at + 1) & (lane_of(first.shape) < at + 3)
                    packed = jnp.concatenate([jnp.where(on, both, packed[:rows]), nothing], axis=0)
                    continue
                end = nothing
                if k in corner_fields:
                    end = corners[k][z]
                    end = jnp.where(lane_of(end[:, :LANES].shape) < LANES // 2, end[:, :LANES], end[:, -LANES:])
                both = pltpu.roll(jnp.concatenate([both, end], axis=0), (at + 2) % LANES, 1)
                packed = jnp.where((lane >= at) & (lane < at + 4), both, packed)
        own_ref[:, tile * LANES : (tile + 1) * LANES] = packed
    odd = lax.axis_index("layer") % 2 == 1
    half = FIELDS // 8
    for n in range(half):
        near, far = (own_ref[:, t * LANES : (t + 1) * LANES] for t in (n, n + half))
        upward = jnp.where(lane % 4 < 2, near, pltpu.roll(far, 2, 1))
        downward = jnp.where(lane % 4 < 2, pltpu.roll(near, LANES - 2, 1), far)
        one_ref[:, n * LANES : (n + 1) * LANES] = jnp.where(odd, downward, upward)
        two_ref[:, n * LANES : (n + 1) * LANES] = jnp.where(odd, upward, downward)


def spread_fields(tiles):
    fields = []
    for tile in tiles:
        for quarter in range(4):
            turn = (LANES - 32 * quarter) % LANES
            fields.append(pltpu.roll(tile, turn, 1) if turn else tile)
    return fields


def side_fields(one, two):
    lane = lane_of((one.shape[0], LANES))
    near, far = [], []
    for n in range(FIELDS // 8):
        span = slice(n * LANES, (n + 1) * LANES)
        left, right = by_side("layer", one[:, span], two[:, span])
        near.append(jnp.where(lane % 4 < 2, left, pltpu.roll(right, 2, 1)))
        far.append(jnp.where(lane % 4 < 2, pltpu.roll(left, LANES - 2, 1), right))
    return spread_fields(near + far)


def flash_rows(source, target, tile_row, flags, vol, slope, operand, comp, press, pore, mass, outs):
    mob_ref, acc_ref, mob_sum, acc_sum = outs
    layer = lax.axis_index("layer")
    depth, _, width = press.shape

    def beside(ref, *lead):
        return jnp.concatenate([ref[(*lead, z, source)] for z in range(depth)], axis=1)

    def store(ref, value, *lead):
        for z in range(depth):
            ref[(*lead, z, target)] = value[:, z * width : (z + 1) * width]

    raw = [beside(comp, i) for i in range(COMPS)]
    inverse = rcp(total_of(raw))
    feed = [raw[i] * inverse for i in range(COMPS)]
    volume = beside(pore)
    acc = [volume * feed[i] - beside(mass, i) for i in range(COMPS)]
    for i in range(COMPS):
        store(acc_ref, acc[i], i)
    store(acc_sum, total_of(acc))
    first, last = flags[layer, 2 * tile_row], flags[layer, 2 * tile_row + 1]

    @pl.when(first + last > 0)
    def _():
        signed, slopes = parameters(vol, slope)
        two = flash(feed, beside(press), signed, slopes, operand[...])
        marked = jnp.where(row_of(feed[0].shape) < ROWS // 2, first, last) > 0
        mobility = [jnp.where(marked, two[i], feed[i]) for i in range(COMPS)]
        for i in range(COMPS):
            store(mob_ref, mobility[i], i)
        store(mob_sum, total_of(mobility))

    @pl.when(first + last == 0)
    def _():
        for i in range(COMPS):
            store(mob_ref, feed[i], i)
        store(mob_sum, total_of(feed))


def edge_cells(
    flags_in, vol_in, slope_in, mix_in, comp, press, pore, mass, tx, ty, tz,
    mob_ref, acc_ref, mob_sum, acc_sum, one_ref, two_ref, operand, comp_i, press_i, pore_i, mass_i,
    flags, vol, slope, mix, comp_s, press_s, pore_s, mass_s, tx_s, ty_s, tz_s, sems, scalar_sems,
):
    depth, rows, _ = press.shape
    fetched = (
        (comp, comp_s), (press, press_s), (pore, pore_s), (mass, mass_s), (tx, tx_s), (ty, ty_s), (tz, tz_s)
    )

    ahead = (comp_i, press_i, pore_i, mass_i)

    def fetch(end, n):
        source, slot = fetched[n]
        at = pl.ds(end * (rows - ROWS), ROWS) if end < 2 else pl.ds(ROWS, rows - 2 * ROWS)
        return pltpu.make_async_copy(
            source.at[:, :, at, :] if len(source.shape) == 4 else source.at[:, at, :],
            slot.at[end] if end < 2 else ahead[n],
            sems.at[end, n],
        )

    scalars = [
        pltpu.make_async_copy(source, slot, scalar_sems.at[n])
        for n, (source, slot) in enumerate(
            ((flags_in, flags), (vol_in, vol), (slope_in, slope), (mix_in, mix))
        )
    ]
    for copy in scalars:
        copy.start()
    for end in range(2):
        for n in range(len(fetched)):
            fetch(end, n).start()
    for copy in scalars:
        copy.wait()
    operand[...] = mixing_operand(mix)
    odd = lax.axis_index("areal") % 2 == 1
    for end in range(2):
        for n in range(len(fetched)):
            fetch(end, n).wait()
        if end == 0:
            for n in range(len(ahead)):
                fetch(2, n).start()
        target = slice(end * ROWS, (end + 1) * ROWS)
        flash_rows(
            slice(None), target, end * (rows // ROWS - 1), flags, vol, slope, operand,
            *(slot.at[end] for _, slot in fetched[:4]), (mob_ref, acc_ref, mob_sum, acc_sum),
        )

        def field(k, z):
            if k < COMPS:
                here = mob_ref[k, z, target]
            elif k in (MOB, ACC):
                here = (mob_sum if k == MOB else acc_sum)[z, target]
            else:
                here = {PRESS: press_s, TX: tx_s, TY: ty_s, TZ: tz_s, PORE: pore_s}[k][end, z]
            return here

        for turn, ref in enumerate((one_ref, two_ref)):
            @pl.when(odd == (end == turn))
            def _():
                pack_rows(field, end == 0, ref, depth)

    for n in range(len(ahead)):
        fetch(2, n).wait()


def inner_cells(flags, vol, slope, operand, comp, press, pore, mass, *outs):
    def tile(t, carry):
        at = pl.ds(pl.multiple_of(t * ROWS, ROWS), ROWS)
        flash_rows(at, at, t + 1, flags, vol, slope, operand, comp, press, pore, mass, outs)
        return carry

    lax.fori_loop(0, press.shape[1] // ROWS, tile, 0)


def by_side(axis, one, two):
    odd = lax.axis_index(axis) % 2 == 1
    return jnp.where(odd, one, two), jnp.where(odd, two, one)


def by_pairs(count, body):
    def pair(t, carry):
        body(2 * t)
        body(2 * t + 1)
        return carry

    lax.fori_loop(0, count // 2, pair, 0)


def near_residual(
    rows_one, rows_two, press, tx, ty, tz, pore,
    edge_mob, edge_acc, edge_mob_sum, edge_acc_sum, mob, acc, mob_sum, acc_sum,
    out_ref, total_ref, diagonal_ref, c_x, c_y, c_z,
    rows_h, fields_h, g_x, g_y, g_z,
):
    depth, rows, width = press.shape
    areal, areals = lax.axis_index("areal"), lax.axis_size("areal")
    tall = rows + ROWS
    full = (tall, width)
    own = slice(0, rows)
    mob, acc, mob_sum, acc_sum = (
        Rows(*both)
        for both in ((edge_mob, mob), (edge_acc, acc), (edge_mob_sum, mob_sum), (edge_acc_sum, acc_sum))
    )
    fields = {MOB: mob_sum, PRESS: press, TX: tx, TY: ty, TZ: tz, PORE: pore, ACC: acc_sum}
    tiles = row_tiles(rows_one, rows_two, range(FIELDS))
    for z in range(depth):
        for i in range(COMPS):
            rows_h[i, z] = tiles[i][z]
        for n, k in enumerate(fields):
            fields_h[n, z] = tiles[k][z]

    end_x = (row_of(full) == rows - 1) & (areal == areals - 1)
    end_y = lane_of(full) == width - 1
    scale = 0.5 * TIME_STEP
    c_z[0] = jnp.zeros(full, jnp.float32)
    g_z[0] = jnp.zeros((rows, width), jnp.float32)

    def update(z):
        m, p, x, y, zz, volume, total = (
            jnp.concatenate([ref[z], fields_h[n, z]], axis=0) for n, ref in enumerate(fields.values())
        )
        up, down = jnp.minimum(z + 1, depth - 1), jnp.maximum(z - 1, 0)
        p_up = jnp.concatenate([press[up], fields_h[1, up]], axis=0)
        p_down = jnp.concatenate([press[down], fields_h[1, down]], axis=0)
        m_up = jnp.concatenate([mob_sum[up], fields_h[0, up]], axis=0)
        strength_x = jnp.where(end_x, 0.0, scale * x)
        strength_y = jnp.where(end_y, 0.0, scale * y)
        strength_z = jnp.where(z < depth - 1, scale, 0.0) * zz
        dx = p - pltpu.roll(p, tall - 1, 0)
        dy = p - pltpu.roll(p, width - 1, 1)
        dz = p - p_up
        cx = strength_x * (m + pltpu.roll(m, tall - 1, 0))
        cy = strength_y * (m + pltpu.roll(m, width - 1, 1))
        cz = strength_z * (m + m_up)
        cz_low = c_z[z]
        gx = strength_x * dx
        g_x[0, z], g_x[1, z] = gx[own], -pltpu.roll(gx, 1, 0)[own]
        g_y[z], g_z[z + 1] = (strength_y * dy)[own], (strength_z * dz)[own]
        c_x[z], c_y[z], c_z[z + 1] = cx, cy, cz
        fx, fy = cx * dx, cy * dy
        total_ref[z] = (
            total
            + (fx - pltpu.roll(fx, 1, 0))
            + (fy - pltpu.roll(fy, 1, 1))
            + (cz * dz + cz_low * (p - p_down))
        )
        diagonal_ref[z] = (
            COMPRESS * volume
            + (cx + pltpu.roll(cx, 1, 0))
            + (cy + pltpu.roll(cy, 1, 1))
            + (cz + cz_low)
        )

    by_pairs(depth, update)

    def residual(z):
        down, up = jnp.maximum(z - 1, 0), jnp.minimum(z + 1, depth - 1)
        gx, gx_low, gy, gz, gz_low = g_x[0, z], g_x[1, z], g_y[z], g_z[z + 1], -g_z[z]
        gy_low = -pltpu.roll(gy, 1, 1)
        middle = (gx + gx_low) + (gy + gy_low) + (gz + gz_low)
        for i in range(COMPS):
            here = mob[i, z]
            tall_here = jnp.concatenate([here, rows_h[i, z]], axis=0)
            out_ref[i, z] = (
                acc[i, z]
                + middle * here
                + gx * pltpu.roll(tall_here, tall - 1, 0)[own]
                + gx_low * pltpu.roll(tall_here, 1, 0)[own]
                + gy * pltpu.roll(here, width - 1, 1)
                + gy_low * pltpu.roll(here, 1, 1)
                + gz * mob[i, up]
                + gz_low * mob[i, down]
            )

    by_pairs(depth, residual)


def finish(
    columns_one, columns_two, packet, press, total_in, diagonal_in, c_x, c_y, c_z, edge_mob, mob, near,
    res_ref, new_ref,
    side_h, edge_h, first, total_ref, inverse_ref, res_s, sems,
):
    depth, rows, width = press.shape
    layer, layers = lax.axis_index("layer"), lax.axis_size("layer")
    areal, areals = lax.axis_index("areal"), lax.axis_size("areal")
    tall = rows + ROWS
    lane = lane_of((tall, LANES))
    at_first, at_last = lane == 0, lane == LANES - 1
    low, high = slice(0, LANES), slice(width - LANES, width)
    FLUX, COUPLE, FACE, NEXT = range(4)
    mob = Rows(edge_mob, mob)

    def edges(which, z):
        both = pltpu.roll(edge_h[which], LANES - 1 - 4 * z, 1)
        return jnp.where(at_first, both, 0.0), jnp.where(at_last, both, 0.0)

    halo = side_fields(columns_one, columns_two)
    here = spread_fields([packet[:, t : t + LANES] for t in range(0, FIELDS * 32, LANES)])
    is_left = lane % 4 == 1
    for i in range(COMPS):
        cells = halo[i][:rows]
        side_h[i] = jnp.where(is_left[:rows], pltpu.roll(cells, LANES - 1, 1), pltpu.roll(cells, 1, 1))
    scale = 0.5 * TIME_STEP

    def turned(x, by):
        return pltpu.roll(x, by % LANES, 1)

    def outer(x):
        return jnp.where(is_left, turned(x, 1), turned(x, -1))

    def inner(x):
        return jnp.where(is_left, turned(x, -1), turned(x, 1))

    m, p = halo[MOB], halo[PRESS]
    strength = scale * halo[TY]
    own_strength = jnp.where(layer < layers - 1, scale, 0.0) * here[TY]
    c_out = jnp.where(is_left, turned(strength, 1), strength) * (m + outer(m))
    s_in = jnp.where(is_left, strength, turned(own_strength, 1))
    c_in = s_in * (m + inner(here[MOB]))
    d_in = p - inner(here[PRESS])
    end_x = (row_of(lane.shape) == rows - 1) & (areal == areals - 1)
    cx = jnp.where(end_x, 0.0, scale * halo[TX]) * (m + pltpu.roll(m, tall - 1, 0))
    cz = jnp.where(lane < 4 * (depth - 1), scale * halo[TZ], 0.0) * (m + turned(m, -4))
    fx = cx * (p - pltpu.roll(p, tall - 1, 0))
    fz = cz * (p - turned(p, -4))
    total = (
        halo[ACC]
        + (c_out * (p - outer(p)) + c_in * d_in)
        + (fx - pltpu.roll(fx, 1, 0))
        + (fz - turned(fz, 4))
    )
    diagonal = (
        COMPRESS * halo[PORE] + (c_out + c_in) + (cx + pltpu.roll(cx, 1, 0)) + (cz + turned(cz, 4))
    )
    usable = diagonal > 0.0
    beside = jnp.where(usable, -total * rcp(jnp.where(usable, diagonal, 1.0)), 0.0)
    for which, value in (
        (FLUX, -c_in * d_in), (COUPLE, c_in), (FACE, -s_in * d_in), (NEXT, c_in * beside)
    ):
        edge_h[which] = jnp.where(is_left, value, turned(value, -2))

    def leave(z):
        return pltpu.make_async_copy(res_s.at[:, z], res_ref.at[:, z], sems.at[z])

    def update(z):
        faces = [face[:rows] for face in edges(FACE, z)]
        for i in range(COMPS):
            side = pltpu.roll(side_h[i], LANES - 2 - 4 * z, 1)
            cells = mob[i, z]
            for span, face in zip((low, high), faces):
                res_s[i, z, :, span] = near[i, z, :, span] + face * (cells[:, span] + side)
        leave(z).start()
        flux, couple = edges(FLUX, z), edges(COUPLE, z)
        for n, span in enumerate((low, high)):
            total = total_in[z, :, span] + flux[n]
            diagonal = diagonal_in[z, :, span] + couple[n]
            usable = diagonal > 0.0
            inverse = rcp(jnp.where(usable, diagonal, 1.0))
            first[z, :, span] = jnp.where(usable, -total * inverse, 0.0)
            total_ref[z, :, span] = total[:rows]
            inverse_ref[z, :, span] = inverse[:rows]

    by_pairs(depth, update)

    def second(z):
        here = first[z]
        up, down = jnp.minimum(z + 1, depth - 1), jnp.maximum(z - 1, 0)
        cx, cy = c_x[z], c_y[z, :rows]
        own = here[:rows]
        gathered = (
            (cx * pltpu.roll(here, tall - 1, 0))[:rows]
            + pltpu.roll(cx * here, 1, 0)[:rows]
            + cy * pltpu.roll(own, width - 1, 1)
            + pltpu.roll(cy * own, 1, 1)
            + (c_z[z + 1, :rows] * first[up, :rows] + c_z[z, :rows] * first[down, :rows])
            - total_ref[z]
        )
        beyond = edges(NEXT, z)
        for n, span in enumerate((low, high)):
            new_ref[z, :, span] = press[z, :, span] + inverse_ref[z, :, span] * (
                gathered[:, span] + beyond[n][:rows]
            )

    by_pairs(depth, second)

    def left(z):
        leave(z).wait()

    by_pairs(depth, left)


def on_device(
    pressure, composition, mass_old, pore_volume, trans_x, trans_y, trans_z,
    volatility, pressure_slope, mixing, two_phase,
):
    depth, rows, width = pressure.shape
    f32 = jnp.float32
    smem = pl.BlockSpec(memory_space=pltpu.SMEM)
    vmem = pl.BlockSpec(memory_space=pltpu.VMEM)
    def params(mib):
        return pltpu.CompilerParams(vmem_limit_bytes=mib * MIB)

    scalars = (two_phase, volatility, pressure_slope, mixing)

    def swapped(block, axis, first):
        count = lax.axis_size(axis)
        pairs = [(i, i + 1) for i in range(first, count - 1, 2)]
        return lax.ppermute(block, axis, pairs + [(j, i) for i, j in pairs])

    whole = jax.ShapeDtypeStruct((COMPS, depth, rows, width), f32)
    sums = jax.ShapeDtypeStruct((depth, rows, width), f32)
    packed = jax.ShapeDtypeStruct((len(UNITS) // 2, DEPTH_SLOTS * depth, width), f32)
    fields = (composition, pressure, pore_volume, mass_old, trans_x, trans_y, trans_z)

    def parts(count):
        planes = jax.ShapeDtypeStruct((COMPS, depth, count, width), f32)
        plane = jax.ShapeDtypeStruct((depth, count, width), f32)
        return [planes, planes, plane, plane]

    between = [jax.ShapeDtypeStruct((*x.shape[:-2], rows - 2 * ROWS, width), f32) for x in fields[:4]]
    *results, operand, comp, press, pore, mass = pl.pallas_call(
        edge_cells,
        in_specs=[pl.BlockSpec(memory_space=pl.ANY)] * (4 + len(fields)),
        out_specs=[vmem] * 11,
        out_shape=parts(2 * ROWS)
        + [packed, packed, jax.ShapeDtypeStruct((PART, DEEP), jnp.bfloat16), *between],
        scratch_shapes=[pltpu.SMEM(x.shape, x.dtype) for x in scalars]
        + [pltpu.VMEM((2, *x.shape[:-2], ROWS, width), f32) for x in fields]
        + [pltpu.SemaphoreType.DMA((3, len(fields))), pltpu.SemaphoreType.DMA((4,))],
        compiler_params=params(24),
        name="edge_cells",
    )(*(pltpu.with_memory_space_constraint(x, pltpu.HBM) for x in (*scalars, *fields)))
    *edge, one, two = results
    rows_one = swapped(one, "areal", 0)
    rows_two = swapped(two, "areal", 1)
    cells = rows * depth * width
    inner = pl.pallas_call(
        inner_cells,
        in_specs=[smem] * 3 + [vmem] * 5,
        out_specs=[vmem] * 4,
        out_shape=parts(rows - 2 * ROWS),
        compiler_params=params(24),
        cost_estimate=pl.CostEstimate(
            flops=450 * cells, transcendentals=95 * cells, bytes_accessed=2 * 39 * cells
        ),
        name="inner_cells",
    )(*scalars[:3], operand, comp, press, pore, mass)
    planes_of = (pressure, trans_x, trans_y, trans_z, pore_volume)

    narrow = jax.ShapeDtypeStruct((rows + ROWS, FIELDS * 16), f32)
    one, two, packet = pl.pallas_call(
        pack_columns,
        in_specs=[vmem] * 15,
        out_specs=[vmem] * 3,
        out_shape=[narrow, narrow, jax.ShapeDtypeStruct((rows + ROWS, FIELDS * 32), f32)],
        compiler_params=params(24),
        name="pack_columns",
    )(rows_one, rows_two, *planes_of, *edge, *inner)
    columns_one = swapped(one, "layer", 0)
    columns_two = swapped(two, "layer", 1)

    tall = jax.ShapeDtypeStruct((depth, rows + ROWS, width), f32)
    above_faces = jax.ShapeDtypeStruct((depth + 1, rows + ROWS, width), f32)
    near, *sweep = pl.pallas_call(
        near_residual,
        in_specs=[vmem] * 15,
        out_specs=[vmem] * 6,
        out_shape=[whole, tall, tall, tall, tall, above_faces],
        scratch_shapes=[
            pltpu.VMEM((COMPS, depth, ROWS, width), f32),
            pltpu.VMEM((FIELDS - COMPS, depth, ROWS, width), f32),
            pltpu.VMEM((2, depth, rows, width), f32),
            pltpu.VMEM((depth, rows, width), f32),
            pltpu.VMEM((depth + 1, rows, width), f32),
        ],
        compiler_params=params(24),
        cost_estimate=pl.CostEstimate(flops=150 * cells, transcendentals=0, bytes_accessed=4 * 31 * cells),
        name="near_residual",
    )(rows_one, rows_two, *planes_of, *edge, *inner)

    return pl.pallas_call(
        finish,
        in_specs=[vmem] * 12,
        out_specs=[pl.BlockSpec(memory_space=pl.ANY), vmem],
        out_shape=[whole, sums],
        scratch_shapes=[
            pltpu.VMEM((COMPS, rows, LANES), f32),
            pltpu.VMEM((4, rows + ROWS, LANES), f32),
            pltpu.VMEM((depth, rows + ROWS, width), f32),
            pltpu.VMEM((depth, rows, width), f32),
            pltpu.VMEM((depth, rows, width), f32),
            pltpu.VMEM((COMPS, depth, rows, width), f32),
            pltpu.SemaphoreType.DMA((depth,)),
        ],
        compiler_params=params(24),
        name="finish",
    )(columns_one, columns_two, packet, pressure, *sweep, edge[0], inner[0], near)


def solution(mesh):
    placed = (
        P(None, "areal", "layer"),
        P(None, None, "areal", "layer"),
        P(None, None, "areal", "layer"),
        P(None, "areal", "layer"),
        P(None, "areal", "layer"),
        P(None, "areal", "layer"),
        P(None, "areal", "layer"),
        P(),
        P(),
        P(),
        P(None, "areal"),
    )
    return jax.shard_map(
        on_device,
        mesh=mesh,
        in_specs=placed,
        out_specs=(P(None, None, "areal", "layer"), P(None, "areal", "layer")),
        check_vma=False,
    )
```

```python
import jax
import jax.numpy as jnp
from jax import lax
from jax.experimental import pallas as pl
from jax.experimental.pallas import tpu as pltpu
from jax.sharding import PartitionSpec as P

SS_ITERS = 3
RR_ITERS = 3
LIGHT = 4
COMPS = 9
FIELDS = 16
MOB, PRESS, TX, TY, TZ, PORE, ACC = range(COMPS, FIELDS)
UNITS = (MOB, PRESS, TX, (0, 1), (2, 3), (4, 5), (6, 7), (8, TY), (TZ, PORE), (ACC, ACC))
DEPTH_SLOTS = 4
TIME_STEP = 4.0
COMPRESS = 0.2
VAPOUR_WEIGHT = 1.0 / 0.25
LANES = 128
ROWS = 8
MIB = 1024 * 1024
PART = (COMPS + 1) * ROWS
DEEP = 256


def rcp(x):
    return pltpu.reciprocal(x, approx=True)


def total_of(terms):
    terms = list(terms)
    while len(terms) > 1:
        terms = [a + b for a, b in zip(terms[::2], terms[1::2])] + (
            [terms[-1]] if len(terms) % 2 else []
        )
    return terms[0]


def split(x):
    high = x.astype(jnp.bfloat16)
    return high, (x - high.astype(jnp.float32)).astype(jnp.bfloat16)


def mixing_operand(mix_ref):
    shape = (ROWS, DEEP)
    lane, row = lane_of(shape), row_of(shape)
    part = lax.div(lane, PART)
    within = lane - PART * part
    column = lax.div(within, ROWS)
    on = (within - ROWS * column == row) & (part < 3)
    blocks = []
    for i in range(COMPS):
        value = jnp.zeros(shape, jnp.float32)
        for j in range(COMPS):
            value = jnp.where(column == j, 2.0 * mix_ref[i, j], value)
        high, low = split(value)
        value = jnp.where(part == 2, low.astype(jnp.float32), high.astype(jnp.float32))
        blocks.append(jnp.where(on, value, 0.0))
    blocks.append(jnp.zeros(shape, jnp.float32))
    return jnp.concatenate(blocks, axis=0).astype(jnp.bfloat16)


def mixed(operand, spread):
    shape = spread[0].shape
    high, low = split(jnp.concatenate(spread + [jnp.zeros(shape, jnp.float32)], axis=0))
    tail = jnp.zeros((DEEP - 3 * PART, shape[1]), jnp.bfloat16)
    out = jnp.dot(
        operand,
        jnp.concatenate([high, low, high, tail], axis=0),
        preferred_element_type=jnp.float32,
    )
    return [out[ROWS * i : ROWS * (i + 1)] for i in range(COMPS)]


def flash(feed, pressure, signed, slope, operand):
    log_press = jnp.log(pressure)
    half_base = [0.5 * signed[i] - (0.5 * slope[i]) * log_press for i in range(COMPS)]
    spread = None
    for outer in range(SS_ITERS):
        if outer == 0:
            half_log = half_base
        else:
            mix = mixed(operand, spread)
            half_log = [half_base[i] - 0.5 * jnp.tanh(mix[i]) for i in range(COMPS)]
        t = [jnp.tanh(half_log[i]) for i in range(COMPS)]
        u = [rcp(t[i]) for i in range(COMPS)]
        psi = None
        for inner in range(RR_ITERS):
            q = t if inner == 0 else [rcp(u[i] + psi) for i in range(COMPS)]
            part = [feed[i] * q[i] for i in range(COMPS)]
            step = total_of(part) * rcp(total_of(part[i] * q[i] for i in range(COMPS)))
            psi = jnp.clip(step if inner == 0 else psi + step, -1.0, 1.0)
        spread = [feed[i] * rcp(u[i] + psi) for i in range(COMPS)]
    liquid_part = (0.25 * (1.0 - psi)) * (1.0 - psi)
    vapour_part = (0.25 * VAPOUR_WEIGHT * (1.0 + psi)) * (1.0 + psi)
    both, apart = vapour_part + liquid_part, vapour_part - liquid_part
    return [spread[i] * (both * u[i] + apart) for i in range(COMPS)]


def parameters(vol_ref, slope_ref):
    signed = [vol_ref[i] if i < LIGHT else -vol_ref[i] for i in range(COMPS)]
    return signed, [slope_ref[i] for i in range(COMPS)]


def lane_of(shape):
    return lax.broadcasted_iota(jnp.int32, shape, len(shape) - 1)


def row_of(shape):
    return lax.broadcasted_iota(jnp.int32, shape, len(shape) - 2)


class Rows:
    def __init__(self, edge, inner):
        self.edge, self.inner = edge, inner

    def __getitem__(self, at):
        at = at if isinstance(at, tuple) else (at,)
        edge = self.edge[at]
        return jnp.concatenate([edge[:ROWS], self.inner[at], edge[ROWS:]], axis=0)


def pack_rows(field, low, out_ref, depth):
    row = None
    for n in range(0, len(UNITS), 2):
        for pair in range(depth // 2):
            tile = None
            for z in (2 * pair, 2 * pair + 1):
                order = (1, 0) if low else (0, 1)
                for which in order:
                    unit = UNITS[n + which]
                    at = 4 * (z % 2) + (2 if low == (which == 0) else 0)
                    first = 0 if low else ROWS - 1
                    if isinstance(unit, tuple):
                        a, b = unit
                        pieces = [(at, a, at - first), (at + 1, b, at + 1 - first)]
                        if not low:
                            pieces = [(at, b, at - first), (at + 1, a, at + 1 - first)]
                    else:
                        pieces = [(at, unit, at if low else at + 2)]
                    for start, k, turn in pieces:
                        here = field(k, z)
                        if row is None:
                            row = row_of(here.shape)
                        if turn % ROWS:
                            here = pltpu.roll(here, turn % ROWS, 0)
                        tile = here if tile is None else jnp.where(row < start, tile, here)
            out_ref[n // 2, pl.ds(pair * ROWS, ROWS), :] = tile


def row_tiles(one, two, wanted, start=0, stop=None):
    shape = one.shape[1:]
    upper = row_of(shape) % DEPTH_SLOTS < 2
    tile_row = row_of((ROWS, shape[1]))
    stop = stop or shape[0] // DEPTH_SLOTS
    tiles = {}
    for n, unit in enumerate(UNITS):
        fields = unit if isinstance(unit, tuple) else (unit,)
        if not any(k in wanted for k in fields):
            continue
        up, down = by_side("areal", one[n // 2], two[n // 2])
        if n % 2:
            up, down = pltpu.roll(up, shape[0] - 2, 0), pltpu.roll(down, 2, 0)
        both = jnp.where(upper, up, down)
        for z in range(start, stop):
            at = (z // 2) * ROWS
            tile = pltpu.roll(both[at : at + ROWS], 6 - 4 * (z % 2), 0)
            if fields[0] in wanted:
                tiles.setdefault(fields[0], []).append(tile)
            if fields[-1] in wanted and fields[-1] != fields[0]:
                other = jnp.where(tile_row < 4, pltpu.roll(tile, ROWS - 1, 0), pltpu.roll(tile, 1, 0))
                tiles.setdefault(fields[-1], []).append(other)
    return tiles


def pack_columns(rows_one, rows_two, *refs):
    (
        press, tx, ty, tz, pore, edge_mob, _, edge_mob_sum, edge_acc_sum, mob, _, mob_sum, acc_sum,
        one_ref, two_ref, own_ref,
    ) = refs
    depth, rows, width = press.shape
    shape = (rows + ROWS, LANES)
    lane = lane_of(shape)
    mob, mob_sum, acc_sum = (
        Rows(*both) for both in ((edge_mob, mob), (edge_mob_sum, mob_sum), (edge_acc_sum, acc_sum))
    )
    corner_fields = {MOB: mob_sum, PRESS: press, TX: tx, TY: ty}
    others = {TZ: tz, PORE: pore, ACC: acc_sum, **corner_fields}
    corners = row_tiles(rows_one, rows_two, corner_fields)
    nothing = jnp.zeros((ROWS, LANES), jnp.float32)
    for tile in range(FIELDS // 4):
        packed = jnp.zeros(shape, jnp.float32)
        for quarter in range(4):
            k = 4 * tile + quarter
            for z in range(depth):
                plane = mob[k, z] if k < COMPS else others[k][z]
                first, last = plane[:, :LANES], plane[:, -LANES:]
                at = 32 * quarter + 4 * z
                both = jnp.where(lane_of(first.shape) < LANES // 2, first, last)
                if k < COMPS:
                    both = pltpu.roll(both, at + 2, 1)
                    on = (lane_of(first.shape) >= at + 1) & (lane_of(first.shape) < at + 3)
                    packed = jnp.concatenate([jnp.where(on, both, packed[:rows]), nothing], axis=0)
                    continue
                end = nothing
                if k in corner_fields:
                    end = corners[k][z]
                    end = jnp.where(lane_of(end[:, :LANES].shape) < LANES // 2, end[:, :LANES], end[:, -LANES:])
                both = pltpu.roll(jnp.concatenate([both, end], axis=0), (at + 2) % LANES, 1)
                packed = jnp.where((lane >= at) & (lane < at + 4), both, packed)
        own_ref[:, tile * LANES : (tile + 1) * LANES] = packed
    odd = lax.axis_index("layer") % 2 == 1
    half = FIELDS // 8
    for n in range(half):
        near, far = (own_ref[:, t * LANES : (t + 1) * LANES] for t in (n, n + half))
        upward = jnp.where(lane % 4 < 2, near, pltpu.roll(far, 2, 1))
        downward = jnp.where(lane % 4 < 2, pltpu.roll(near, LANES - 2, 1), far)
        one_ref[:, n * LANES : (n + 1) * LANES] = jnp.where(odd, downward, upward)
        two_ref[:, n * LANES : (n + 1) * LANES] = jnp.where(odd, upward, downward)


def spread_fields(tiles):
    fields = []
    for tile in tiles:
        for quarter in range(4):
            turn = (LANES - 32 * quarter) % LANES
            fields.append(pltpu.roll(tile, turn, 1) if turn else tile)
    return fields


def side_fields(one, two):
    lane = lane_of((one.shape[0], LANES))
    near, far = [], []
    for n in range(FIELDS // 8):
        span = slice(n * LANES, (n + 1) * LANES)
        left, right = by_side("layer", one[:, span], two[:, span])
        near.append(jnp.where(lane % 4 < 2, left, pltpu.roll(right, 2, 1)))
        far.append(jnp.where(lane % 4 < 2, pltpu.roll(left, LANES - 2, 1), right))
    return spread_fields(near + far)


def flash_rows(source, target, tile_row, flags, vol, slope, operand, comp, press, pore, mass, outs, ready=None):
    mob_ref, acc_ref, mob_sum, acc_sum = outs
    layer = lax.axis_index("layer")
    depth, _, width = press.shape

    def beside(ref, *lead):
        return jnp.concatenate([ref[(*lead, z, source)] for z in range(depth)], axis=1)

    def store(ref, value, *lead):
        for z in range(depth):
            ref[(*lead, z, target)] = value[:, z * width : (z + 1) * width]

    raw = [beside(comp, i) for i in range(COMPS)]
    inverse = rcp(total_of(raw))
    feed = [raw[i] * inverse for i in range(COMPS)]
    first, last = flags[layer, 2 * tile_row], flags[layer, 2 * tile_row + 1]

    @pl.when(first + last > 0)
    def _():
        signed, slopes = parameters(vol, slope)
        two = flash(feed, beside(press), signed, slopes, operand[...])
        marked = jnp.where(row_of(feed[0].shape) < ROWS // 2, first, last) > 0
        mobility = [jnp.where(marked, two[i], feed[i]) for i in range(COMPS)]
        for i in range(COMPS):
            store(mob_ref, mobility[i], i)
        store(mob_sum, total_of(mobility))

    @pl.when(first + last == 0)
    def _():
        for i in range(COMPS):
            store(mob_ref, feed[i], i)
        store(mob_sum, total_of(feed))

    if ready:
        ready()
    volume = beside(pore)
    acc = [volume * feed[i] - beside(mass, i) for i in range(COMPS)]
    for i in range(COMPS):
        store(acc_ref, acc[i], i)
    store(acc_sum, total_of(acc))


def edge_cells(
    flags_in, vol_in, slope_in, mix_in, comp, press, pore, mass, tx, ty, tz,
    mob_ref, acc_ref, mob_sum, acc_sum, one_ref, two_ref, operand, comp_i, press_i, pore_i, mass_i,
    flags, vol, slope, mix, comp_s, press_s, pore_s, mass_s, tx_s, ty_s, tz_s, sems, scalar_sems,
):
    depth, rows, _ = press.shape
    fetched = (
        (comp, comp_s), (press, press_s), (pore, pore_s), (mass, mass_s), (tx, tx_s), (ty, ty_s), (tz, tz_s)
    )

    ahead = (comp_i, press_i, pore_i, mass_i)

    def fetch(end, n):
        source, slot = fetched[n]
        at = pl.ds(end * (rows - ROWS), ROWS) if end < 2 else pl.ds(ROWS, rows - 2 * ROWS)
        return pltpu.make_async_copy(
            source.at[:, :, at, :] if len(source.shape) == 4 else source.at[:, at, :],
            slot.at[end] if end < 2 else ahead[n],
            sems.at[end, n],
        )

    scalars = [
        pltpu.make_async_copy(source, slot, scalar_sems.at[n])
        for n, (source, slot) in enumerate(
            ((flags_in, flags), (vol_in, vol), (slope_in, slope), (mix_in, mix))
        )
    ]
    early, late = (0, 1), range(2, len(fetched))
    for copy in scalars:
        copy.start()
    for n in early:
        fetch(0, n).start()
    for copy in scalars:
        copy.wait()
    operand[...] = mixing_operand(mix)
    odd = lax.axis_index("areal") % 2 == 1
    for end in range(2):
        for n in early:
            fetch(end, n).wait()
        if end == 0:
            for n in late:
                fetch(0, n).start()
            for n in range(len(fetched)):
                fetch(1, n).start()
        else:
            for n in range(len(ahead)):
                fetch(2, n).start()

        def ready():
            for n in late:
                fetch(end, n).wait()

        target = slice(end * ROWS, (end + 1) * ROWS)
        flash_rows(
            slice(None), target, end * (rows // ROWS - 1), flags, vol, slope, operand,
            *(slot.at[end] for _, slot in fetched[:4]), (mob_ref, acc_ref, mob_sum, acc_sum), ready,
        )

        def field(k, z):
            if k < COMPS:
                here = mob_ref[k, z, target]
            elif k in (MOB, ACC):
                here = (mob_sum if k == MOB else acc_sum)[z, target]
            else:
                here = {PRESS: press_s, TX: tx_s, TY: ty_s, TZ: tz_s, PORE: pore_s}[k][end, z]
            return here

        for turn, ref in enumerate((one_ref, two_ref)):
            @pl.when(odd == (end == turn))
            def _():
                pack_rows(field, end == 0, ref, depth)

    for n in range(len(ahead)):
        fetch(2, n).wait()


def inner_cells(flags, vol, slope, operand, comp, press, pore, mass, *outs):
    def tile(t, carry):
        at = pl.ds(pl.multiple_of(t * ROWS, ROWS), ROWS)
        flash_rows(at, at, t + 1, flags, vol, slope, operand, comp, press, pore, mass, outs)
        return carry

    lax.fori_loop(0, press.shape[1] // ROWS, tile, 0)


def by_side(axis, one, two):
    odd = lax.axis_index(axis) % 2 == 1
    return jnp.where(odd, one, two), jnp.where(odd, two, one)


def by_pairs(count, body):
    def pair(t, carry):
        body(2 * t)
        body(2 * t + 1)
        return carry

    lax.fori_loop(0, count // 2, pair, 0)


def near_residual(
    rows_one, rows_two, press, tx, ty, tz, pore,
    edge_mob, edge_acc, edge_mob_sum, edge_acc_sum, mob, acc, mob_sum, acc_sum,
    out_ref, total_ref, diagonal_ref, c_x, c_y, c_z,
    rows_h, fields_h, g_x, g_y, g_z,
):
    depth, rows, width = press.shape
    areal, areals = lax.axis_index("areal"), lax.axis_size("areal")
    tall = rows + ROWS
    full = (tall, width)
    own = slice(0, rows)
    mob, acc, mob_sum, acc_sum = (
        Rows(*both)
        for both in ((edge_mob, mob), (edge_acc, acc), (edge_mob_sum, mob_sum), (edge_acc_sum, acc_sum))
    )
    fields = {MOB: mob_sum, PRESS: press, TX: tx, TY: ty, TZ: tz, PORE: pore, ACC: acc_sum}
    tiles = row_tiles(rows_one, rows_two, range(FIELDS))
    for z in range(depth):
        for i in range(COMPS):
            rows_h[i, z] = tiles[i][z]
        for n, k in enumerate(fields):
            fields_h[n, z] = tiles[k][z]

    end_x = (row_of(full) == rows - 1) & (areal == areals - 1)
    end_y = lane_of(full) == width - 1
    scale = 0.5 * TIME_STEP
    c_z[0] = jnp.zeros(full, jnp.float32)
    g_z[0] = jnp.zeros((rows, width), jnp.float32)

    def update(z):
        m, p, x, y, zz, volume, total = (
            jnp.concatenate([ref[z], fields_h[n, z]], axis=0) for n, ref in enumerate(fields.values())
        )
        up, down = jnp.minimum(z + 1, depth - 1), jnp.maximum(z - 1, 0)
        p_up = jnp.concatenate([press[up], fields_h[1, up]], axis=0)
        p_down = jnp.concatenate([press[down], fields_h[1, down]], axis=0)
        m_up = jnp.concatenate([mob_sum[up], fields_h[0, up]], axis=0)
        strength_x = jnp.where(end_x, 0.0, scale * x)
        strength_y = jnp.where(end_y, 0.0, scale * y)
        strength_z = jnp.where(z < depth - 1, scale, 0.0) * zz
        dx = p - pltpu.roll(p, tall - 1, 0)
        dy = p - pltpu.roll(p, width - 1, 1)
        dz = p - p_up
        cx = strength_x * (m + pltpu.roll(m, tall - 1, 0))
        cy = strength_y * (m + pltpu.roll(m, width - 1, 1))
        cz = strength_z * (m + m_up)
        cz_low = c_z[z]
        gx = strength_x * dx
        g_x[0, z], g_x[1, z] = gx[own], -pltpu.roll(gx, 1, 0)[own]
        g_y[z], g_z[z + 1] = (strength_y * dy)[own], (strength_z * dz)[own]
        c_x[z], c_y[z], c_z[z + 1] = cx, cy, cz
        fx, fy = cx * dx, cy * dy
        total_ref[z] = (
            total
            + (fx - pltpu.roll(fx, 1, 0))
            + (fy - pltpu.roll(fy, 1, 1))
            + (cz * dz + cz_low * (p - p_down))
        )
        diagonal_ref[z] = (
            COMPRESS * volume
            + (cx + pltpu.roll(cx, 1, 0))
            + (cy + pltpu.roll(cy, 1, 1))
            + (cz + cz_low)
        )

    by_pairs(depth, update)

    def residual(z):
        down, up = jnp.maximum(z - 1, 0), jnp.minimum(z + 1, depth - 1)
        gx, gx_low, gy, gz, gz_low = g_x[0, z], g_x[1, z], g_y[z], g_z[z + 1], -g_z[z]
        gy_low = -pltpu.roll(gy, 1, 1)
        middle = (gx + gx_low) + (gy + gy_low) + (gz + gz_low)
        for i in range(COMPS):
            here = mob[i, z]
            tall_here = jnp.concatenate([here, rows_h[i, z]], axis=0)
            out_ref[i, z] = (
                acc[i, z]
                + middle * here
                + gx * pltpu.roll(tall_here, tall - 1, 0)[own]
                + gx_low * pltpu.roll(tall_here, 1, 0)[own]
                + gy * pltpu.roll(here, width - 1, 1)
                + gy_low * pltpu.roll(here, 1, 1)
                + gz * mob[i, up]
                + gz_low * mob[i, down]
            )

    by_pairs(depth, residual)


def finish(
    columns_one, columns_two, packet, press, total_in, diagonal_in, c_x, c_y, c_z, edge_mob, mob, near,
    res_ref, new_ref,
    side_h, edge_h, first, total_ref, inverse_ref, res_s, sems,
):
    depth, rows, width = press.shape
    layer, layers = lax.axis_index("layer"), lax.axis_size("layer")
    areal, areals = lax.axis_index("areal"), lax.axis_size("areal")
    tall = rows + ROWS
    lane = lane_of((tall, LANES))
    at_first, at_last = lane == 0, lane == LANES - 1
    low, high = slice(0, LANES), slice(width - LANES, width)
    FLUX, COUPLE, FACE, NEXT = range(4)
    mob = Rows(edge_mob, mob)

    def edges(which, z):
        both = pltpu.roll(edge_h[which], LANES - 1 - 4 * z, 1)
        return jnp.where(at_first, both, 0.0), jnp.where(at_last, both, 0.0)

    halo = side_fields(columns_one, columns_two)
    here = spread_fields([packet[:, t : t + LANES] for t in range(0, FIELDS * 32, LANES)])
    is_left = lane % 4 == 1
    for i in range(COMPS):
        cells = halo[i][:rows]
        side_h[i] = jnp.where(is_left[:rows], pltpu.roll(cells, LANES - 1, 1), pltpu.roll(cells, 1, 1))
    scale = 0.5 * TIME_STEP

    def turned(x, by):
        return pltpu.roll(x, by % LANES, 1)

    def outer(x):
        return jnp.where(is_left, turned(x, 1), turned(x, -1))

    def inner(x):
        return jnp.where(is_left, turned(x, -1), turned(x, 1))

    m, p = halo[MOB], halo[PRESS]
    strength = scale * halo[TY]
    own_strength = jnp.where(layer < layers - 1, scale, 0.0) * here[TY]
    c_out = jnp.where(is_left, turned(strength, 1), strength) * (m + outer(m))
    s_in = jnp.where(is_left, strength, turned(own_strength, 1))
    c_in = s_in * (m + inner(here[MOB]))
    d_in = p - inner(here[PRESS])
    end_x = (row_of(lane.shape) == rows - 1) & (areal == areals - 1)
    cx = jnp.where(end_x, 0.0, scale * halo[TX]) * (m + pltpu.roll(m, tall - 1, 0))
    cz = jnp.where(lane < 4 * (depth - 1), scale * halo[TZ], 0.0) * (m + turned(m, -4))
    fx = cx * (p - pltpu.roll(p, tall - 1, 0))
    fz = cz * (p - turned(p, -4))
    total = (
        halo[ACC]
        + (c_out * (p - outer(p)) + c_in * d_in)
        + (fx - pltpu.roll(fx, 1, 0))
        + (fz - turned(fz, 4))
    )
    diagonal = (
        COMPRESS * halo[PORE] + (c_out + c_in) + (cx + pltpu.roll(cx, 1, 0)) + (cz + turned(cz, 4))
    )
    usable = diagonal > 0.0
    beside = jnp.where(usable, -total * rcp(jnp.where(usable, diagonal, 1.0)), 0.0)
    for which, value in (
        (FLUX, -c_in * d_in), (COUPLE, c_in), (FACE, -s_in * d_in), (NEXT, c_in * beside)
    ):
        edge_h[which] = jnp.where(is_left, value, turned(value, -2))

    def leave(z):
        return pltpu.make_async_copy(res_s.at[:, z], res_ref.at[:, z], sems.at[z])

    def update(z):
        faces = [face[:rows] for face in edges(FACE, z)]
        for i in range(COMPS):
            side = pltpu.roll(side_h[i], LANES - 2 - 4 * z, 1)
            cells = mob[i, z]
            for span, face in zip((low, high), faces):
                res_s[i, z, :, span] = near[i, z, :, span] + face * (cells[:, span] + side)
        leave(z).start()
        flux, couple = edges(FLUX, z), edges(COUPLE, z)
        for n, span in enumerate((low, high)):
            total = total_in[z, :, span] + flux[n]
            diagonal = diagonal_in[z, :, span] + couple[n]
            usable = diagonal > 0.0
            inverse = rcp(jnp.where(usable, diagonal, 1.0))
            first[z, :, span] = jnp.where(usable, -total * inverse, 0.0)
            total_ref[z, :, span] = total[:rows]
            inverse_ref[z, :, span] = inverse[:rows]

    by_pairs(depth, update)

    def second(z):
        here = first[z]
        up, down = jnp.minimum(z + 1, depth - 1), jnp.maximum(z - 1, 0)
        cx, cy = c_x[z], c_y[z, :rows]
        own = here[:rows]
        gathered = (
            (cx * pltpu.roll(here, tall - 1, 0))[:rows]
            + pltpu.roll(cx * here, 1, 0)[:rows]
            + cy * pltpu.roll(own, width - 1, 1)
            + pltpu.roll(cy * own, 1, 1)
            + (c_z[z + 1, :rows] * first[up, :rows] + c_z[z, :rows] * first[down, :rows])
            - total_ref[z]
        )
        beyond = edges(NEXT, z)
        for n, span in enumerate((low, high)):
            new_ref[z, :, span] = press[z, :, span] + inverse_ref[z, :, span] * (
                gathered[:, span] + beyond[n][:rows]
            )

    by_pairs(depth, second)

    def left(z):
        leave(z).wait()

    by_pairs(depth, left)


def on_device(
    pressure, composition, mass_old, pore_volume, trans_x, trans_y, trans_z,
    volatility, pressure_slope, mixing, two_phase,
):
    depth, rows, width = pressure.shape
    f32 = jnp.float32
    smem = pl.BlockSpec(memory_space=pltpu.SMEM)
    vmem = pl.BlockSpec(memory_space=pltpu.VMEM)
    def params(mib):
        return pltpu.CompilerParams(vmem_limit_bytes=mib * MIB)

    scalars = (two_phase, volatility, pressure_slope, mixing)

    def swapped(block, axis, first):
        count = lax.axis_size(axis)
        pairs = [(i, i + 1) for i in range(first, count - 1, 2)]
        return lax.ppermute(block, axis, pairs + [(j, i) for i, j in pairs])

    whole = jax.ShapeDtypeStruct((COMPS, depth, rows, width), f32)
    sums = jax.ShapeDtypeStruct((depth, rows, width), f32)
    packed = jax.ShapeDtypeStruct((len(UNITS) // 2, DEPTH_SLOTS * depth, width), f32)
    fields = (composition, pressure, pore_volume, mass_old, trans_x, trans_y, trans_z)

    def parts(count):
        planes = jax.ShapeDtypeStruct((COMPS, depth, count, width), f32)
        plane = jax.ShapeDtypeStruct((depth, count, width), f32)
        return [planes, planes, plane, plane]

    between = [jax.ShapeDtypeStruct((*x.shape[:-2], rows - 2 * ROWS, width), f32) for x in fields[:4]]
    *results, operand, comp, press, pore, mass = pl.pallas_call(
        edge_cells,
        in_specs=[pl.BlockSpec(memory_space=pl.ANY)] * (4 + len(fields)),
        out_specs=[vmem] * 11,
        out_shape=parts(2 * ROWS)
        + [packed, packed, jax.ShapeDtypeStruct((PART, DEEP), jnp.bfloat16), *between],
        scratch_shapes=[pltpu.SMEM(x.shape, x.dtype) for x in scalars]
        + [pltpu.VMEM((2, *x.shape[:-2], ROWS, width), f32) for x in fields]
        + [pltpu.SemaphoreType.DMA((3, len(fields))), pltpu.SemaphoreType.DMA((4,))],
        compiler_params=params(24),
        name="edge_cells",
    )(*(pltpu.with_memory_space_constraint(x, pltpu.HBM) for x in (*scalars, *fields)))
    *edge, one, two = results
    rows_two = swapped(two, "areal", 1)
    rows_one = swapped(one, "areal", 0)
    cells = rows * depth * width
    inner = pl.pallas_call(
        inner_cells,
        in_specs=[smem] * 3 + [vmem] * 5,
        out_specs=[vmem] * 4,
        out_shape=parts(rows - 2 * ROWS),
        compiler_params=params(24),
        cost_estimate=pl.CostEstimate(
            flops=450 * cells, transcendentals=95 * cells, bytes_accessed=2 * 39 * cells
        ),
        name="inner_cells",
    )(*scalars[:3], operand, comp, press, pore, mass)
    planes_of = (pressure, trans_x, trans_y, trans_z, pore_volume)

    narrow = jax.ShapeDtypeStruct((rows + ROWS, FIELDS * 16), f32)
    one, two, packet = pl.pallas_call(
        pack_columns,
        in_specs=[vmem] * 15,
        out_specs=[vmem] * 3,
        out_shape=[narrow, narrow, jax.ShapeDtypeStruct((rows + ROWS, FIELDS * 32), f32)],
        compiler_params=params(24),
        name="pack_columns",
    )(rows_one, rows_two, *planes_of, *edge, *inner)
    columns_one = swapped(one, "layer", 0)
    columns_two = swapped(two, "layer", 1)

    tall = jax.ShapeDtypeStruct((depth, rows + ROWS, width), f32)
    above_faces = jax.ShapeDtypeStruct((depth + 1, rows + ROWS, width), f32)
    near, *sweep = pl.pallas_call(
        near_residual,
        in_specs=[vmem] * 15,
        out_specs=[vmem] * 6,
        out_shape=[whole, tall, tall, tall, tall, above_faces],
        scratch_shapes=[
            pltpu.VMEM((COMPS, depth, ROWS, width), f32),
            pltpu.VMEM((FIELDS - COMPS, depth, ROWS, width), f32),
            pltpu.VMEM((2, depth, rows, width), f32),
            pltpu.VMEM((depth, rows, width), f32),
            pltpu.VMEM((depth + 1, rows, width), f32),
        ],
        compiler_params=params(24),
        cost_estimate=pl.CostEstimate(flops=150 * cells, transcendentals=0, bytes_accessed=4 * 31 * cells),
        name="near_residual",
    )(rows_one, rows_two, *planes_of, *edge, *inner)

    return pl.pallas_call(
        finish,
        in_specs=[vmem] * 12,
        out_specs=[pl.BlockSpec(memory_space=pl.ANY), vmem],
        out_shape=[whole, sums],
        scratch_shapes=[
            pltpu.VMEM((COMPS, rows, LANES), f32),
            pltpu.VMEM((4, rows + ROWS, LANES), f32),
            pltpu.VMEM((depth, rows + ROWS, width), f32),
            pltpu.VMEM((depth, rows, width), f32),
            pltpu.VMEM((depth, rows, width), f32),
            pltpu.VMEM((COMPS, depth, rows, width), f32),
            pltpu.SemaphoreType.DMA((depth,)),
        ],
        compiler_params=params(24),
        name="finish",
    )(columns_one, columns_two, packet, pressure, *sweep, edge[0], inner[0], near)


def solution(mesh):
    placed = (
        P(None, "areal", "layer"),
        P(None, None, "areal", "layer"),
        P(None, None, "areal", "layer"),
        P(None, "areal", "layer"),
        P(None, "areal", "layer"),
        P(None, "areal", "layer"),
        P(None, "areal", "layer"),
        P(),
        P(),
        P(),
        P(None, "areal"),
    )
    return jax.shard_map(
        on_device,
        mesh=mesh,
        in_specs=placed,
        out_specs=(P(None, None, "areal", "layer"), P(None, "areal", "layer")),
        check_vma=False,
    )
```

```python
import jax
import jax.numpy as jnp
from jax import lax
from jax.experimental import pallas as pl
from jax.experimental.pallas import tpu as pltpu
from jax.sharding import PartitionSpec as P

SS_ITERS = 3
RR_ITERS = 3
LIGHT = 4
COMPS = 9
FIELDS = 16
MOB, PRESS, TX, TY, TZ, PORE, ACC = range(COMPS, FIELDS)
UNITS = (MOB, PRESS, TX, (0, 1), (2, 3), (4, 5), (6, 7), (8, TY), (TZ, PORE), (ACC, ACC))
DEPTH_SLOTS = 4
TIME_STEP = 4.0
COMPRESS = 0.2
VAPOUR_WEIGHT = 1.0 / 0.25
LANES = 128
ROWS = 8
MIB = 1024 * 1024
PART = (COMPS + 1) * ROWS
DEEP = 256


def rcp(x):
    return pltpu.reciprocal(x, approx=True)


def total_of(terms):
    terms = list(terms)
    while len(terms) > 1:
        terms = [a + b for a, b in zip(terms[::2], terms[1::2])] + (
            [terms[-1]] if len(terms) % 2 else []
        )
    return terms[0]


def split(x):
    high = x.astype(jnp.bfloat16)
    return high, (x - high.astype(jnp.float32)).astype(jnp.bfloat16)


def mixing_operand(mix_ref):
    shape = (ROWS, DEEP)
    lane, row = lane_of(shape), row_of(shape)
    part = lax.div(lane, PART)
    within = lane - PART * part
    column = lax.div(within, ROWS)
    on = (within - ROWS * column == row) & (part < 3)
    blocks = []
    for i in range(COMPS):
        value = jnp.zeros(shape, jnp.float32)
        for j in range(COMPS):
            value = jnp.where(column == j, 2.0 * mix_ref[i, j], value)
        high, low = split(value)
        value = jnp.where(part == 2, low.astype(jnp.float32), high.astype(jnp.float32))
        blocks.append(jnp.where(on, value, 0.0))
    blocks.append(jnp.zeros(shape, jnp.float32))
    return jnp.concatenate(blocks, axis=0).astype(jnp.bfloat16)


def mixed(operand, spread):
    shape = spread[0].shape
    high, low = split(jnp.concatenate(spread + [jnp.zeros(shape, jnp.float32)], axis=0))
    tail = jnp.zeros((DEEP - 3 * PART, shape[1]), jnp.bfloat16)
    out = jnp.dot(
        operand,
        jnp.concatenate([high, low, high, tail], axis=0),
        preferred_element_type=jnp.float32,
    )
    return [out[ROWS * i : ROWS * (i + 1)] for i in range(COMPS)]


def flash(feed, pressure, signed, slope, operand):
    log_press = jnp.log(pressure)
    half_base = [0.5 * signed[i] - (0.5 * slope[i]) * log_press for i in range(COMPS)]
    spread = None
    for outer in range(SS_ITERS):
        if outer == 0:
            half_log = half_base
        else:
            mix = mixed(operand, spread)
            half_log = [half_base[i] - 0.5 * jnp.tanh(mix[i]) for i in range(COMPS)]
        t = [jnp.tanh(half_log[i]) for i in range(COMPS)]
        u = [rcp(t[i]) for i in range(COMPS)]
        psi = None
        for inner in range(RR_ITERS):
            q = t if inner == 0 else [rcp(u[i] + psi) for i in range(COMPS)]
            part = [feed[i] * q[i] for i in range(COMPS)]
            step = total_of(part) * rcp(total_of(part[i] * q[i] for i in range(COMPS)))
            psi = jnp.clip(step if inner == 0 else psi + step, -1.0, 1.0)
        spread = [feed[i] * rcp(u[i] + psi) for i in range(COMPS)]
    liquid_part = (0.25 * (1.0 - psi)) * (1.0 - psi)
    vapour_part = (0.25 * VAPOUR_WEIGHT * (1.0 + psi)) * (1.0 + psi)
    both, apart = vapour_part + liquid_part, vapour_part - liquid_part
    return [spread[i] * (both * u[i] + apart) for i in range(COMPS)]


def parameters(vol_ref, slope_ref):
    signed = [vol_ref[i] if i < LIGHT else -vol_ref[i] for i in range(COMPS)]
    return signed, [slope_ref[i] for i in range(COMPS)]


def lane_of(shape):
    return lax.broadcasted_iota(jnp.int32, shape, len(shape) - 1)


def row_of(shape):
    return lax.broadcasted_iota(jnp.int32, shape, len(shape) - 2)


class Rows:
    def __init__(self, edge, inner):
        self.edge, self.inner = edge, inner

    def __getitem__(self, at):
        at = at if isinstance(at, tuple) else (at,)
        edge = self.edge[at]
        return jnp.concatenate([edge[:ROWS], self.inner[at], edge[ROWS:]], axis=0)


def pack_rows(field, low, out_ref, depth):
    row = None
    for n in range(0, len(UNITS), 2):
        for pair in range(depth // 2):
            tile = None
            for z in (2 * pair, 2 * pair + 1):
                order = (1, 0) if low else (0, 1)
                for which in order:
                    unit = UNITS[n + which]
                    at = 4 * (z % 2) + (2 if low == (which == 0) else 0)
                    first = 0 if low else ROWS - 1
                    if isinstance(unit, tuple):
                        a, b = unit
                        pieces = [(at, a, at - first), (at + 1, b, at + 1 - first)]
                        if not low:
                            pieces = [(at, b, at - first), (at + 1, a, at + 1 - first)]
                    else:
                        pieces = [(at, unit, at if low else at + 2)]
                    for start, k, turn in pieces:
                        here = field(k, z)
                        if row is None:
                            row = row_of(here.shape)
                        if turn % ROWS:
                            here = pltpu.roll(here, turn % ROWS, 0)
                        tile = here if tile is None else jnp.where(row < start, tile, here)
            out_ref[n // 2, pl.ds(pair * ROWS, ROWS), :] = tile


def row_tiles(one, two, wanted, start=0, stop=None):
    shape = one.shape[1:]
    upper = row_of(shape) % DEPTH_SLOTS < 2
    tile_row = row_of((ROWS, shape[1]))
    stop = stop or shape[0] // DEPTH_SLOTS
    tiles = {}
    for n, unit in enumerate(UNITS):
        fields = unit if isinstance(unit, tuple) else (unit,)
        if not any(k in wanted for k in fields):
            continue
        up, down = by_side("areal", one[n // 2], two[n // 2])
        if n % 2:
            up, down = pltpu.roll(up, shape[0] - 2, 0), pltpu.roll(down, 2, 0)
        both = jnp.where(upper, up, down)
        for z in range(start, stop):
            at = (z // 2) * ROWS
            tile = pltpu.roll(both[at : at + ROWS], 6 - 4 * (z % 2), 0)
            if fields[0] in wanted:
                tiles.setdefault(fields[0], []).append(tile)
            if fields[-1] in wanted and fields[-1] != fields[0]:
                other = jnp.where(tile_row < 4, pltpu.roll(tile, ROWS - 1, 0), pltpu.roll(tile, 1, 0))
                tiles.setdefault(fields[-1], []).append(other)
    return tiles


def pack_columns(rows_two, rows_one, *refs):
    (
        press, tx, ty, tz, pore, edge_mob, _, edge_mob_sum, edge_acc_sum, mob, _, mob_sum, acc_sum,
        one_ref, two_ref, own_ref,
    ) = refs
    depth, rows, width = press.shape
    shape = (rows + ROWS, LANES)
    lane = lane_of(shape)
    mob, mob_sum, acc_sum = (
        Rows(*both) for both in ((edge_mob, mob), (edge_mob_sum, mob_sum), (edge_acc_sum, acc_sum))
    )
    corner_fields = {MOB: mob_sum, PRESS: press, TX: tx, TY: ty}
    others = {TZ: tz, PORE: pore, ACC: acc_sum, **corner_fields}
    corners = row_tiles(rows_one, rows_two, corner_fields)
    nothing = jnp.zeros((ROWS, LANES), jnp.float32)
    for tile in range(FIELDS // 4):
        packed = jnp.zeros(shape, jnp.float32)
        for quarter in range(4):
            k = 4 * tile + quarter
            for z in range(depth):
                plane = mob[k, z] if k < COMPS else others[k][z]
                first, last = plane[:, :LANES], plane[:, -LANES:]
                at = 32 * quarter + 4 * z
                both = jnp.where(lane_of(first.shape) < LANES // 2, first, last)
                if k < COMPS:
                    both = pltpu.roll(both, at + 2, 1)
                    on = (lane_of(first.shape) >= at + 1) & (lane_of(first.shape) < at + 3)
                    packed = jnp.concatenate([jnp.where(on, both, packed[:rows]), nothing], axis=0)
                    continue
                end = nothing
                if k in corner_fields:
                    end = corners[k][z]
                    end = jnp.where(lane_of(end[:, :LANES].shape) < LANES // 2, end[:, :LANES], end[:, -LANES:])
                both = pltpu.roll(jnp.concatenate([both, end], axis=0), (at + 2) % LANES, 1)
                packed = jnp.where((lane >= at) & (lane < at + 4), both, packed)
        own_ref[:, tile * LANES : (tile + 1) * LANES] = packed
    odd = lax.axis_index("layer") % 2 == 1
    half = FIELDS // 8
    for n in range(half):
        near, far = (own_ref[:, t * LANES : (t + 1) * LANES] for t in (n, n + half))
        upward = jnp.where(lane % 4 < 2, near, pltpu.roll(far, 2, 1))
        downward = jnp.where(lane % 4 < 2, pltpu.roll(near, LANES - 2, 1), far)
        one_ref[:, n * LANES : (n + 1) * LANES] = jnp.where(odd, downward, upward)
        two_ref[:, n * LANES : (n + 1) * LANES] = jnp.where(odd, upward, downward)


def spread_fields(tiles):
    fields = []
    for tile in tiles:
        for quarter in range(4):
            turn = (LANES - 32 * quarter) % LANES
            fields.append(pltpu.roll(tile, turn, 1) if turn else tile)
    return fields


def side_fields(one, two):
    lane = lane_of((one.shape[0], LANES))
    near, far = [], []
    for n in range(FIELDS // 8):
        span = slice(n * LANES, (n + 1) * LANES)
        left, right = by_side("layer", one[:, span], two[:, span])
        near.append(jnp.where(lane % 4 < 2, left, pltpu.roll(right, 2, 1)))
        far.append(jnp.where(lane % 4 < 2, pltpu.roll(left, LANES - 2, 1), right))
    return spread_fields(near + far)


def flash_rows(rows, flags, vol, slope, operand, outs, ready=None):
    mob_ref, acc_ref, mob_sum, acc_sum = outs
    layer = lax.axis_index("layer")
    depth, _, width = mob_sum.shape
    signed, slopes = parameters(vol, slope)

    def beside(ref, source, *lead):
        return jnp.concatenate([ref[(*lead, z, source)] for z in range(depth)], axis=1)

    def store(ref, value, target, *lead):
        for z in range(depth):
            ref[(*lead, z, target)] = value[:, z * width : (z + 1) * width]

    def put(mobility, target):
        for i in range(COMPS):
            store(mob_ref, mobility[i], target, i)
        store(mob_sum, total_of(mobility), target)

    feeds, some, marks = [], [], []
    for source, _, tile_row, (comp, *_) in rows:
        raw = [beside(comp, source, i) for i in range(COMPS)]
        inverse = rcp(total_of(raw))
        feeds.append([raw[i] * inverse for i in range(COMPS)])
        first, last = flags[layer, 2 * tile_row], flags[layer, 2 * tile_row + 1]
        some.append(first + last > 0)
        marks.append(jnp.where(row_of(raw[0].shape) < ROWS // 2, first, last))

    def flashed(which):
        feed = [jnp.concatenate([feeds[n][i] for n in which], axis=1) for i in range(COMPS)]
        pressure = jnp.concatenate([beside(rows[n][3][1], rows[n][0]) for n in which], axis=1)
        two = flash(feed, pressure, signed, slopes, operand[...])
        marked = jnp.concatenate([marks[n] for n in which], axis=1) > 0
        for m, n in enumerate(which):
            span = slice(m * depth * width, (m + 1) * depth * width)
            put([jnp.where(marked, two[i], feed[i])[:, span] for i in range(COMPS)], rows[n][1])

    @pl.when(some[0] & some[1])
    def _():
        flashed((0, 1))

    for n in range(2):
        @pl.when(some[n] & jnp.logical_not(some[1 - n]))
        def _():
            flashed((n,))

        @pl.when(jnp.logical_not(some[n]))
        def _():
            put(feeds[n], rows[n][1])

    if ready:
        ready()
    for feed, (source, target, _, (_, _, pore, mass)) in zip(feeds, rows):
        volume = beside(pore, source)
        acc = [volume * feed[i] - beside(mass, source, i) for i in range(COMPS)]
        for i in range(COMPS):
            store(acc_ref, acc[i], target, i)
        store(acc_sum, total_of(acc), target)


def edge_cells(
    flags_in, vol_in, slope_in, mix_in, comp, press, pore, mass, tx, ty, tz,
    mob_ref, acc_ref, mob_sum, acc_sum, one_ref, two_ref, operand, comp_i, press_i, pore_i, mass_i,
    flags, vol, slope, mix, comp_s, press_s, pore_s, mass_s, tx_s, ty_s, tz_s, sems, scalar_sems,
):
    depth, rows, _ = press.shape
    fetched = (
        (comp, comp_s), (press, press_s), (pore, pore_s), (mass, mass_s), (tx, tx_s), (ty, ty_s), (tz, tz_s)
    )

    ahead = (comp_i, press_i, pore_i, mass_i)

    def fetch(end, n):
        source, slot = fetched[n]
        at = pl.ds(end * (rows - ROWS), ROWS) if end < 2 else pl.ds(ROWS, rows - 2 * ROWS)
        return pltpu.make_async_copy(
            source.at[:, :, at, :] if len(source.shape) == 4 else source.at[:, at, :],
            slot.at[end] if end < 2 else ahead[n],
            sems.at[end, n],
        )

    scalars = [
        pltpu.make_async_copy(source, slot, scalar_sems.at[n])
        for n, (source, slot) in enumerate(
            ((flags_in, flags), (vol_in, vol), (slope_in, slope), (mix_in, mix))
        )
    ]
    early, late = (0, 1), range(2, len(fetched))
    early, late = (0, 1), range(2, len(fetched))
    for copy in scalars:
        copy.start()
    for end in range(2):
        for n in early:
            fetch(end, n).start()
    for copy in scalars:
        copy.wait()
    operand[...] = mixing_operand(mix)
    for end in range(2):
        for n in early:
            fetch(end, n).wait()
    for end in range(2):
        for n in late:
            fetch(end, n).start()
    for n in range(len(ahead)):
        fetch(2, n).start()

    def ready():
        for end in range(2):
            for n in late:
                fetch(end, n).wait()

    targets = [slice(end * ROWS, (end + 1) * ROWS) for end in range(2)]
    flash_rows(
        [
            (slice(None), targets[end], end * (rows // ROWS - 1), [slot.at[end] for _, slot in fetched[:4]])
            for end in range(2)
        ],
        flags, vol, slope, operand, (mob_ref, acc_ref, mob_sum, acc_sum), ready,
    )
    odd = lax.axis_index("areal") % 2 == 1
    for end in range(2):
        def field(k, z):
            if k < COMPS:
                here = mob_ref[k, z, targets[end]]
            elif k in (MOB, ACC):
                here = (mob_sum if k == MOB else acc_sum)[z, targets[end]]
            else:
                here = {PRESS: press_s, TX: tx_s, TY: ty_s, TZ: tz_s, PORE: pore_s}[k][end, z]
            return here

        for turn, ref in enumerate((one_ref, two_ref)):
            @pl.when(odd == (end == turn))
            def _():
                pack_rows(field, end == 0, ref, depth)

    for n in range(len(ahead)):
        fetch(2, n).wait()


def inner_cells(flags, vol, slope, operand, comp, press, pore, mass, *outs):
    ins = (comp, press, pore, mass)

    def pair(t, carry):
        at = [pl.ds(pl.multiple_of((2 * t + n) * ROWS, ROWS), ROWS) for n in range(2)]
        flash_rows(
            [(at[n], at[n], 2 * t + n + 1, ins) for n in range(2)], flags, vol, slope, operand, outs
        )
        return carry

    lax.fori_loop(0, press.shape[1] // (2 * ROWS), pair, 0)


def by_side(axis, one, two):
    odd = lax.axis_index(axis) % 2 == 1
    return jnp.where(odd, one, two), jnp.where(odd, two, one)


def by_pairs(count, body):
    def pair(t, carry):
        body(2 * t)
        body(2 * t + 1)
        return carry

    lax.fori_loop(0, count // 2, pair, 0)


def near_residual(
    rows_two, rows_one, press, tx, ty, tz, pore,
    edge_mob, edge_acc, edge_mob_sum, edge_acc_sum, mob, acc, mob_sum, acc_sum,
    out_ref, total_ref, diagonal_ref, c_x, c_y, c_z,
    rows_h, fields_h, g_x, g_y, g_z,
):
    depth, rows, width = press.shape
    areal, areals = lax.axis_index("areal"), lax.axis_size("areal")
    tall = rows + ROWS
    full = (tall, width)
    own = slice(0, rows)
    mob, acc, mob_sum, acc_sum = (
        Rows(*both)
        for both in ((edge_mob, mob), (edge_acc, acc), (edge_mob_sum, mob_sum), (edge_acc_sum, acc_sum))
    )
    fields = {MOB: mob_sum, PRESS: press, TX: tx, TY: ty, TZ: tz, PORE: pore, ACC: acc_sum}
    tiles = row_tiles(rows_one, rows_two, range(FIELDS))
    for z in range(depth):
        for i in range(COMPS):
            rows_h[i, z] = tiles[i][z]
        for n, k in enumerate(fields):
            fields_h[n, z] = tiles[k][z]

    end_x = (row_of(full) == rows - 1) & (areal == areals - 1)
    end_y = lane_of(full) == width - 1
    scale = 0.5 * TIME_STEP
    c_z[0] = jnp.zeros(full, jnp.float32)
    g_z[0] = jnp.zeros((rows, width), jnp.float32)

    def update(z):
        m, p, x, y, zz, volume, total = (
            jnp.concatenate([ref[z], fields_h[n, z]], axis=0) for n, ref in enumerate(fields.values())
        )
        up, down = jnp.minimum(z + 1, depth - 1), jnp.maximum(z - 1, 0)
        p_up = jnp.concatenate([press[up], fields_h[1, up]], axis=0)
        p_down = jnp.concatenate([press[down], fields_h[1, down]], axis=0)
        m_up = jnp.concatenate([mob_sum[up], fields_h[0, up]], axis=0)
        strength_x = jnp.where(end_x, 0.0, scale * x)
        strength_y = jnp.where(end_y, 0.0, scale * y)
        strength_z = jnp.where(z < depth - 1, scale, 0.0) * zz
        dx = p - pltpu.roll(p, tall - 1, 0)
        dy = p - pltpu.roll(p, width - 1, 1)
        dz = p - p_up
        cx = strength_x * (m + pltpu.roll(m, tall - 1, 0))
        cy = strength_y * (m + pltpu.roll(m, width - 1, 1))
        cz = strength_z * (m + m_up)
        cz_low = c_z[z]
        gx = strength_x * dx
        g_x[0, z], g_x[1, z] = gx[own], -pltpu.roll(gx, 1, 0)[own]
        g_y[z], g_z[z + 1] = (strength_y * dy)[own], (strength_z * dz)[own]
        c_x[z], c_y[z], c_z[z + 1] = cx, cy, cz
        fx, fy = cx * dx, cy * dy
        total_ref[z] = (
            total
            + (fx - pltpu.roll(fx, 1, 0))
            + (fy - pltpu.roll(fy, 1, 1))
            + (cz * dz + cz_low * (p - p_down))
        )
        diagonal_ref[z] = (
            COMPRESS * volume
            + (cx + pltpu.roll(cx, 1, 0))
            + (cy + pltpu.roll(cy, 1, 1))
            + (cz + cz_low)
        )

    by_pairs(depth, update)

    def residual(z):
        down, up = jnp.maximum(z - 1, 0), jnp.minimum(z + 1, depth - 1)
        gx, gx_low, gy, gz, gz_low = g_x[0, z], g_x[1, z], g_y[z], g_z[z + 1], -g_z[z]
        gy_low = -pltpu.roll(gy, 1, 1)
        middle = (gx + gx_low) + (gy + gy_low) + (gz + gz_low)
        for i in range(COMPS):
            here = mob[i, z]
            tall_here = jnp.concatenate([here, rows_h[i, z]], axis=0)
            out_ref[i, z] = (
                acc[i, z]
                + middle * here
                + gx * pltpu.roll(tall_here, tall - 1, 0)[own]
                + gx_low * pltpu.roll(tall_here, 1, 0)[own]
                + gy * pltpu.roll(here, width - 1, 1)
                + gy_low * pltpu.roll(here, 1, 1)
                + gz * mob[i, up]
                + gz_low * mob[i, down]
            )

    by_pairs(depth, residual)


def finish(
    columns_one, columns_two, packet, press, total_in, diagonal_in, c_x, c_y, c_z, edge_mob, mob, near,
    res_ref, new_ref,
    side_h, edge_h, first, total_ref, inverse_ref, res_s, sems,
):
    depth, rows, width = press.shape
    layer, layers = lax.axis_index("layer"), lax.axis_size("layer")
    areal, areals = lax.axis_index("areal"), lax.axis_size("areal")
    tall = rows + ROWS
    lane = lane_of((tall, LANES))
    at_first, at_last = lane == 0, lane == LANES - 1
    low, high = slice(0, LANES), slice(width - LANES, width)
    FLUX, COUPLE, FACE, NEXT = range(4)
    mob = Rows(edge_mob, mob)

    def edges(which, z):
        both = pltpu.roll(edge_h[which], LANES - 1 - 4 * z, 1)
        return jnp.where(at_first, both, 0.0), jnp.where(at_last, both, 0.0)

    halo = side_fields(columns_one, columns_two)
    here = spread_fields([packet[:, t : t + LANES] for t in range(0, FIELDS * 32, LANES)])
    is_left = lane % 4 == 1
    for i in range(COMPS):
        cells = halo[i][:rows]
        side_h[i] = jnp.where(is_left[:rows], pltpu.roll(cells, LANES - 1, 1), pltpu.roll(cells, 1, 1))
    scale = 0.5 * TIME_STEP

    def turned(x, by):
        return pltpu.roll(x, by % LANES, 1)

    def outer(x):
        return jnp.where(is_left, turned(x, 1), turned(x, -1))

    def inner(x):
        return jnp.where(is_left, turned(x, -1), turned(x, 1))

    m, p = halo[MOB], halo[PRESS]
    strength = scale * halo[TY]
    own_strength = jnp.where(layer < layers - 1, scale, 0.0) * here[TY]
    c_out = jnp.where(is_left, turned(strength, 1), strength) * (m + outer(m))
    s_in = jnp.where(is_left, strength, turned(own_strength, 1))
    c_in = s_in * (m + inner(here[MOB]))
    d_in = p - inner(here[PRESS])
    end_x = (row_of(lane.shape) == rows - 1) & (areal == areals - 1)
    cx = jnp.where(end_x, 0.0, scale * halo[TX]) * (m + pltpu.roll(m, tall - 1, 0))
    cz = jnp.where(lane < 4 * (depth - 1), scale * halo[TZ], 0.0) * (m + turned(m, -4))
    fx = cx * (p - pltpu.roll(p, tall - 1, 0))
    fz = cz * (p - turned(p, -4))
    total = (
        halo[ACC]
        + (c_out * (p - outer(p)) + c_in * d_in)
        + (fx - pltpu.roll(fx, 1, 0))
        + (fz - turned(fz, 4))
    )
    diagonal = (
        COMPRESS * halo[PORE] + (c_out + c_in) + (cx + pltpu.roll(cx, 1, 0)) + (cz + turned(cz, 4))
    )
    usable = diagonal > 0.0
    beside = jnp.where(usable, -total * rcp(jnp.where(usable, diagonal, 1.0)), 0.0)
    for which, value in (
        (FLUX, -c_in * d_in), (COUPLE, c_in), (FACE, -s_in * d_in), (NEXT, c_in * beside)
    ):
        edge_h[which] = jnp.where(is_left, value, turned(value, -2))

    def leave(z):
        return pltpu.make_async_copy(res_s.at[:, z], res_ref.at[:, z], sems.at[z])

    def update(z):
        faces = [face[:rows] for face in edges(FACE, z)]
        for i in range(COMPS):
            side = pltpu.roll(side_h[i], LANES - 2 - 4 * z, 1)
            cells = mob[i, z]
            for span, face in zip((low, high), faces):
                res_s[i, z, :, span] = near[i, z, :, span] + face * (cells[:, span] + side)
        leave(z).start()
        flux, couple = edges(FLUX, z), edges(COUPLE, z)
        for n, span in enumerate((low, high)):
            total = total_in[z, :, span] + flux[n]
            diagonal = diagonal_in[z, :, span] + couple[n]
            usable = diagonal > 0.0
            inverse = rcp(jnp.where(usable, diagonal, 1.0))
            first[z, :, span] = jnp.where(usable, -total * inverse, 0.0)
            total_ref[z, :, span] = total[:rows]
            inverse_ref[z, :, span] = inverse[:rows]

    by_pairs(depth, update)

    def second(z):
        here = first[z]
        up, down = jnp.minimum(z + 1, depth - 1), jnp.maximum(z - 1, 0)
        cx, cy = c_x[z], c_y[z, :rows]
        own = here[:rows]
        gathered = (
            (cx * pltpu.roll(here, tall - 1, 0))[:rows]
            + pltpu.roll(cx * here, 1, 0)[:rows]
            + cy * pltpu.roll(own, width - 1, 1)
            + pltpu.roll(cy * own, 1, 1)
            + (c_z[z + 1, :rows] * first[up, :rows] + c_z[z, :rows] * first[down, :rows])
            - total_ref[z]
        )
        beyond = edges(NEXT, z)
        for n, span in enumerate((low, high)):
            new_ref[z, :, span] = press[z, :, span] + inverse_ref[z, :, span] * (
                gathered[:, span] + beyond[n][:rows]
            )

    by_pairs(depth, second)

    def left(z):
        leave(z).wait()

    by_pairs(depth, left)


def on_device(
    pressure, composition, mass_old, pore_volume, trans_x, trans_y, trans_z,
    volatility, pressure_slope, mixing, two_phase,
):
    depth, rows, width = pressure.shape
    f32 = jnp.float32
    smem = pl.BlockSpec(memory_space=pltpu.SMEM)
    vmem = pl.BlockSpec(memory_space=pltpu.VMEM)
    def params(mib):
        return pltpu.CompilerParams(vmem_limit_bytes=mib * MIB)

    scalars = (two_phase, volatility, pressure_slope, mixing)

    def swapped(block, axis, first):
        count = lax.axis_size(axis)
        pairs = [(i, i + 1) for i in range(first, count - 1, 2)]
        return lax.ppermute(block, axis, pairs + [(j, i) for i, j in pairs])

    whole = jax.ShapeDtypeStruct((COMPS, depth, rows, width), f32)
    sums = jax.ShapeDtypeStruct((depth, rows, width), f32)
    packed = jax.ShapeDtypeStruct((len(UNITS) // 2, DEPTH_SLOTS * depth, width), f32)
    fields = (composition, pressure, pore_volume, mass_old, trans_x, trans_y, trans_z)

    def parts(count):
        planes = jax.ShapeDtypeStruct((COMPS, depth, count, width), f32)
        plane = jax.ShapeDtypeStruct((depth, count, width), f32)
        return [planes, planes, plane, plane]

    between = [jax.ShapeDtypeStruct((*x.shape[:-2], rows - 2 * ROWS, width), f32) for x in fields[:4]]
    *results, operand, comp, press, pore, mass = pl.pallas_call(
        edge_cells,
        in_specs=[pl.BlockSpec(memory_space=pl.ANY)] * (4 + len(fields)),
        out_specs=[vmem] * 11,
        out_shape=parts(2 * ROWS)
        + [packed, packed, jax.ShapeDtypeStruct((PART, DEEP), jnp.bfloat16), *between],
        scratch_shapes=[pltpu.SMEM(x.shape, x.dtype) for x in scalars]
        + [pltpu.VMEM((2, *x.shape[:-2], ROWS, width), f32) for x in fields]
        + [pltpu.SemaphoreType.DMA((3, len(fields))), pltpu.SemaphoreType.DMA((4,))],
        compiler_params=params(24),
        name="edge_cells",
    )(*(pltpu.with_memory_space_constraint(x, pltpu.HBM) for x in (*scalars, *fields)))
    *edge, one, two = results
    rows_two = swapped(two, "areal", 1)
    rows_one = swapped(one, "areal", 0)
    cells = rows * depth * width
    inner = pl.pallas_call(
        inner_cells,
        in_specs=[smem] * 3 + [vmem] * 5,
        out_specs=[vmem] * 4,
        out_shape=parts(rows - 2 * ROWS),
        compiler_params=params(24),
        cost_estimate=pl.CostEstimate(
            flops=450 * cells, transcendentals=95 * cells, bytes_accessed=2 * 39 * cells
        ),
        name="inner_cells",
    )(*scalars[:3], operand, comp, press, pore, mass)
    planes_of = (pressure, trans_x, trans_y, trans_z, pore_volume)

    narrow = jax.ShapeDtypeStruct((rows + ROWS, FIELDS * 16), f32)
    one, two, packet = pl.pallas_call(
        pack_columns,
        in_specs=[vmem] * 15,
        out_specs=[vmem] * 3,
        out_shape=[narrow, narrow, jax.ShapeDtypeStruct((rows + ROWS, FIELDS * 32), f32)],
        compiler_params=params(24),
        name="pack_columns",
    )(rows_two, rows_one, *planes_of, *edge, *inner)
    columns_one = swapped(one, "layer", 0)
    columns_two = swapped(two, "layer", 1)

    tall = jax.ShapeDtypeStruct((depth, rows + ROWS, width), f32)
    above_faces = jax.ShapeDtypeStruct((depth + 1, rows + ROWS, width), f32)
    near, *sweep = pl.pallas_call(
        near_residual,
        in_specs=[vmem] * 15,
        out_specs=[vmem] * 6,
        out_shape=[whole, tall, tall, tall, tall, above_faces],
        scratch_shapes=[
            pltpu.VMEM((COMPS, depth, ROWS, width), f32),
            pltpu.VMEM((FIELDS - COMPS, depth, ROWS, width), f32),
            pltpu.VMEM((2, depth, rows, width), f32),
            pltpu.VMEM((depth, rows, width), f32),
            pltpu.VMEM((depth + 1, rows, width), f32),
        ],
        compiler_params=params(24),
        cost_estimate=pl.CostEstimate(flops=150 * cells, transcendentals=0, bytes_accessed=4 * 31 * cells),
        name="near_residual",
    )(rows_two, rows_one, *planes_of, *edge, *inner)

    return pl.pallas_call(
        finish,
        in_specs=[vmem] * 12,
        out_specs=[pl.BlockSpec(memory_space=pl.ANY), vmem],
        out_shape=[whole, sums],
        scratch_shapes=[
            pltpu.VMEM((COMPS, rows, LANES), f32),
            pltpu.VMEM((4, rows + ROWS, LANES), f32),
            pltpu.VMEM((depth, rows + ROWS, width), f32),
            pltpu.VMEM((depth, rows, width), f32),
            pltpu.VMEM((depth, rows, width), f32),
            pltpu.VMEM((COMPS, depth, rows, width), f32),
            pltpu.SemaphoreType.DMA((depth,)),
        ],
        compiler_params=params(24),
        name="finish",
    )(columns_one, columns_two, packet, pressure, *sweep, edge[0], inner[0], near)


def solution(mesh):
    placed = (
        P(None, "areal", "layer"),
        P(None, None, "areal", "layer"),
        P(None, None, "areal", "layer"),
        P(None, "areal", "layer"),
        P(None, "areal", "layer"),
        P(None, "areal", "layer"),
        P(None, "areal", "layer"),
        P(),
        P(),
        P(),
        P(None, "areal"),
    )
    return jax.shard_map(
        on_device,
        mesh=mesh,
        in_specs=placed,
        out_specs=(P(None, None, "areal", "layer"), P(None, "areal", "layer")),
        check_vma=False,
    )
```

```python
import jax
import jax.numpy as jnp
from jax import lax
from jax.experimental import pallas as pl
from jax.experimental.pallas import tpu as pltpu
from jax.sharding import PartitionSpec as P

SS_ITERS = 3
RR_ITERS = 3
LIGHT = 4
COMPS = 9
FIELDS = 16
MOB, PRESS, TX, TY, TZ, PORE, ACC = range(COMPS, FIELDS)
UNITS = (MOB, PRESS, TX, (0, 1), (2, 3), (4, 5), (6, 7), (8, TY), (TZ, PORE), (ACC, ACC))
DEPTH_SLOTS = 4
TIME_STEP = 4.0
COMPRESS = 0.2
VAPOUR_WEIGHT = 1.0 / 0.25
LANES = 128
ROWS = 8
MIB = 1024 * 1024
PART = (COMPS + 1) * ROWS
DEEP = 256


def rcp(x):
    return pltpu.reciprocal(x, approx=True)


def total_of(terms):
    terms = list(terms)
    while len(terms) > 1:
        terms = [a + b for a, b in zip(terms[::2], terms[1::2])] + (
            [terms[-1]] if len(terms) % 2 else []
        )
    return terms[0]


def split(x):
    high = x.astype(jnp.bfloat16)
    return high, (x - high.astype(jnp.float32)).astype(jnp.bfloat16)


def mixing_operand(mix_ref):
    shape = (ROWS, DEEP)
    lane, row = lane_of(shape), row_of(shape)
    part = lax.div(lane, PART)
    within = lane - PART * part
    column = lax.div(within, ROWS)
    on = (within - ROWS * column == row) & (part < 3)
    blocks = []
    for i in range(COMPS):
        value = jnp.zeros(shape, jnp.float32)
        for j in range(COMPS):
            value = jnp.where(column == j, 2.0 * mix_ref[i, j], value)
        high, low = split(value)
        value = jnp.where(part == 2, low.astype(jnp.float32), high.astype(jnp.float32))
        blocks.append(jnp.where(on, value, 0.0))
    blocks.append(jnp.zeros(shape, jnp.float32))
    return jnp.concatenate(blocks, axis=0).astype(jnp.bfloat16)


def mixed(operand, spread):
    shape = spread[0].shape
    high, low = split(jnp.concatenate(spread + [jnp.zeros(shape, jnp.float32)], axis=0))
    tail = jnp.zeros((DEEP - 3 * PART, shape[1]), jnp.bfloat16)
    out = jnp.dot(
        operand,
        jnp.concatenate([high, low, high, tail], axis=0),
        preferred_element_type=jnp.float32,
    )
    return [out[ROWS * i : ROWS * (i + 1)] for i in range(COMPS)]


def flash(feed, pressure, signed, slope, operand):
    log_press = jnp.log(pressure)
    half_base = [0.5 * signed[i] - (0.5 * slope[i]) * log_press for i in range(COMPS)]
    spread = None
    for outer in range(SS_ITERS):
        if outer == 0:
            half_log = half_base
        else:
            mix = mixed(operand, spread)
            half_log = [half_base[i] - 0.5 * jnp.tanh(mix[i]) for i in range(COMPS)]
        t = [jnp.tanh(half_log[i]) for i in range(COMPS)]
        u = [rcp(t[i]) for i in range(COMPS)]
        psi = None
        for inner in range(RR_ITERS):
            q = t if inner == 0 else [rcp(u[i] + psi) for i in range(COMPS)]
            part = [feed[i] * q[i] for i in range(COMPS)]
            step = total_of(part) * rcp(total_of(part[i] * q[i] for i in range(COMPS)))
            psi = jnp.clip(step if inner == 0 else psi + step, -1.0, 1.0)
        spread = [feed[i] * rcp(u[i] + psi) for i in range(COMPS)]
    liquid_part = (0.25 * (1.0 - psi)) * (1.0 - psi)
    vapour_part = (0.25 * VAPOUR_WEIGHT * (1.0 + psi)) * (1.0 + psi)
    both, apart = vapour_part + liquid_part, vapour_part - liquid_part
    return [spread[i] * (both * u[i] + apart) for i in range(COMPS)]


def parameters(vol_ref, slope_ref):
    signed = [vol_ref[i] if i < LIGHT else -vol_ref[i] for i in range(COMPS)]
    return signed, [slope_ref[i] for i in range(COMPS)]


def lane_of(shape):
    return lax.broadcasted_iota(jnp.int32, shape, len(shape) - 1)


def row_of(shape):
    return lax.broadcasted_iota(jnp.int32, shape, len(shape) - 2)


class Rows:
    def __init__(self, edge, inner):
        self.edge, self.inner = edge, inner

    def __getitem__(self, at):
        at = at if isinstance(at, tuple) else (at,)
        edge = self.edge[at]
        return jnp.concatenate([edge[:ROWS], self.inner[at], edge[ROWS:]], axis=0)


def pack_rows(field, low, out_ref, depth):
    row = None
    for n in range(0, len(UNITS), 2):
        for pair in range(depth // 2):
            tile = None
            for z in (2 * pair, 2 * pair + 1):
                order = (1, 0) if low else (0, 1)
                for which in order:
                    unit = UNITS[n + which]
                    at = 4 * (z % 2) + (2 if low == (which == 0) else 0)
                    first = 0 if low else ROWS - 1
                    if isinstance(unit, tuple):
                        a, b = unit
                        pieces = [(at, a, at - first), (at + 1, b, at + 1 - first)]
                        if not low:
                            pieces = [(at, b, at - first), (at + 1, a, at + 1 - first)]
                    else:
                        pieces = [(at, unit, at if low else at + 2)]
                    for start, k, turn in pieces:
                        here = field(k, z)
                        if row is None:
                            row = row_of(here.shape)
                        if turn % ROWS:
                            here = pltpu.roll(here, turn % ROWS, 0)
                        tile = here if tile is None else jnp.where(row < start, tile, here)
            out_ref[n // 2, pl.ds(pair * ROWS, ROWS), :] = tile


def row_tiles(one, two, wanted, start=0, stop=None):
    shape = one.shape[1:]
    upper = row_of(shape) % DEPTH_SLOTS < 2
    tile_row = row_of((ROWS, shape[1]))
    stop = stop or shape[0] // DEPTH_SLOTS
    tiles = {}
    for n, unit in enumerate(UNITS):
        fields = unit if isinstance(unit, tuple) else (unit,)
        if not any(k in wanted for k in fields):
            continue
        up, down = by_side("areal", one[n // 2], two[n // 2])
        if n % 2:
            up, down = pltpu.roll(up, shape[0] - 2, 0), pltpu.roll(down, 2, 0)
        both = jnp.where(upper, up, down)
        for z in range(start, stop):
            at = (z // 2) * ROWS
            tile = pltpu.roll(both[at : at + ROWS], 6 - 4 * (z % 2), 0)
            if fields[0] in wanted:
                tiles.setdefault(fields[0], []).append(tile)
            if fields[-1] in wanted and fields[-1] != fields[0]:
                other = jnp.where(tile_row < 4, pltpu.roll(tile, ROWS - 1, 0), pltpu.roll(tile, 1, 0))
                tiles.setdefault(fields[-1], []).append(other)
    return tiles


def pack_columns(rows_two, rows_one, *refs):
    (
        press, tx, ty, tz, pore, edge_mob, _, edge_mob_sum, edge_acc_sum, mob, _, mob_sum, acc_sum,
        one_ref, two_ref, own_ref,
    ) = refs
    depth, rows, width = press.shape
    shape = (rows + ROWS, LANES)
    lane = lane_of(shape)
    mob, mob_sum, acc_sum = (
        Rows(*both) for both in ((edge_mob, mob), (edge_mob_sum, mob_sum), (edge_acc_sum, acc_sum))
    )
    corner_fields = {MOB: mob_sum, PRESS: press, TX: tx, TY: ty}
    others = {TZ: tz, PORE: pore, ACC: acc_sum, **corner_fields}
    corners = row_tiles(rows_one, rows_two, corner_fields)
    nothing = jnp.zeros((ROWS, LANES), jnp.float32)
    for tile in range(FIELDS // 4):
        packed = jnp.zeros(shape, jnp.float32)
        for quarter in range(4):
            k = 4 * tile + quarter
            for z in range(depth):
                plane = mob[k, z] if k < COMPS else others[k][z]
                first, last = plane[:, :LANES], plane[:, -LANES:]
                at = 32 * quarter + 4 * z
                both = jnp.where(lane_of(first.shape) < LANES // 2, first, last)
                if k < COMPS:
                    both = pltpu.roll(both, at + 2, 1)
                    on = (lane_of(first.shape) >= at + 1) & (lane_of(first.shape) < at + 3)
                    packed = jnp.concatenate([jnp.where(on, both, packed[:rows]), nothing], axis=0)
                    continue
                end = nothing
                if k in corner_fields:
                    end = corners[k][z]
                    end = jnp.where(lane_of(end[:, :LANES].shape) < LANES // 2, end[:, :LANES], end[:, -LANES:])
                both = pltpu.roll(jnp.concatenate([both, end], axis=0), (at + 2) % LANES, 1)
                packed = jnp.where((lane >= at) & (lane < at + 4), both, packed)
        own_ref[:, tile * LANES : (tile + 1) * LANES] = packed
    odd = lax.axis_index("layer") % 2 == 1
    half = FIELDS // 8
    for n in range(half):
        near, far = (own_ref[:, t * LANES : (t + 1) * LANES] for t in (n, n + half))
        upward = jnp.where(lane % 4 < 2, near, pltpu.roll(far, 2, 1))
        downward = jnp.where(lane % 4 < 2, pltpu.roll(near, LANES - 2, 1), far)
        one_ref[:, n * LANES : (n + 1) * LANES] = jnp.where(odd, downward, upward)
        two_ref[:, n * LANES : (n + 1) * LANES] = jnp.where(odd, upward, downward)


def spread_fields(tiles):
    fields = []
    for tile in tiles:
        for quarter in range(4):
            turn = (LANES - 32 * quarter) % LANES
            fields.append(pltpu.roll(tile, turn, 1) if turn else tile)
    return fields


def side_fields(one, two):
    lane = lane_of((one.shape[0], LANES))
    near, far = [], []
    for n in range(FIELDS // 8):
        span = slice(n * LANES, (n + 1) * LANES)
        left, right = by_side("layer", one[:, span], two[:, span])
        near.append(jnp.where(lane % 4 < 2, left, pltpu.roll(right, 2, 1)))
        far.append(jnp.where(lane % 4 < 2, pltpu.roll(left, LANES - 2, 1), right))
    return spread_fields(near + far)


def flash_rows(source, target, tile_row, flags, vol, slope, operand, comp, press, pore, mass, outs, ready=None):
    mob_ref, acc_ref, mob_sum, acc_sum = outs
    layer = lax.axis_index("layer")
    depth, _, width = press.shape

    def beside(ref, *lead):
        return jnp.concatenate([ref[(*lead, z, source)] for z in range(depth)], axis=1)

    def store(ref, value, *lead):
        for z in range(depth):
            ref[(*lead, z, target)] = value[:, z * width : (z + 1) * width]

    raw = [beside(comp, i) for i in range(COMPS)]
    inverse = rcp(total_of(raw))
    feed = [raw[i] * inverse for i in range(COMPS)]
    first, last = flags[layer, 2 * tile_row], flags[layer, 2 * tile_row + 1]

    @pl.when(first + last > 0)
    def _():
        signed, slopes = parameters(vol, slope)
        two = flash(feed, beside(press), signed, slopes, operand[...])
        marked = jnp.where(row_of(feed[0].shape) < ROWS // 2, first, last) > 0
        mobility = [jnp.where(marked, two[i], feed[i]) for i in range(COMPS)]
        for i in range(COMPS):
            store(mob_ref, mobility[i], i)
        store(mob_sum, total_of(mobility))

    @pl.when(first + last == 0)
    def _():
        for i in range(COMPS):
            store(mob_ref, feed[i], i)
        store(mob_sum, total_of(feed))

    if ready:
        ready()
    volume = beside(pore)
    acc = [volume * feed[i] - beside(mass, i) for i in range(COMPS)]
    for i in range(COMPS):
        store(acc_ref, acc[i], i)
    store(acc_sum, total_of(acc))


def edge_cells(
    flags_in, vol_in, slope_in, mix_in, comp, press, pore, mass, tx, ty, tz,
    mob_ref, acc_ref, mob_sum, acc_sum, one_ref, two_ref, operand, comp_i, press_i, pore_i, mass_i,
    flags, vol, slope, mix, comp_s, press_s, pore_s, mass_s, tx_s, ty_s, tz_s, sems, scalar_sems,
):
    depth, rows, _ = press.shape
    fetched = (
        (comp, comp_s), (press, press_s), (pore, pore_s), (mass, mass_s), (tx, tx_s), (ty, ty_s), (tz, tz_s)
    )

    ahead = (comp_i, press_i, pore_i, mass_i)

    def fetch(end, n):
        source, slot = fetched[n]
        at = pl.ds(end * (rows - ROWS), ROWS) if end < 2 else pl.ds(ROWS, rows - 2 * ROWS)
        return pltpu.make_async_copy(
            source.at[:, :, at, :] if len(source.shape) == 4 else source.at[:, at, :],
            slot.at[end] if end < 2 else ahead[n],
            sems.at[end, n],
        )

    scalars = [
        pltpu.make_async_copy(source, slot, scalar_sems.at[n])
        for n, (source, slot) in enumerate(
            ((flags_in, flags), (vol_in, vol), (slope_in, slope), (mix_in, mix))
        )
    ]
    early, late = (0, 1), range(2, len(fetched))
    for copy in scalars:
        copy.start()
    for n in early:
        fetch(0, n).start()
    for copy in scalars:
        copy.wait()
    operand[...] = mixing_operand(mix)
    odd = lax.axis_index("areal") % 2 == 1
    for end in range(2):
        for n in early:
            fetch(end, n).wait()
        if end == 0:
            for n in late:
                fetch(0, n).start()
            for n in range(len(fetched)):
                fetch(1, n).start()
        else:
            for n in range(len(ahead)):
                fetch(2, n).start()

        def ready():
            for n in late:
                fetch(end, n).wait()

        target = slice(end * ROWS, (end + 1) * ROWS)
        flash_rows(
            slice(None), target, end * (rows // ROWS - 1), flags, vol, slope, operand,
            *(slot.at[end] for _, slot in fetched[:4]), (mob_ref, acc_ref, mob_sum, acc_sum), ready,
        )

        def field(k, z):
            if k < COMPS:
                here = mob_ref[k, z, target]
            elif k in (MOB, ACC):
                here = (mob_sum if k == MOB else acc_sum)[z, target]
            else:
                here = {PRESS: press_s, TX: tx_s, TY: ty_s, TZ: tz_s, PORE: pore_s}[k][end, z]
            return here

        for turn, ref in enumerate((one_ref, two_ref)):
            @pl.when(odd == (end == turn))
            def _():
                pack_rows(field, end == 0, ref, depth)

    for n in range(len(ahead)):
        fetch(2, n).wait()


def inner_cells(flags, vol, slope, operand, comp, press, pore, mass, *outs):
    def tile(t, carry):
        at = pl.ds(pl.multiple_of(t * ROWS, ROWS), ROWS)
        flash_rows(at, at, t + 1, flags, vol, slope, operand, comp, press, pore, mass, outs)
        return carry

    lax.fori_loop(0, press.shape[1] // ROWS, tile, 0)


def by_side(axis, one, two):
    odd = lax.axis_index(axis) % 2 == 1
    return jnp.where(odd, one, two), jnp.where(odd, two, one)


def by_pairs(count, body):
    def pair(t, carry):
        body(2 * t)
        body(2 * t + 1)
        return carry

    lax.fori_loop(0, count // 2, pair, 0)


def near_residual(
    rows_two, rows_one, press, tx, ty, tz, pore,
    edge_mob, edge_acc, edge_mob_sum, edge_acc_sum, mob, acc, mob_sum, acc_sum,
    out_ref, total_ref, diagonal_ref, c_x, c_y, c_z,
    rows_h, fields_h, g_x, g_y, g_z,
):
    depth, rows, width = press.shape
    areal, areals = lax.axis_index("areal"), lax.axis_size("areal")
    tall = rows + ROWS
    full = (tall, width)
    own = slice(0, rows)
    mob, acc, mob_sum, acc_sum = (
        Rows(*both)
        for both in ((edge_mob, mob), (edge_acc, acc), (edge_mob_sum, mob_sum), (edge_acc_sum, acc_sum))
    )
    fields = {MOB: mob_sum, PRESS: press, TX: tx, TY: ty, TZ: tz, PORE: pore, ACC: acc_sum}
    tiles = row_tiles(rows_one, rows_two, range(FIELDS))
    for z in range(depth):
        for i in range(COMPS):
            rows_h[i, z] = tiles[i][z]
        for n, k in enumerate(fields):
            fields_h[n, z] = tiles[k][z]

    end_x = (row_of(full) == rows - 1) & (areal == areals - 1)
    end_y = lane_of(full) == width - 1
    scale = 0.5 * TIME_STEP
    c_z[0] = jnp.zeros(full, jnp.float32)
    g_z[0] = jnp.zeros((rows, width), jnp.float32)

    def update(z):
        m, p, x, y, zz, volume, total = (
            jnp.concatenate([ref[z], fields_h[n, z]], axis=0) for n, ref in enumerate(fields.values())
        )
        up, down = jnp.minimum(z + 1, depth - 1), jnp.maximum(z - 1, 0)
        p_up = jnp.concatenate([press[up], fields_h[1, up]], axis=0)
        p_down = jnp.concatenate([press[down], fields_h[1, down]], axis=0)
        m_up = jnp.concatenate([mob_sum[up], fields_h[0, up]], axis=0)
        strength_x = jnp.where(end_x, 0.0, scale * x)
        strength_y = jnp.where(end_y, 0.0, scale * y)
        strength_z = jnp.where(z < depth - 1, scale, 0.0) * zz
        dx = p - pltpu.roll(p, tall - 1, 0)
        dy = p - pltpu.roll(p, width - 1, 1)
        dz = p - p_up
        cx = strength_x * (m + pltpu.roll(m, tall - 1, 0))
        cy = strength_y * (m + pltpu.roll(m, width - 1, 1))
        cz = strength_z * (m + m_up)
        cz_low = c_z[z]
        gx = strength_x * dx
        g_x[0, z], g_x[1, z] = gx[own], -pltpu.roll(gx, 1, 0)[own]
        g_y[z], g_z[z + 1] = (strength_y * dy)[own], (strength_z * dz)[own]
        c_x[z], c_y[z], c_z[z + 1] = cx, cy, cz
        fx, fy = cx * dx, cy * dy
        total_ref[z] = (
            total
            + (fx - pltpu.roll(fx, 1, 0))
            + (fy - pltpu.roll(fy, 1, 1))
            + (cz * dz + cz_low * (p - p_down))
        )
        diagonal_ref[z] = (
            COMPRESS * volume
            + (cx + pltpu.roll(cx, 1, 0))
            + (cy + pltpu.roll(cy, 1, 1))
            + (cz + cz_low)
        )

    by_pairs(depth, update)

    def residual(z):
        down, up = jnp.maximum(z - 1, 0), jnp.minimum(z + 1, depth - 1)
        gx, gx_low, gy, gz, gz_low = g_x[0, z], g_x[1, z], g_y[z], g_z[z + 1], -g_z[z]
        gy_low = -pltpu.roll(gy, 1, 1)
        middle = (gx + gx_low) + (gy + gy_low) + (gz + gz_low)
        for i in range(COMPS):
            here = mob[i, z]
            tall_here = jnp.concatenate([here, rows_h[i, z]], axis=0)
            out_ref[i, z] = (
                acc[i, z]
                + middle * here
                + gx * pltpu.roll(tall_here, tall - 1, 0)[own]
                + gx_low * pltpu.roll(tall_here, 1, 0)[own]
                + gy * pltpu.roll(here, width - 1, 1)
                + gy_low * pltpu.roll(here, 1, 1)
                + gz * mob[i, up]
                + gz_low * mob[i, down]
            )

    by_pairs(depth, residual)


def finish(
    columns_one, columns_two, packet, press, total_in, diagonal_in, c_x, c_y, c_z, edge_mob, mob, near,
    res_ref, new_ref,
    side_h, edge_h, first, total_ref, inverse_ref, res_s, new_s, sems,
):
    depth, rows, width = press.shape
    layer, layers = lax.axis_index("layer"), lax.axis_size("layer")
    areal, areals = lax.axis_index("areal"), lax.axis_size("areal")
    tall = rows + ROWS
    lane = lane_of((tall, LANES))
    at_first, at_last = lane == 0, lane == LANES - 1
    low, high = slice(0, LANES), slice(width - LANES, width)
    FLUX, COUPLE, FACE, NEXT = range(4)
    mob = Rows(edge_mob, mob)

    def edges(which, z):
        both = pltpu.roll(edge_h[which], LANES - 1 - 4 * z, 1)
        return jnp.where(at_first, both, 0.0), jnp.where(at_last, both, 0.0)

    halo = side_fields(columns_one, columns_two)
    here = spread_fields([packet[:, t : t + LANES] for t in range(0, FIELDS * 32, LANES)])
    is_left = lane % 4 == 1
    for i in range(COMPS):
        cells = halo[i][:rows]
        side_h[i] = jnp.where(is_left[:rows], pltpu.roll(cells, LANES - 1, 1), pltpu.roll(cells, 1, 1))
    scale = 0.5 * TIME_STEP

    def turned(x, by):
        return pltpu.roll(x, by % LANES, 1)

    def outer(x):
        return jnp.where(is_left, turned(x, 1), turned(x, -1))

    def inner(x):
        return jnp.where(is_left, turned(x, -1), turned(x, 1))

    m, p = halo[MOB], halo[PRESS]
    strength = scale * halo[TY]
    own_strength = jnp.where(layer < layers - 1, scale, 0.0) * here[TY]
    c_out = jnp.where(is_left, turned(strength, 1), strength) * (m + outer(m))
    s_in = jnp.where(is_left, strength, turned(own_strength, 1))
    c_in = s_in * (m + inner(here[MOB]))
    d_in = p - inner(here[PRESS])
    end_x = (row_of(lane.shape) == rows - 1) & (areal == areals - 1)
    cx = jnp.where(end_x, 0.0, scale * halo[TX]) * (m + pltpu.roll(m, tall - 1, 0))
    cz = jnp.where(lane < 4 * (depth - 1), scale * halo[TZ], 0.0) * (m + turned(m, -4))
    fx = cx * (p - pltpu.roll(p, tall - 1, 0))
    fz = cz * (p - turned(p, -4))
    total = (
        halo[ACC]
        + (c_out * (p - outer(p)) + c_in * d_in)
        + (fx - pltpu.roll(fx, 1, 0))
        + (fz - turned(fz, 4))
    )
    diagonal = (
        COMPRESS * halo[PORE] + (c_out + c_in) + (cx + pltpu.roll(cx, 1, 0)) + (cz + turned(cz, 4))
    )
    usable = diagonal > 0.0
    beside = jnp.where(usable, -total * rcp(jnp.where(usable, diagonal, 1.0)), 0.0)
    for which, value in (
        (FLUX, -c_in * d_in), (COUPLE, c_in), (FACE, -s_in * d_in), (NEXT, c_in * beside)
    ):
        edge_h[which] = jnp.where(is_left, value, turned(value, -2))

    def leave(z):
        return pltpu.make_async_copy(res_s.at[:, z], res_ref.at[:, z], sems.at[0, z])

    def leave_new(z):
        return pltpu.make_async_copy(new_s.at[z], new_ref.at[z], sems.at[1, z])

    def update(z):
        faces = [face[:rows] for face in edges(FACE, z)]
        for i in range(COMPS):
            side = pltpu.roll(side_h[i], LANES - 2 - 4 * z, 1)
            cells = mob[i, z]
            for span, face in zip((low, high), faces):
                res_s[i, z, :, span] = near[i, z, :, span] + face * (cells[:, span] + side)
        leave(z).start()
        flux, couple = edges(FLUX, z), edges(COUPLE, z)
        for n, span in enumerate((low, high)):
            total = total_in[z, :, span] + flux[n]
            diagonal = diagonal_in[z, :, span] + couple[n]
            usable = diagonal > 0.0
            inverse = rcp(jnp.where(usable, diagonal, 1.0))
            first[z, :, span] = jnp.where(usable, -total * inverse, 0.0)
            total_ref[z, :, span] = total[:rows]
            inverse_ref[z, :, span] = inverse[:rows]

    by_pairs(depth, update)

    def second(z):
        here = first[z]
        up, down = jnp.minimum(z + 1, depth - 1), jnp.maximum(z - 1, 0)
        cx, cy = c_x[z], c_y[z, :rows]
        own = here[:rows]
        gathered = (
            (cx * pltpu.roll(here, tall - 1, 0))[:rows]
            + pltpu.roll(cx * here, 1, 0)[:rows]
            + cy * pltpu.roll(own, width - 1, 1)
            + pltpu.roll(cy * own, 1, 1)
            + (c_z[z + 1, :rows] * first[up, :rows] + c_z[z, :rows] * first[down, :rows])
            - total_ref[z]
        )
        beyond = edges(NEXT, z)
        for n, span in enumerate((low, high)):
            new_s[z, :, span] = press[z, :, span] + inverse_ref[z, :, span] * (
                gathered[:, span] + beyond[n][:rows]
            )
        leave_new(z).start()

    by_pairs(depth, second)

    def left(z):
        leave(z).wait()
        leave_new(z).wait()

    by_pairs(depth, left)


def on_device(
    pressure, composition, mass_old, pore_volume, trans_x, trans_y, trans_z,
    volatility, pressure_slope, mixing, two_phase,
):
    depth, rows, width = pressure.shape
    f32 = jnp.float32
    smem = pl.BlockSpec(memory_space=pltpu.SMEM)
    vmem = pl.BlockSpec(memory_space=pltpu.VMEM)
    def params(mib):
        return pltpu.CompilerParams(vmem_limit_bytes=mib * MIB)

    scalars = (two_phase, volatility, pressure_slope, mixing)

    def swapped(block, axis, first):
        count = lax.axis_size(axis)
        pairs = [(i, i + 1) for i in range(first, count - 1, 2)]
        return lax.ppermute(block, axis, pairs + [(j, i) for i, j in pairs])

    whole = jax.ShapeDtypeStruct((COMPS, depth, rows, width), f32)
    sums = jax.ShapeDtypeStruct((depth, rows, width), f32)
    packed = jax.ShapeDtypeStruct((len(UNITS) // 2, DEPTH_SLOTS * depth, width), f32)
    fields = (composition, pressure, pore_volume, mass_old, trans_x, trans_y, trans_z)

    def parts(count):
        planes = jax.ShapeDtypeStruct((COMPS, depth, count, width), f32)
        plane = jax.ShapeDtypeStruct((depth, count, width), f32)
        return [planes, planes, plane, plane]

    between = [jax.ShapeDtypeStruct((*x.shape[:-2], rows - 2 * ROWS, width), f32) for x in fields[:4]]
    *results, operand, comp, press, pore, mass = pl.pallas_call(
        edge_cells,
        in_specs=[pl.BlockSpec(memory_space=pl.ANY)] * (4 + len(fields)),
        out_specs=[vmem] * 11,
        out_shape=parts(2 * ROWS)
        + [packed, packed, jax.ShapeDtypeStruct((PART, DEEP), jnp.bfloat16), *between],
        scratch_shapes=[pltpu.SMEM(x.shape, x.dtype) for x in scalars]
        + [pltpu.VMEM((2, *x.shape[:-2], ROWS, width), f32) for x in fields]
        + [pltpu.SemaphoreType.DMA((3, len(fields))), pltpu.SemaphoreType.DMA((4,))],
        compiler_params=params(24),
        name="edge_cells",
    )(*(pltpu.with_memory_space_constraint(x, pltpu.HBM) for x in (*scalars, *fields)))
    *edge, one, two = results
    rows_two = swapped(two, "areal", 1)
    rows_one = swapped(one, "areal", 0)
    cells = rows * depth * width
    inner = pl.pallas_call(
        inner_cells,
        in_specs=[smem] * 3 + [vmem] * 5,
        out_specs=[vmem] * 4,
        out_shape=parts(rows - 2 * ROWS),
        compiler_params=params(24),
        cost_estimate=pl.CostEstimate(
            flops=450 * cells, transcendentals=95 * cells, bytes_accessed=2 * 39 * cells
        ),
        name="inner_cells",
    )(*scalars[:3], operand, comp, press, pore, mass)
    planes_of = (pressure, trans_x, trans_y, trans_z, pore_volume)

    narrow = jax.ShapeDtypeStruct((rows + ROWS, FIELDS * 16), f32)
    one, two, packet = pl.pallas_call(
        pack_columns,
        in_specs=[vmem] * 15,
        out_specs=[vmem] * 3,
        out_shape=[narrow, narrow, jax.ShapeDtypeStruct((rows + ROWS, FIELDS * 32), f32)],
        compiler_params=params(24),
        name="pack_columns",
    )(rows_two, rows_one, *planes_of, *edge, *inner)
    columns_one = swapped(one, "layer", 0)
    columns_two = swapped(two, "layer", 1)

    tall = jax.ShapeDtypeStruct((depth, rows + ROWS, width), f32)
    above_faces = jax.ShapeDtypeStruct((depth + 1, rows + ROWS, width), f32)
    near, *sweep = pl.pallas_call(
        near_residual,
        in_specs=[vmem] * 15,
        out_specs=[vmem] * 6,
        out_shape=[whole, tall, tall, tall, tall, above_faces],
        scratch_shapes=[
            pltpu.VMEM((COMPS, depth, ROWS, width), f32),
            pltpu.VMEM((FIELDS - COMPS, depth, ROWS, width), f32),
            pltpu.VMEM((2, depth, rows, width), f32),
            pltpu.VMEM((depth, rows, width), f32),
            pltpu.VMEM((depth + 1, rows, width), f32),
        ],
        compiler_params=params(24),
        cost_estimate=pl.CostEstimate(flops=150 * cells, transcendentals=0, bytes_accessed=4 * 31 * cells),
        name="near_residual",
    )(rows_two, rows_one, *planes_of, *edge, *inner)

    return pl.pallas_call(
        finish,
        in_specs=[vmem] * 12,
        out_specs=[pl.BlockSpec(memory_space=pl.ANY)] * 2,
        out_shape=[whole, sums],
        scratch_shapes=[
            pltpu.VMEM((COMPS, rows, LANES), f32),
            pltpu.VMEM((4, rows + ROWS, LANES), f32),
            pltpu.VMEM((depth, rows + ROWS, width), f32),
            pltpu.VMEM((depth, rows, width), f32),
            pltpu.VMEM((depth, rows, width), f32),
            pltpu.VMEM((COMPS, depth, rows, width), f32),
            pltpu.VMEM((depth, rows, width), f32),
            pltpu.SemaphoreType.DMA((2, depth)),
        ],
        compiler_params=params(24),
        name="finish",
    )(columns_one, columns_two, packet, pressure, *sweep, edge[0], inner[0], near)


def solution(mesh):
    placed = (
        P(None, "areal", "layer"),
        P(None, None, "areal", "layer"),
        P(None, None, "areal", "layer"),
        P(None, "areal", "layer"),
        P(None, "areal", "layer"),
        P(None, "areal", "layer"),
        P(None, "areal", "layer"),
        P(),
        P(),
        P(),
        P(None, "areal"),
    )
    return jax.shard_map(
        on_device,
        mesh=mesh,
        in_specs=placed,
        out_specs=(P(None, None, "areal", "layer"), P(None, "areal", "layer")),
        check_vma=False,
    )
```

```python
import jax
import jax.numpy as jnp
from jax import lax
from jax.experimental import pallas as pl
from jax.experimental.pallas import tpu as pltpu
from jax.sharding import PartitionSpec as P

SS_ITERS = 3
RR_ITERS = 3
LIGHT = 4
COMPS = 9
FIELDS = 16
MOB, PRESS, TX, TY, TZ, PORE, ACC = range(COMPS, FIELDS)
UNITS = ((0, 1), (2, 3), (4, 5), (6, 7), (8, MOB), (PRESS, TX), (TY, TZ), (PORE, ACC))
DEPTH_SLOTS = 4
TIME_STEP = 4.0
COMPRESS = 0.2
VAPOUR_WEIGHT = 1.0 / 0.25
LANES = 128
ROWS = 8
MIB = 1024 * 1024
PART = (COMPS + 1) * ROWS
DEEP = 256


def rcp(x):
    return pltpu.reciprocal(x, approx=True)


def total_of(terms):
    terms = list(terms)
    while len(terms) > 1:
        terms = [a + b for a, b in zip(terms[::2], terms[1::2])] + (
            [terms[-1]] if len(terms) % 2 else []
        )
    return terms[0]


def split(x):
    high = x.astype(jnp.bfloat16)
    return high, (x - high.astype(jnp.float32)).astype(jnp.bfloat16)


def mixing_operand(mix_ref):
    shape = (ROWS, DEEP)
    lane, row = lane_of(shape), row_of(shape)
    part = lax.div(lane, PART)
    within = lane - PART * part
    column = lax.div(within, ROWS)
    on = (within - ROWS * column == row) & (part < 3)
    blocks = []
    for i in range(COMPS):
        value = jnp.zeros(shape, jnp.float32)
        for j in range(COMPS):
            value = jnp.where(column == j, 2.0 * mix_ref[i, j], value)
        high, low = split(value)
        value = jnp.where(part == 2, low.astype(jnp.float32), high.astype(jnp.float32))
        blocks.append(jnp.where(on, value, 0.0))
    blocks.append(jnp.zeros(shape, jnp.float32))
    return jnp.concatenate(blocks, axis=0).astype(jnp.bfloat16)


def mixed(operand, spread):
    shape = spread[0].shape
    high, low = split(jnp.concatenate(spread + [jnp.zeros(shape, jnp.float32)], axis=0))
    tail = jnp.zeros((DEEP - 3 * PART, shape[1]), jnp.bfloat16)
    out = jnp.dot(
        operand,
        jnp.concatenate([high, low, high, tail], axis=0),
        preferred_element_type=jnp.float32,
    )
    return [out[ROWS * i : ROWS * (i + 1)] for i in range(COMPS)]


def flash(feed, pressure, signed, slope, operand):
    log_press = jnp.log(pressure)
    half_base = [0.5 * signed[i] - (0.5 * slope[i]) * log_press for i in range(COMPS)]
    spread = None
    for outer in range(SS_ITERS):
        if outer == 0:
            half_log = half_base
        else:
            mix = mixed(operand, spread)
            half_log = [half_base[i] - 0.5 * jnp.tanh(mix[i]) for i in range(COMPS)]
        t = [jnp.tanh(half_log[i]) for i in range(COMPS)]
        u = [rcp(t[i]) for i in range(COMPS)]
        psi = None
        for inner in range(RR_ITERS):
            q = t if inner == 0 else [rcp(u[i] + psi) for i in range(COMPS)]
            part = [feed[i] * q[i] for i in range(COMPS)]
            step = total_of(part) * rcp(total_of(part[i] * q[i] for i in range(COMPS)))
            psi = jnp.clip(step if inner == 0 else psi + step, -1.0, 1.0)
        spread = [feed[i] * rcp(u[i] + psi) for i in range(COMPS)]
    liquid_part = (0.25 * (1.0 - psi)) * (1.0 - psi)
    vapour_part = (0.25 * VAPOUR_WEIGHT * (1.0 + psi)) * (1.0 + psi)
    both, apart = vapour_part + liquid_part, vapour_part - liquid_part
    return [spread[i] * (both * u[i] + apart) for i in range(COMPS)]


def parameters(vol_ref, slope_ref):
    signed = [vol_ref[i] if i < LIGHT else -vol_ref[i] for i in range(COMPS)]
    return signed, [slope_ref[i] for i in range(COMPS)]


def lane_of(shape):
    return lax.broadcasted_iota(jnp.int32, shape, len(shape) - 1)


def row_of(shape):
    return lax.broadcasted_iota(jnp.int32, shape, len(shape) - 2)


class Rows:
    def __init__(self, edge, inner):
        self.edge, self.inner = edge, inner

    def __getitem__(self, at):
        at = at if isinstance(at, tuple) else (at,)
        edge = self.edge[at]
        return jnp.concatenate([edge[:ROWS], self.inner[at], edge[ROWS:]], axis=0)


def pack_rows(field, low, out_ref, depth):
    row = None
    for n in range(0, len(UNITS), 2):
        for pair in range(depth // 2):
            tile = None
            for z in (2 * pair, 2 * pair + 1):
                order = (1, 0) if low else (0, 1)
                for which in order:
                    unit = UNITS[n + which]
                    at = 4 * (z % 2) + (2 if low == (which == 0) else 0)
                    first = 0 if low else ROWS - 1
                    if isinstance(unit, tuple):
                        a, b = unit
                        pieces = [(at, a, at - first), (at + 1, b, at + 1 - first)]
                        if not low:
                            pieces = [(at, b, at - first), (at + 1, a, at + 1 - first)]
                    else:
                        pieces = [(at, unit, at if low else at + 2)]
                    for start, k, turn in pieces:
                        here = field(k, z)
                        if row is None:
                            row = row_of(here.shape)
                        if turn % ROWS:
                            here = pltpu.roll(here, turn % ROWS, 0)
                        tile = here if tile is None else jnp.where(row < start, tile, here)
            out_ref[n // 2, pl.ds(pair * ROWS, ROWS), :] = tile


def row_tiles(one, two, wanted, start=0, stop=None):
    shape = one.shape[1:]
    upper = row_of(shape) % DEPTH_SLOTS < 2
    tile_row = row_of((ROWS, shape[1]))
    stop = stop or shape[0] // DEPTH_SLOTS
    tiles = {}
    for n, unit in enumerate(UNITS):
        fields = unit if isinstance(unit, tuple) else (unit,)
        if not any(k in wanted for k in fields):
            continue
        up, down = by_side("areal", one[n // 2], two[n // 2])
        if n % 2:
            up, down = pltpu.roll(up, shape[0] - 2, 0), pltpu.roll(down, 2, 0)
        both = jnp.where(upper, up, down)
        for z in range(start, stop):
            at = (z // 2) * ROWS
            tile = pltpu.roll(both[at : at + ROWS], 6 - 4 * (z % 2), 0)
            if fields[0] in wanted:
                tiles.setdefault(fields[0], []).append(tile)
            if fields[-1] in wanted and fields[-1] != fields[0]:
                other = jnp.where(tile_row < 4, pltpu.roll(tile, ROWS - 1, 0), pltpu.roll(tile, 1, 0))
                tiles.setdefault(fields[-1], []).append(other)
    return tiles


def pack_columns(rows_two, rows_one, *refs):
    (
        press, tx, ty, tz, pore, edge_mob, _, edge_mob_sum, edge_acc_sum, mob, _, mob_sum, acc_sum,
        one_ref, two_ref, own_ref,
    ) = refs
    depth, rows, width = press.shape
    shape = (rows + ROWS, LANES)
    lane = lane_of(shape)
    mob, mob_sum, acc_sum = (
        Rows(*both) for both in ((edge_mob, mob), (edge_mob_sum, mob_sum), (edge_acc_sum, acc_sum))
    )
    corner_fields = {MOB: mob_sum, PRESS: press, TX: tx, TY: ty}
    others = {TZ: tz, PORE: pore, ACC: acc_sum, **corner_fields}
    corners = row_tiles(rows_one, rows_two, corner_fields)
    nothing = jnp.zeros((ROWS, LANES), jnp.float32)
    for tile in range(FIELDS // 4):
        packed = jnp.zeros(shape, jnp.float32)
        for quarter in range(4):
            k = 4 * tile + quarter
            for z in range(depth):
                plane = mob[k, z] if k < COMPS else others[k][z]
                first, last = plane[:, :LANES], plane[:, -LANES:]
                at = 32 * quarter + 4 * z
                both = jnp.where(lane_of(first.shape) < LANES // 2, first, last)
                if k < COMPS:
                    both = pltpu.roll(both, at + 2, 1)
                    on = (lane_of(first.shape) >= at + 1) & (lane_of(first.shape) < at + 3)
                    packed = jnp.concatenate([jnp.where(on, both, packed[:rows]), nothing], axis=0)
                    continue
                end = nothing
                if k in corner_fields:
                    end = corners[k][z]
                    end = jnp.where(lane_of(end[:, :LANES].shape) < LANES // 2, end[:, :LANES], end[:, -LANES:])
                both = pltpu.roll(jnp.concatenate([both, end], axis=0), (at + 2) % LANES, 1)
                packed = jnp.where((lane >= at) & (lane < at + 4), both, packed)
        own_ref[:, tile * LANES : (tile + 1) * LANES] = packed
    odd = lax.axis_index("layer") % 2 == 1
    half = FIELDS // 8
    for n in range(half):
        near, far = (own_ref[:, t * LANES : (t + 1) * LANES] for t in (n, n + half))
        upward = jnp.where(lane % 4 < 2, near, pltpu.roll(far, 2, 1))
        downward = jnp.where(lane % 4 < 2, pltpu.roll(near, LANES - 2, 1), far)
        one_ref[:, n * LANES : (n + 1) * LANES] = jnp.where(odd, downward, upward)
        two_ref[:, n * LANES : (n + 1) * LANES] = jnp.where(odd, upward, downward)


def spread_fields(tiles):
    fields = []
    for tile in tiles:
        for quarter in range(4):
            turn = (LANES - 32 * quarter) % LANES
            fields.append(pltpu.roll(tile, turn, 1) if turn else tile)
    return fields


def side_fields(one, two):
    lane = lane_of((one.shape[0], LANES))
    near, far = [], []
    for n in range(FIELDS // 8):
        span = slice(n * LANES, (n + 1) * LANES)
        left, right = by_side("layer", one[:, span], two[:, span])
        near.append(jnp.where(lane % 4 < 2, left, pltpu.roll(right, 2, 1)))
        far.append(jnp.where(lane % 4 < 2, pltpu.roll(left, LANES - 2, 1), right))
    return spread_fields(near + far)


def flash_rows(source, target, tile_row, flags, vol, slope, operand, comp, press, pore, mass, outs, ready=None):
    mob_ref, acc_ref, mob_sum, acc_sum = outs
    layer = lax.axis_index("layer")
    depth, _, width = press.shape

    def beside(ref, *lead):
        return jnp.concatenate([ref[(*lead, z, source)] for z in range(depth)], axis=1)

    def store(ref, value, *lead):
        for z in range(depth):
            ref[(*lead, z, target)] = value[:, z * width : (z + 1) * width]

    raw = [beside(comp, i) for i in range(COMPS)]
    inverse = rcp(total_of(raw))
    feed = [raw[i] * inverse for i in range(COMPS)]
    first, last = flags[layer, 2 * tile_row], flags[layer, 2 * tile_row + 1]

    @pl.when(first + last > 0)
    def _():
        signed, slopes = parameters(vol, slope)
        two = flash(feed, beside(press), signed, slopes, operand[...])
        marked = jnp.where(row_of(feed[0].shape) < ROWS // 2, first, last) > 0
        mobility = [jnp.where(marked, two[i], feed[i]) for i in range(COMPS)]
        for i in range(COMPS):
            store(mob_ref, mobility[i], i)
        store(mob_sum, total_of(mobility))

    @pl.when(first + last == 0)
    def _():
        for i in range(COMPS):
            store(mob_ref, feed[i], i)
        store(mob_sum, total_of(feed))

    if ready:
        ready()
    volume = beside(pore)
    acc = [volume * feed[i] - beside(mass, i) for i in range(COMPS)]
    for i in range(COMPS):
        store(acc_ref, acc[i], i)
    store(acc_sum, total_of(acc))


def edge_cells(
    flags_in, vol_in, slope_in, mix_in, comp, press, pore, mass, tx, ty, tz,
    mob_ref, acc_ref, mob_sum, acc_sum, one_ref, two_ref, operand, comp_i, press_i, pore_i, mass_i,
    flags, vol, slope, mix, comp_s, press_s, pore_s, mass_s, tx_s, ty_s, tz_s, sems, scalar_sems,
):
    depth, rows, _ = press.shape
    fetched = (
        (comp, comp_s), (press, press_s), (pore, pore_s), (mass, mass_s), (tx, tx_s), (ty, ty_s), (tz, tz_s)
    )

    ahead = (comp_i, press_i, pore_i, mass_i)

    def fetch(end, n):
        source, slot = fetched[n]
        at = pl.ds(end * (rows - ROWS), ROWS) if end < 2 else pl.ds(ROWS, rows - 2 * ROWS)
        return pltpu.make_async_copy(
            source.at[:, :, at, :] if len(source.shape) == 4 else source.at[:, at, :],
            slot.at[end] if end < 2 else ahead[n],
            sems.at[end, n],
        )

    scalars = [
        pltpu.make_async_copy(source, slot, scalar_sems.at[n])
        for n, (source, slot) in enumerate(
            ((flags_in, flags), (vol_in, vol), (slope_in, slope), (mix_in, mix))
        )
    ]
    early, late = (0, 1), range(2, len(fetched))
    for copy in scalars:
        copy.start()
    for n in early:
        fetch(0, n).start()
    for copy in scalars:
        copy.wait()
    operand[...] = mixing_operand(mix)
    odd = lax.axis_index("areal") % 2 == 1
    for end in range(2):
        for n in early:
            fetch(end, n).wait()
        if end == 0:
            for n in late:
                fetch(0, n).start()
            for n in range(len(fetched)):
                fetch(1, n).start()
        else:
            for n in range(len(ahead)):
                fetch(2, n).start()

        def ready():
            for n in late:
                fetch(end, n).wait()

        target = slice(end * ROWS, (end + 1) * ROWS)
        flash_rows(
            slice(None), target, end * (rows // ROWS - 1), flags, vol, slope, operand,
            *(slot.at[end] for _, slot in fetched[:4]), (mob_ref, acc_ref, mob_sum, acc_sum), ready,
        )

        def field(k, z):
            if k < COMPS:
                return mob_ref[k, z, target]
            if k == MOB:
                return mob_sum[z, target]
            if k in (PORE, ACC):
                m, p = mob_sum[z, target], press_s[end, z]
                behind = ROWS - 1 if end == 0 else 1
                strength = (0.5 * TIME_STEP) * tx_s[end, z]
                if end == 1:
                    strength = pltpu.roll(strength, 1, 0)
                couple = strength * (m + pltpu.roll(m, behind, 0))
                if k == PORE:
                    return COMPRESS * pore_s[end, z] + couple
                return acc_sum[z, target] + couple * (p - pltpu.roll(p, behind, 0))
            return {PRESS: press_s, TX: tx_s, TY: ty_s, TZ: tz_s}[k][end, z]

        for turn, ref in enumerate((one_ref, two_ref)):
            @pl.when(odd == (end == turn))
            def _():
                pack_rows(field, end == 0, ref, depth)

    for n in range(len(ahead)):
        fetch(2, n).wait()


def inner_cells(flags, vol, slope, operand, comp, press, pore, mass, *outs):
    def tile(t, carry):
        at = pl.ds(pl.multiple_of(t * ROWS, ROWS), ROWS)
        flash_rows(at, at, t + 1, flags, vol, slope, operand, comp, press, pore, mass, outs)
        return carry

    lax.fori_loop(0, press.shape[1] // ROWS, tile, 0)


def by_side(axis, one, two):
    odd = lax.axis_index(axis) % 2 == 1
    return jnp.where(odd, one, two), jnp.where(odd, two, one)


def by_pairs(count, body):
    def pair(t, carry):
        body(2 * t)
        body(2 * t + 1)
        return carry

    lax.fori_loop(0, count // 2, pair, 0)


def near_residual(
    rows_two, rows_one, press, tx, ty, tz, pore,
    edge_mob, edge_acc, edge_mob_sum, edge_acc_sum, mob, acc, mob_sum, acc_sum,
    out_ref, total_ref, diagonal_ref, c_x, c_y, c_z,
    rows_h, fields_h, g_x, g_y, g_z,
):
    depth, rows, width = press.shape
    areal, areals = lax.axis_index("areal"), lax.axis_size("areal")
    tall = rows + ROWS
    full = (tall, width)
    own = slice(0, rows)
    mob, acc, mob_sum, acc_sum = (
        Rows(*both)
        for both in ((edge_mob, mob), (edge_acc, acc), (edge_mob_sum, mob_sum), (edge_acc_sum, acc_sum))
    )
    fields = {MOB: mob_sum, PRESS: press, TX: tx, TY: ty, TZ: tz, PORE: pore, ACC: acc_sum}
    tiles = row_tiles(rows_one, rows_two, range(FIELDS))
    for z in range(depth):
        for i in range(COMPS):
            rows_h[i, z] = tiles[i][z]
        for n, k in enumerate(fields):
            tile = tiles[k][z]
            if k == TX:
                tile = jnp.where(row_of(tile.shape) == ROWS - 1, tile, 0.0)
            fields_h[n, z] = tile

    end_x = (row_of(full) == rows - 1) & (areal == areals - 1)
    end_y = lane_of(full) == width - 1
    scale = 0.5 * TIME_STEP
    c_z[0] = jnp.zeros(full, jnp.float32)
    g_z[0] = jnp.zeros((rows, width), jnp.float32)

    def update(z):
        m, p, x, y, zz, volume, total = (
            jnp.concatenate([COMPRESS * ref[z] if ref is pore else ref[z], fields_h[n, z]], axis=0)
            for n, ref in enumerate(fields.values())
        )
        up, down = jnp.minimum(z + 1, depth - 1), jnp.maximum(z - 1, 0)
        p_up = jnp.concatenate([press[up], fields_h[1, up]], axis=0)
        p_down = jnp.concatenate([press[down], fields_h[1, down]], axis=0)
        m_up = jnp.concatenate([mob_sum[up], fields_h[0, up]], axis=0)
        strength_x = jnp.where(end_x, 0.0, scale * x)
        strength_y = jnp.where(end_y, 0.0, scale * y)
        strength_z = jnp.where(z < depth - 1, scale, 0.0) * zz
        dx = p - pltpu.roll(p, tall - 1, 0)
        dy = p - pltpu.roll(p, width - 1, 1)
        dz = p - p_up
        cx = strength_x * (m + pltpu.roll(m, tall - 1, 0))
        cy = strength_y * (m + pltpu.roll(m, width - 1, 1))
        cz = strength_z * (m + m_up)
        cz_low = c_z[z]
        gx = strength_x * dx
        g_x[0, z], g_x[1, z] = gx[own], -pltpu.roll(gx, 1, 0)[own]
        g_y[z], g_z[z + 1] = (strength_y * dy)[own], (strength_z * dz)[own]
        c_x[z], c_y[z], c_z[z + 1] = cx, cy, cz
        fx, fy = cx * dx, cy * dy
        total_ref[z] = (
            total
            + (fx - pltpu.roll(fx, 1, 0))
            + (fy - pltpu.roll(fy, 1, 1))
            + (cz * dz + cz_low * (p - p_down))
        )
        diagonal_ref[z] = (
            volume
            + (cx + pltpu.roll(cx, 1, 0))
            + (cy + pltpu.roll(cy, 1, 1))
            + (cz + cz_low)
        )

    by_pairs(depth, update)

    def residual(z):
        down, up = jnp.maximum(z - 1, 0), jnp.minimum(z + 1, depth - 1)
        gx, gx_low, gy, gz, gz_low = g_x[0, z], g_x[1, z], g_y[z], g_z[z + 1], -g_z[z]
        gy_low = -pltpu.roll(gy, 1, 1)
        middle = (gx + gx_low) + (gy + gy_low) + (gz + gz_low)
        for i in range(COMPS):
            here = mob[i, z]
            tall_here = jnp.concatenate([here, rows_h[i, z]], axis=0)
            out_ref[i, z] = (
                acc[i, z]
                + middle * here
                + gx * pltpu.roll(tall_here, tall - 1, 0)[own]
                + gx_low * pltpu.roll(tall_here, 1, 0)[own]
                + gy * pltpu.roll(here, width - 1, 1)
                + gy_low * pltpu.roll(here, 1, 1)
                + gz * mob[i, up]
                + gz_low * mob[i, down]
            )

    by_pairs(depth, residual)


def finish(
    columns_one, columns_two, packet, press, total_in, diagonal_in, c_x, c_y, c_z, edge_mob, mob, near,
    res_ref, new_ref,
    side_h, edge_h, first, total_ref, inverse_ref, res_s, new_s, sems,
):
    depth, rows, width = press.shape
    layer, layers = lax.axis_index("layer"), lax.axis_size("layer")
    areal, areals = lax.axis_index("areal"), lax.axis_size("areal")
    tall = rows + ROWS
    lane = lane_of((tall, LANES))
    at_first, at_last = lane == 0, lane == LANES - 1
    low, high = slice(0, LANES), slice(width - LANES, width)
    FLUX, COUPLE, FACE, NEXT = range(4)
    mob = Rows(edge_mob, mob)

    def edges(which, z):
        both = pltpu.roll(edge_h[which], LANES - 1 - 4 * z, 1)
        return jnp.where(at_first, both, 0.0), jnp.where(at_last, both, 0.0)

    halo = side_fields(columns_one, columns_two)
    here = spread_fields([packet[:, t : t + LANES] for t in range(0, FIELDS * 32, LANES)])
    is_left = lane % 4 == 1
    for i in range(COMPS):
        cells = halo[i][:rows]
        side_h[i] = jnp.where(is_left[:rows], pltpu.roll(cells, LANES - 1, 1), pltpu.roll(cells, 1, 1))
    scale = 0.5 * TIME_STEP

    def turned(x, by):
        return pltpu.roll(x, by % LANES, 1)

    def outer(x):
        return jnp.where(is_left, turned(x, 1), turned(x, -1))

    def inner(x):
        return jnp.where(is_left, turned(x, -1), turned(x, 1))

    m, p = halo[MOB], halo[PRESS]
    strength = scale * halo[TY]
    own_strength = jnp.where(layer < layers - 1, scale, 0.0) * here[TY]
    c_out = jnp.where(is_left, turned(strength, 1), strength) * (m + outer(m))
    s_in = jnp.where(is_left, strength, turned(own_strength, 1))
    c_in = s_in * (m + inner(here[MOB]))
    d_in = p - inner(here[PRESS])
    end_x = (row_of(lane.shape) == rows - 1) & (areal == areals - 1)
    cx = jnp.where(end_x, 0.0, scale * halo[TX]) * (m + pltpu.roll(m, tall - 1, 0))
    cz = jnp.where(lane < 4 * (depth - 1), scale * halo[TZ], 0.0) * (m + turned(m, -4))
    fx = cx * (p - pltpu.roll(p, tall - 1, 0))
    fz = cz * (p - turned(p, -4))
    total = (
        halo[ACC]
        + (c_out * (p - outer(p)) + c_in * d_in)
        + (fx - pltpu.roll(fx, 1, 0))
        + (fz - turned(fz, 4))
    )
    diagonal = (
        COMPRESS * halo[PORE] + (c_out + c_in) + (cx + pltpu.roll(cx, 1, 0)) + (cz + turned(cz, 4))
    )
    usable = diagonal > 0.0
    beside = jnp.where(usable, -total * rcp(jnp.where(usable, diagonal, 1.0)), 0.0)
    for which, value in (
        (FLUX, -c_in * d_in), (COUPLE, c_in), (FACE, -s_in * d_in), (NEXT, c_in * beside)
    ):
        edge_h[which] = jnp.where(is_left, value, turned(value, -2))

    def leave(z):
        return pltpu.make_async_copy(res_s.at[:, z], res_ref.at[:, z], sems.at[0, z])

    def leave_new(z):
        return pltpu.make_async_copy(new_s.at[z], new_ref.at[z], sems.at[1, z])

    def update(z):
        faces = [face[:rows] for face in edges(FACE, z)]
        for i in range(COMPS):
            side = pltpu.roll(side_h[i], LANES - 2 - 4 * z, 1)
            cells = mob[i, z]
            for span, face in zip((low, high), faces):
                res_s[i, z, :, span] = near[i, z, :, span] + face * (cells[:, span] + side)
        leave(z).start()
        flux, couple = edges(FLUX, z), edges(COUPLE, z)
        for n, span in enumerate((low, high)):
            total = total_in[z, :, span] + flux[n]
            diagonal = diagonal_in[z, :, span] + couple[n]
            usable = diagonal > 0.0
            inverse = rcp(jnp.where(usable, diagonal, 1.0))
            first[z, :, span] = jnp.where(usable, -total * inverse, 0.0)
            total_ref[z, :, span] = total[:rows]
            inverse_ref[z, :, span] = inverse[:rows]

    by_pairs(depth, update)

    def second(z):
        here = first[z]
        up, down = jnp.minimum(z + 1, depth - 1), jnp.maximum(z - 1, 0)
        cx, cy = c_x[z], c_y[z, :rows]
        own = here[:rows]
        gathered = (
            (cx * pltpu.roll(here, tall - 1, 0))[:rows]
            + pltpu.roll(cx * here, 1, 0)[:rows]
            + cy * pltpu.roll(own, width - 1, 1)
            + pltpu.roll(cy * own, 1, 1)
            + (c_z[z + 1, :rows] * first[up, :rows] + c_z[z, :rows] * first[down, :rows])
            - total_ref[z]
        )
        beyond = edges(NEXT, z)
        for n, span in enumerate((low, high)):
            new_s[z, :, span] = press[z, :, span] + inverse_ref[z, :, span] * (
                gathered[:, span] + beyond[n][:rows]
            )
        leave_new(z).start()

    by_pairs(depth, second)

    def left(z):
        leave(z).wait()
        leave_new(z).wait()

    by_pairs(depth, left)


def on_device(
    pressure, composition, mass_old, pore_volume, trans_x, trans_y, trans_z,
    volatility, pressure_slope, mixing, two_phase,
):
    depth, rows, width = pressure.shape
    f32 = jnp.float32
    smem = pl.BlockSpec(memory_space=pltpu.SMEM)
    vmem = pl.BlockSpec(memory_space=pltpu.VMEM)
    def params(mib):
        return pltpu.CompilerParams(vmem_limit_bytes=mib * MIB)

    scalars = (two_phase, volatility, pressure_slope, mixing)

    def swapped(block, axis, first):
        count = lax.axis_size(axis)
        pairs = [(i, i + 1) for i in range(first, count - 1, 2)]
        return lax.ppermute(block, axis, pairs + [(j, i) for i, j in pairs])

    whole = jax.ShapeDtypeStruct((COMPS, depth, rows, width), f32)
    sums = jax.ShapeDtypeStruct((depth, rows, width), f32)
    packed = jax.ShapeDtypeStruct((len(UNITS) // 2, DEPTH_SLOTS * depth, width), f32)
    fields = (composition, pressure, pore_volume, mass_old, trans_x, trans_y, trans_z)

    def parts(count):
        planes = jax.ShapeDtypeStruct((COMPS, depth, count, width), f32)
        plane = jax.ShapeDtypeStruct((depth, count, width), f32)
        return [planes, planes, plane, plane]

    between = [jax.ShapeDtypeStruct((*x.shape[:-2], rows - 2 * ROWS, width), f32) for x in fields[:4]]
    *results, operand, comp, press, pore, mass = pl.pallas_call(
        edge_cells,
        in_specs=[pl.BlockSpec(memory_space=pl.ANY)] * (4 + len(fields)),
        out_specs=[vmem] * 11,
        out_shape=parts(2 * ROWS)
        + [packed, packed, jax.ShapeDtypeStruct((PART, DEEP), jnp.bfloat16), *between],
        scratch_shapes=[pltpu.SMEM(x.shape, x.dtype) for x in scalars]
        + [pltpu.VMEM((2, *x.shape[:-2], ROWS, width), f32) for x in fields]
        + [pltpu.SemaphoreType.DMA((3, len(fields))), pltpu.SemaphoreType.DMA((4,))],
        compiler_params=params(24),
        name="edge_cells",
    )(*(pltpu.with_memory_space_constraint(x, pltpu.HBM) for x in (*scalars, *fields)))
    *edge, one, two = results
    rows_two = swapped(two, "areal", 1)
    rows_one = swapped(one, "areal", 0)
    cells = rows * depth * width
    inner = pl.pallas_call(
        inner_cells,
        in_specs=[smem] * 3 + [vmem] * 5,
        out_specs=[vmem] * 4,
        out_shape=parts(rows - 2 * ROWS),
        compiler_params=params(24),
        cost_estimate=pl.CostEstimate(
            flops=450 * cells, transcendentals=95 * cells, bytes_accessed=2 * 39 * cells
        ),
        name="inner_cells",
    )(*scalars[:3], operand, comp, press, pore, mass)
    planes_of = (pressure, trans_x, trans_y, trans_z, pore_volume)

    narrow = jax.ShapeDtypeStruct((rows + ROWS, FIELDS * 16), f32)
    one, two, packet = pl.pallas_call(
        pack_columns,
        in_specs=[vmem] * 15,
        out_specs=[vmem] * 3,
        out_shape=[narrow, narrow, jax.ShapeDtypeStruct((rows + ROWS, FIELDS * 32), f32)],
        compiler_params=params(24),
        name="pack_columns",
    )(rows_two, rows_one, *planes_of, *edge, *inner)
    columns_one = swapped(one, "layer", 0)
    columns_two = swapped(two, "layer", 1)

    tall = jax.ShapeDtypeStruct((depth, rows + ROWS, width), f32)
    above_faces = jax.ShapeDtypeStruct((depth + 1, rows + ROWS, width), f32)
    near, *sweep = pl.pallas_call(
        near_residual,
        in_specs=[vmem] * 15,
        out_specs=[vmem] * 6,
        out_shape=[whole, tall, tall, tall, tall, above_faces],
        scratch_shapes=[
            pltpu.VMEM((COMPS, depth, ROWS, width), f32),
            pltpu.VMEM((FIELDS - COMPS, depth, ROWS, width), f32),
            pltpu.VMEM((2, depth, rows, width), f32),
            pltpu.VMEM((depth, rows, width), f32),
            pltpu.VMEM((depth + 1, rows, width), f32),
        ],
        compiler_params=params(24),
        cost_estimate=pl.CostEstimate(flops=150 * cells, transcendentals=0, bytes_accessed=4 * 31 * cells),
        name="near_residual",
    )(rows_two, rows_one, *planes_of, *edge, *inner)

    return pl.pallas_call(
        finish,
        in_specs=[vmem] * 12,
        out_specs=[pl.BlockSpec(memory_space=pl.ANY)] * 2,
        out_shape=[whole, sums],
        scratch_shapes=[
            pltpu.VMEM((COMPS, rows, LANES), f32),
            pltpu.VMEM((4, rows + ROWS, LANES), f32),
            pltpu.VMEM((depth, rows + ROWS, width), f32),
            pltpu.VMEM((depth, rows, width), f32),
            pltpu.VMEM((depth, rows, width), f32),
            pltpu.VMEM((COMPS, depth, rows, width), f32),
            pltpu.VMEM((depth, rows, width), f32),
            pltpu.SemaphoreType.DMA((2, depth)),
        ],
        compiler_params=params(24),
        name="finish",
    )(columns_one, columns_two, packet, pressure, *sweep, edge[0], inner[0], near)


def solution(mesh):
    placed = (
        P(None, "areal", "layer"),
        P(None, None, "areal", "layer"),
        P(None, None, "areal", "layer"),
        P(None, "areal", "layer"),
        P(None, "areal", "layer"),
        P(None, "areal", "layer"),
        P(None, "areal", "layer"),
        P(),
        P(),
        P(),
        P(None, "areal"),
    )
    return jax.shard_map(
        on_device,
        mesh=mesh,
        in_specs=placed,
        out_specs=(P(None, None, "areal", "layer"), P(None, "areal", "layer")),
        check_vma=False,
    )
```

```python
import jax
import jax.numpy as jnp
from jax import lax
from jax.experimental import pallas as pl
from jax.experimental.pallas import tpu as pltpu
from jax.sharding import PartitionSpec as P

SS_ITERS = 3
RR_ITERS = 3
LIGHT = 4
COMPS = 9
FIELDS = 16
MOB, PRESS, TX, TY, TZ, PORE, ACC = range(COMPS, FIELDS)
UNITS = ((0, 1), (2, 3), (4, 5), (6, 7), (8, MOB), (PRESS, TX), (TY, TZ), (PORE, ACC))
DEPTH_SLOTS = 4
TIME_STEP = 4.0
COMPRESS = 0.2
VAPOUR_WEIGHT = 1.0 / 0.25
LANES = 128
ROWS = 8
MIB = 1024 * 1024
PART = (COMPS + 1) * ROWS
DEEP = 256


def rcp(x):
    return pltpu.reciprocal(x, approx=True)


def total_of(terms):
    terms = list(terms)
    while len(terms) > 1:
        terms = [a + b for a, b in zip(terms[::2], terms[1::2])] + (
            [terms[-1]] if len(terms) % 2 else []
        )
    return terms[0]


def split(x):
    high = x.astype(jnp.bfloat16)
    return high, (x - high.astype(jnp.float32)).astype(jnp.bfloat16)


def mixing_operand(mix_ref):
    shape = (ROWS, DEEP)
    lane, row = lane_of(shape), row_of(shape)
    part = lax.div(lane, PART)
    within = lane - PART * part
    column = lax.div(within, ROWS)
    on = (within - ROWS * column == row) & (part < 3)
    blocks = []
    for i in range(COMPS):
        value = jnp.zeros(shape, jnp.float32)
        for j in range(COMPS):
            value = jnp.where(column == j, 2.0 * mix_ref[i, j], value)
        high, low = split(value)
        value = jnp.where(part == 2, low.astype(jnp.float32), high.astype(jnp.float32))
        blocks.append(jnp.where(on, value, 0.0))
    blocks.append(jnp.zeros(shape, jnp.float32))
    return jnp.concatenate(blocks, axis=0).astype(jnp.bfloat16)


def mixed(operand, spread):
    shape = spread[0].shape
    high, low = split(jnp.concatenate(spread + [jnp.zeros(shape, jnp.float32)], axis=0))
    tail = jnp.zeros((DEEP - 3 * PART, shape[1]), jnp.bfloat16)
    out = jnp.dot(
        operand,
        jnp.concatenate([high, low, high, tail], axis=0),
        preferred_element_type=jnp.float32,
    )
    return [out[ROWS * i : ROWS * (i + 1)] for i in range(COMPS)]


def flash(feed, pressure, signed, slope, operand):
    log_press = jnp.log(pressure)
    half_base = [0.5 * signed[i] - (0.5 * slope[i]) * log_press for i in range(COMPS)]
    spread = None
    for outer in range(SS_ITERS):
        if outer == 0:
            half_log = half_base
        else:
            mix = mixed(operand, spread)
            half_log = [half_base[i] - 0.5 * jnp.tanh(mix[i]) for i in range(COMPS)]
        t = [jnp.tanh(half_log[i]) for i in range(COMPS)]
        u = [rcp(t[i]) for i in range(COMPS)]
        psi = None
        for inner in range(RR_ITERS):
            q = t if inner == 0 else [rcp(u[i] + psi) for i in range(COMPS)]
            part = [feed[i] * q[i] for i in range(COMPS)]
            step = total_of(part) * rcp(total_of(part[i] * q[i] for i in range(COMPS)))
            psi = jnp.clip(step if inner == 0 else psi + step, -1.0, 1.0)
        spread = [feed[i] * rcp(u[i] + psi) for i in range(COMPS)]
    liquid_part = (0.25 * (1.0 - psi)) * (1.0 - psi)
    vapour_part = (0.25 * VAPOUR_WEIGHT * (1.0 + psi)) * (1.0 + psi)
    both, apart = vapour_part + liquid_part, vapour_part - liquid_part
    return [spread[i] * (both * u[i] + apart) for i in range(COMPS)]


def parameters(vol_ref, slope_ref):
    signed = [vol_ref[i] if i < LIGHT else -vol_ref[i] for i in range(COMPS)]
    return signed, [slope_ref[i] for i in range(COMPS)]


def lane_of(shape):
    return lax.broadcasted_iota(jnp.int32, shape, len(shape) - 1)


def row_of(shape):
    return lax.broadcasted_iota(jnp.int32, shape, len(shape) - 2)


class Rows:
    def __init__(self, edge, inner):
        self.edge, self.inner = edge, inner

    def __getitem__(self, at):
        at = at if isinstance(at, tuple) else (at,)
        edge = self.edge[at]
        return jnp.concatenate([edge[:ROWS], self.inner[at], edge[ROWS:]], axis=0)


def pack_rows(field, low, out_ref, depth):
    row = None
    for n in range(0, len(UNITS), 2):
        for pair in range(depth // 2):
            tile = None
            for z in (2 * pair, 2 * pair + 1):
                order = (1, 0) if low else (0, 1)
                for which in order:
                    unit = UNITS[n + which]
                    at = 4 * (z % 2) + (2 if low == (which == 0) else 0)
                    first = 0 if low else ROWS - 1
                    if isinstance(unit, tuple):
                        a, b = unit
                        pieces = [(at, a, at - first), (at + 1, b, at + 1 - first)]
                        if not low:
                            pieces = [(at, b, at - first), (at + 1, a, at + 1 - first)]
                    else:
                        pieces = [(at, unit, at if low else at + 2)]
                    for start, k, turn in pieces:
                        here = field(k, z)
                        if row is None:
                            row = row_of(here.shape)
                        if turn % ROWS:
                            here = pltpu.roll(here, turn % ROWS, 0)
                        tile = here if tile is None else jnp.where(row < start, tile, here)
            out_ref[n // 2, pl.ds(pair * ROWS, ROWS), :] = tile


def row_tiles(one, two, wanted, start=0, stop=None):
    shape = one.shape[1:]
    upper = row_of(shape) % DEPTH_SLOTS < 2
    tile_row = row_of((ROWS, shape[1]))
    stop = stop or shape[0] // DEPTH_SLOTS
    tiles = {}
    for n, unit in enumerate(UNITS):
        fields = unit if isinstance(unit, tuple) else (unit,)
        if not any(k in wanted for k in fields):
            continue
        up, down = by_side("areal", one[n // 2], two[n // 2])
        if n % 2:
            up, down = pltpu.roll(up, shape[0] - 2, 0), pltpu.roll(down, 2, 0)
        both = jnp.where(upper, up, down)
        for z in range(start, stop):
            at = (z // 2) * ROWS
            tile = pltpu.roll(both[at : at + ROWS], 6 - 4 * (z % 2), 0)
            if fields[0] in wanted:
                tiles.setdefault(fields[0], []).append(tile)
            if fields[-1] in wanted and fields[-1] != fields[0]:
                other = jnp.where(tile_row < 4, pltpu.roll(tile, ROWS - 1, 0), pltpu.roll(tile, 1, 0))
                tiles.setdefault(fields[-1], []).append(other)
    return tiles


def pack_columns(rows_two, rows_one, *refs):
    (
        press, tx, ty, tz, pore, edge_mob, _, edge_mob_sum, edge_acc_sum, mob, _, mob_sum, acc_sum,
        one_ref, two_ref, own_ref,
    ) = refs
    depth, rows, width = press.shape
    shape = (rows + ROWS, LANES)
    lane = lane_of(shape)
    mob, mob_sum, acc_sum = (
        Rows(*both) for both in ((edge_mob, mob), (edge_mob_sum, mob_sum), (edge_acc_sum, acc_sum))
    )
    corner_fields = {MOB: mob_sum, PRESS: press, TX: tx, TY: ty}
    others = {TZ: tz, PORE: pore, ACC: acc_sum, **corner_fields}
    corners = row_tiles(rows_one, rows_two, corner_fields)
    nothing = jnp.zeros((ROWS, LANES), jnp.float32)
    for tile in range(FIELDS // 4):
        packed = jnp.zeros(shape, jnp.float32)
        for quarter in range(4):
            k = 4 * tile + quarter
            for z in range(depth):
                plane = mob[k, z] if k < COMPS else others[k][z]
                first, last = plane[:, :LANES], plane[:, -LANES:]
                at = 32 * quarter + 4 * z
                both = jnp.where(lane_of(first.shape) < LANES // 2, first, last)
                if k < COMPS:
                    both = pltpu.roll(both, at + 2, 1)
                    on = (lane_of(first.shape) >= at + 1) & (lane_of(first.shape) < at + 3)
                    packed = jnp.concatenate([jnp.where(on, both, packed[:rows]), nothing], axis=0)
                    continue
                end = nothing
                if k in corner_fields:
                    end = corners[k][z]
                    end = jnp.where(lane_of(end[:, :LANES].shape) < LANES // 2, end[:, :LANES], end[:, -LANES:])
                both = pltpu.roll(jnp.concatenate([both, end], axis=0), (at + 2) % LANES, 1)
                packed = jnp.where((lane >= at) & (lane < at + 4), both, packed)
        own_ref[:, tile * LANES : (tile + 1) * LANES] = packed
    odd = lax.axis_index("layer") % 2 == 1
    half = FIELDS // 8
    for n in range(half):
        near, far = (own_ref[:, t * LANES : (t + 1) * LANES] for t in (n, n + half))
        upward = jnp.where(lane % 4 < 2, near, pltpu.roll(far, 2, 1))
        downward = jnp.where(lane % 4 < 2, pltpu.roll(near, LANES - 2, 1), far)
        one_ref[:, n * LANES : (n + 1) * LANES] = jnp.where(odd, downward, upward)
        two_ref[:, n * LANES : (n + 1) * LANES] = jnp.where(odd, upward, downward)


def spread_fields(tiles):
    fields = []
    for tile in tiles:
        for quarter in range(4):
            turn = (LANES - 32 * quarter) % LANES
            fields.append(pltpu.roll(tile, turn, 1) if turn else tile)
    return fields


def side_fields(one, two):
    lane = lane_of((one.shape[0], LANES))
    near, far = [], []
    for n in range(FIELDS // 8):
        span = slice(n * LANES, (n + 1) * LANES)
        left, right = by_side("layer", one[:, span], two[:, span])
        near.append(jnp.where(lane % 4 < 2, left, pltpu.roll(right, 2, 1)))
        far.append(jnp.where(lane % 4 < 2, pltpu.roll(left, LANES - 2, 1), right))
    return spread_fields(near + far)


def flash_rows(source, target, tile_row, flags, vol, slope, operand, comp, press, pore, mass, outs, ready=None):
    mob_ref, acc_ref, mob_sum, acc_sum = outs
    layer = lax.axis_index("layer")
    depth, _, width = press.shape

    def beside(ref, *lead):
        return jnp.concatenate([ref[(*lead, z, source)] for z in range(depth)], axis=1)

    def store(ref, value, *lead):
        for z in range(depth):
            ref[(*lead, z, target)] = value[:, z * width : (z + 1) * width]

    raw = [beside(comp, i) for i in range(COMPS)]
    inverse = rcp(total_of(raw))
    feed = [raw[i] * inverse for i in range(COMPS)]
    first, last = flags[layer, 2 * tile_row], flags[layer, 2 * tile_row + 1]

    @pl.when(first + last > 0)
    def _():
        signed, slopes = parameters(vol, slope)
        two = flash(feed, beside(press), signed, slopes, operand[...])
        marked = jnp.where(row_of(feed[0].shape) < ROWS // 2, first, last) > 0
        mobility = [jnp.where(marked, two[i], feed[i]) for i in range(COMPS)]
        for i in range(COMPS):
            store(mob_ref, mobility[i], i)
        store(mob_sum, total_of(mobility))

    @pl.when(first + last == 0)
    def _():
        for i in range(COMPS):
            store(mob_ref, feed[i], i)
        store(mob_sum, total_of(feed))

    if ready:
        ready()
    volume = beside(pore)
    acc = [volume * feed[i] - beside(mass, i) for i in range(COMPS)]
    for i in range(COMPS):
        store(acc_ref, acc[i], i)
    store(acc_sum, total_of(acc))


def edge_cells(
    flags_in, vol_in, slope_in, mix_in, comp, press, pore, mass, tx, ty, tz,
    mob_ref, acc_ref, mob_sum, acc_sum, one_ref, two_ref, operand, comp_i, press_i, pore_i, mass_i,
    flags, vol, slope, mix, comp_s, press_s, pore_s, mass_s, tx_s, ty_s, tz_s, sems, scalar_sems,
):
    depth, rows, _ = press.shape
    fetched = (
        (comp, comp_s), (press, press_s), (pore, pore_s), (mass, mass_s), (tx, tx_s), (ty, ty_s), (tz, tz_s)
    )

    ahead = (comp_i, press_i, pore_i, mass_i)

    def fetch(end, n):
        source, slot = fetched[n]
        at = pl.ds(end * (rows - ROWS), ROWS) if end < 2 else pl.ds(ROWS, rows - 2 * ROWS)
        return pltpu.make_async_copy(
            source.at[:, :, at, :] if len(source.shape) == 4 else source.at[:, at, :],
            slot.at[end] if end < 2 else ahead[n],
            sems.at[end, n],
        )

    scalars = [
        pltpu.make_async_copy(source, slot, scalar_sems.at[n])
        for n, (source, slot) in enumerate(
            ((flags_in, flags), (vol_in, vol), (slope_in, slope), (mix_in, mix))
        )
    ]
    early, late = (0, 1), range(2, len(fetched))
    for copy in scalars:
        copy.start()
    for n in early:
        fetch(0, n).start()
    for copy in scalars:
        copy.wait()
    operand[...] = mixing_operand(mix)
    odd = lax.axis_index("areal") % 2 == 1
    for end in range(2):
        for n in early:
            fetch(end, n).wait()
        if end == 0:
            for n in late:
                fetch(0, n).start()
            for n in range(len(fetched)):
                fetch(1, n).start()
        else:
            for n in range(len(ahead)):
                fetch(2, n).start()

        def ready():
            for n in late:
                fetch(end, n).wait()

        target = slice(end * ROWS, (end + 1) * ROWS)
        flash_rows(
            slice(None), target, end * (rows // ROWS - 1), flags, vol, slope, operand,
            *(slot.at[end] for _, slot in fetched[:4]), (mob_ref, acc_ref, mob_sum, acc_sum), ready,
        )

        def field(k, z):
            if k < COMPS:
                return mob_ref[k, z, target]
            if k == MOB:
                return mob_sum[z, target]
            if k in (PORE, ACC):
                m, p = mob_sum[z, target], press_s[end, z]
                behind = ROWS - 1 if end == 0 else 1
                strength = (0.5 * TIME_STEP) * tx_s[end, z]
                if end == 1:
                    strength = pltpu.roll(strength, 1, 0)
                couple = strength * (m + pltpu.roll(m, behind, 0))
                if k == PORE:
                    return COMPRESS * pore_s[end, z] + couple
                return acc_sum[z, target] + couple * (p - pltpu.roll(p, behind, 0))
            return {PRESS: press_s, TX: tx_s, TY: ty_s, TZ: tz_s}[k][end, z]

        for turn, ref in enumerate((one_ref, two_ref)):
            @pl.when(odd == (end == turn))
            def _():
                pack_rows(field, end == 0, ref, depth)

    for n in range(len(ahead)):
        fetch(2, n).wait()


def inner_cells(flags, vol, slope, operand, comp, press, pore, mass, *outs):
    def tile(t, carry):
        at = pl.ds(pl.multiple_of(t * ROWS, ROWS), ROWS)
        flash_rows(at, at, t + 1, flags, vol, slope, operand, comp, press, pore, mass, outs)
        return carry

    lax.fori_loop(0, press.shape[1] // ROWS, tile, 0)


def by_side(axis, one, two):
    odd = lax.axis_index(axis) % 2 == 1
    return jnp.where(odd, one, two), jnp.where(odd, two, one)


def by_pairs(count, body):
    def pair(t, carry):
        body(2 * t)
        body(2 * t + 1)
        return carry

    lax.fori_loop(0, count // 2, pair, 0)


def near_residual(
    rows_two, rows_one, press, tx, ty, tz, pore,
    edge_mob, edge_acc, edge_mob_sum, edge_acc_sum, mob, acc, mob_sum, acc_sum,
    out_ref, total_ref, diagonal_ref, c_x, c_y, c_z,
    rows_h, fields_h, g_x, g_y, g_z,
):
    depth, rows, width = press.shape
    areal, areals = lax.axis_index("areal"), lax.axis_size("areal")
    tall = rows + ROWS
    full = (tall, width)
    own = slice(0, rows)
    mob, acc, mob_sum, acc_sum = (
        Rows(*both)
        for both in ((edge_mob, mob), (edge_acc, acc), (edge_mob_sum, mob_sum), (edge_acc_sum, acc_sum))
    )
    fields = {MOB: mob_sum, PRESS: press, TX: tx, TY: ty, TZ: tz, PORE: pore, ACC: acc_sum}
    tiles = row_tiles(rows_one, rows_two, range(FIELDS))
    for z in range(depth):
        for i in range(COMPS):
            rows_h[i, z] = tiles[i][z]
        for n, k in enumerate(fields):
            tile = tiles[k][z]
            if k == TX:
                tile = jnp.where(row_of(tile.shape) == ROWS - 1, tile, 0.0)
            fields_h[n, z] = tile

    end_x = (row_of(full) == rows - 1) & (areal == areals - 1)
    end_y = lane_of(full) == width - 1
    scale = 0.5 * TIME_STEP
    c_z[0] = jnp.zeros(full, jnp.float32)
    g_z[0] = jnp.zeros((rows, width), jnp.float32)

    def update(z):
        m, p, x, y, zz, volume, total = (
            jnp.concatenate([COMPRESS * ref[z] if ref is pore else ref[z], fields_h[n, z]], axis=0)
            for n, ref in enumerate(fields.values())
        )
        up, down = jnp.minimum(z + 1, depth - 1), jnp.maximum(z - 1, 0)
        p_up = jnp.concatenate([press[up], fields_h[1, up]], axis=0)
        p_down = jnp.concatenate([press[down], fields_h[1, down]], axis=0)
        m_up = jnp.concatenate([mob_sum[up], fields_h[0, up]], axis=0)
        strength_x = jnp.where(end_x, 0.0, scale * x)
        strength_y = jnp.where(end_y, 0.0, scale * y)
        strength_z = jnp.where(z < depth - 1, scale, 0.0) * zz
        dx = p - pltpu.roll(p, tall - 1, 0)
        dy = p - pltpu.roll(p, width - 1, 1)
        dz = p - p_up
        cx = strength_x * (m + pltpu.roll(m, tall - 1, 0))
        cy = strength_y * (m + pltpu.roll(m, width - 1, 1))
        cz = strength_z * (m + m_up)
        cz_low = c_z[z]
        gx = strength_x * dx
        g_x[0, z], g_x[1, z] = gx[own], -pltpu.roll(gx, 1, 0)[own]
        g_y[z], g_z[z + 1] = (strength_y * dy)[own], (strength_z * dz)[own]
        c_x[z], c_y[z], c_z[z + 1] = cx, cy, cz
        fx, fy = cx * dx, cy * dy
        total_ref[z] = (
            total
            + (fx - pltpu.roll(fx, 1, 0))
            + (fy - pltpu.roll(fy, 1, 1))
            + (cz * dz + cz_low * (p - p_down))
        )
        diagonal_ref[z] = (
            volume
            + (cx + pltpu.roll(cx, 1, 0))
            + (cy + pltpu.roll(cy, 1, 1))
            + (cz + cz_low)
        )

    by_pairs(depth, update)

    def residual(z):
        down, up = jnp.maximum(z - 1, 0), jnp.minimum(z + 1, depth - 1)
        gx, gx_low, gy, gz, gz_low = g_x[0, z], g_x[1, z], g_y[z], g_z[z + 1], -g_z[z]
        gy_low = -pltpu.roll(gy, 1, 1)
        middle = (gx + gx_low) + (gy + gy_low) + (gz + gz_low)
        for i in range(COMPS):
            here = mob[i, z]
            tall_here = jnp.concatenate([here, rows_h[i, z]], axis=0)
            out_ref[i, z] = (
                acc[i, z]
                + middle * here
                + gx * pltpu.roll(tall_here, tall - 1, 0)[own]
                + gx_low * pltpu.roll(tall_here, 1, 0)[own]
                + gy * pltpu.roll(here, width - 1, 1)
                + gy_low * pltpu.roll(here, 1, 1)
                + gz * mob[i, up]
                + gz_low * mob[i, down]
            )

    by_pairs(depth, residual)


def finish(
    columns_two, columns_one, packet, press, total_in, diagonal_in, c_x, c_y, c_z, edge_mob, mob, near,
    res_ref, new_ref,
    side_h, edge_h, first, total_ref, inverse_ref, res_s, new_s, sems,
):
    depth, rows, width = press.shape
    layer, layers = lax.axis_index("layer"), lax.axis_size("layer")
    areal, areals = lax.axis_index("areal"), lax.axis_size("areal")
    tall = rows + ROWS
    lane = lane_of((tall, LANES))
    at_first, at_last = lane == 0, lane == LANES - 1
    low, high = slice(0, LANES), slice(width - LANES, width)
    FLUX, COUPLE, FACE, NEXT = range(4)
    mob = Rows(edge_mob, mob)

    def edges(which, z):
        both = pltpu.roll(edge_h[which], LANES - 1 - 4 * z, 1)
        return jnp.where(at_first, both, 0.0), jnp.where(at_last, both, 0.0)

    halo = side_fields(columns_one, columns_two)
    here = spread_fields([packet[:, t : t + LANES] for t in range(0, FIELDS * 32, LANES)])
    is_left = lane % 4 == 1
    for i in range(COMPS):
        cells = halo[i][:rows]
        side_h[i] = jnp.where(is_left[:rows], pltpu.roll(cells, LANES - 1, 1), pltpu.roll(cells, 1, 1))
    scale = 0.5 * TIME_STEP

    def turned(x, by):
        return pltpu.roll(x, by % LANES, 1)

    def outer(x):
        return jnp.where(is_left, turned(x, 1), turned(x, -1))

    def inner(x):
        return jnp.where(is_left, turned(x, -1), turned(x, 1))

    m, p = halo[MOB], halo[PRESS]
    strength = scale * halo[TY]
    own_strength = jnp.where(layer < layers - 1, scale, 0.0) * here[TY]
    c_out = jnp.where(is_left, turned(strength, 1), strength) * (m + outer(m))
    s_in = jnp.where(is_left, strength, turned(own_strength, 1))
    c_in = s_in * (m + inner(here[MOB]))
    d_in = p - inner(here[PRESS])
    end_x = (row_of(lane.shape) == rows - 1) & (areal == areals - 1)
    cx = jnp.where(end_x, 0.0, scale * halo[TX]) * (m + pltpu.roll(m, tall - 1, 0))
    cz = jnp.where(lane < 4 * (depth - 1), scale * halo[TZ], 0.0) * (m + turned(m, -4))
    fx = cx * (p - pltpu.roll(p, tall - 1, 0))
    fz = cz * (p - turned(p, -4))
    total = (
        halo[ACC]
        + (c_out * (p - outer(p)) + c_in * d_in)
        + (fx - pltpu.roll(fx, 1, 0))
        + (fz - turned(fz, 4))
    )
    diagonal = (
        COMPRESS * halo[PORE] + (c_out + c_in) + (cx + pltpu.roll(cx, 1, 0)) + (cz + turned(cz, 4))
    )
    usable = diagonal > 0.0
    beside = jnp.where(usable, -total * rcp(jnp.where(usable, diagonal, 1.0)), 0.0)
    for which, value in (
        (FLUX, -c_in * d_in), (COUPLE, c_in), (FACE, -s_in * d_in), (NEXT, c_in * beside)
    ):
        edge_h[which] = jnp.where(is_left, value, turned(value, -2))

    def leave(z):
        return pltpu.make_async_copy(res_s.at[:, z], res_ref.at[:, z], sems.at[0, z])

    def leave_new(z):
        return pltpu.make_async_copy(new_s.at[z], new_ref.at[z], sems.at[1, z])

    def update(z):
        faces = [face[:rows] for face in edges(FACE, z)]
        for i in range(COMPS):
            side = pltpu.roll(side_h[i], LANES - 2 - 4 * z, 1)
            cells = mob[i, z]
            for span, face in zip((low, high), faces):
                res_s[i, z, :, span] = near[i, z, :, span] + face * (cells[:, span] + side)
        leave(z).start()
        flux, couple = edges(FLUX, z), edges(COUPLE, z)
        for n, span in enumerate((low, high)):
            total = total_in[z, :, span] + flux[n]
            diagonal = diagonal_in[z, :, span] + couple[n]
            usable = diagonal > 0.0
            inverse = rcp(jnp.where(usable, diagonal, 1.0))
            first[z, :, span] = jnp.where(usable, -total * inverse, 0.0)
            total_ref[z, :, span] = total[:rows]
            inverse_ref[z, :, span] = inverse[:rows]

    by_pairs(depth, update)

    def second(z):
        here = first[z]
        up, down = jnp.minimum(z + 1, depth - 1), jnp.maximum(z - 1, 0)
        cx, cy = c_x[z], c_y[z, :rows]
        own = here[:rows]
        gathered = (
            (cx * pltpu.roll(here, tall - 1, 0))[:rows]
            + pltpu.roll(cx * here, 1, 0)[:rows]
            + cy * pltpu.roll(own, width - 1, 1)
            + pltpu.roll(cy * own, 1, 1)
            + (c_z[z + 1, :rows] * first[up, :rows] + c_z[z, :rows] * first[down, :rows])
            - total_ref[z]
        )
        beyond = edges(NEXT, z)
        for n, span in enumerate((low, high)):
            new_s[z, :, span] = press[z, :, span] + inverse_ref[z, :, span] * (
                gathered[:, span] + beyond[n][:rows]
            )
        leave_new(z).start()

    by_pairs(depth, second)

    def left(z):
        leave(z).wait()
        leave_new(z).wait()

    by_pairs(depth, left)


def on_device(
    pressure, composition, mass_old, pore_volume, trans_x, trans_y, trans_z,
    volatility, pressure_slope, mixing, two_phase,
):
    depth, rows, width = pressure.shape
    f32 = jnp.float32
    smem = pl.BlockSpec(memory_space=pltpu.SMEM)
    vmem = pl.BlockSpec(memory_space=pltpu.VMEM)
    def params(mib):
        return pltpu.CompilerParams(vmem_limit_bytes=mib * MIB)

    scalars = (two_phase, volatility, pressure_slope, mixing)

    def swapped(block, axis, first):
        count = lax.axis_size(axis)
        pairs = [(i, i + 1) for i in range(first, count - 1, 2)]
        return lax.ppermute(block, axis, pairs + [(j, i) for i, j in pairs])

    whole = jax.ShapeDtypeStruct((COMPS, depth, rows, width), f32)
    sums = jax.ShapeDtypeStruct((depth, rows, width), f32)
    packed = jax.ShapeDtypeStruct((len(UNITS) // 2, DEPTH_SLOTS * depth, width), f32)
    fields = (composition, pressure, pore_volume, mass_old, trans_x, trans_y, trans_z)

    def parts(count):
        planes = jax.ShapeDtypeStruct((COMPS, depth, count, width), f32)
        plane = jax.ShapeDtypeStruct((depth, count, width), f32)
        return [planes, planes, plane, plane]

    between = [jax.ShapeDtypeStruct((*x.shape[:-2], rows - 2 * ROWS, width), f32) for x in fields[:4]]
    *results, operand, comp, press, pore, mass = pl.pallas_call(
        edge_cells,
        in_specs=[pl.BlockSpec(memory_space=pl.ANY)] * (4 + len(fields)),
        out_specs=[vmem] * 11,
        out_shape=parts(2 * ROWS)
        + [packed, packed, jax.ShapeDtypeStruct((PART, DEEP), jnp.bfloat16), *between],
        scratch_shapes=[pltpu.SMEM(x.shape, x.dtype) for x in scalars]
        + [pltpu.VMEM((2, *x.shape[:-2], ROWS, width), f32) for x in fields]
        + [pltpu.SemaphoreType.DMA((3, len(fields))), pltpu.SemaphoreType.DMA((4,))],
        compiler_params=params(24),
        name="edge_cells",
    )(*(pltpu.with_memory_space_constraint(x, pltpu.HBM) for x in (*scalars, *fields)))
    *edge, one, two = results
    rows_two = swapped(two, "areal", 1)
    rows_one = swapped(one, "areal", 0)
    cells = rows * depth * width
    inner = pl.pallas_call(
        inner_cells,
        in_specs=[smem] * 3 + [vmem] * 5,
        out_specs=[vmem] * 4,
        out_shape=parts(rows - 2 * ROWS),
        compiler_params=params(24),
        cost_estimate=pl.CostEstimate(
            flops=450 * cells, transcendentals=95 * cells, bytes_accessed=2 * 39 * cells
        ),
        name="inner_cells",
    )(*scalars[:3], operand, comp, press, pore, mass)
    planes_of = (pressure, trans_x, trans_y, trans_z, pore_volume)

    narrow = jax.ShapeDtypeStruct((rows + ROWS, FIELDS * 16), f32)
    one, two, packet = pl.pallas_call(
        pack_columns,
        in_specs=[vmem] * 15,
        out_specs=[vmem] * 3,
        out_shape=[narrow, narrow, jax.ShapeDtypeStruct((rows + ROWS, FIELDS * 32), f32)],
        compiler_params=params(24),
        name="pack_columns",
    )(rows_two, rows_one, *planes_of, *edge, *inner)
    columns_two = swapped(two, "layer", 1)
    columns_one = swapped(one, "layer", 0)

    tall = jax.ShapeDtypeStruct((depth, rows + ROWS, width), f32)
    above_faces = jax.ShapeDtypeStruct((depth + 1, rows + ROWS, width), f32)
    near, *sweep = pl.pallas_call(
        near_residual,
        in_specs=[vmem] * 15,
        out_specs=[vmem] * 6,
        out_shape=[whole, tall, tall, tall, tall, above_faces],
        scratch_shapes=[
            pltpu.VMEM((COMPS, depth, ROWS, width), f32),
            pltpu.VMEM((FIELDS - COMPS, depth, ROWS, width), f32),
            pltpu.VMEM((2, depth, rows, width), f32),
            pltpu.VMEM((depth, rows, width), f32),
            pltpu.VMEM((depth + 1, rows, width), f32),
        ],
        compiler_params=params(24),
        cost_estimate=pl.CostEstimate(flops=150 * cells, transcendentals=0, bytes_accessed=4 * 31 * cells),
        name="near_residual",
    )(rows_two, rows_one, *planes_of, *edge, *inner)

    return pl.pallas_call(
        finish,
        in_specs=[vmem] * 12,
        out_specs=[pl.BlockSpec(memory_space=pl.ANY)] * 2,
        out_shape=[whole, sums],
        scratch_shapes=[
            pltpu.VMEM((COMPS, rows, LANES), f32),
            pltpu.VMEM((4, rows + ROWS, LANES), f32),
            pltpu.VMEM((depth, rows + ROWS, width), f32),
            pltpu.VMEM((depth, rows, width), f32),
            pltpu.VMEM((depth, rows, width), f32),
            pltpu.VMEM((COMPS, depth, rows, width), f32),
            pltpu.VMEM((depth, rows, width), f32),
            pltpu.SemaphoreType.DMA((2, depth)),
        ],
        compiler_params=params(24),
        name="finish",
    )(columns_two, columns_one, packet, pressure, *sweep, edge[0], inner[0], near)


def solution(mesh):
    placed = (
        P(None, "areal", "layer"),
        P(None, None, "areal", "layer"),
        P(None, None, "areal", "layer"),
        P(None, "areal", "layer"),
        P(None, "areal", "layer"),
        P(None, "areal", "layer"),
        P(None, "areal", "layer"),
        P(),
        P(),
        P(),
        P(None, "areal"),
    )
    return jax.shard_map(
        on_device,
        mesh=mesh,
        in_specs=placed,
        out_specs=(P(None, None, "areal", "layer"), P(None, "areal", "layer")),
        check_vma=False,
    )
```

```python
import jax
import jax.numpy as jnp
from jax import lax
from jax.experimental import pallas as pl
from jax.experimental.pallas import tpu as pltpu
from jax.sharding import PartitionSpec as P

SS_ITERS = 3
RR_ITERS = 3
LIGHT = 4
COMPS = 9
FIELDS = 16
MOB, PRESS, TX, TY, TZ, PORE, ACC = range(COMPS, FIELDS)
UNITS = ((0, 1), (2, 3), (4, 5), (6, 7), (8, MOB), (PRESS, TX), (TY, TZ), (PORE, ACC))
DEPTH_SLOTS = 4
TIME_STEP = 4.0
COMPRESS = 0.2
VAPOUR_WEIGHT = 1.0 / 0.25
LANES = 128
ROWS = 8
MIB = 1024 * 1024
PART = (COMPS + 1) * ROWS
DEEP = 256


def rcp(x):
    return pltpu.reciprocal(x, approx=True)


def total_of(terms):
    terms = list(terms)
    while len(terms) > 1:
        terms = [a + b for a, b in zip(terms[::2], terms[1::2])] + (
            [terms[-1]] if len(terms) % 2 else []
        )
    return terms[0]


def split(x):
    high = x.astype(jnp.bfloat16)
    return high, (x - high.astype(jnp.float32)).astype(jnp.bfloat16)


def mixing_operand(mix_ref):
    shape = (ROWS, DEEP)
    lane, row = lane_of(shape), row_of(shape)
    part = lax.div(lane, PART)
    within = lane - PART * part
    column = lax.div(within, ROWS)
    on = (within - ROWS * column == row) & (part < 3)
    blocks = []
    for i in range(COMPS):
        value = jnp.zeros(shape, jnp.float32)
        for j in range(COMPS):
            value = jnp.where(column == j, 2.0 * mix_ref[i, j], value)
        high, low = split(value)
        value = jnp.where(part == 2, low.astype(jnp.float32), high.astype(jnp.float32))
        blocks.append(jnp.where(on, value, 0.0))
    blocks.append(jnp.zeros(shape, jnp.float32))
    return jnp.concatenate(blocks, axis=0).astype(jnp.bfloat16)


def mixed(operand, spread):
    shape = spread[0].shape
    high, low = split(jnp.concatenate(spread + [jnp.zeros(shape, jnp.float32)], axis=0))
    tail = jnp.zeros((DEEP - 3 * PART, shape[1]), jnp.bfloat16)
    out = jnp.dot(
        operand,
        jnp.concatenate([high, low, high, tail], axis=0),
        preferred_element_type=jnp.float32,
    )
    return [out[ROWS * i : ROWS * (i + 1)] for i in range(COMPS)]


def flash(feed, pressure, signed, slope, operand):
    log_press = jnp.log(pressure)
    half_base = [0.5 * signed[i] - (0.5 * slope[i]) * log_press for i in range(COMPS)]
    spread = None
    for outer in range(SS_ITERS):
        if outer == 0:
            half_log = half_base
        else:
            mix = mixed(operand, spread)
            half_log = [half_base[i] - 0.5 * jnp.tanh(mix[i]) for i in range(COMPS)]
        t = [jnp.tanh(half_log[i]) for i in range(COMPS)]
        u = [rcp(t[i]) for i in range(COMPS)]
        psi = None
        for inner in range(RR_ITERS):
            q = t if inner == 0 else [rcp(u[i] + psi) for i in range(COMPS)]
            part = [feed[i] * q[i] for i in range(COMPS)]
            step = total_of(part) * rcp(total_of(part[i] * q[i] for i in range(COMPS)))
            psi = jnp.clip(step if inner == 0 else psi + step, -1.0, 1.0)
        spread = [feed[i] * rcp(u[i] + psi) for i in range(COMPS)]
    liquid_part = (0.25 * (1.0 - psi)) * (1.0 - psi)
    vapour_part = (0.25 * VAPOUR_WEIGHT * (1.0 + psi)) * (1.0 + psi)
    both, apart = vapour_part + liquid_part, vapour_part - liquid_part
    return [spread[i] * (both * u[i] + apart) for i in range(COMPS)]


def parameters(vol_ref, slope_ref):
    signed = [vol_ref[i] if i < LIGHT else -vol_ref[i] for i in range(COMPS)]
    return signed, [slope_ref[i] for i in range(COMPS)]


def lane_of(shape):
    return lax.broadcasted_iota(jnp.int32, shape, len(shape) - 1)


def row_of(shape):
    return lax.broadcasted_iota(jnp.int32, shape, len(shape) - 2)


class Rows:
    def __init__(self, edge, inner):
        self.edge, self.inner = edge, inner

    def __getitem__(self, at):
        at = at if isinstance(at, tuple) else (at,)
        edge = self.edge[at]
        return jnp.concatenate([edge[:ROWS], self.inner[at], edge[ROWS:]], axis=0)


def pack_rows(field, low, out_ref, depth):
    row = None
    for n in range(0, len(UNITS), 2):
        for pair in range(depth // 2):
            tile = None
            for z in (2 * pair, 2 * pair + 1):
                order = (1, 0) if low else (0, 1)
                for which in order:
                    unit = UNITS[n + which]
                    at = 4 * (z % 2) + (2 if low == (which == 0) else 0)
                    first = 0 if low else ROWS - 1
                    if isinstance(unit, tuple):
                        a, b = unit
                        pieces = [(at, a, at - first), (at + 1, b, at + 1 - first)]
                        if not low:
                            pieces = [(at, b, at - first), (at + 1, a, at + 1 - first)]
                    else:
                        pieces = [(at, unit, at if low else at + 2)]
                    for start, k, turn in pieces:
                        here = field(k, z)
                        if row is None:
                            row = row_of(here.shape)
                        if turn % ROWS:
                            here = pltpu.roll(here, turn % ROWS, 0)
                        tile = here if tile is None else jnp.where(row < start, tile, here)
            out_ref[n // 2, pl.ds(pair * ROWS, ROWS), :] = tile


def row_tiles(one, two, wanted, start=0, stop=None):
    shape = one.shape[1:]
    upper = row_of(shape) % DEPTH_SLOTS < 2
    tile_row = row_of((ROWS, shape[1]))
    stop = stop or shape[0] // DEPTH_SLOTS
    tiles = {}
    for n, unit in enumerate(UNITS):
        fields = unit if isinstance(unit, tuple) else (unit,)
        if not any(k in wanted for k in fields):
            continue
        up, down = by_side("areal", one[n // 2], two[n // 2])
        if n % 2:
            up, down = pltpu.roll(up, shape[0] - 2, 0), pltpu.roll(down, 2, 0)
        both = jnp.where(upper, up, down)
        for z in range(start, stop):
            at = (z // 2) * ROWS
            tile = pltpu.roll(both[at : at + ROWS], 6 - 4 * (z % 2), 0)
            if fields[0] in wanted:
                tiles.setdefault(fields[0], []).append(tile)
            if fields[-1] in wanted and fields[-1] != fields[0]:
                other = jnp.where(tile_row < 4, pltpu.roll(tile, ROWS - 1, 0), pltpu.roll(tile, 1, 0))
                tiles.setdefault(fields[-1], []).append(other)
    return tiles


def pack_columns(rows_two, rows_one, *refs):
    (
        press, tx, ty, tz, pore, edge_mob, _, edge_mob_sum, edge_acc_sum, mob, _, mob_sum, acc_sum,
        one_ref, two_ref, own_ref,
    ) = refs
    depth, rows, width = press.shape
    shape = (rows + ROWS, LANES)
    lane = lane_of(shape)
    mob, mob_sum, acc_sum = (
        Rows(*both) for both in ((edge_mob, mob), (edge_mob_sum, mob_sum), (edge_acc_sum, acc_sum))
    )
    corner_fields = {MOB: mob_sum, PRESS: press, TX: tx, TY: ty}
    others = {TZ: tz, PORE: pore, ACC: acc_sum, **corner_fields}
    corners = row_tiles(rows_one, rows_two, corner_fields)
    nothing = jnp.zeros((ROWS, LANES), jnp.float32)
    for tile in range(FIELDS // 4):
        packed = jnp.zeros(shape, jnp.float32)
        for quarter in range(4):
            k = 4 * tile + quarter
            for z in range(depth):
                plane = mob[k, z] if k < COMPS else others[k][z]
                first, last = plane[:, :LANES], plane[:, -LANES:]
                at = 32 * quarter + 4 * z
                both = jnp.where(lane_of(first.shape) < LANES // 2, first, last)
                if k < COMPS:
                    both = pltpu.roll(both, at + 2, 1)
                    on = (lane_of(first.shape) >= at + 1) & (lane_of(first.shape) < at + 3)
                    packed = jnp.concatenate([jnp.where(on, both, packed[:rows]), nothing], axis=0)
                    continue
                end = nothing
                if k in corner_fields:
                    end = corners[k][z]
                    end = jnp.where(lane_of(end[:, :LANES].shape) < LANES // 2, end[:, :LANES], end[:, -LANES:])
                both = pltpu.roll(jnp.concatenate([both, end], axis=0), (at + 2) % LANES, 1)
                packed = jnp.where((lane >= at) & (lane < at + 4), both, packed)
        own_ref[:, tile * LANES : (tile + 1) * LANES] = packed
    odd = lax.axis_index("layer") % 2 == 1
    half = FIELDS // 8
    for n in range(half):
        near, far = (own_ref[:, t * LANES : (t + 1) * LANES] for t in (n, n + half))
        upward = jnp.where(lane % 4 < 2, near, pltpu.roll(far, 2, 1))
        downward = jnp.where(lane % 4 < 2, pltpu.roll(near, LANES - 2, 1), far)
        one_ref[:, n * LANES : (n + 1) * LANES] = jnp.where(odd, downward, upward)
        two_ref[:, n * LANES : (n + 1) * LANES] = jnp.where(odd, upward, downward)


def spread_fields(tiles):
    fields = []
    for tile in tiles:
        for quarter in range(4):
            turn = (LANES - 32 * quarter) % LANES
            fields.append(pltpu.roll(tile, turn, 1) if turn else tile)
    return fields


def side_fields(one, two):
    lane = lane_of((one.shape[0], LANES))
    near, far = [], []
    for n in range(FIELDS // 8):
        span = slice(n * LANES, (n + 1) * LANES)
        left, right = by_side("layer", one[:, span], two[:, span])
        near.append(jnp.where(lane % 4 < 2, left, pltpu.roll(right, 2, 1)))
        far.append(jnp.where(lane % 4 < 2, pltpu.roll(left, LANES - 2, 1), right))
    return spread_fields(near + far)


def flash_rows(source, target, tile_row, flags, vol, slope, operand, comp, press, pore, mass, outs, ready=None):
    mob_ref, acc_ref, mob_sum, acc_sum = outs
    layer = lax.axis_index("layer")
    depth, _, width = press.shape

    def beside(ref, *lead):
        return jnp.concatenate([ref[(*lead, z, source)] for z in range(depth)], axis=1)

    def store(ref, value, *lead):
        for z in range(depth):
            ref[(*lead, z, target)] = value[:, z * width : (z + 1) * width]

    raw = [beside(comp, i) for i in range(COMPS)]
    inverse = rcp(total_of(raw))
    feed = [raw[i] * inverse for i in range(COMPS)]
    first, last = flags[layer, 2 * tile_row], flags[layer, 2 * tile_row + 1]

    @pl.when(first + last > 0)
    def _():
        signed, slopes = parameters(vol, slope)
        two = flash(feed, beside(press), signed, slopes, operand[...])
        marked = jnp.where(row_of(feed[0].shape) < ROWS // 2, first, last) > 0
        mobility = [jnp.where(marked, two[i], feed[i]) for i in range(COMPS)]
        for i in range(COMPS):
            store(mob_ref, mobility[i], i)
        store(mob_sum, total_of(mobility))

    @pl.when(first + last == 0)
    def _():
        for i in range(COMPS):
            store(mob_ref, feed[i], i)
        store(mob_sum, total_of(feed))

    if ready:
        ready()
    volume = beside(pore)
    acc = [volume * feed[i] - beside(mass, i) for i in range(COMPS)]
    for i in range(COMPS):
        store(acc_ref, acc[i], i)
    store(acc_sum, total_of(acc))


def edge_cells(
    flags_in, vol_in, slope_in, mix_in, comp, press, pore, mass, tx, ty, tz,
    mob_ref, acc_ref, mob_sum, acc_sum, one_ref, two_ref, operand, comp_i, press_i, pore_i, mass_i,
    flags, vol, slope, mix, comp_s, press_s, pore_s, mass_s, tx_s, ty_s, tz_s, sems, scalar_sems,
):
    depth, rows, _ = press.shape
    fetched = (
        (comp, comp_s), (press, press_s), (pore, pore_s), (mass, mass_s), (tx, tx_s), (ty, ty_s), (tz, tz_s)
    )

    ahead = (comp_i, press_i, pore_i, mass_i)

    def fetch(end, n):
        source, slot = fetched[n]
        at = pl.ds(end * (rows - ROWS), ROWS) if end < 2 else pl.ds(ROWS, rows - 2 * ROWS)
        return pltpu.make_async_copy(
            source.at[:, :, at, :] if len(source.shape) == 4 else source.at[:, at, :],
            slot.at[end] if end < 2 else ahead[n],
            sems.at[end, n],
        )

    scalars = [
        pltpu.make_async_copy(source, slot, scalar_sems.at[n])
        for n, (source, slot) in enumerate(
            ((flags_in, flags), (vol_in, vol), (slope_in, slope), (mix_in, mix))
        )
    ]
    early, late = (0, 1), range(2, len(fetched))
    for copy in scalars:
        copy.start()
    for n in early:
        fetch(0, n).start()
    for copy in scalars:
        copy.wait()
    operand[...] = mixing_operand(mix)
    odd = lax.axis_index("areal") % 2 == 1
    for end in range(2):
        for n in early:
            fetch(end, n).wait()
        if end == 0:
            for n in late:
                fetch(0, n).start()
            for n in range(len(fetched)):
                fetch(1, n).start()
        else:
            for n in range(len(ahead)):
                fetch(2, n).start()

        def ready():
            for n in late:
                fetch(end, n).wait()

        target = slice(end * ROWS, (end + 1) * ROWS)
        flash_rows(
            slice(None), target, end * (rows // ROWS - 1), flags, vol, slope, operand,
            *(slot.at[end] for _, slot in fetched[:4]), (mob_ref, acc_ref, mob_sum, acc_sum), ready,
        )

        def field(k, z):
            if k < COMPS:
                return mob_ref[k, z, target]
            if k == MOB:
                return mob_sum[z, target]
            if k in (PORE, ACC):
                m, p = mob_sum[z, target], press_s[end, z]
                behind = ROWS - 1 if end == 0 else 1
                strength = (0.5 * TIME_STEP) * tx_s[end, z]
                if end == 1:
                    strength = pltpu.roll(strength, 1, 0)
                couple = strength * (m + pltpu.roll(m, behind, 0))
                if k == PORE:
                    return COMPRESS * pore_s[end, z] + couple
                return acc_sum[z, target] + couple * (p - pltpu.roll(p, behind, 0))
            return {PRESS: press_s, TX: tx_s, TY: ty_s, TZ: tz_s}[k][end, z]

        for turn, ref in enumerate((one_ref, two_ref)):
            @pl.when(odd == (end == turn))
            def _():
                pack_rows(field, end == 0, ref, depth)

    for n in range(len(ahead)):
        fetch(2, n).wait()


def inner_cells(flags, vol, slope, operand, comp, press, pore, mass, *outs):
    def tile(t, carry):
        at = pl.ds(pl.multiple_of(t * ROWS, ROWS), ROWS)
        flash_rows(at, at, t + 1, flags, vol, slope, operand, comp, press, pore, mass, outs)
        return carry

    lax.fori_loop(0, press.shape[1] // ROWS, tile, 0)


def by_side(axis, one, two):
    odd = lax.axis_index(axis) % 2 == 1
    return jnp.where(odd, one, two), jnp.where(odd, two, one)


def by_turns(count, each, body):
    def turn(t, carry):
        for n in range(each):
            body(each * t + n)
        return carry

    lax.fori_loop(0, count // each, turn, 0)


def near_residual(
    rows_two, rows_one, press, tx, ty, tz, pore,
    edge_mob, edge_acc, edge_mob_sum, edge_acc_sum, mob, acc, mob_sum, acc_sum,
    out_ref, total_ref, diagonal_ref, c_x, c_y, c_z,
    rows_h, fields_h, g_x, g_y, g_z,
):
    depth, rows, width = press.shape
    areal, areals = lax.axis_index("areal"), lax.axis_size("areal")
    tall = rows + ROWS
    full = (tall, width)
    own = slice(0, rows)
    mob, acc, mob_sum, acc_sum = (
        Rows(*both)
        for both in ((edge_mob, mob), (edge_acc, acc), (edge_mob_sum, mob_sum), (edge_acc_sum, acc_sum))
    )
    fields = {MOB: mob_sum, PRESS: press, TX: tx, TY: ty, TZ: tz, PORE: pore, ACC: acc_sum}
    tiles = row_tiles(rows_one, rows_two, range(FIELDS))
    for z in range(depth):
        for i in range(COMPS):
            rows_h[i, z] = tiles[i][z]
        for n, k in enumerate(fields):
            tile = tiles[k][z]
            if k == TX:
                tile = jnp.where(row_of(tile.shape) == ROWS - 1, tile, 0.0)
            fields_h[n, z] = tile

    end_x = (row_of(full) == rows - 1) & (areal == areals - 1)
    end_y = lane_of(full) == width - 1
    scale = 0.5 * TIME_STEP
    c_z[0] = jnp.zeros(full, jnp.float32)
    g_z[0] = jnp.zeros((rows, width), jnp.float32)

    def update(z):
        m, p, x, y, zz, volume, total = (
            jnp.concatenate([COMPRESS * ref[z] if ref is pore else ref[z], fields_h[n, z]], axis=0)
            for n, ref in enumerate(fields.values())
        )
        up, down = jnp.minimum(z + 1, depth - 1), jnp.maximum(z - 1, 0)
        p_up = jnp.concatenate([press[up], fields_h[1, up]], axis=0)
        p_down = jnp.concatenate([press[down], fields_h[1, down]], axis=0)
        m_up = jnp.concatenate([mob_sum[up], fields_h[0, up]], axis=0)
        strength_x = jnp.where(end_x, 0.0, scale * x)
        strength_y = jnp.where(end_y, 0.0, scale * y)
        strength_z = jnp.where(z < depth - 1, scale, 0.0) * zz
        dx = p - pltpu.roll(p, tall - 1, 0)
        dy = p - pltpu.roll(p, width - 1, 1)
        dz = p - p_up
        cx = strength_x * (m + pltpu.roll(m, tall - 1, 0))
        cy = strength_y * (m + pltpu.roll(m, width - 1, 1))
        cz = strength_z * (m + m_up)
        cz_low = c_z[z]
        gx = strength_x * dx
        g_x[0, z], g_x[1, z] = gx[own], -pltpu.roll(gx, 1, 0)[own]
        g_y[z], g_z[z + 1] = (strength_y * dy)[own], (strength_z * dz)[own]
        c_x[z], c_y[z], c_z[z + 1] = cx, cy, cz
        fx, fy = cx * dx, cy * dy
        total_ref[z] = (
            total
            + (fx - pltpu.roll(fx, 1, 0))
            + (fy - pltpu.roll(fy, 1, 1))
            + (cz * dz + cz_low * (p - p_down))
        )
        diagonal_ref[z] = (
            volume
            + (cx + pltpu.roll(cx, 1, 0))
            + (cy + pltpu.roll(cy, 1, 1))
            + (cz + cz_low)
        )

    by_turns(depth, 4, update)

    def residual(z):
        down, up = jnp.maximum(z - 1, 0), jnp.minimum(z + 1, depth - 1)
        gx, gx_low, gy, gz, gz_low = g_x[0, z], g_x[1, z], g_y[z], g_z[z + 1], -g_z[z]
        gy_low = -pltpu.roll(gy, 1, 1)
        middle = (gx + gx_low) + (gy + gy_low) + (gz + gz_low)
        for i in range(COMPS):
            here = mob[i, z]
            tall_here = jnp.concatenate([here, rows_h[i, z]], axis=0)
            out_ref[i, z] = (
                acc[i, z]
                + middle * here
                + gx * pltpu.roll(tall_here, tall - 1, 0)[own]
                + gx_low * pltpu.roll(tall_here, 1, 0)[own]
                + gy * pltpu.roll(here, width - 1, 1)
                + gy_low * pltpu.roll(here, 1, 1)
                + gz * mob[i, up]
                + gz_low * mob[i, down]
            )

    by_turns(depth, 2, residual)


def finish(
    columns_one, columns_two, packet, press, total_in, diagonal_in, c_x, c_y, c_z, edge_mob, mob, near,
    res_ref, new_ref,
    side_h, edge_h, first, total_ref, inverse_ref, res_s, new_s, sems,
):
    depth, rows, width = press.shape
    layer, layers = lax.axis_index("layer"), lax.axis_size("layer")
    areal, areals = lax.axis_index("areal"), lax.axis_size("areal")
    tall = rows + ROWS
    lane = lane_of((tall, LANES))
    at_first, at_last = lane == 0, lane == LANES - 1
    low, high = slice(0, LANES), slice(width - LANES, width)
    FLUX, COUPLE, FACE, NEXT = range(4)
    mob = Rows(edge_mob, mob)

    def edges(which, z):
        both = pltpu.roll(edge_h[which], LANES - 1 - 4 * z, 1)
        return jnp.where(at_first, both, 0.0), jnp.where(at_last, both, 0.0)

    halo = side_fields(columns_one, columns_two)
    here = spread_fields([packet[:, t : t + LANES] for t in range(0, FIELDS * 32, LANES)])
    is_left = lane % 4 == 1
    for i in range(COMPS):
        cells = halo[i][:rows]
        side_h[i] = jnp.where(is_left[:rows], pltpu.roll(cells, LANES - 1, 1), pltpu.roll(cells, 1, 1))
    scale = 0.5 * TIME_STEP

    def turned(x, by):
        return pltpu.roll(x, by % LANES, 1)

    def outer(x):
        return jnp.where(is_left, turned(x, 1), turned(x, -1))

    def inner(x):
        return jnp.where(is_left, turned(x, -1), turned(x, 1))

    m, p = halo[MOB], halo[PRESS]
    strength = scale * halo[TY]
    own_strength = jnp.where(layer < layers - 1, scale, 0.0) * here[TY]
    c_out = jnp.where(is_left, turned(strength, 1), strength) * (m + outer(m))
    s_in = jnp.where(is_left, strength, turned(own_strength, 1))
    c_in = s_in * (m + inner(here[MOB]))
    d_in = p - inner(here[PRESS])
    end_x = (row_of(lane.shape) == rows - 1) & (areal == areals - 1)
    cx = jnp.where(end_x, 0.0, scale * halo[TX]) * (m + pltpu.roll(m, tall - 1, 0))
    cz = jnp.where(lane < 4 * (depth - 1), scale * halo[TZ], 0.0) * (m + turned(m, -4))
    fx = cx * (p - pltpu.roll(p, tall - 1, 0))
    fz = cz * (p - turned(p, -4))
    total = (
        halo[ACC]
        + (c_out * (p - outer(p)) + c_in * d_in)
        + (fx - pltpu.roll(fx, 1, 0))
        + (fz - turned(fz, 4))
    )
    diagonal = (
        COMPRESS * halo[PORE] + (c_out + c_in) + (cx + pltpu.roll(cx, 1, 0)) + (cz + turned(cz, 4))
    )
    usable = diagonal > 0.0
    beside = jnp.where(usable, -total * rcp(jnp.where(usable, diagonal, 1.0)), 0.0)
    for which, value in (
        (FLUX, -c_in * d_in), (COUPLE, c_in), (FACE, -s_in * d_in), (NEXT, c_in * beside)
    ):
        edge_h[which] = jnp.where(is_left, value, turned(value, -2))

    def leave(z):
        return pltpu.make_async_copy(res_s.at[:, z], res_ref.at[:, z], sems.at[0, z])

    def leave_new(z):
        return pltpu.make_async_copy(new_s.at[z], new_ref.at[z], sems.at[1, z])

    def update(z):
        faces = [face[:rows] for face in edges(FACE, z)]
        for i in range(COMPS):
            side = pltpu.roll(side_h[i], LANES - 2 - 4 * z, 1)
            cells = mob[i, z]
            for span, face in zip((low, high), faces):
                res_s[i, z, :, span] = near[i, z, :, span] + face * (cells[:, span] + side)
        leave(z).start()
        flux, couple = edges(FLUX, z), edges(COUPLE, z)
        for n, span in enumerate((low, high)):
            total = total_in[z, :, span] + flux[n]
            diagonal = diagonal_in[z, :, span] + couple[n]
            usable = diagonal > 0.0
            inverse = rcp(jnp.where(usable, diagonal, 1.0))
            first[z, :, span] = jnp.where(usable, -total * inverse, 0.0)
            total_ref[z, :, span] = total[:rows]
            inverse_ref[z, :, span] = inverse[:rows]

    by_turns(depth, 4, update)

    def second(z):
        here = first[z]
        up, down = jnp.minimum(z + 1, depth - 1), jnp.maximum(z - 1, 0)
        cx, cy = c_x[z], c_y[z, :rows]
        own = here[:rows]
        gathered = (
            (cx * pltpu.roll(here, tall - 1, 0))[:rows]
            + pltpu.roll(cx * here, 1, 0)[:rows]
            + cy * pltpu.roll(own, width - 1, 1)
            + pltpu.roll(cy * own, 1, 1)
            + (c_z[z + 1, :rows] * first[up, :rows] + c_z[z, :rows] * first[down, :rows])
            - total_ref[z]
        )
        beyond = edges(NEXT, z)
        for n, span in enumerate((low, high)):
            new_s[z, :, span] = press[z, :, span] + inverse_ref[z, :, span] * (
                gathered[:, span] + beyond[n][:rows]
            )
        leave_new(z).start()

    by_turns(depth, 4, second)

    def left(z):
        leave(z).wait()
        leave_new(z).wait()

    by_turns(depth, 8, left)


def on_device(
    pressure, composition, mass_old, pore_volume, trans_x, trans_y, trans_z,
    volatility, pressure_slope, mixing, two_phase,
):
    depth, rows, width = pressure.shape
    f32 = jnp.float32
    smem = pl.BlockSpec(memory_space=pltpu.SMEM)
    vmem = pl.BlockSpec(memory_space=pltpu.VMEM)
    def params(mib):
        return pltpu.CompilerParams(vmem_limit_bytes=mib * MIB)

    scalars = (two_phase, volatility, pressure_slope, mixing)

    def swapped(block, axis, first):
        count = lax.axis_size(axis)
        pairs = [(i, i + 1) for i in range(first, count - 1, 2)]
        return lax.ppermute(block, axis, pairs + [(j, i) for i, j in pairs])

    whole = jax.ShapeDtypeStruct((COMPS, depth, rows, width), f32)
    sums = jax.ShapeDtypeStruct((depth, rows, width), f32)
    packed = jax.ShapeDtypeStruct((len(UNITS) // 2, DEPTH_SLOTS * depth, width), f32)
    fields = (composition, pressure, pore_volume, mass_old, trans_x, trans_y, trans_z)

    def parts(count):
        planes = jax.ShapeDtypeStruct((COMPS, depth, count, width), f32)
        plane = jax.ShapeDtypeStruct((depth, count, width), f32)
        return [planes, planes, plane, plane]

    between = [jax.ShapeDtypeStruct((*x.shape[:-2], rows - 2 * ROWS, width), f32) for x in fields[:4]]
    *results, operand, comp, press, pore, mass = pl.pallas_call(
        edge_cells,
        in_specs=[pl.BlockSpec(memory_space=pl.ANY)] * (4 + len(fields)),
        out_specs=[vmem] * 11,
        out_shape=parts(2 * ROWS)
        + [packed, packed, jax.ShapeDtypeStruct((PART, DEEP), jnp.bfloat16), *between],
        scratch_shapes=[pltpu.SMEM(x.shape, x.dtype) for x in scalars]
        + [pltpu.VMEM((2, *x.shape[:-2], ROWS, width), f32) for x in fields]
        + [pltpu.SemaphoreType.DMA((3, len(fields))), pltpu.SemaphoreType.DMA((4,))],
        compiler_params=params(24),
        name="edge_cells",
    )(*(pltpu.with_memory_space_constraint(x, pltpu.HBM) for x in (*scalars, *fields)))
    *edge, one, two = results
    rows_two = swapped(two, "areal", 1)
    rows_one = swapped(one, "areal", 0)
    cells = rows * depth * width
    inner = pl.pallas_call(
        inner_cells,
        in_specs=[smem] * 3 + [vmem] * 5,
        out_specs=[vmem] * 4,
        out_shape=parts(rows - 2 * ROWS),
        compiler_params=params(24),
        cost_estimate=pl.CostEstimate(
            flops=450 * cells, transcendentals=95 * cells, bytes_accessed=2 * 39 * cells
        ),
        name="inner_cells",
    )(*scalars[:3], operand, comp, press, pore, mass)
    planes_of = (pressure, trans_x, trans_y, trans_z, pore_volume)

    narrow = jax.ShapeDtypeStruct((rows + ROWS, FIELDS * 16), f32)
    one, two, packet = pl.pallas_call(
        pack_columns,
        in_specs=[vmem] * 15,
        out_specs=[vmem] * 3,
        out_shape=[narrow, narrow, jax.ShapeDtypeStruct((rows + ROWS, FIELDS * 32), f32)],
        compiler_params=params(24),
        name="pack_columns",
    )(rows_two, rows_one, *planes_of, *edge, *inner)
    columns_one = swapped(one, "layer", 0)
    columns_two = swapped(two, "layer", 1)

    tall = jax.ShapeDtypeStruct((depth, rows + ROWS, width), f32)
    above_faces = jax.ShapeDtypeStruct((depth + 1, rows + ROWS, width), f32)
    near, *sweep = pl.pallas_call(
        near_residual,
        in_specs=[vmem] * 15,
        out_specs=[vmem] * 6,
        out_shape=[whole, tall, tall, tall, tall, above_faces],
        scratch_shapes=[
            pltpu.VMEM((COMPS, depth, ROWS, width), f32),
            pltpu.VMEM((FIELDS - COMPS, depth, ROWS, width), f32),
            pltpu.VMEM((2, depth, rows, width), f32),
            pltpu.VMEM((depth, rows, width), f32),
            pltpu.VMEM((depth + 1, rows, width), f32),
        ],
        compiler_params=params(24),
        cost_estimate=pl.CostEstimate(flops=150 * cells, transcendentals=0, bytes_accessed=4 * 31 * cells),
        name="near_residual",
    )(rows_two, rows_one, *planes_of, *edge, *inner)

    return pl.pallas_call(
        finish,
        in_specs=[vmem] * 12,
        out_specs=[pl.BlockSpec(memory_space=pl.ANY)] * 2,
        out_shape=[whole, sums],
        scratch_shapes=[
            pltpu.VMEM((COMPS, rows, LANES), f32),
            pltpu.VMEM((4, rows + ROWS, LANES), f32),
            pltpu.VMEM((depth, rows + ROWS, width), f32),
            pltpu.VMEM((depth, rows, width), f32),
            pltpu.VMEM((depth, rows, width), f32),
            pltpu.VMEM((COMPS, depth, rows, width), f32),
            pltpu.VMEM((depth, rows, width), f32),
            pltpu.SemaphoreType.DMA((2, depth)),
        ],
        compiler_params=params(24),
        name="finish",
    )(columns_one, columns_two, packet, pressure, *sweep, edge[0], inner[0], near)


def solution(mesh):
    placed = (
        P(None, "areal", "layer"),
        P(None, None, "areal", "layer"),
        P(None, None, "areal", "layer"),
        P(None, "areal", "layer"),
        P(None, "areal", "layer"),
        P(None, "areal", "layer"),
        P(None, "areal", "layer"),
        P(),
        P(),
        P(),
        P(None, "areal"),
    )
    return jax.shard_map(
        on_device,
        mesh=mesh,
        in_specs=placed,
        out_specs=(P(None, None, "areal", "layer"), P(None, "areal", "layer")),
        check_vma=False,
    )
```
